32 devices in a mesh: rows: 8 (over z, y), tp: 4 (over x, core).
Axes of the slice: x: 2, y: 2, z: 4, core: 2. Of those that a mesh axis runs over, the one named last changes fastest.
Arguments:
- frames: bfloat16 [8192, 768], P(('rows', 'tp')), may hold values from -6 to 6
- seg_starts: int32 [8, 6], P('rows'), may hold values from 0 to 1023, as said below
- conv_weight: bfloat16 [128, 48, 768], P(None, None, 'tp'), may hold values from -0.078125 to 0.078125
- conv_bias: bfloat16 [768], P('tp'), may hold values from -3 to 3
- norm_gain0: bfloat16 [768], replicated, may hold values from 0.099609375 to 1.8984375
- norm_bias0: bfloat16 [768], replicated, may hold values from -1.75 to 1.75
- qkv_weight: bfloat16 [768, 3, 768], P(None, None, 'tp'), may hold values from -0.21875 to 0.21875
- qv_bias: bfloat16 [2, 768], P(None, 'tp'), may hold values from -3 to 3
- out_weight: bfloat16 [768, 768], P('tp'), may hold values from -0.875 to 0.875
- out_bias: bfloat16 [768], replicated, may hold values from -1.75 to 1.75
- norm_gain1: bfloat16 [768], replicated, may hold values from 0.099609375 to 1.8984375
- norm_bias1: bfloat16 [768], replicated, may hold values from -1.75 to 1.75
- up_weight: bfloat16 [768, 3072], P(None, 'tp'), may hold values from -0.21875 to 0.21875
- up_bias: bfloat16 [3072], P('tp'), may hold values from -3 to 3
- down_weight: bfloat16 [3072, 768], P('tp'), may hold values from -0.109375 to 0.109375
- down_bias: bfloat16 [768], replicated, may hold values from -1.75 to 1.75
- norm_gain2: bfloat16 [768], replicated, may hold values from 0.099609375 to 1.8984375
- norm_bias2: bfloat16 [768], replicated, may hold values from -1.75 to 1.75
- cotangent: bfloat16 [8192, 768], P(('rows', 'tp')), may hold values from -6 to 6
Outputs:
- block_out: bfloat16 [8192, 768], P(('rows', 'tp'))
- frames_grad: float32 [8192, 768], P(('rows', 'tp'))
- conv_weight_grad: float32 [128, 48, 768], P(None, None, 'tp')
- conv_bias_grad: float32 [768], P('tp')
- norm_gain0_grad: float32 [768], replicated
- norm_bias0_grad: float32 [768], replicated
- qkv_weight_grad: float32 [768, 3, 768], P(None, None, 'tp')
- qv_bias_grad: float32 [2, 768], P(None, 'tp')
- out_weight_grad: float32 [768, 768], P('tp')
- out_bias_grad: float32 [768], replicated
- norm_gain1_grad: float32 [768], replicated
- norm_bias1_grad: float32 [768], replicated
- up_weight_grad: float32 [768, 3072], P(None, 'tp')
- up_bias_grad: float32 [3072], P('tp')
- down_weight_grad: float32 [3072, 768], P('tp')
- down_bias_grad: float32 [768], replicated
- norm_gain2_grad: float32 [768], replicated
- norm_bias2_grad: float32 [768], replicated
The draws below stay inside these ranges and needn't reach their ends.
Inputs may be any that keep to these rules, and one draw needn't show every extreme that they name: Each row of seg_starts begins with 0 and rises strictly; utterance j of a packed row covers frames seg_starts[r, j] up to the next start or 1024.
All inputs are finite; a program needn't handle non-finite values.
Results may differ from the reference program's by a relative error of at most 0.02.
Values may be sent and summed in bfloat16 or wider, within the bound.
No kernel may reach another device: no remote copies, remote signals or barrier semaphores. Data moves between devices by JAX's collectives and lax.ppermute only.
A program may use at most 192 MiB of HBM per device.

```python
import jax
import jax.numpy as jnp
from jax import lax

D = 768
H = 12
HD = 64
FF = 3072
KER = 128
GROUPS = 16
LEN = 1024
SEG = 6
PIECE = 256
PACKROWS = 8
TOKENS = 8192


def starts_row(row_key):
    key_list = jax.random.split(row_key, 5)
    extra_cuts = SEG - 3
    quarter_piece = PIECE // 4
    low_cut = jax.random.randint(key_list[0], (), quarter_piece, PIECE, dtype=jnp.int32)
    high_cut = jax.random.randint(key_list[1], (), LEN - PIECE + 1, LEN - quarter_piece + 1, dtype=jnp.int32)
    step_index = jnp.arange(extra_cuts, dtype=jnp.int32)
    before_cuts = jnp.sort(jax.random.randint(key_list[2], (extra_cuts,), 0, low_cut - extra_cuts, dtype=jnp.int32)) + step_index + 1
    after_cuts = jnp.sort(jax.random.randint(key_list[3], (extra_cuts,), 0, LEN - high_cut - extra_cuts, dtype=jnp.int32)) + step_index + high_cut + 1
    before_count = jax.random.randint(key_list[4], (), 0, extra_cuts + 1, dtype=jnp.int32)
    before_cuts = jnp.where(step_index < before_count, before_cuts, LEN)
    after_cuts = jnp.where(step_index < extra_cuts - before_count, after_cuts, LEN)
    all_cuts = jnp.concatenate([jnp.zeros((1,), jnp.int32), jnp.stack([low_cut, high_cut]), before_cuts, after_cuts])
    return jnp.sort(all_cuts)[:SEG]


def draw_seg_starts(key, part):
    key = jax.random.fold_in(key, 7)
    return jax.vmap(starts_row)(jax.random.split(key, PACKROWS))


def levels(stream_key, shape, pieces, least, high):
    def one(dim, shards_of):
        steps = jax.random.uniform(jax.random.fold_in(jax.random.fold_in(stream_key, 6), dim), (shards_of,), jnp.float32, least / len(pieces), high / len(pieces))
        return jnp.repeat(jnp.exp(steps), shape[dim] // shards_of).reshape((-1,) + (1,) * (len(shape) - dim - 1))

    gain = one(*pieces[0])
    for cut in pieces[1:]:
        gain = gain * one(*cut)
    return gain


def noise(key, shape, deviation, most, pieces=(), kind=jnp.bfloat16):
    values = jax.random.normal(key, shape, jnp.float32) * deviation
    if len(pieces) > 0:
        values = levels(key, shape, pieces, -0.22, 0.18) * values
    return jnp.clip(values, min=-most, max=most).astype(kind)


def setup_inputs(seed: int = 0) -> dict:
    splits = jax.random.split(jax.random.key(seed), 20)
    frames = noise(splits[0], (TOKENS, D), 1.0, 6.0, ((0, 32),))
    seg_starts = draw_seg_starts(jax.random.fold_in(splits[19], 71), 0)
    conv_weight = noise(splits[2], (KER, D // GROUPS, D), (KER * D // GROUPS) ** -0.5, 0.078125, ((2, 4),))
    conv_bias = noise(splits[3], (D,), 0.5, 3.0, ((0, 4),))
    norm_gain0 = jnp.clip(1.0 + 0.18 * jax.random.normal(splits[4], (D,), jnp.float32), 0.099609375, 1.8984375).astype(jnp.bfloat16)
    norm_bias0 = noise(splits[5], (D,), 0.3, 1.75)
    qkv_weight = noise(splits[6], (D, 3, D), D ** -0.5, 0.21875, ((2, 4),))
    qv_bias = noise(splits[7], (2, D), 0.5, 3.0, ((1, 4),))
    out_weight = noise(splits[8], (D, D), (D // 16) ** -0.5, 0.875, ((0, 4),))
    out_bias = noise(splits[9], (D,), 0.3, 1.75)
    norm_gain1 = jnp.clip(1.0 + 0.18 * jax.random.normal(splits[10], (D,), jnp.float32), 0.099609375, 1.8984375).astype(jnp.bfloat16)
    norm_bias1 = noise(splits[11], (D,), 0.3, 1.75)
    up_weight = noise(splits[12], (D, FF), D ** -0.5, 0.21875, ((1, 4),))
    up_bias = noise(splits[13], (FF,), 0.5, 3.0, ((0, 4),))
    down_weight = noise(splits[14], (FF, D), FF ** -0.5, 0.109375, ((0, 4),))
    down_bias = noise(splits[15], (D,), 0.3, 1.75)
    norm_gain2 = jnp.clip(1.0 + 0.18 * jax.random.normal(splits[16], (D,), jnp.float32), 0.099609375, 1.8984375).astype(jnp.bfloat16)
    norm_bias2 = noise(splits[17], (D,), 0.3, 1.75)
    cotangent = noise(splits[18], (TOKENS, D), 1.0, 6.0, ((0, 32),))
    return dict(frames=frames, seg_starts=seg_starts, conv_weight=conv_weight, conv_bias=conv_bias, norm_gain0=norm_gain0, norm_bias0=norm_bias0, qkv_weight=qkv_weight, qv_bias=qv_bias, out_weight=out_weight, out_bias=out_bias, norm_gain1=norm_gain1, norm_bias1=norm_bias1, up_weight=up_weight, up_bias=up_bias, down_weight=down_weight, down_bias=down_bias, norm_gain2=norm_gain2, norm_bias2=norm_bias2, cotangent=cotangent)


HIGHEST = lax.Precision.HIGHEST
EPSILON = 1e-05
MASKED = -1000000000.0

@jax.custom_vjp
def low(v):
    return lax.optimization_barrier(v.astype(jnp.bfloat16)).astype(jnp.float32)

@jax.custom_vjp
def low_back(v):
    return v

def low_keep(v):
    return (low(v), None)

def low_pass(kept, grad):
    return (grad,)

def back_keep(v):
    return (v, None)

def back_low(kept, grad):
    return (low(grad),)
low.defvjp(low_keep, low_pass)
low_back.defvjp(back_keep, back_low)

def product(matrix_a, matrix_b):
    return jnp.dot(matrix_a, matrix_b, precision=HIGHEST, preferred_element_type=jnp.float32)

def layer_norm(inputs, norm_gain, norm_bias):
    centered = inputs - lax.optimization_barrier(jnp.mean(inputs, axis=-1, keepdims=True))
    inv_std = lax.rsqrt(lax.optimization_barrier(jnp.mean(centered * centered, axis=-1, keepdims=True)) + EPSILON)
    return centered * inv_std * norm_gain + norm_bias

def windows(window):
    tap_count = window.shape[0] // 2
    repeated = jnp.tile(window, (tap_count + 1,) + (1,) * (window.ndim - 1))
    trimmed = repeated[:tap_count * (2 * tap_count + 1)]
    return trimmed.reshape((tap_count, 2 * tap_count + 1) + window.shape[1:])[:, :tap_count]

def conv_row(signal, segment, conv_weight):
    half_ker = KER // 2
    group_width = D // GROUPS
    padded = jnp.pad(signal, ((half_ker, half_ker), (0, 0)))
    seg_padded = jnp.pad(segment, (half_ker, half_ker), constant_values=-1)
    kernel = conv_weight.reshape(KER, group_width, GROUPS, group_width)

    def one_block(block_index):
        row_start = block_index * KER
        window = lax.dynamic_slice_in_dim(padded, row_start, 2 * KER, 0)
        seg_window = lax.dynamic_slice_in_dim(seg_padded, row_start, 2 * KER, 0)
        seg_out = lax.dynamic_slice_in_dim(segment, row_start, KER, 0)
        same_seg = windows(seg_window[:, None])[:, :, 0] == seg_out[:, None]
        patches = jnp.where(same_seg[:, :, None], windows(window), 0.0)
        patches = patches.reshape(KER, KER, GROUPS, group_width)
        return jnp.einsum('tkgc,kcgo->tgo', patches, kernel, precision=HIGHEST).reshape(KER, D)
    blocks = lax.map(jax.checkpoint(one_block), jnp.arange(LEN // KER, dtype=jnp.int32))
    return blocks.reshape(LEN, D)

def attend_row(queries, key_vals, value_vals, segment):
    q_block = min(LEN, 512)

    def one_block(block_index):
        row_start = block_index * q_block
        query_block = lax.dynamic_slice_in_dim(queries, row_start, q_block, 0)
        seg_block = lax.dynamic_slice_in_dim(segment, row_start, q_block, 0)
        scores = jnp.einsum('qhd,khd->hqk', query_block, key_vals, precision=HIGHEST)
        same_seg = seg_block[:, None] == segment[None, :]
        scores = low_back(jnp.where(same_seg[None], scores, MASKED))
        attn_probs = jax.nn.softmax(scores, axis=-1)
        mixed_heads = jnp.einsum('hqk,khd->qhd', low(attn_probs), value_vals, precision=HIGHEST)
        return mixed_heads.reshape(q_block, D)
    blocks = lax.map(jax.checkpoint(one_block), jnp.arange(LEN // q_block, dtype=jnp.int32))
    return blocks.reshape(LEN, D)

def layer_row(frames_row, starts, weights):
    conv_weight, conv_bias, norm_gain0, norm_bias0, qkv_weight, qv_bias, out_weight, out_bias, norm_gain1, norm_bias1, up_weight, up_bias, down_weight, down_bias, norm_gain2, norm_bias2 = weights
    positions = jnp.arange(LEN, dtype=jnp.int32)
    segment = lax.optimization_barrier(jnp.sum((positions[:, None] >= starts[None, :]).astype(jnp.int32), axis=1, dtype=jnp.int32)) - 1
    conv_pre = low_back(conv_row(frames_row, segment, conv_weight)) + conv_bias
    mixed_low = low_back(low(jax.nn.gelu(conv_pre, approximate=False)))
    normed0 = layer_norm(frames_row + mixed_low, norm_gain0, norm_bias0)
    normed0_low = low(normed0)
    projected = low_back(product(normed0_low, qkv_weight.reshape(D, 3 * D))).reshape(LEN, 3, D)
    queries = low((projected[:, 0] + qv_bias[0]) * HD ** (-0.5))
    key_vals = low(projected[:, 1])
    value_vals = low(projected[:, 2] + qv_bias[1])
    attended = attend_row(queries.reshape(LEN, H, HD), key_vals.reshape(LEN, H, HD), value_vals.reshape(LEN, H, HD), segment)
    attended = low_back(low(attended))
    normed1 = layer_norm(normed0 + low_back(product(attended, out_weight)) + out_bias, norm_gain1, norm_bias1)
    normed1_low = low(normed1)
    up_pre = low_back(product(normed1_low, up_weight)) + up_bias
    activated = low_back(low(jax.nn.gelu(up_pre, approximate=False)))
    return layer_norm(normed1 + low_back(product(activated, down_weight)) + down_bias, norm_gain2, norm_bias2)

def reference(frames, seg_starts, conv_weight, conv_bias, norm_gain0, norm_bias0, qkv_weight, qv_bias, out_weight, out_bias, norm_gain1, norm_bias1, up_weight, up_bias, down_weight, down_bias, norm_gain2, norm_bias2, cotangent):
    inputs = tuple((argument.astype(jnp.float32) for argument in (frames, conv_weight, conv_bias, norm_gain0, norm_bias0, qkv_weight, qv_bias, out_weight, out_bias, norm_gain1, norm_bias1, up_weight, up_bias, down_weight, down_bias, norm_gain2, norm_bias2)))

    def forward(frames_in, *weights):

        def one_row(row_pair):
            return layer_row(row_pair[0], row_pair[1], weights)
        rows_out = lax.map(jax.checkpoint(one_row), (frames_in.reshape(PACKROWS, LEN, D), seg_starts))
        return rows_out.reshape(TOKENS, D)
    block_out, pull_back = jax.vjp(forward, *inputs)
    gradients = pull_back(cotangent.astype(jnp.float32))
    return (block_out.astype(jnp.bfloat16), gradients[0], gradients[1], gradients[2], gradients[3], gradients[4], gradients[5], gradients[6], gradients[7], gradients[8], gradients[9], gradients[10], gradients[11], gradients[12], gradients[13], gradients[14], gradients[15], gradients[16])
```

```python
import jax
import jax.numpy as jnp
from jax import lax
from jax.experimental import pallas as pl
from jax.experimental.pallas import tpu as pltpu
from jax.sharding import PartitionSpec as P

D = 768
HD = 64
KER = 128
GROUPS = 16
LEN = 1024

EPSILON = 1e-05
MASKED = -1000000000.0
ROOT_HALF = 0.7071067811865476
INV_ROOT_TAU = 0.3989422804014327


def gelu_slope(inputs):
    return 0.5 * (1.0 + lax.erf(inputs * ROOT_HALF)) + inputs * INV_ROOT_TAU * jnp.exp(
        -0.5 * inputs * inputs
    )


def norm_forward(inputs, norm_gain, norm_bias):
    centered = inputs - jnp.mean(inputs, axis=-1, keepdims=True)
    inv_std = lax.rsqrt(jnp.mean(centered * centered, axis=-1, keepdims=True) + EPSILON)
    normed = centered * inv_std
    return (normed * norm_gain + norm_bias, normed, inv_std)


def norm_backward(grad_out, normed, inv_std, norm_gain):
    scaled = grad_out * norm_gain
    grad_in = inv_std * (
        scaled
        - jnp.mean(scaled, axis=-1, keepdims=True)
        - normed * jnp.mean(scaled * normed, axis=-1, keepdims=True)
    )
    return (grad_in, jnp.sum(grad_out * normed, axis=0), jnp.sum(grad_out, axis=0))


GW = 48
PH = 5
QN, PN = 17, 16
CORE = QN * PN
NJ = 27
LEAD = 13
EXT = (QN + NJ - 1) * PN
LANES = 256
GAP = KER // 2
SLOTS = PH * CORE
BF = jnp.bfloat16
F32 = jnp.float32

def iota(shape, dim):
    return lax.broadcasted_iota(jnp.int32, shape, dim)

def spread_slots(segments):
    place = jnp.arange(LEN, dtype=jnp.int32) + GAP * segments
    block = place // PH
    return place % PH * CORE + block % QN * PN + block // QN

def extension():
    row, col = iota((EXT, CORE), 0), iota((EXT, CORE), 1)
    want = QN * (row % PN) + row // PN - LEAD
    have = QN * (col % PN) + col // PN
    return (want == have).astype(BF)

def lane_map(group, rows, offset):
    row, lane = iota((rows, LANES), 0), iota((rows, LANES), 1)
    return (row == GW * group + lane % GW) & (lane < PH * GW)

def wprep_kernel(w_ref, out_ref, wide_ref):
    g = pl.program_id(0)
    before = PH * GW
    after = wide_ref.shape[0] - before - KER * GW
    wide_ref[0:before, :] = jnp.zeros((before, LANES), BF)
    wide_ref[before + KER * GW :, :] = jnp.zeros((after, LANES), BF)
    spread = lane_map(g, 4 * GW, 0).astype(BF)
    chunk = 768

    def widen(step, carry):
        start = pl.multiple_of(step * chunk, chunk)
        part = jnp.dot(w_ref[pl.ds(start, chunk), :], spread, preferred_element_type=F32)
        wide_ref[pl.ds(pl.multiple_of(start + before, 16), chunk), :] = part.astype(BF)
        return carry

    lax.fori_loop(0, KER * GW // chunk, widen, 0)
    lane = iota((1, LANES), 1)
    masks = [(lane // GW == i).astype(F32).astype(BF) for i in range(PH)]

    def place(j, carry):
        total = None
        for i in range(PH):
            start = pl.multiple_of(before + PH * GW * j - GW * (1 + i), 16)
            part = wide_ref[pl.ds(start, PH * GW), :] * masks[i]
            total = part if total is None else total + part
        out_ref[0, pl.ds(pl.multiple_of(j * LANES, LANES), PH * GW), :] = total
        out_ref[0, pl.ds(pl.multiple_of(j * LANES + PH * GW, 16), LANES - PH * GW), :] = jnp.zeros(
            (LANES - PH * GW, LANES), BF
        )
        return carry

    lax.fori_loop(0, NJ, place, 0)

def wprep(kernel_flat, groups, **kw):
    return pl.pallas_call(
        wprep_kernel,
        grid=(groups,),
        in_specs=[pl.BlockSpec((KER * GW, groups * GW), lambda g: (0, 0))],
        out_specs=pl.BlockSpec((1, NJ * LANES, LANES), lambda g: (g, 0, 0)),
        out_shape=jax.ShapeDtypeStruct((groups, NJ * LANES, LANES), BF),
        scratch_shapes=[pltpu.VMEM((PH * GW + KER * GW + 288, LANES), BF)],
        compiler_params=pltpu.CompilerParams(vmem_limit_bytes=40 * 2**20),
    )(kernel_flat)

def phi_pair(v):
    cdf = 0.5 * (1.0 + lax.erf(v * ROOT_HALF))
    return v * cdf, cdf + v * INV_ROOT_TAU * jnp.exp(-0.5 * v * v)

def unfold_lanes(values, group, i, groups):
    row, col = iota((LANES, groups * GW), 0), iota((LANES, groups * GW), 1)
    pick = ((row // GW == i) & (col == GW * group + row % GW)).astype(F32).astype(BF)
    return jnp.dot(values, pick, preferred_element_type=F32).astype(BF)

def conv_fwd_kernel(sig_ref, put_ref, take_ref, ext_ref, wt_ref, bias_ref,
                    mixed_ref, slope_ref, core_ref, slots_ref, wide_ref, back_ref):
    g = pl.program_id(0)
    groups = pl.num_programs(0)
    width = sig_ref.shape[1]

    @pl.when(g == 0)
    def _():
        slots_ref[...] = jnp.dot(put_ref[...], sig_ref[...], preferred_element_type=F32).astype(BF)
        back_ref[...] = jnp.zeros_like(back_ref)

    core = jnp.zeros((CORE, LANES), F32)
    row, lane = iota((width, LANES), 0), iota((width, LANES), 1)
    for i in range(PH):
        pick = ((lane // GW == i) & (row == GW * g + lane % GW)).astype(F32).astype(BF)
        core = core + jnp.dot(slots_ref[i * CORE:(i + 1) * CORE, :], pick, preferred_element_type=F32)
    core = core.astype(BF)
    core_ref[0] = core
    wide_ref[...] = jnp.dot(ext_ref[...], core, preferred_element_type=F32).astype(BF)
    total = jnp.zeros((CORE, LANES), F32)
    for j in range(NJ):
        total = total + jnp.dot(wide_ref[PN * j:PN * j + CORE, :], wt_ref[0, j * LANES:(j + 1) * LANES, :],
                                preferred_element_type=F32)
    value, slope = phi_pair(total + bias_ref[0])
    slope_ref[0] = slope
    value = value.astype(BF)
    for i in range(PH):
        rows = slice(i * CORE, (i + 1) * CORE)
        back_ref[rows, :] = back_ref[rows, :] + unfold_lanes(value, g, i, width // GW)

    @pl.when(g == groups - 1)
    def _():
        mixed_ref[...] = jnp.dot(take_ref[...], back_ref[...], preferred_element_type=F32).astype(BF)

def conv_fwd(signal, put, take, ext, wt, bias_lanes):
    groups = wt.shape[0]
    width = signal.shape[1]
    whole = lambda shape: pl.BlockSpec(shape, lambda g: (0,) * len(shape))
    return pl.pallas_call(
        conv_fwd_kernel,
        grid=(groups,),
        in_specs=[whole((LEN, width)), whole((SLOTS, LEN)), whole((LEN, SLOTS)), whole((EXT, CORE)),
                  pl.BlockSpec((1, NJ * LANES, LANES), lambda g: (g, 0, 0)),
                  pl.BlockSpec((1, 1, LANES), lambda g: (g, 0, 0))],
        out_specs=[whole((LEN, width)), pl.BlockSpec((1, CORE, LANES), lambda g: (g, 0, 0)),
                   pl.BlockSpec((1, CORE, LANES), lambda g: (g, 0, 0))],
        out_shape=[jax.ShapeDtypeStruct((LEN, width), BF), jax.ShapeDtypeStruct((groups, CORE, LANES), F32),
                   jax.ShapeDtypeStruct((groups, CORE, LANES), BF)],
        scratch_shapes=[pltpu.VMEM((SLOTS, width), BF), pltpu.VMEM((EXT, LANES), BF), pltpu.VMEM((SLOTS, width), BF)],
        compiler_params=pltpu.CompilerParams(vmem_limit_bytes=48 * 2**20),
    )(signal, put, take, ext, wt, bias_lanes)

def conv_grad_kernel(grad_ref, put_ref, slope_ref, ext_ref, wide_ref, half_ref, bias_ref, slots_ref):
    g = pl.program_id(0)
    width = grad_ref.shape[1]

    @pl.when(g == 0)
    def _():
        slots_ref[...] = jnp.dot(put_ref[...], grad_ref[...], preferred_element_type=F32).astype(BF)

    core = jnp.zeros((CORE, LANES), F32)
    row, lane = iota((width, LANES), 0), iota((width, LANES), 1)
    for i in range(PH):
        pick = ((lane // GW == i) & (row == GW * g + lane % GW)).astype(F32).astype(BF)
        core = core + jnp.dot(slots_ref[i * CORE:(i + 1) * CORE, :], pick, preferred_element_type=F32)
    grad = core * slope_ref[0]
    bias_ref[0] = jnp.sum(grad, axis=0, keepdims=True)
    low = grad.astype(BF)
    wide_ref[0] = jnp.dot(ext_ref[...], low, preferred_element_type=F32).astype(BF)
    half = GW // 2
    row, lane = iota((LANES, 128), 0), iota((LANES, 128), 1)
    for h in range(2):
        pick = ((lane < PH * half) & (row == lane // half * GW + lane % half + h * half)).astype(F32).astype(BF)
        half_ref[h] = jnp.dot(low, pick, preferred_element_type=F32).astype(BF)

def conv_grad(mixed_grad, put, slope, ext):
    groups = slope.shape[0]
    width = mixed_grad.shape[1]
    whole = lambda shape: pl.BlockSpec(shape, lambda g: (0,) * len(shape))
    return pl.pallas_call(
        conv_grad_kernel,
        grid=(groups,),
        in_specs=[whole((LEN, width)), whole((SLOTS, LEN)), pl.BlockSpec((1, CORE, LANES), lambda g: (g, 0, 0)), whole((EXT, CORE))],
        out_specs=[pl.BlockSpec((1, EXT, LANES), lambda g: (g, 0, 0)), pl.BlockSpec((2, CORE, 128), lambda g: (g, 0, 0)),
                   pl.BlockSpec((1, 1, LANES), lambda g: (g, 0, 0))],
        out_shape=[jax.ShapeDtypeStruct((groups, EXT, LANES), BF), jax.ShapeDtypeStruct((2 * groups, CORE, 128), BF),
                   jax.ShapeDtypeStruct((groups, 1, LANES), F32)],
        scratch_shapes=[pltpu.VMEM((SLOTS, width), BF)],
        compiler_params=pltpu.CompilerParams(vmem_limit_bytes=48 * 2**20),
    )(mixed_grad, put, slope, ext)

def signal_grad_kernel(wide_ref, wt_ref, take_ref, out_ref, back_ref):
    g = pl.program_id(0)
    width = out_ref.shape[1]

    @pl.when(g == 0)
    def _():
        back_ref[...] = jnp.zeros_like(back_ref)

    total = jnp.zeros((CORE, LANES), F32)
    for j in range(NJ):
        m = NJ - 1 - j
        total = total + lax.dot_general(wide_ref[0, PN * j:PN * j + CORE, :], wt_ref[0, m * LANES:(m + 1) * LANES, :],
                                        (((1,), (1,)), ((), ())), preferred_element_type=F32)
    value = total.astype(BF)
    for i in range(PH):
        rows = slice(i * CORE, (i + 1) * CORE)
        back_ref[rows, :] = back_ref[rows, :] + unfold_lanes(value, g, i, width // GW)

    @pl.when(g == pl.num_programs(0) - 1)
    def _():
        out_ref[...] = jnp.dot(take_ref[...], back_ref[...], preferred_element_type=F32).astype(BF)

def signal_grad(wide, wt, take):
    groups = wt.shape[0]
    width = groups * GW
    whole = lambda shape: pl.BlockSpec(shape, lambda g: (0,) * len(shape))
    return pl.pallas_call(
        signal_grad_kernel,
        grid=(groups,),
        in_specs=[pl.BlockSpec((1, EXT, LANES), lambda g: (g, 0, 0)), pl.BlockSpec((1, NJ * LANES, LANES), lambda g: (g, 0, 0)), whole((LEN, SLOTS))],
        out_specs=whole((LEN, width)),
        out_shape=jax.ShapeDtypeStruct((LEN, width), BF),
        scratch_shapes=[pltpu.VMEM((SLOTS, width), BF)],
        compiler_params=pltpu.CompilerParams(vmem_limit_bytes=48 * 2**20),
    )(wide, wt, take)

HALF = GW // 2
NM = 26

def kernel_grad_kernel(sig_ref, grad_ref, ext_ref, out_ref, wide_ref, turned_ref, parts_ref):
    packs = sig_ref.shape[0]
    for r in range(packs):
        wide_ref[r] = jnp.dot(ext_ref[...], sig_ref[r], preferred_element_type=F32).astype(BF)
        turned_ref[:, r * CORE:(r + 1) * CORE] = grad_ref[r].astype(F32).T.astype(BF)

    def one_offset(j, carry):
        total = jnp.zeros((128, LANES), F32)
        for r in range(packs):
            start = pl.multiple_of(PN * j, PN)
            total = total + jnp.dot(turned_ref[:, r * CORE:(r + 1) * CORE], wide_ref[r, pl.ds(start, CORE), :],
                                    preferred_element_type=F32)
        parts_ref[j] = total
        return carry

    lax.fori_loop(0, NJ, one_offset, 0)
    lane = iota((HALF, LANES), 1)

    def one_block(m, carry):
        total = jnp.zeros((HALF, LANES), F32)
        for i in range(PH):
            rows = slice(HALF * i, HALF * (i + 1))
            here = pltpu.roll(parts_ref[m, rows, :], LANES - GW * (1 + i), 1)
            if i == PH - 1:
                after = parts_ref[m + 1, rows, :]
            else:
                after = pltpu.roll(parts_ref[m + 1, rows, :], GW * (PH - 1 - i), 1)
            total = total + jnp.where(lane < GW * (PH - 1 - i), here, after)
        out_ref[m] = jnp.where(lane < PH * GW, total, 0.0)
        return carry

    lax.fori_loop(0, NM, one_block, 0)

def kernel_grad(sig, grad, ext):
    packs = sig.shape[0]
    return pl.pallas_call(
        kernel_grad_kernel,
        out_shape=jax.ShapeDtypeStruct((NM, HALF, LANES), F32),
        scratch_shapes=[pltpu.VMEM((packs, EXT, LANES), BF), pltpu.VMEM((128, packs * CORE), BF), pltpu.VMEM((NJ, 128, LANES), F32)],
        compiler_params=pltpu.CompilerParams(vmem_limit_bytes=48 * 2**20),
    )(sig, grad, ext)

def assemble_kernel(part_ref, out_ref):
    block = part_ref[:, 0].astype(F32).reshape(-1, LANES)
    out_ref[...] = block.T[:PH * GW, :]

def assemble(parts):
    n = parts.shape[0]
    return pl.pallas_call(
        assemble_kernel,
        grid=(NM,),
        in_specs=[pl.BlockSpec((n, 1, HALF, LANES), lambda m: (0, m, 0, 0))],
        out_specs=pl.BlockSpec((PH * GW, n * HALF), lambda m: (m, 0)),
        out_shape=jax.ShapeDtypeStruct((KER * GW, n * HALF), F32),
    )(parts)


def team_groups(row_count, team):
    if row_count == team:
        return None
    return [list(range(first, first + team)) for first in range(0, row_count, team)]


def cross_groups(row_count, team):
    return [list(range(first, row_count, team)) for first in range(team)]


def attention_forward(queries, key_low, value_low, segments, heads_here):
    pack_count = segments.shape[0]
    q_block = min(LEN, 512)
    per_pack = LEN // q_block
    head_shape = (pack_count, LEN, heads_here, HD)
    query_all = queries.reshape(head_shape)
    key_all = key_low.reshape(head_shape)
    value_all = value_low.reshape(head_shape)
    zero_index = jnp.zeros((), jnp.int32)

    def one_block(block_index):
        pack_index = block_index // per_pack
        row_start = block_index % per_pack * q_block
        query_block = lax.dynamic_slice(
            query_all, (pack_index, row_start, zero_index, zero_index), (1, q_block, heads_here, HD)
        )[0]
        pack_keys = lax.dynamic_index_in_dim(key_all, pack_index, 0, keepdims=False)
        pack_values = lax.dynamic_index_in_dim(value_all, pack_index, 0, keepdims=False)
        pack_seg = lax.dynamic_index_in_dim(segments, pack_index, 0, keepdims=False)
        seg_block = lax.dynamic_slice_in_dim(pack_seg, row_start, q_block, 0)
        scores = jnp.einsum(
            "qhd,khd->hqk", query_block, pack_keys, preferred_element_type=jnp.float32
        )
        scores = jnp.where((seg_block[:, None] == pack_seg[None, :])[None], scores, MASKED)
        top_score = jnp.max(scores, axis=-1, keepdims=True)
        exp_scores = jnp.exp(scores - top_score)
        row_total = jnp.sum(exp_scores, axis=-1, keepdims=True)
        attn_probs = (exp_scores / row_total).astype(jnp.bfloat16)
        result = jnp.einsum(
            "hqk,khd->qhd", attn_probs, pack_values, preferred_element_type=jnp.float32
        )
        return (result.reshape(q_block, -1), (top_score + jnp.log(row_total))[:, :, 0])

    blocks, log_sums = lax.map(one_block, jnp.arange(pack_count * per_pack, dtype=jnp.int32))
    return (blocks.reshape(pack_count * LEN, -1), log_sums)


def attention_backward(queries, key_low, value_low, attended_grad, log_sums, segments, heads_here):
    pack_count = segments.shape[0]
    q_block = min(LEN, 512)
    per_pack = LEN // q_block
    head_shape = (pack_count, LEN, heads_here, HD)
    query_all = queries.reshape(head_shape)
    key_all = key_low.reshape(head_shape)
    value_all = value_low.reshape(head_shape)
    grad_all = attended_grad.reshape(head_shape)
    sums_all = log_sums.reshape(pack_count, per_pack, heads_here, q_block)

    def one_pack(pack_index):
        pack_query = lax.dynamic_index_in_dim(query_all, pack_index, 0, keepdims=False)
        pack_keys = lax.dynamic_index_in_dim(key_all, pack_index, 0, keepdims=False)
        pack_values = lax.dynamic_index_in_dim(value_all, pack_index, 0, keepdims=False)
        pack_grad = lax.dynamic_index_in_dim(grad_all, pack_index, 0, keepdims=False)
        pack_seg = lax.dynamic_index_in_dim(segments, pack_index, 0, keepdims=False)
        pack_sums = lax.dynamic_index_in_dim(sums_all, pack_index, 0, keepdims=False)

        def one_block(totals, block_index):
            key_grad, value_grad = totals
            row_start = block_index * q_block
            query_block = lax.dynamic_slice_in_dim(pack_query, row_start, q_block, 0)
            grad_block = lax.dynamic_slice_in_dim(pack_grad, row_start, q_block, 0)
            seg_block = lax.dynamic_slice_in_dim(pack_seg, row_start, q_block, 0)
            sum_block = lax.dynamic_index_in_dim(pack_sums, block_index, 0, keepdims=False)
            scores = jnp.einsum(
                "qhd,khd->hqk", query_block, pack_keys, preferred_element_type=jnp.float32
            )
            scores = jnp.where((seg_block[:, None] == pack_seg[None, :])[None], scores, MASKED)
            attn_probs = jnp.exp(scores - sum_block[:, :, None])
            value_grad = value_grad + jnp.einsum(
                "hqk,qhd->khd",
                attn_probs.astype(jnp.bfloat16),
                grad_block,
                preferred_element_type=jnp.float32,
            )
            prob_grad = jnp.einsum(
                "qhd,khd->hqk", grad_block, pack_values, preferred_element_type=jnp.float32
            )
            row_delta = jnp.sum(attn_probs * prob_grad, axis=-1, keepdims=True)
            score_grad = (attn_probs * (prob_grad - row_delta)).astype(jnp.bfloat16)
            query_grad = jnp.einsum(
                "hqk,khd->qhd", score_grad, pack_keys, preferred_element_type=jnp.float32
            )
            key_grad = key_grad + jnp.einsum(
                "hqk,qhd->khd", score_grad, query_block, preferred_element_type=jnp.float32
            )
            return ((key_grad, value_grad), query_grad.reshape(q_block, -1))

        zeros_kv = jnp.zeros((LEN, heads_here, HD), jnp.float32)
        (key_grad, value_grad), query_grad = lax.scan(
            one_block, (zeros_kv, zeros_kv), jnp.arange(per_pack, dtype=jnp.int32)
        )
        return (query_grad.reshape(LEN, -1), key_grad.reshape(LEN, -1), value_grad.reshape(LEN, -1))

    query_grad, key_grad, value_grad = lax.map(one_pack, jnp.arange(pack_count, dtype=jnp.int32))
    total_rows = pack_count * LEN
    return (
        query_grad.reshape(total_rows, -1),
        key_grad.reshape(total_rows, -1),
        value_grad.reshape(total_rows, -1),
    )


def rows_total(gradients):
    return lax.psum(
        (
            gradients[0],
            gradients[1],
            gradients[2],
            gradients[3],
            gradients[4],
            gradients[5],
            gradients[6],
        ),
        "rows",
    )


def norm_total(gradients):
    return lax.psum(
        (
            gradients[0],
            gradients[1],
            gradients[2],
            gradients[3],
            gradients[4],
            gradients[5],
            gradients[6],
            gradients[7],
        ),
        ("rows", "tp"),
    )


def on_device(
    frames,
    seg_starts,
    conv_weight,
    conv_bias,
    norm_gain0,
    norm_bias0,
    qkv_weight,
    qv_bias,
    out_weight,
    out_bias,
    norm_gain1,
    norm_bias1,
    up_weight,
    up_bias,
    down_weight,
    down_bias,
    norm_gain2,
    norm_bias2,
    cotangent,
):
    pack_count = seg_starts.shape[0]
    total_rows = pack_count * LEN
    group_width = D // GROUPS
    head_cols = qkv_weight.shape[2]
    heads_here = head_cols // HD
    q_scale = HD ** (-0.5)
    groups_here = conv_weight.shape[2] // group_width
    team = 2 * groups_here
    row_count = lax.axis_size("rows")
    teams = team_groups(row_count, team)
    qkv_flat = qkv_weight.reshape(D, -1)
    positions = jnp.arange(LEN, dtype=jnp.int32)
    segments = (
        jnp.sum(
            (positions[None, :, None] >= seg_starts[:, None, :]).astype(jnp.int32),
            axis=2,
            dtype=jnp.int32,
        )
        - 1
    )
    gain_conv = norm_gain0.astype(jnp.float32)
    bias_conv = norm_bias0.astype(jnp.float32)
    gain_attn = norm_gain1.astype(jnp.float32)
    bias_attn = norm_bias1.astype(jnp.float32)
    gain_ffn = norm_gain2.astype(jnp.float32)
    bias_ffn = norm_bias2.astype(jnp.float32)
    bias_out = out_bias.astype(jnp.float32)
    bias_down = down_bias.astype(jnp.float32)
    channels = lax.all_to_all(frames, "tp", split_axis=1, concat_axis=0, tiled=True)
    slots = spread_slots(segments[0])
    put = (iota((SLOTS, LEN), 0) == slots[None, :]).astype(BF)
    take = (slots[:, None] == iota((LEN, SLOTS), 1)).astype(BF)
    ext = extension()
    toeplitz = wprep(conv_weight.reshape(KER * group_width, -1), groups_here)
    bias_lanes = jnp.tile(conv_bias.astype(F32).reshape(groups_here, 1, group_width), (1, 1, PH))
    bias_lanes = jnp.pad(bias_lanes, ((0, 0), (0, 0), (0, LANES - PH * group_width)))
    mixed_low, slope, core = conv_fwd(channels, put, take, ext, toeplitz, bias_lanes)
    core_all = lax.all_to_all(
        jnp.repeat(core, 2, axis=0), "rows", 0, 0, axis_index_groups=teams, tiled=True
    )
    mixed_rows = lax.all_to_all(mixed_low, "tp", split_axis=0, concat_axis=1, tiled=True)
    normed0, hat_conv, inv_conv = norm_forward(
        frames.astype(jnp.float32) + mixed_rows.astype(jnp.float32), gain_conv, bias_conv
    )
    normed0_full = lax.all_gather(normed0.astype(jnp.bfloat16), "tp", axis=0, tiled=True)
    projected = jnp.dot(normed0_full, qkv_flat, preferred_element_type=jnp.float32).reshape(
        total_rows, 3, head_cols
    )
    bias_qv = qv_bias.astype(jnp.float32)
    queries = ((projected[:, 0] + bias_qv[0]) * q_scale).astype(jnp.bfloat16)
    key_low = projected[:, 1].astype(jnp.bfloat16)
    value_low = (projected[:, 2] + bias_qv[1]).astype(jnp.bfloat16)
    attended, log_sums = attention_forward(queries, key_low, value_low, segments, heads_here)
    attended_low = attended.astype(jnp.bfloat16)
    piece_rows = attended_low
    attn_sum = lax.psum_scatter(
        jnp.dot(piece_rows, out_weight, preferred_element_type=jnp.float32).astype(jnp.bfloat16),
        "tp",
        scatter_dimension=0,
        tiled=True,
    ).astype(jnp.float32)
    normed1, hat_attn, inv_attn = norm_forward(normed0 + attn_sum + bias_out, gain_attn, bias_attn)
    normed1_full = lax.all_gather(normed1.astype(jnp.bfloat16), "tp", axis=0, tiled=True)
    up_pre = jnp.dot(normed1_full, up_weight, preferred_element_type=jnp.float32) + up_bias.astype(
        jnp.float32
    )
    activated = jax.nn.gelu(up_pre, approximate=False).astype(jnp.bfloat16)
    piece_rows = activated
    ffn_sum = lax.psum_scatter(
        jnp.dot(piece_rows, down_weight, preferred_element_type=jnp.float32).astype(jnp.bfloat16),
        "tp",
        scatter_dimension=0,
        tiled=True,
    ).astype(jnp.float32)
    block_out, hat_ffn, inv_ffn = norm_forward(normed1 + ffn_sum + bias_down, gain_ffn, bias_ffn)
    grad2, gain2_grad, bias2_grad = norm_backward(
        cotangent.astype(jnp.float32), hat_ffn, inv_ffn, gain_ffn
    )
    down_bias_grad = jnp.sum(grad2, axis=0)
    grad2_full = lax.all_gather(grad2.astype(jnp.bfloat16), "tp", axis=0, tiled=True)
    down_grad = jnp.einsum("rf,rd->fd", activated, grad2_full, preferred_element_type=jnp.float32)
    act_grad = jnp.einsum("rd,fd->rf", grad2_full, down_weight, preferred_element_type=jnp.float32)
    up_grad_pre = act_grad * gelu_slope(up_pre)
    up_bias_grad = jnp.sum(up_grad_pre, axis=0)
    up_low = up_grad_pre.astype(jnp.bfloat16)
    up_grad = jnp.einsum("rd,rf->df", normed1_full, up_low, preferred_element_type=jnp.float32)
    piece_rows = up_low
    ffn_back = lax.psum_scatter(
        jnp.einsum("rf,df->rd", piece_rows, up_weight, preferred_element_type=jnp.float32).astype(
            jnp.bfloat16
        ),
        "tp",
        scatter_dimension=0,
        tiled=True,
    ).astype(jnp.float32)
    grad1, gain1_grad, bias1_grad = norm_backward(grad2 + ffn_back, hat_attn, inv_attn, gain_attn)
    out_bias_grad = jnp.sum(grad1, axis=0)
    grad1_full = lax.all_gather(grad1.astype(jnp.bfloat16), "tp", axis=0, tiled=True)
    out_grad = jnp.einsum("rh,rd->hd", attended_low, grad1_full, preferred_element_type=jnp.float32)
    attended_grad = jnp.einsum(
        "rd,hd->rh", grad1_full, out_weight, preferred_element_type=jnp.float32
    ).astype(jnp.bfloat16)
    query_grad, key_grad, value_grad = attention_backward(
        queries, key_low, value_low, attended_grad, log_sums, segments, heads_here
    )
    query_grad = query_grad * q_scale
    qv_grad = jnp.stack([jnp.sum(query_grad, axis=0), jnp.sum(value_grad, axis=0)])
    proj_grad = (
        jnp.stack([query_grad, key_grad, value_grad], axis=1)
        .astype(jnp.bfloat16)
        .reshape(total_rows, -1)
    )
    qkv_grad = jnp.einsum(
        "rd,rc->dc", normed0_full, proj_grad, preferred_element_type=jnp.float32
    ).reshape(D, 3, head_cols)
    piece_rows = proj_grad
    attn_back = lax.psum_scatter(
        jnp.einsum("rc,dc->rd", piece_rows, qkv_flat, preferred_element_type=jnp.float32).astype(
            jnp.bfloat16
        ),
        "tp",
        scatter_dimension=0,
        tiled=True,
    ).astype(jnp.float32)
    grad0, gain0_grad, bias0_grad = norm_backward(grad1 + attn_back, hat_conv, inv_conv, gain_conv)
    mixed_grad = lax.all_to_all(
        grad0.astype(jnp.bfloat16), "tp", split_axis=1, concat_axis=0, tiled=True
    )
    wide, halves, conv_bias_grad = conv_grad(mixed_grad, put, slope, ext)
    conv_bias_grad = conv_bias_grad[:, 0, : PH * group_width].reshape(groups_here, PH, group_width)
    conv_bias_grad = jnp.sum(conv_bias_grad, axis=1).reshape(-1)
    halves_all = lax.all_to_all(halves, "rows", 0, 0, axis_index_groups=teams, tiled=True)
    kernel_part = kernel_grad(core_all, halves_all, ext)
    if teams is not None:
        kernel_part = lax.psum(
            kernel_part, "rows", axis_index_groups=cross_groups(row_count, team)
        )
    kernel_parts = lax.all_gather(kernel_part.astype(BF), "rows", axis_index_groups=teams)
    kernel_total = assemble(kernel_parts).reshape(KER, group_width, -1)
    signal_back = signal_grad(wide, toeplitz, take)
    frames_back = lax.all_to_all(
        signal_back, "tp", split_axis=0, concat_axis=1, tiled=True
    ).astype(F32)
    frames_grad = grad0 + frames_back
    conv_bias_grad, qkv_grad, qv_grad, out_grad, up_grad, up_bias_grad, down_grad = (
        rows_total(
            (
                conv_bias_grad,
                qkv_grad,
                qv_grad,
                out_grad,
                up_grad,
                up_bias_grad,
                down_grad,
            )
        )
    )
    (
        gain0_grad,
        bias0_grad,
        out_bias_grad,
        gain1_grad,
        bias1_grad,
        down_bias_grad,
        gain2_grad,
        bias2_grad,
    ) = norm_total(
        (
            gain0_grad,
            bias0_grad,
            out_bias_grad,
            gain1_grad,
            bias1_grad,
            down_bias_grad,
            gain2_grad,
            bias2_grad,
        )
    )
    return (
        block_out.astype(jnp.bfloat16),
        frames_grad,
        kernel_total,
        conv_bias_grad,
        gain0_grad,
        bias0_grad,
        qkv_grad,
        qv_grad,
        out_grad,
        out_bias_grad,
        gain1_grad,
        bias1_grad,
        up_grad,
        up_bias_grad,
        down_grad,
        down_bias_grad,
        gain2_grad,
        bias2_grad,
    )


def solution(mesh):
    return jax.shard_map(
        on_device,
        mesh=mesh,
        in_specs=(
            P(("rows", "tp"), None),
            P("rows", None),
            P(None, None, "tp"),
            P("tp"),
            P(),
            P(),
            P(None, None, "tp"),
            P(None, "tp"),
            P("tp", None),
            P(),
            P(),
            P(),
            P(None, "tp"),
            P("tp"),
            P("tp", None),
            P(),
            P(),
            P(),
            P(("rows", "tp"), None),
        ),
        out_specs=(
            P(("rows", "tp"), None),
            P(("rows", "tp"), None),
            P(None, None, "tp"),
            P("tp"),
            P(),
            P(),
            P(None, None, "tp"),
            P(None, "tp"),
            P("tp", None),
            P(),
            P(),
            P(),
            P(None, "tp"),
            P("tp"),
            P("tp", None),
            P(),
            P(),
            P(),
        ),
        check_vma=False,
    )
```

```python
import jax
import jax.numpy as jnp
from jax import lax
from jax.experimental import pallas as pl
from jax.experimental.pallas import tpu as pltpu
from jax.sharding import PartitionSpec as P

D = 768
HD = 64
KER = 128
GROUPS = 16
LEN = 1024

EPSILON = 1e-05
MASKED = -1000000000.0
ROOT_HALF = 0.7071067811865476
INV_ROOT_TAU = 0.3989422804014327


def gelu_slope(inputs):
    return 0.5 * (1.0 + lax.erf(inputs * ROOT_HALF)) + inputs * INV_ROOT_TAU * jnp.exp(
        -0.5 * inputs * inputs
    )


def norm_forward(inputs, norm_gain, norm_bias):
    centered = inputs - jnp.mean(inputs, axis=-1, keepdims=True)
    inv_std = lax.rsqrt(jnp.mean(centered * centered, axis=-1, keepdims=True) + EPSILON)
    normed = centered * inv_std
    return (normed * norm_gain + norm_bias, normed, inv_std)


def norm_backward(grad_out, normed, inv_std, norm_gain):
    scaled = grad_out * norm_gain
    grad_in = inv_std * (
        scaled
        - jnp.mean(scaled, axis=-1, keepdims=True)
        - normed * jnp.mean(scaled * normed, axis=-1, keepdims=True)
    )
    return (grad_in, jnp.sum(grad_out * normed, axis=0), jnp.sum(grad_out, axis=0))


GW = 48
PH = 5
QN, PN = 17, 16
CORE = QN * PN
NJ = 27
LEAD = 13
EXT = (QN + NJ - 1) * PN
LANES = 256
GAP = KER // 2
SLOTS = PH * CORE
BF = jnp.bfloat16
F32 = jnp.float32

def iota(shape, dim):
    return lax.broadcasted_iota(jnp.int32, shape, dim)

def spread_slots(segments):
    place = jnp.arange(LEN, dtype=jnp.int32) + GAP * segments
    block = place // PH
    return place % PH * CORE + block % QN * PN + block // QN

def extension():
    row, col = iota((EXT, CORE), 0), iota((EXT, CORE), 1)
    want = QN * (row % PN) + row // PN - LEAD
    have = QN * (col % PN) + col // PN
    return (want == have).astype(BF)

def lane_map(group, rows, offset):
    row, lane = iota((rows, LANES), 0), iota((rows, LANES), 1)
    return (row == GW * group + lane % GW) & (lane < PH * GW)

def wprep_kernel(w_ref, out_ref, wide_ref):
    g = pl.program_id(0)
    before = PH * GW
    after = wide_ref.shape[0] - before - KER * GW
    wide_ref[0:before, :] = jnp.zeros((before, LANES), BF)
    wide_ref[before + KER * GW :, :] = jnp.zeros((after, LANES), BF)
    spread = lane_map(g, 4 * GW, 0).astype(BF)
    chunk = 768

    def widen(step, carry):
        start = pl.multiple_of(step * chunk, chunk)
        part = jnp.dot(w_ref[pl.ds(start, chunk), :], spread, preferred_element_type=F32)
        wide_ref[pl.ds(pl.multiple_of(start + before, 16), chunk), :] = part.astype(BF)
        return carry

    lax.fori_loop(0, KER * GW // chunk, widen, 0)
    lane = iota((1, LANES), 1)
    masks = [(lane // GW == i).astype(F32).astype(BF) for i in range(PH)]

    def place(j, carry):
        total = None
        for i in range(PH):
            start = pl.multiple_of(before + PH * GW * j - GW * (1 + i), 16)
            part = wide_ref[pl.ds(start, PH * GW), :] * masks[i]
            total = part if total is None else total + part
        out_ref[0, pl.ds(pl.multiple_of(j * LANES, LANES), PH * GW), :] = total
        out_ref[0, pl.ds(pl.multiple_of(j * LANES + PH * GW, 16), LANES - PH * GW), :] = jnp.zeros(
            (LANES - PH * GW, LANES), BF
        )
        return carry

    lax.fori_loop(0, NJ, place, 0)

def wprep(kernel_flat, groups, **kw):
    return pl.pallas_call(
        wprep_kernel,
        grid=(groups,),
        in_specs=[pl.BlockSpec((KER * GW, groups * GW), lambda g: (0, 0))],
        out_specs=pl.BlockSpec((1, NJ * LANES, LANES), lambda g: (g, 0, 0)),
        out_shape=jax.ShapeDtypeStruct((groups, NJ * LANES, LANES), BF),
        scratch_shapes=[pltpu.VMEM((PH * GW + KER * GW + 288, LANES), BF)],
        compiler_params=pltpu.CompilerParams(vmem_limit_bytes=40 * 2**20),
    )(kernel_flat)

def phi_pair(v):
    cdf = 0.5 * (1.0 + lax.erf(v * ROOT_HALF))
    return v * cdf, cdf + v * INV_ROOT_TAU * jnp.exp(-0.5 * v * v)

def unfold_lanes(values, group, i, groups):
    row, col = iota((LANES, groups * GW), 0), iota((LANES, groups * GW), 1)
    pick = ((row // GW == i) & (col == GW * group + row % GW)).astype(F32).astype(BF)
    return jnp.dot(values, pick, preferred_element_type=F32).astype(BF)

def conv_fwd_kernel(sig_ref, put_ref, take_ref, ext_ref, wt_ref, bias_ref,
                    mixed_ref, slope_ref, core_ref, slots_ref, wide_ref, back_ref):
    g = pl.program_id(0)
    groups = pl.num_programs(0)
    width = sig_ref.shape[1]

    @pl.when(g == 0)
    def _():
        slots_ref[...] = jnp.dot(put_ref[...], sig_ref[...], preferred_element_type=F32).astype(BF)
        back_ref[...] = jnp.zeros_like(back_ref)

    core = jnp.zeros((CORE, LANES), F32)
    row, lane = iota((width, LANES), 0), iota((width, LANES), 1)
    for i in range(PH):
        pick = ((lane // GW == i) & (row == GW * g + lane % GW)).astype(F32).astype(BF)
        core = core + jnp.dot(slots_ref[i * CORE:(i + 1) * CORE, :], pick, preferred_element_type=F32)
    core = core.astype(BF)
    core_ref[0] = core
    wide_ref[...] = jnp.dot(ext_ref[...], core, preferred_element_type=F32).astype(BF)
    total = jnp.zeros((CORE, LANES), F32)
    for j in range(NJ):
        total = total + jnp.dot(wide_ref[PN * j:PN * j + CORE, :], wt_ref[0, j * LANES:(j + 1) * LANES, :],
                                preferred_element_type=F32)
    value, slope = phi_pair(total + bias_ref[0])
    slope_ref[0] = slope
    value = value.astype(BF)
    for i in range(PH):
        rows = slice(i * CORE, (i + 1) * CORE)
        back_ref[rows, :] = back_ref[rows, :] + unfold_lanes(value, g, i, width // GW)

    @pl.when(g == groups - 1)
    def _():
        mixed_ref[...] = jnp.dot(take_ref[...], back_ref[...], preferred_element_type=F32).astype(BF)

def conv_fwd(signal, put, take, ext, wt, bias_lanes):
    groups = wt.shape[0]
    width = signal.shape[1]
    whole = lambda shape: pl.BlockSpec(shape, lambda g: (0,) * len(shape))
    return pl.pallas_call(
        conv_fwd_kernel,
        grid=(groups,),
        in_specs=[whole((LEN, width)), whole((SLOTS, LEN)), whole((LEN, SLOTS)), whole((EXT, CORE)),
                  pl.BlockSpec((1, NJ * LANES, LANES), lambda g: (g, 0, 0)),
                  pl.BlockSpec((1, 1, LANES), lambda g: (g, 0, 0))],
        out_specs=[whole((LEN, width)), pl.BlockSpec((1, CORE, LANES), lambda g: (g, 0, 0)),
                   pl.BlockSpec((1, CORE, LANES), lambda g: (g, 0, 0))],
        out_shape=[jax.ShapeDtypeStruct((LEN, width), BF), jax.ShapeDtypeStruct((groups, CORE, LANES), F32),
                   jax.ShapeDtypeStruct((groups, CORE, LANES), BF)],
        scratch_shapes=[pltpu.VMEM((SLOTS, width), BF), pltpu.VMEM((EXT, LANES), BF), pltpu.VMEM((SLOTS, width), BF)],
        compiler_params=pltpu.CompilerParams(vmem_limit_bytes=48 * 2**20),
    )(signal, put, take, ext, wt, bias_lanes)

def conv_grad_kernel(grad_ref, put_ref, slope_ref, ext_ref, wide_ref, half_ref, bias_ref, slots_ref):
    g = pl.program_id(0)
    width = grad_ref.shape[1]

    @pl.when(g == 0)
    def _():
        slots_ref[...] = jnp.dot(put_ref[...], grad_ref[...], preferred_element_type=F32).astype(BF)

    core = jnp.zeros((CORE, LANES), F32)
    row, lane = iota((width, LANES), 0), iota((width, LANES), 1)
    for i in range(PH):
        pick = ((lane // GW == i) & (row == GW * g + lane % GW)).astype(F32).astype(BF)
        core = core + jnp.dot(slots_ref[i * CORE:(i + 1) * CORE, :], pick, preferred_element_type=F32)
    grad = core * slope_ref[0]
    bias_ref[0] = jnp.sum(grad, axis=0, keepdims=True)
    low = grad.astype(BF)
    wide_ref[0] = jnp.dot(ext_ref[...], low, preferred_element_type=F32).astype(BF)
    half = GW // 2
    row, lane = iota((LANES, 128), 0), iota((LANES, 128), 1)
    for h in range(2):
        pick = ((lane < PH * half) & (row == lane // half * GW + lane % half + h * half)).astype(F32).astype(BF)
        half_ref[h] = jnp.dot(low, pick, preferred_element_type=F32).astype(BF)

def conv_grad(mixed_grad, put, slope, ext):
    groups = slope.shape[0]
    width = mixed_grad.shape[1]
    whole = lambda shape: pl.BlockSpec(shape, lambda g: (0,) * len(shape))
    return pl.pallas_call(
        conv_grad_kernel,
        grid=(groups,),
        in_specs=[whole((LEN, width)), whole((SLOTS, LEN)), pl.BlockSpec((1, CORE, LANES), lambda g: (g, 0, 0)), whole((EXT, CORE))],
        out_specs=[pl.BlockSpec((1, EXT, LANES), lambda g: (g, 0, 0)), pl.BlockSpec((2, CORE, 128), lambda g: (g, 0, 0)),
                   pl.BlockSpec((1, 1, LANES), lambda g: (g, 0, 0))],
        out_shape=[jax.ShapeDtypeStruct((groups, EXT, LANES), BF), jax.ShapeDtypeStruct((2 * groups, CORE, 128), BF),
                   jax.ShapeDtypeStruct((groups, 1, LANES), F32)],
        scratch_shapes=[pltpu.VMEM((SLOTS, width), BF)],
        compiler_params=pltpu.CompilerParams(vmem_limit_bytes=48 * 2**20),
    )(mixed_grad, put, slope, ext)

def signal_grad_kernel(wide_ref, wt_ref, take_ref, out_ref, back_ref):
    g = pl.program_id(0)
    width = out_ref.shape[1]

    @pl.when(g == 0)
    def _():
        back_ref[...] = jnp.zeros_like(back_ref)

    total = jnp.zeros((CORE, LANES), F32)
    for j in range(NJ):
        m = NJ - 1 - j
        total = total + lax.dot_general(wide_ref[0, PN * j:PN * j + CORE, :], wt_ref[0, m * LANES:(m + 1) * LANES, :],
                                        (((1,), (1,)), ((), ())), preferred_element_type=F32)
    value = total.astype(BF)
    for i in range(PH):
        rows = slice(i * CORE, (i + 1) * CORE)
        back_ref[rows, :] = back_ref[rows, :] + unfold_lanes(value, g, i, width // GW)

    @pl.when(g == pl.num_programs(0) - 1)
    def _():
        out_ref[...] = jnp.dot(take_ref[...], back_ref[...], preferred_element_type=F32).astype(BF)

def signal_grad(wide, wt, take):
    groups = wt.shape[0]
    width = groups * GW
    whole = lambda shape: pl.BlockSpec(shape, lambda g: (0,) * len(shape))
    return pl.pallas_call(
        signal_grad_kernel,
        grid=(groups,),
        in_specs=[pl.BlockSpec((1, EXT, LANES), lambda g: (g, 0, 0)), pl.BlockSpec((1, NJ * LANES, LANES), lambda g: (g, 0, 0)), whole((LEN, SLOTS))],
        out_specs=whole((LEN, width)),
        out_shape=jax.ShapeDtypeStruct((LEN, width), BF),
        scratch_shapes=[pltpu.VMEM((SLOTS, width), BF)],
        compiler_params=pltpu.CompilerParams(vmem_limit_bytes=48 * 2**20),
    )(wide, wt, take)

HALF = GW // 2
NM = 26

def kernel_grad_kernel(sig_ref, grad_ref, ext_ref, out_ref, wide_ref, turned_ref, parts_ref):
    packs = sig_ref.shape[0]
    for r in range(packs):
        wide_ref[r] = jnp.dot(ext_ref[...], sig_ref[r], preferred_element_type=F32).astype(BF)
        turned_ref[:, r * CORE:(r + 1) * CORE] = grad_ref[r].astype(F32).T.astype(BF)

    def one_offset(j, carry):
        total = jnp.zeros((128, LANES), F32)
        for r in range(packs):
            start = pl.multiple_of(PN * j, PN)
            total = total + jnp.dot(turned_ref[:, r * CORE:(r + 1) * CORE], wide_ref[r, pl.ds(start, CORE), :],
                                    preferred_element_type=F32)
        parts_ref[j] = total
        return carry

    lax.fori_loop(0, NJ, one_offset, 0)
    lane = iota((HALF, LANES), 1)

    def one_block(m, carry):
        total = jnp.zeros((HALF, LANES), F32)
        for i in range(PH):
            rows = slice(HALF * i, HALF * (i + 1))
            here = pltpu.roll(parts_ref[m, rows, :], LANES - GW * (1 + i), 1)
            if i == PH - 1:
                after = parts_ref[m + 1, rows, :]
            else:
                after = pltpu.roll(parts_ref[m + 1, rows, :], GW * (PH - 1 - i), 1)
            total = total + jnp.where(lane < GW * (PH - 1 - i), here, after)
        out_ref[m] = jnp.where(lane < PH * GW, total, 0.0)
        return carry

    lax.fori_loop(0, NM, one_block, 0)

def kernel_grad(sig, grad, ext):
    packs = sig.shape[0]
    return pl.pallas_call(
        kernel_grad_kernel,
        out_shape=jax.ShapeDtypeStruct((NM, HALF, LANES), F32),
        scratch_shapes=[pltpu.VMEM((packs, EXT, LANES), BF), pltpu.VMEM((128, packs * CORE), BF), pltpu.VMEM((NJ, 128, LANES), F32)],
        compiler_params=pltpu.CompilerParams(vmem_limit_bytes=48 * 2**20),
    )(sig, grad, ext)

def assemble_kernel(part_ref, out_ref):
    block = part_ref[:, 0].astype(F32).reshape(-1, LANES)
    out_ref[...] = block.T[:PH * GW, :]

def assemble(parts):
    n = parts.shape[0]
    return pl.pallas_call(
        assemble_kernel,
        grid=(NM,),
        in_specs=[pl.BlockSpec((n, 1, HALF, LANES), lambda m: (0, m, 0, 0))],
        out_specs=pl.BlockSpec((PH * GW, n * HALF), lambda m: (m, 0)),
        out_shape=jax.ShapeDtypeStruct((KER * GW, n * HALF), F32),
    )(parts)


def team_groups(row_count, team):
    if row_count == team:
        return None
    return [list(range(first, first + team)) for first in range(0, row_count, team)]


def cross_groups(row_count, team):
    return [list(range(first, row_count, team)) for first in range(team)]


def attention_forward(queries, key_low, value_low, segments, heads_here):
    pack_count = segments.shape[0]
    q_block = min(LEN, 512)
    per_pack = LEN // q_block
    head_shape = (pack_count, LEN, heads_here, HD)
    query_all = queries.reshape(head_shape)
    key_all = key_low.reshape(head_shape)
    value_all = value_low.reshape(head_shape)
    zero_index = jnp.zeros((), jnp.int32)

    def one_block(block_index):
        pack_index = block_index // per_pack
        row_start = block_index % per_pack * q_block
        query_block = lax.dynamic_slice(
            query_all, (pack_index, row_start, zero_index, zero_index), (1, q_block, heads_here, HD)
        )[0]
        pack_keys = lax.dynamic_index_in_dim(key_all, pack_index, 0, keepdims=False)
        pack_values = lax.dynamic_index_in_dim(value_all, pack_index, 0, keepdims=False)
        pack_seg = lax.dynamic_index_in_dim(segments, pack_index, 0, keepdims=False)
        seg_block = lax.dynamic_slice_in_dim(pack_seg, row_start, q_block, 0)
        scores = jnp.einsum(
            "qhd,khd->hqk", query_block, pack_keys, preferred_element_type=jnp.float32
        )
        scores = jnp.where((seg_block[:, None] == pack_seg[None, :])[None], scores, MASKED)
        top_score = jnp.max(scores, axis=-1, keepdims=True)
        exp_scores = jnp.exp(scores - top_score)
        row_total = jnp.sum(exp_scores, axis=-1, keepdims=True)
        attn_probs = (exp_scores / row_total).astype(jnp.bfloat16)
        result = jnp.einsum(
            "hqk,khd->qhd", attn_probs, pack_values, preferred_element_type=jnp.float32
        )
        return (result.reshape(q_block, -1), (top_score + jnp.log(row_total))[:, :, 0])

    blocks, log_sums = lax.map(one_block, jnp.arange(pack_count * per_pack, dtype=jnp.int32))
    return (blocks.reshape(pack_count * LEN, -1), log_sums)


def attention_backward(queries, key_low, value_low, attended_grad, log_sums, segments, heads_here):
    pack_count = segments.shape[0]
    q_block = min(LEN, 512)
    per_pack = LEN // q_block
    head_shape = (pack_count, LEN, heads_here, HD)
    query_all = queries.reshape(head_shape)
    key_all = key_low.reshape(head_shape)
    value_all = value_low.reshape(head_shape)
    grad_all = attended_grad.reshape(head_shape)
    sums_all = log_sums.reshape(pack_count, per_pack, heads_here, q_block)

    def one_pack(pack_index):
        pack_query = lax.dynamic_index_in_dim(query_all, pack_index, 0, keepdims=False)
        pack_keys = lax.dynamic_index_in_dim(key_all, pack_index, 0, keepdims=False)
        pack_values = lax.dynamic_index_in_dim(value_all, pack_index, 0, keepdims=False)
        pack_grad = lax.dynamic_index_in_dim(grad_all, pack_index, 0, keepdims=False)
        pack_seg = lax.dynamic_index_in_dim(segments, pack_index, 0, keepdims=False)
        pack_sums = lax.dynamic_index_in_dim(sums_all, pack_index, 0, keepdims=False)

        def one_block(totals, block_index):
            key_grad, value_grad = totals
            row_start = block_index * q_block
            query_block = lax.dynamic_slice_in_dim(pack_query, row_start, q_block, 0)
            grad_block = lax.dynamic_slice_in_dim(pack_grad, row_start, q_block, 0)
            seg_block = lax.dynamic_slice_in_dim(pack_seg, row_start, q_block, 0)
            sum_block = lax.dynamic_index_in_dim(pack_sums, block_index, 0, keepdims=False)
            scores = jnp.einsum(
                "qhd,khd->hqk", query_block, pack_keys, preferred_element_type=jnp.float32
            )
            scores = jnp.where((seg_block[:, None] == pack_seg[None, :])[None], scores, MASKED)
            attn_probs = jnp.exp(scores - sum_block[:, :, None])
            value_grad = value_grad + jnp.einsum(
                "hqk,qhd->khd",
                attn_probs.astype(jnp.bfloat16),
                grad_block,
                preferred_element_type=jnp.float32,
            )
            prob_grad = jnp.einsum(
                "qhd,khd->hqk", grad_block, pack_values, preferred_element_type=jnp.float32
            )
            row_delta = jnp.sum(attn_probs * prob_grad, axis=-1, keepdims=True)
            score_grad = (attn_probs * (prob_grad - row_delta)).astype(jnp.bfloat16)
            query_grad = jnp.einsum(
                "hqk,khd->qhd", score_grad, pack_keys, preferred_element_type=jnp.float32
            )
            key_grad = key_grad + jnp.einsum(
                "hqk,qhd->khd", score_grad, query_block, preferred_element_type=jnp.float32
            )
            return ((key_grad, value_grad), query_grad.reshape(q_block, -1))

        zeros_kv = jnp.zeros((LEN, heads_here, HD), jnp.float32)
        (key_grad, value_grad), query_grad = lax.scan(
            one_block, (zeros_kv, zeros_kv), jnp.arange(per_pack, dtype=jnp.int32)
        )
        return (query_grad.reshape(LEN, -1), key_grad.reshape(LEN, -1), value_grad.reshape(LEN, -1))

    query_grad, key_grad, value_grad = lax.map(one_pack, jnp.arange(pack_count, dtype=jnp.int32))
    total_rows = pack_count * LEN
    return (
        query_grad.reshape(total_rows, -1),
        key_grad.reshape(total_rows, -1),
        value_grad.reshape(total_rows, -1),
    )


def swap(value, bit):
    return lax.ppermute(value, "tp", [(i, i ^ bit) for i in range(lax.axis_size("tp"))])


def gather_pieces(value):
    across = swap(value, 2)
    return [value, swap(value, 1), across, swap(across, 1)]


def scatter_sum(pieces):
    half = pieces[0].shape[0]
    near = swap(jnp.concatenate([pieces[3], pieces[1]], axis=0), 1)
    across = (pieces[2].astype(F32) + near[:half].astype(F32)).astype(BF)
    far = swap(across, 2)
    return pieces[0].astype(F32) + near[half:].astype(F32) + far.astype(F32)


def exchange(pieces):
    near = swap(jnp.concatenate([pieces[1], pieces[3]], axis=0), 1)
    rows = pieces[0].shape[0]
    far = swap(jnp.concatenate([pieces[2], near[rows:]], axis=0), 2)
    return [pieces[0], near[:rows], far[:rows], far[rows:]]


def split_pieces(value):
    rows = value.shape[0] // 4
    return [value[m * rows : (m + 1) * rows] for m in range(4)]


def sum_rows(value, steps):
    me = lax.axis_index("rows")
    count = lax.axis_size("rows")
    for bit in steps:
        upper = (me >> bit) & 1
        half = value.shape[0] // 2
        keep = lax.dynamic_slice_in_dim(value, upper * half, half, 0)
        send = lax.dynamic_slice_in_dim(value, (1 - upper) * half, half, 0)
        other = lax.ppermute(send, "rows", [(i, i ^ (1 << bit)) for i in range(count)])
        value = (keep.astype(F32) + other.astype(F32)).astype(BF)
    for bit in reversed(steps):
        upper = (me >> bit) & 1
        other = lax.ppermute(value, "rows", [(i, i ^ (1 << bit)) for i in range(count)])
        value = jnp.where(
            upper == 0,
            jnp.concatenate([value, other], axis=0),
            jnp.concatenate([other, value], axis=0),
        )
    return value


def on_device(
    frames,
    seg_starts,
    conv_weight,
    conv_bias,
    norm_gain0,
    norm_bias0,
    qkv_weight,
    qv_bias,
    out_weight,
    out_bias,
    norm_gain1,
    norm_bias1,
    up_weight,
    up_bias,
    down_weight,
    down_bias,
    norm_gain2,
    norm_bias2,
    cotangent,
):
    pack_count = seg_starts.shape[0]
    total_rows = pack_count * LEN
    group_width = D // GROUPS
    head_cols = qkv_weight.shape[2]
    heads_here = head_cols // HD
    q_scale = HD ** (-0.5)
    groups_here = conv_weight.shape[2] // group_width
    team = 2 * groups_here
    row_count = lax.axis_size("rows")
    teams = team_groups(row_count, team)
    qkv_flat = qkv_weight.reshape(D, -1)
    positions = jnp.arange(LEN, dtype=jnp.int32)
    segments = (
        jnp.sum(
            (positions[None, :, None] >= seg_starts[:, None, :]).astype(jnp.int32),
            axis=2,
            dtype=jnp.int32,
        )
        - 1
    )
    gain_conv = norm_gain0.astype(jnp.float32)
    bias_conv = norm_bias0.astype(jnp.float32)
    gain_attn = norm_gain1.astype(jnp.float32)
    bias_attn = norm_bias1.astype(jnp.float32)
    gain_ffn = norm_gain2.astype(jnp.float32)
    bias_ffn = norm_bias2.astype(jnp.float32)
    bias_out = out_bias.astype(jnp.float32)
    bias_down = down_bias.astype(jnp.float32)
    channels = lax.all_to_all(frames, "tp", split_axis=1, concat_axis=0, tiled=True)
    slots = spread_slots(segments[0])
    put = (iota((SLOTS, LEN), 0) == slots[None, :]).astype(BF)
    take = (slots[:, None] == iota((LEN, SLOTS), 1)).astype(BF)
    ext = extension()
    toeplitz = wprep(conv_weight.reshape(KER * group_width, -1), groups_here)
    bias_lanes = jnp.tile(conv_bias.astype(F32).reshape(groups_here, 1, group_width), (1, 1, PH))
    bias_lanes = jnp.pad(bias_lanes, ((0, 0), (0, 0), (0, LANES - PH * group_width)))
    mixed_low, slope, core = conv_fwd(channels, put, take, ext, toeplitz, bias_lanes)
    core_all = lax.all_to_all(
        jnp.repeat(core, 2, axis=0), "rows", 0, 0, axis_index_groups=teams, tiled=True
    )
    mixed_rows = lax.all_to_all(mixed_low, "tp", split_axis=0, concat_axis=1, tiled=True)
    normed0, hat_conv, inv_conv = norm_forward(
        frames.astype(jnp.float32) + mixed_rows.astype(jnp.float32), gain_conv, bias_conv
    )
    me = lax.axis_index("tp")
    order = [me ^ m for m in range(4)]
    piece = total_rows // 4
    seg_own = jnp.concatenate(
        [lax.dynamic_slice_in_dim(segments, m * piece, piece, 1) for m in order], axis=1
    )
    out_pieces = gather_pieces(out_weight)
    out_all = jnp.concatenate(out_pieces, axis=0)
    normed0_full = jnp.concatenate(gather_pieces(normed0.astype(BF)), axis=0)
    projected = jnp.dot(normed0_full, qkv_flat, preferred_element_type=jnp.float32).reshape(
        total_rows, 3, head_cols
    )
    bias_qv = qv_bias.astype(jnp.float32)
    queries = ((projected[:, 0] + bias_qv[0]) * q_scale).astype(jnp.bfloat16)
    key_low = projected[:, 1].astype(jnp.bfloat16)
    value_low = (projected[:, 2] + bias_qv[1]).astype(jnp.bfloat16)
    attended, log_sums = attention_forward(queries, key_low, value_low, seg_own, heads_here)
    attended_low = attended.astype(jnp.bfloat16)
    attended_rows = exchange(split_pieces(attended_low))
    attn_sum = jnp.dot(
        jnp.concatenate(attended_rows, axis=1), out_all, preferred_element_type=F32
    )
    normed1, hat_attn, inv_attn = norm_forward(normed0 + attn_sum + bias_out, gain_attn, bias_attn)
    normed1_full = jnp.concatenate(gather_pieces(normed1.astype(BF)), axis=0)
    up_pre = jnp.dot(normed1_full, up_weight, preferred_element_type=jnp.float32) + up_bias.astype(
        jnp.float32
    )
    activated = jax.nn.gelu(up_pre, approximate=False).astype(jnp.bfloat16)
    ffn_sum = scatter_sum(
        split_pieces(jnp.dot(activated, down_weight, preferred_element_type=F32).astype(BF))
    )
    block_out, hat_ffn, inv_ffn = norm_forward(normed1 + ffn_sum + bias_down, gain_ffn, bias_ffn)
    grad2, gain2_grad, bias2_grad = norm_backward(
        cotangent.astype(jnp.float32), hat_ffn, inv_ffn, gain_ffn
    )
    down_bias_grad = jnp.sum(grad2, axis=0)
    grad2_full = jnp.concatenate(gather_pieces(grad2.astype(BF)), axis=0)
    down_grad = jnp.einsum("rf,rd->fd", activated, grad2_full, preferred_element_type=jnp.float32)
    act_grad = jnp.einsum("rd,fd->rf", grad2_full, down_weight, preferred_element_type=jnp.float32)
    up_grad_pre = act_grad * gelu_slope(up_pre)
    up_bias_grad = jnp.sum(up_grad_pre, axis=0)
    up_low = up_grad_pre.astype(jnp.bfloat16)
    up_grad = jnp.einsum("rd,rf->df", normed1_full, up_low, preferred_element_type=jnp.float32)
    ffn_back = scatter_sum(
        split_pieces(
            jnp.einsum("rf,df->rd", up_low, up_weight, preferred_element_type=F32).astype(BF)
        )
    )
    steps = list(range(row_count.bit_length() - 1))
    down_total = sum_rows(down_grad.astype(BF), steps).astype(F32)
    up_total = sum_rows(up_grad.astype(BF), steps).astype(F32)
    grad1, gain1_grad, bias1_grad = norm_backward(grad2 + ffn_back, hat_attn, inv_attn, gain_attn)
    out_bias_grad = jnp.sum(grad1, axis=0)
    grad1_low = grad1.astype(BF)
    attended_back = jnp.einsum("rd,hd->rh", grad1_low, out_all, preferred_element_type=F32)
    attended_back = attended_back.astype(BF)
    attended_grad = jnp.concatenate(
        exchange([attended_back[:, m * head_cols : (m + 1) * head_cols] for m in range(4)]), axis=0
    )
    grad1_full = jnp.concatenate(gather_pieces(grad1_low), axis=0)
    out_grad = jnp.einsum("rh,rd->hd", attended_low, grad1_full, preferred_element_type=jnp.float32)
    query_grad, key_grad, value_grad = attention_backward(
        queries, key_low, value_low, attended_grad, log_sums, seg_own, heads_here
    )
    query_grad = query_grad * q_scale
    qv_grad = jnp.stack([jnp.sum(query_grad, axis=0), jnp.sum(value_grad, axis=0)])
    proj_grad = (
        jnp.stack([query_grad, key_grad, value_grad], axis=1)
        .astype(jnp.bfloat16)
        .reshape(total_rows, -1)
    )
    qkv_grad = jnp.einsum(
        "rd,rc->dc", normed0_full, proj_grad, preferred_element_type=jnp.float32
    )
    attn_back = scatter_sum(
        split_pieces(
            jnp.einsum("rc,dc->rd", proj_grad, qkv_flat, preferred_element_type=F32).astype(BF)
        )
    )
    tail = jnp.concatenate([qkv_grad.reshape(-1, D), out_grad], axis=0).astype(BF)
    tail = sum_rows(tail, steps).astype(F32)
    qkv_rows = qkv_grad.size // D
    qkv_total = tail[:qkv_rows].reshape(D, 3, head_cols)
    out_total = tail[qkv_rows:]
    grad0, gain0_grad, bias0_grad = norm_backward(grad1 + attn_back, hat_conv, inv_conv, gain_conv)
    mixed_grad = lax.all_to_all(
        grad0.astype(jnp.bfloat16), "tp", split_axis=1, concat_axis=0, tiled=True
    )
    wide, halves, conv_bias_grad = conv_grad(mixed_grad, put, slope, ext)
    conv_bias_grad = conv_bias_grad[:, 0, : PH * group_width].reshape(groups_here, PH, group_width)
    conv_bias_grad = jnp.sum(conv_bias_grad, axis=1).reshape(-1)
    halves_all = lax.all_to_all(halves, "rows", 0, 0, axis_index_groups=teams, tiled=True)
    kernel_part = kernel_grad(core_all, halves_all, ext)
    if teams is not None:
        kernel_part = lax.psum(
            kernel_part, "rows", axis_index_groups=cross_groups(row_count, team)
        )
    rows_small = [conv_bias_grad, qv_grad, up_bias_grad]
    all_small = [
        gain0_grad, bias0_grad, out_bias_grad, gain1_grad, bias1_grad, down_bias_grad, gain2_grad,
        bias2_grad,
    ]
    shared = jnp.stack(all_small)
    shared = shared + swap(shared, 1)
    shared = shared + swap(shared, 2)
    small = jnp.concatenate([shared.reshape(-1)] + [v.reshape(-1) for v in rows_small])
    kernel_parts = lax.all_gather(kernel_part.astype(BF), "rows", axis_index_groups=teams)
    small = jnp.sum(lax.all_gather(small, "rows"), axis=0)
    kernel_total = assemble(kernel_parts).reshape(KER, group_width, -1)
    signal_back = signal_grad(wide, toeplitz, take)
    frames_back = lax.all_to_all(
        signal_back, "tp", split_axis=0, concat_axis=1, tiled=True
    ).astype(F32)
    frames_grad = grad0 + frames_back
    sizes = [v.size for v in all_small + rows_small]
    ends = [sum(sizes[: i + 1]) for i in range(len(sizes))]
    cuts = [small[end - size : end] for size, end in zip(sizes, ends)]
    gain0_grad, bias0_grad, out_bias_grad, gain1_grad, bias1_grad = cuts[:5]
    down_bias_grad, gain2_grad, bias2_grad, conv_bias_grad, qv_grad, up_bias_grad = cuts[5:]
    qv_grad = qv_grad.reshape(2, head_cols)
    return (
        block_out.astype(jnp.bfloat16),
        frames_grad,
        kernel_total,
        conv_bias_grad,
        gain0_grad,
        bias0_grad,
        qkv_total,
        qv_grad,
        out_total,
        out_bias_grad,
        gain1_grad,
        bias1_grad,
        up_total,
        up_bias_grad,
        down_total,
        down_bias_grad,
        gain2_grad,
        bias2_grad,
    )


def solution(mesh):
    return jax.shard_map(
        on_device,
        mesh=mesh,
        in_specs=(
            P(("rows", "tp"), None),
            P("rows", None),
            P(None, None, "tp"),
            P("tp"),
            P(),
            P(),
            P(None, None, "tp"),
            P(None, "tp"),
            P("tp", None),
            P(),
            P(),
            P(),
            P(None, "tp"),
            P("tp"),
            P("tp", None),
            P(),
            P(),
            P(),
            P(("rows", "tp"), None),
        ),
        out_specs=(
            P(("rows", "tp"), None),
            P(("rows", "tp"), None),
            P(None, None, "tp"),
            P("tp"),
            P(),
            P(),
            P(None, None, "tp"),
            P(None, "tp"),
            P("tp", None),
            P(),
            P(),
            P(),
            P(None, "tp"),
            P("tp"),
            P("tp", None),
            P(),
            P(),
            P(),
        ),
        check_vma=False,
    )
```

```python
import functools

import jax
import jax.numpy as jnp
from jax import lax
from jax.experimental import pallas as pl
from jax.experimental.pallas import tpu as pltpu
from jax.sharding import PartitionSpec as P

D = 768
HD = 64
KER = 128
GROUPS = 16
LEN = 1024

EPSILON = 1e-05
ROOT_HALF = 0.7071067811865476
INV_ROOT_TAU = 0.3989422804014327
MASK_ROOT = 16384.0

GW = D // GROUPS
HALF = GW // 2
PH = 5
QN, PN = 17, 16
CORE = QN * PN
NJ = 27
LEAD = 13
EXT = (QN + NJ - 1) * PN
LANES = 256
GAP = KER // 2
SLOTS = PH * CORE
NM = 26

ORDER = (0, 2, 1, 3)

BF = jnp.bfloat16
F32 = jnp.float32


def iota(shape, dim):
    return lax.broadcasted_iota(jnp.int32, shape, dim)


def full(shape):
    return pl.BlockSpec(shape, lambda *index: (0,) * len(shape))


def block(shape, index_map):
    return pl.BlockSpec(shape, index_map)


def params(mib):
    return pltpu.CompilerParams(vmem_limit_bytes=58 * 2**20)


def cost(microseconds):
    return pl.CostEstimate(
        flops=int(microseconds * 1.1e9), bytes_accessed=int(microseconds * 1e6), transcendentals=0
    )


def dot(left, right):
    return jnp.dot(left, right, preferred_element_type=F32)


def dot_turned(left, right):
    return lax.dot_general(left, right, (((1,), (1,)), ((), ())), preferred_element_type=F32)


def phi_pair(v):
    cdf = 0.5 * (1.0 + lax.erf(v * ROOT_HALF))
    return v * cdf, cdf + v * INV_ROOT_TAU * jnp.exp(-0.5 * v * v)


def norm_stats(inputs):
    centered = inputs - jnp.mean(inputs, axis=-1, keepdims=True)
    inv_std = lax.rsqrt(jnp.mean(centered * centered, axis=-1, keepdims=True) + EPSILON)
    return centered * inv_std, inv_std


def norm_backward(grad_out, normed, inv_std, norm_gain):
    scaled = grad_out * norm_gain
    grad_in = inv_std * (
        scaled
        - jnp.mean(scaled, axis=-1, keepdims=True)
        - normed * jnp.mean(scaled * normed, axis=-1, keepdims=True)
    )
    return (grad_in, jnp.sum(grad_out * normed, axis=0), jnp.sum(grad_out, axis=0))


def spread_slots(segments):
    place = jnp.arange(LEN, dtype=jnp.int32) + GAP * segments
    at = place // PH
    return place % PH * CORE + at % QN * PN + at // QN


def extension():
    row, col = iota((EXT, CORE), 0), iota((EXT, CORE), 1)
    want = QN * (row % PN) + row // PN - LEAD
    have = QN * (col % PN) + col // PN
    return (want == have).astype(BF)


def toeplitz_kernel(w_ref, out_ref, wide_ref):
    g = pl.program_id(0)
    before = PH * GW
    after = wide_ref.shape[0] - before - KER * GW
    row, lane = iota((w_ref.shape[1], LANES), 0), iota((w_ref.shape[1], LANES), 1)
    spread = ((row == GW * g + lane % GW) & (lane < PH * GW)).astype(F32).astype(BF)
    wide_ref[0:before, :] = jnp.zeros((before, LANES), BF)
    wide_ref[before + KER * GW :, :] = jnp.zeros((after, LANES), BF)
    wide_ref[before : before + KER * GW, :] = dot(w_ref[...], spread).astype(BF)
    lane = iota((1, LANES), 1)
    masks = [(lane // GW == i).astype(F32).astype(BF) for i in range(PH)]

    def place(j, carry):
        total = None
        for i in range(PH):
            start = pl.multiple_of(before + PH * GW * j - GW * (1 + i), 16)
            part = wide_ref[pl.ds(start, PH * GW), :] * masks[i]
            total = part if total is None else total + part
        out_ref[0, pl.ds(pl.multiple_of(j * LANES, LANES), PH * GW), :] = total
        out_ref[0, pl.ds(pl.multiple_of(j * LANES + PH * GW, 16), LANES - PH * GW), :] = jnp.zeros(
            (LANES - PH * GW, LANES), BF
        )
        return carry

    lax.fori_loop(0, NJ, place, 0)


def toeplitz_weights(kernel_flat, groups):
    return pl.pallas_call(
        toeplitz_kernel,
        grid=(groups,),
        in_specs=[full((KER * GW, groups * GW))],
        out_specs=block((1, NJ * LANES, LANES), lambda g: (g, 0, 0)),
        out_shape=jax.ShapeDtypeStruct((groups, NJ * LANES, LANES), BF),
        scratch_shapes=[pltpu.VMEM((PH * GW + KER * GW + 288, LANES), BF)],
        compiler_params=params(20),
        cost_estimate=cost(11),
    )(kernel_flat)


def fold_in(slots_ref, g):
    width = slots_ref.shape[1]
    row, lane = iota((width, LANES), 0), iota((width, LANES), 1)
    core = jnp.zeros((CORE, LANES), F32)
    for i in range(PH):
        pick = ((lane // GW == i) & (row == GW * g + lane % GW)).astype(F32).astype(BF)
        core = core + dot(slots_ref[i * CORE : (i + 1) * CORE, :], pick)
    return core


def fold_out(values, back_ref, g):
    width = back_ref.shape[1]
    row, col = iota((LANES, width), 0), iota((LANES, width), 1)
    for i in range(PH):
        pick = ((row // GW == i) & (col == GW * g + row % GW)).astype(F32).astype(BF)
        here = slice(i * CORE, (i + 1) * CORE)
        back_ref[here, :] = back_ref[here, :] + dot(values, pick).astype(BF)


def unspread(back_ref, put_ref):
    turned = back_ref[...].astype(F32).T.astype(BF)
    return dot(turned, put_ref[...]).T.astype(BF)


def conv_kernel(sig_ref, put_ref, ext_ref, wt_ref, bias_ref,
                mixed_ref, slope_ref, core_ref, slots_ref, wide_ref, back_ref):
    g = pl.program_id(0)

    @pl.when(g == 0)
    def _():
        slots_ref[...] = dot(put_ref[...], sig_ref[...]).astype(BF)
        back_ref[...] = jnp.zeros_like(back_ref)

    core = fold_in(slots_ref, g).astype(BF)
    core_ref[0] = core
    wide_ref[...] = dot(ext_ref[...], core).astype(BF)
    total = jnp.zeros((CORE, LANES), F32)
    for j in range(NJ):
        total = total + dot(
            wide_ref[PN * j : PN * j + CORE, :], wt_ref[0, j * LANES : (j + 1) * LANES, :]
        )
    value, slope = phi_pair(total + bias_ref[0])
    slope_ref[0] = slope
    fold_out(value.astype(BF), back_ref, g)

    @pl.when(g == pl.num_programs(0) - 1)
    def _():
        mixed_ref[...] = unspread(back_ref, put_ref)


def conv(signal, put, ext, toeplitz, bias_lanes):
    groups = toeplitz.shape[0]
    width = signal.shape[1]
    return pl.pallas_call(
        conv_kernel,
        grid=(groups,),
        in_specs=[
            full((LEN, width)),
            full((SLOTS, LEN)),
            full((EXT, CORE)),
            block((1, NJ * LANES, LANES), lambda g: (g, 0, 0)),
            block((1, 1, LANES), lambda g: (g, 0, 0)),
        ],
        out_specs=[
            full((LEN, width)),
            block((1, CORE, LANES), lambda g: (g, 0, 0)),
            block((1, CORE, LANES), lambda g: (g, 0, 0)),
        ],
        out_shape=[
            jax.ShapeDtypeStruct((LEN, width), BF),
            jax.ShapeDtypeStruct((groups, CORE, LANES), F32),
            jax.ShapeDtypeStruct((groups, CORE, LANES), BF),
        ],
        scratch_shapes=[
            pltpu.VMEM((SLOTS, width), BF),
            pltpu.VMEM((EXT, LANES), BF),
            pltpu.VMEM((SLOTS, width), BF),
        ],
        compiler_params=params(28),
        cost_estimate=cost(14),
    )(signal, put, ext, toeplitz, bias_lanes)


def conv_grad_kernel(grad_ref, put_ref, slope_ref, ext_ref, wide_ref, half_ref, bias_ref, slots_ref):
    g = pl.program_id(0)

    @pl.when(g == 0)
    def _():
        slots_ref[...] = dot(put_ref[...], grad_ref[...]).astype(BF)

    grad = fold_in(slots_ref, g) * slope_ref[0]
    bias_ref[0] = jnp.sum(grad, axis=0, keepdims=True)
    low = grad.astype(BF)
    wide_ref[0] = dot(ext_ref[...], low).astype(BF)
    row, lane = iota((LANES, 128), 0), iota((LANES, 128), 1)
    for h in range(2):
        pick = (lane < PH * HALF) & (row == lane // HALF * GW + lane % HALF + h * HALF)
        half_ref[h] = dot(low, pick.astype(F32).astype(BF)).astype(BF)


def conv_grad(mixed_grad, put, slope, ext):
    groups = slope.shape[0]
    width = mixed_grad.shape[1]
    return pl.pallas_call(
        conv_grad_kernel,
        grid=(groups,),
        in_specs=[
            full((LEN, width)),
            full((SLOTS, LEN)),
            block((1, CORE, LANES), lambda g: (g, 0, 0)),
            full((EXT, CORE)),
        ],
        out_specs=[
            block((1, EXT, LANES), lambda g: (g, 0, 0)),
            block((2, CORE, 128), lambda g: (g, 0, 0)),
            block((1, 1, LANES), lambda g: (g, 0, 0)),
        ],
        out_shape=[
            jax.ShapeDtypeStruct((groups, EXT, LANES), BF),
            jax.ShapeDtypeStruct((2 * groups, CORE, 128), BF),
            jax.ShapeDtypeStruct((groups, 1, LANES), F32),
        ],
        scratch_shapes=[pltpu.VMEM((SLOTS, width), BF)],
        compiler_params=params(20),
        cost_estimate=cost(7),
    )(mixed_grad, put, slope, ext)


def signal_grad_kernel(wide_ref, wt_ref, put_ref, out_ref, back_ref):
    g = pl.program_id(0)

    @pl.when(g == 0)
    def _():
        back_ref[...] = jnp.zeros_like(back_ref)

    total = jnp.zeros((CORE, LANES), F32)
    for j in range(NJ):
        m = NJ - 1 - j
        total = total + dot_turned(
            wide_ref[0, PN * j : PN * j + CORE, :], wt_ref[0, m * LANES : (m + 1) * LANES, :]
        )
    fold_out(total.astype(BF), back_ref, g)

    @pl.when(g == pl.num_programs(0) - 1)
    def _():
        out_ref[...] = unspread(back_ref, put_ref)


def signal_grad(wide, toeplitz, put):
    groups = toeplitz.shape[0]
    width = groups * GW
    return pl.pallas_call(
        signal_grad_kernel,
        grid=(groups,),
        in_specs=[
            block((1, EXT, LANES), lambda g: (g, 0, 0)),
            block((1, NJ * LANES, LANES), lambda g: (g, 0, 0)),
            full((SLOTS, LEN)),
        ],
        out_specs=full((LEN, width)),
        out_shape=jax.ShapeDtypeStruct((LEN, width), BF),
        scratch_shapes=[pltpu.VMEM((SLOTS, width), BF)],
        compiler_params=params(24),
        cost_estimate=cost(10),
    )(wide, toeplitz, put)


def tap_grad_kernel(sig_ref, grad_ref, ext_ref, out_ref, wide_ref, turned_ref, parts_ref, rows_ref):
    packs = sig_ref.shape[0]
    for r in range(packs):
        wide_ref[r] = dot(ext_ref[...], sig_ref[r]).astype(BF)
        turned_ref[:, r * CORE : (r + 1) * CORE] = grad_ref[r].astype(F32).T.astype(BF)

    def one_offset(j, carry):
        total = jnp.zeros((128, LANES), F32)
        start = pl.multiple_of(PN * j, PN)
        for r in range(packs):
            total = total + dot(
                turned_ref[:, r * CORE : (r + 1) * CORE], wide_ref[r, pl.ds(start, CORE), :]
            )
        parts_ref[j] = total
        return carry

    lax.fori_loop(0, NJ, one_offset, 0)
    lane = iota((HALF, LANES), 1)

    def one_block(m, carry):
        total = jnp.zeros((HALF, LANES), F32)
        for i in range(PH):
            rows = slice(HALF * i, HALF * (i + 1))
            here = pltpu.roll(parts_ref[m, rows, :], LANES - GW * (1 + i), 1)
            after = parts_ref[m + 1, rows, :]
            if i < PH - 1:
                after = pltpu.roll(after, GW * (PH - 1 - i), 1)
            total = total + jnp.where(lane < GW * (PH - 1 - i), here, after)
        place = pl.ds(pl.multiple_of(PH * GW * m, 8), PH * GW)
        rows_ref[place, 0:HALF] = total.T[: PH * GW, :]
        return carry

    lax.fori_loop(0, NM, one_block, 0)
    for c in range(GW):
        taps = rows_ref[pl.ds(c, KER, stride=GW), :]
        out_ref[c * HALF : (c + 1) * HALF, :] = taps.T[:HALF, :]


def tap_grad(sig, grad, ext):
    packs = sig.shape[0]
    return pl.pallas_call(
        tap_grad_kernel,
        out_shape=jax.ShapeDtypeStruct((GW * HALF, KER), F32),
        scratch_shapes=[
            pltpu.VMEM((packs, EXT, LANES), BF),
            pltpu.VMEM((128, packs * CORE), BF),
            pltpu.VMEM((NJ, 128, LANES), F32),
            pltpu.VMEM((NM * PH * GW, 128), F32),
        ],
        compiler_params=params(28),
        cost_estimate=cost(14),
    )(sig, grad, ext)


def assemble_kernel(at_ref, a_ref, b_ref, out_ref, wide_ref):
    step = pl.program_id(0)
    packs = a_ref.shape[0]
    per_step = out_ref.shape[0]
    half_steps = pl.num_programs(0) // 2

    def place(held_ref, which):
        for r in range(packs):
            wide_ref[...] = held_ref[at_ref[which, r]].astype(F32)
            for c in range(per_step):
                out_ref[c, r * HALF : (r + 1) * HALF, :] = wide_ref[c * HALF : (c + 1) * HALF, :]

    @pl.when(step < half_steps)
    def _():
        place(a_ref, 0)

    @pl.when(step >= half_steps)
    def _():
        place(b_ref, 1)


def assemble(order, held_a, held_b):
    packs = held_a.shape[0]
    steps = 4
    per_step = GW // steps
    rows = per_step * HALF
    half = steps // 2
    return pl.pallas_call(
        assemble_kernel,
        grid=(steps,),
        in_specs=[
            pl.BlockSpec(memory_space=pltpu.SMEM),
            block((packs, rows, KER), lambda s: (0, jnp.minimum(s, half - 1), 0)),
            block((packs, rows, KER), lambda s: (0, jnp.maximum(s - half, 0), 0)),
        ],
        out_specs=block((per_step, packs * HALF, KER), lambda s: (s, 0, 0)),
        out_shape=jax.ShapeDtypeStruct((GW, packs * HALF, KER), F32),
        scratch_shapes=[pltpu.VMEM((rows, KER), F32)],
        compiler_params=params(16),
        cost_estimate=cost(4),
    )(order, held_a, held_b)


def head_rows(turned, head, heads):
    pieces = [jnp.zeros((HD, turned.shape[1]), turned.dtype) for _ in range(heads)]
    pieces[head] = turned[HD * head : HD * (head + 1), :]
    return jnp.concatenate(pieces + [turned[HD * heads :, :]], axis=0)


def attention_kernel(q_block, heads, *refs):
    me_ref = refs[0]
    mixed = refs[1:5]
    frames = refs[5:9]
    (gain_ref, bias_ref, wq_ref, wk_ref, wv_ref, qb_ref, vb_ref, featq_ref, featk_ref) = refs[9:18]
    (att_ref, own_ref, hat_ref, inv_ref, all_out, low_out, q_out, qt_out, k_out, v_out, ot_ref,
     lse_ref) = refs[18:30]
    all_ref, low_ref, q_ref, qt_ref, k_ref, v_ref, vt_ref, sems = refs[30:]
    rows = frames[0].shape[0]
    part = mixed[0].shape[1]
    width = frames[0].shape[1]
    scale = HD ** (-0.5)
    me = me_ref[0]
    row, lane = iota((part, width), 0), iota((part, width), 1)
    spots = [(lane == row + part * (me ^ m)).astype(F32).astype(BF) for m in ORDER]
    for n in range(4):
        here = slice(n * rows, (n + 1) * rows)
        start = pl.multiple_of((me ^ ORDER[n]) * rows, rows)
        total = frames[n][...].astype(F32)
        for ref, spot in zip(mixed, spots):
            total = total + dot(ref[pl.ds(start, rows), :], spot)
        hat, inv = norm_stats(total)
        normed = hat * gain_ref[...] + bias_ref[...]
        if n == 0:
            own_ref[...] = normed
            hat_ref[...] = hat
            inv_ref[...] = jnp.broadcast_to(inv, inv_ref.shape)
        all_ref[here, :] = normed
        normed = normed.astype(BF)
        low_ref[here, :] = normed
        query = (dot_turned(normed, wq_ref[...]) + qb_ref[...]) * scale
        query = query + featq_ref[here, :].astype(F32)
        q_ref[here, :] = query.astype(BF)
        qt_ref[:, here] = query.T.astype(BF)
        key = dot_turned(normed, wk_ref[...])
        k_ref[here, :] = (key + featk_ref[here, :].astype(F32)).astype(BF)
        value = dot_turned(normed, wv_ref[...]) + vb_ref[...]
        v_ref[here, :] = value.astype(BF)
        vt_ref[:, here] = value.T.astype(BF)
    held = [all_ref, low_ref, q_ref, qt_ref, k_ref, v_ref]
    kept = [all_out, low_out, q_out, qt_out, k_out, v_out]
    copies = [
        pltpu.make_async_copy(src, dst, sems.at[i]) for i, (src, dst) in enumerate(zip(held, kept))
    ]
    for copy in copies:
        copy.start()
    total = 4 * rows
    for head in range(heads):
        for start in range(0, total, q_block):
            cols = slice(start, start + q_block)
            turned = head_rows(qt_ref[:, cols], head, heads)
            scores = dot(k_ref[...], turned)
            top = jnp.max(scores, axis=0, keepdims=True)
            weights = jnp.exp(scores - top)
            sums = jnp.sum(weights, axis=0, keepdims=True)
            value = dot(vt_ref[HD * head : HD * (head + 1), :], weights.astype(BF))
            ot_ref[HD * head : HD * (head + 1), cols] = value / sums
            lse_ref[head : head + 1, cols] = top + jnp.log(sums)
    lse_ref[heads:, :] = jnp.zeros((8 - heads, total), F32)
    for n in range(4):
        here = slice(n * rows, (n + 1) * rows)
        att_ref[here, :] = ot_ref[:, here].T.astype(BF)
    for copy in copies:
        copy.wait()


def attention(me, mixed, frames, norm, weights, biases, features, heads, q_block=512):
    rows, width = frames[0].shape
    total = 4 * rows
    cols = heads * HD
    vmem = pl.BlockSpec(memory_space=pltpu.VMEM)
    away = pl.BlockSpec(memory_space=pl.ANY)
    held = [
        ((total, width), F32),
        ((total, width), BF),
        ((total, LANES), BF),
        ((LANES, total), BF),
        ((total, LANES), BF),
        ((total, LANES), BF),
    ]
    return pl.pallas_call(
        functools.partial(attention_kernel, q_block, heads),
        in_specs=[pl.BlockSpec(memory_space=pltpu.SMEM)] + [vmem] * 17,
        out_specs=[vmem] * 4 + [away] * 6 + [vmem] * 2,
        out_shape=[
            jax.ShapeDtypeStruct((total, cols), BF),
            jax.ShapeDtypeStruct((rows, width), F32),
            jax.ShapeDtypeStruct((rows, width), F32),
            jax.ShapeDtypeStruct((rows, 128), F32),
        ]
        + [jax.ShapeDtypeStruct(shape, kind) for shape, kind in held]
        + [jax.ShapeDtypeStruct((cols, total), F32), jax.ShapeDtypeStruct((8, total), F32)],
        scratch_shapes=[pltpu.VMEM(shape, kind) for shape, kind in held]
        + [pltpu.VMEM((LANES, total), BF), pltpu.SemaphoreType.DMA((len(held),))],
        compiler_params=params(40),
        cost_estimate=cost(14),
    )(me, *mixed, *frames, *norm, *weights, *biases, *features)


def attention_grad_kernel(q_block, heads, *refs):
    pieces = refs[:4]
    (q_ref, qt_ref, k_ref, v_ref, ot_ref, lse_ref, wq_ref, wk_ref, wv_ref,
     back_ref, gq_ref, gk_ref, gv_ref, sum_ref,
     go_ref, got_ref, kt_ref, delta_ref, dqt_ref, dk_ref, dv_ref) = refs[4:]
    rows = pieces[0].shape[0]
    total = 4 * rows
    cols_all = heads * HD
    scale = HD ** (-0.5)
    go_ref[...] = jnp.zeros_like(go_ref)
    for n in range(4):
        go_ref[n * rows : (n + 1) * rows, :cols_all] = pieces[n][...]
    got_ref[...] = go_ref[...].astype(F32).T.astype(BF)
    kt_ref[...] = k_ref[...].astype(F32).T.astype(BF)
    for head in range(heads):
        own = slice(HD * head, HD * (head + 1))
        delta_ref[head : head + 1, :] = jnp.sum(
            got_ref[own, :].astype(F32) * ot_ref[own, :], axis=0, keepdims=True
        )
    lane = iota((1, LANES), 1)
    for head in range(heads):
        own = slice(HD * head, HD * (head + 1))
        mask = (lane // HD == head).astype(F32).astype(BF)
        for start in range(0, total, q_block):
            cols = slice(start, start + q_block)
            scores = dot(k_ref[...], head_rows(qt_ref[:, cols], head, heads))
            probs = jnp.exp(scores - lse_ref[head : head + 1, cols])
            prob_grad = dot(v_ref[...], head_rows(got_ref[:, cols], head, heads))
            score_grad = (probs * (prob_grad - delta_ref[head : head + 1, cols])).astype(BF)
            value_part = dot(probs.astype(BF), go_ref[cols, :] * mask)
            key_part = dot(score_grad, q_ref[cols, :] * mask)
            if head == 0 and start == 0:
                dv_ref[...] = value_part
                dk_ref[...] = key_part
            else:
                dv_ref[...] += value_part
                dk_ref[...] += key_part
            dqt_ref[own, cols] = dot(kt_ref[own, :], score_grad)
    dqt_ref[cols_all:, :] = jnp.zeros((LANES - cols_all, total), F32)
    sums_q = jnp.zeros((1, LANES), F32)
    sums_v = jnp.zeros((1, LANES), F32)
    for n in range(4):
        here = slice(n * rows, (n + 1) * rows)
        query_grad = dqt_ref[:, here].T * scale
        value_grad = dv_ref[here, :]
        sums_q = sums_q + jnp.sum(query_grad, axis=0, keepdims=True)
        sums_v = sums_v + jnp.sum(value_grad, axis=0, keepdims=True)
        low_q = query_grad.astype(BF)
        low_k = dk_ref[here, :].astype(BF)
        low_v = value_grad.astype(BF)
        gq_ref[here, :] = low_q[:, :cols_all]
        gk_ref[here, :] = low_k[:, :cols_all]
        gv_ref[here, :] = low_v[:, :cols_all]
        back = dot(low_q, wq_ref[...]) + dot(low_k, wk_ref[...]) + dot(low_v, wv_ref[...])
        back_ref[here, :] = back.astype(BF)
    sum_ref[0:1, :] = sums_q
    sum_ref[1:2, :] = sums_v
    sum_ref[2:, :] = jnp.zeros((6, LANES), F32)


def attention_grad(pieces, saved, weights, heads, q_block=512):
    rows, cols = pieces[0].shape
    total = 4 * rows
    width = weights[0].shape[1]
    return pl.pallas_call(
        functools.partial(attention_grad_kernel, q_block, heads),
        out_shape=[
            jax.ShapeDtypeStruct((total, width), BF),
            jax.ShapeDtypeStruct((total, cols), BF),
            jax.ShapeDtypeStruct((total, cols), BF),
            jax.ShapeDtypeStruct((total, cols), BF),
            jax.ShapeDtypeStruct((8, LANES), F32),
        ],
        scratch_shapes=[
            pltpu.VMEM((total, LANES), BF),
            pltpu.VMEM((LANES, total), BF),
            pltpu.VMEM((LANES, total), BF),
            pltpu.VMEM((8, total), F32),
            pltpu.VMEM((LANES, total), F32),
            pltpu.VMEM((total, LANES), F32),
            pltpu.VMEM((total, LANES), F32),
        ],
        compiler_params=params(40),
        cost_estimate=cost(13),
    )(*pieces, *saved, *weights)


def feed_kernel(a0_ref, a1_ref, a2_ref, a3_ref, normed_ref, ow_ref, ob_ref, gain_ref, bias_ref,
                up_ref, ub_ref, down_ref,
                low_ref, act_ref, slope_ref, sum_ref, own_ref, hat_ref, inv_ref):
    n = pl.program_id(0)
    part = a0_ref.shape[1]
    total = normed_ref[...] + ob_ref[...]
    for i, ref in enumerate((a0_ref, a1_ref, a2_ref, a3_ref)):
        total = total + dot(ref[...], ow_ref[i * part : (i + 1) * part, :])
    hat, inv = norm_stats(total)
    normed = hat * gain_ref[...] + bias_ref[...]

    @pl.when(n == 0)
    def _():
        own_ref[...] = normed
        hat_ref[...] = hat
        inv_ref[...] = jnp.broadcast_to(inv, inv_ref.shape)

    low = normed.astype(BF)
    low_ref[...] = low
    value, slope = phi_pair(dot(low, up_ref[...]) + ub_ref[...])
    slope_ref[...] = slope
    value = value.astype(BF)
    act_ref[...] = value
    sum_ref[...] = dot(value, down_ref[...]).astype(BF)


def feed(attended, normed, out_all, out_bias, norm, up_weight, up_bias, down_weight):
    total, width = normed.shape
    rows = total // 4
    part = attended[0].shape[1]
    units = up_weight.shape[1]
    here = lambda n: (n, 0)
    return pl.pallas_call(
        feed_kernel,
        grid=(4,),
        in_specs=[block((rows, part), lambda n, i=i: (n ^ i, 0)) for i in range(4)]
        + [
            block((rows, width), here),
            full((width, width)),
            full((1, width)),
            full((1, width)),
            full((1, width)),
            full((width, units)),
            full((1, units)),
            full((units, width)),
        ],
        out_specs=[
            block((rows, width), here),
            block((rows, units), here),
            block((rows, units), here),
            block((rows, width), here),
            full((rows, width)),
            full((rows, width)),
            full((rows, 128)),
        ],
        out_shape=[
            jax.ShapeDtypeStruct((total, width), BF),
            jax.ShapeDtypeStruct((total, units), BF),
            jax.ShapeDtypeStruct((total, units), F32),
            jax.ShapeDtypeStruct((total, width), BF),
            jax.ShapeDtypeStruct((rows, width), F32),
            jax.ShapeDtypeStruct((rows, width), F32),
            jax.ShapeDtypeStruct((rows, 128), F32),
        ],
        compiler_params=params(32),
        cost_estimate=cost(10),
    )(*attended, normed, out_all, out_bias, *norm, up_weight, up_bias, down_weight)


def feed_grad_kernel(g0_ref, g1_ref, g2_ref, g3_ref, slope_ref, up_ref, down_ref,
                     all_ref, low_ref, sum_ref, bias_ref):
    n = pl.program_id(0)
    for i, ref in enumerate((g0_ref, g1_ref, g2_ref, g3_ref)):

        @pl.when(n == i)
        def _():
            all_ref[...] = ref[...]

    grad = dot_turned(all_ref[...], down_ref[...]) * slope_ref[...]

    @pl.when(n == 0)
    def _():
        bias_ref[...] = jnp.zeros_like(bias_ref)

    bias_ref[...] += jnp.sum(grad, axis=0, keepdims=True)
    low = grad.astype(BF)
    low_ref[...] = low
    sum_ref[...] = dot_turned(low, up_ref[...]).astype(BF)


def feed_grad(grads, slope, up_weight, down_weight):
    total, units = slope.shape
    rows, width = grads[0].shape
    here = lambda n: (n, 0)
    return pl.pallas_call(
        feed_grad_kernel,
        grid=(4,),
        in_specs=[full((rows, width))] * 4
        + [block((rows, units), here), full((width, units)), full((units, width))],
        out_specs=[
            block((rows, width), here),
            block((rows, units), here),
            block((rows, width), here),
            full((1, units)),
        ],
        out_shape=[
            jax.ShapeDtypeStruct((total, width), BF),
            jax.ShapeDtypeStruct((total, units), BF),
            jax.ShapeDtypeStruct((total, width), BF),
            jax.ShapeDtypeStruct((1, units), F32),
        ],
        compiler_params=params(24),
        cost_estimate=cost(6),
    )(*grads, slope, up_weight, down_weight)


def swap(value, bit):
    return lax.ppermute(value, "tp", [(i, i ^ bit) for i in range(lax.axis_size("tp"))])


def gather_pieces(value):
    across = swap(value, 2)
    return [value, across, swap(value, 1), swap(across, 1)]


def scatter_sum(terms):
    half = terms.shape[0] // 2
    piece = half // 2
    pair = terms[:half].astype(F32) + swap(terms[half:], 1).astype(F32)
    return pair[:piece] + swap(pair[piece:].astype(BF), 2).astype(F32)


def exchange(blocks):
    rows = blocks[0].shape[0]
    near = swap(jnp.concatenate(blocks[2:], axis=0), 1)
    far = swap(jnp.concatenate([blocks[1], near[rows:]], axis=0), 2)
    return [blocks[0], far[:rows], near[:rows], far[rows:]]


def after(value, *others):
    return lax.optimization_barrier((value, *others))[0]


def all_after(values, *others):
    return list(lax.optimization_barrier((*values, *others))[: len(values)])


def team_groups(row_count, team):
    if row_count == team:
        return None
    return [list(range(first, first + team)) for first in range(0, row_count, team)]


def cross_groups(row_count, team):
    return [list(range(first, row_count, team)) for first in range(team)]


def pair_rows(value, mask):
    count = lax.axis_size("rows")
    return lax.ppermute(value, "rows", [(i, i ^ mask) for i in range(count)])


def row_steps(team):
    me = lax.axis_index("rows")
    bits = [(me >> i) & 1 for i in range(team.bit_length() - 1)]
    if team == 8:
        return [(1, bits[0]), (2, bits[1] ^ bits[2]), (6, bits[2])]
    return [(1 << i, bit) for i, bit in enumerate(bits)]


def halve(value, mask, side):
    half = value.shape[0] // 2
    kept = lax.dynamic_slice_in_dim(value, side * half, half, 0)
    sent = lax.dynamic_slice_in_dim(value, (1 - side) * half, half, 0)
    return kept, pair_rows(sent, mask)


def add_low(kept, came):
    return (kept.astype(F32) + came.astype(F32)).astype(BF)


def gather_team(value, masks):
    held, offsets = value[None], [0]
    for mask in masks:
        held = jnp.concatenate([held, pair_rows(held, mask)], axis=0)
        offsets = offsets + [x ^ mask for x in offsets]
    return held, offsets


def on_device(
    frames,
    seg_starts,
    conv_weight,
    conv_bias,
    norm_gain0,
    norm_bias0,
    qkv_weight,
    qv_bias,
    out_weight,
    out_bias,
    norm_gain1,
    norm_bias1,
    up_weight,
    up_bias,
    down_weight,
    down_bias,
    norm_gain2,
    norm_bias2,
    cotangent,
):
    head_cols = qkv_weight.shape[2]
    heads_here = head_cols // HD
    groups_here = conv_weight.shape[2] // GW
    team = 2 * groups_here
    row_count = lax.axis_size("rows")
    teams = team_groups(row_count, team)
    me = lax.axis_index("tp")
    own_row = lax.axis_index("rows") % team
    positions = jnp.arange(LEN, dtype=jnp.int32)
    segments = (
        jnp.sum((positions[:, None] >= seg_starts[0][None, :]).astype(jnp.int32), axis=1) - 1
    )
    line = lambda value: value.astype(F32).reshape(1, -1)

    channels = lax.all_to_all(frames, "tp", split_axis=1, concat_axis=0, tiled=True)
    slots = spread_slots(segments)
    put = (iota((SLOTS, LEN), 0) == slots[None, :]).astype(BF)
    ext = extension()
    conv_flat = conv_weight.reshape(KER * GW, -1)
    toeplitz = toeplitz_weights(conv_flat, groups_here)
    bias_lanes = jnp.tile(conv_bias.astype(F32).reshape(groups_here, 1, GW), (1, 1, PH))
    bias_lanes = jnp.pad(bias_lanes, ((0, 0), (0, 0), (0, LANES - PH * GW)))
    frames_pieces = gather_pieces(frames)
    out_pieces = gather_pieces(out_weight)
    out_all = jnp.concatenate(out_pieces, axis=0)
    signal = after(channels, *frames_pieces, out_all)
    mixed_low, slope0, core = conv(signal, put, ext, toeplitz, bias_lanes)

    seg_rows = segments.reshape(4, -1)
    seg_own = jnp.concatenate(
        [lax.dynamic_index_in_dim(seg_rows, me ^ m, 0, keepdims=False) for m in ORDER]
    )
    lane = jnp.arange(LANES, dtype=jnp.int32)[None, :] - head_cols
    in_seg = lane == seg_own[:, None]
    of_seg = (lane >= 0) & (lane < seg_starts.shape[1])
    features = [
        jnp.where(in_seg, MASK_ROOT, 0.0).astype(BF),
        jnp.where(of_seg & ~in_seg, -MASK_ROOT, 0.0).astype(BF),
    ]
    qkv_padded = jnp.pad(
        qkv_weight.transpose(1, 2, 0), ((0, 0), (0, LANES - head_cols), (0, 0))
    )
    qkv_parts = [qkv_padded[0], qkv_padded[1], qkv_padded[2]]
    qv_padded = jnp.pad(qv_bias.astype(F32), ((0, 0), (0, LANES - head_cols)))
    gain0 = line(norm_gain0)
    mixed_pieces = gather_pieces(mixed_low)
    core_all = lax.all_to_all(
        jnp.repeat(core, 2, axis=0), "rows", 0, 0, axis_index_groups=teams, tiled=True
    )
    (attended, normed0, hat0, inv0, normed0_all, normed0_low, *saved) = attention(
        me.reshape(1).astype(jnp.int32),
        mixed_pieces,
        frames_pieces,
        [gain0, line(norm_bias0)],
        qkv_parts,
        [qv_padded[0:1], qv_padded[1:2]],
        features,
        heads_here,
    )

    attended = after(attended, core_all)
    attended_pieces = gather_pieces(attended)
    gain1 = line(norm_gain1)
    normed1_low, activated, slope1, ffn_terms, normed1, hat1, inv1 = feed(
        attended_pieces,
        normed0_all,
        out_all,
        line(out_bias),
        [gain1, line(norm_bias1)],
        up_weight,
        line(up_bias),
        down_weight,
    )
    ffn_sum = scatter_sum(ffn_terms)
    gain2 = line(norm_gain2)
    hat2, inv2 = norm_stats(normed1 + ffn_sum + line(down_bias))
    block_out = (hat2 * gain2 + line(norm_bias2)).astype(BF)

    grad2, gain2_grad, bias2_grad = norm_backward(cotangent.astype(F32), hat2, inv2, gain2)
    down_bias_grad = jnp.sum(grad2, axis=0)
    grad2_all, up_low, up_terms, up_bias_grad = feed_grad(
        gather_pieces(grad2.astype(BF)), slope1, up_weight, down_weight
    )
    ffn_back = scatter_sum(up_terms)
    down_grad = jnp.einsum("rf,rd->fd", activated, grad2_all, preferred_element_type=F32)
    up_grad = jnp.einsum("rd,rf->df", normed1_low, up_low, preferred_element_type=F32)
    feed_grads = jnp.stack([down_grad.astype(BF), up_grad.astype(BF)])
    ffn_back = after(ffn_back, feed_grads)
    feed_total = lax.psum(feed_grads, "rows")
    grad1, gain1_grad, bias1_grad = norm_backward(grad2 + ffn_back, hat1, inv1[:, :1], gain1)
    out_bias_grad = jnp.sum(grad1, axis=0)

    grad1_low = grad1.astype(BF)
    attended_back = jnp.einsum("rd,hd->rh", grad1_low, out_all, preferred_element_type=F32)
    attended_back = attended_back.astype(BF)
    attended_grad = exchange(
        [attended_back[:, i * head_cols : (i + 1) * head_cols] for i in range(4)]
    )
    back, query_grad, key_grad, value_grad, qv_sums = attention_grad(
        attended_grad, saved, qkv_parts, heads_here
    )
    grad1_pieces = gather_pieces(after(grad1_low, *attended_grad))
    back = after(back, *grad1_pieces)
    attn_back = scatter_sum(back)
    out_grad = jnp.einsum(
        "rh,rd->hd", attended, jnp.concatenate(grad1_pieces, axis=0), preferred_element_type=F32
    )
    turned_grads = [
        jnp.einsum("rc,rd->cd", part, normed0_low, preferred_element_type=F32).astype(BF)
        for part in (query_grad, key_grad, value_grad)
    ]
    tail = jnp.concatenate(turned_grads + [out_grad.astype(BF)], axis=0)
    attn_back = after(attn_back, tail)
    qv_grad = qv_sums[:2, :head_cols]
    grad0, gain0_grad, bias0_grad = norm_backward(grad1 + attn_back, hat0, inv0[:, :1], gain0)

    mixed_grad = lax.all_to_all(
        grad0.astype(BF), "tp", split_axis=1, concat_axis=0, tiled=True
    )
    tail = after(tail, grad0)
    steps = row_steps(team)
    tail_kept, tail_came = halve(tail, *steps[1])
    toeplitz = toeplitz_weights(after(conv_flat, grad0), groups_here)
    mixed_grad = after(mixed_grad, toeplitz)
    wide, halves, conv_bias_grad = conv_grad(mixed_grad, put, slope0, ext)
    conv_bias_grad = conv_bias_grad[:, 0, : PH * GW].reshape(groups_here, PH, GW)
    conv_bias_grad = jnp.sum(conv_bias_grad, axis=1).reshape(-1)
    halves_all = lax.all_to_all(halves, "rows", 0, 0, axis_index_groups=teams, tiled=True)
    tail_kept, tail_came = halve(
        add_low(after(tail_kept, halves), tail_came), *steps[2]
    )
    signal_back = signal_grad(wide, toeplitz, put)
    frames_back = lax.all_to_all(signal_back, "tp", split_axis=0, concat_axis=1, tiled=True)
    frames_grad = grad0 + frames_back.astype(F32)
    tail_kept, tail_came = halve(
        add_low(after(tail_kept, signal_back), tail_came), *steps[0]
    )
    halves_all = after(halves_all, signal_back, tail_kept)
    kernel_part = tap_grad(core_all, halves_all, ext)
    tail_part = add_low(tail_kept, after(tail_came, kernel_part))
    kernel_part = after(kernel_part, feed_total)

    all_small = [
        gain0_grad, bias0_grad, out_bias_grad, gain1_grad, bias1_grad, down_bias_grad, gain2_grad,
        bias2_grad,
    ]
    rows_small = [conv_bias_grad, qv_grad, up_bias_grad]
    shared = jnp.stack(all_small)
    shared = shared + swap(shared, 1)
    shared = shared + swap(shared, 2)
    small = jnp.concatenate([shared.reshape(-1)] + [v.reshape(-1) for v in rows_small])
    small_size = small.size
    small = jnp.pad(small, (0, -small_size % (16 * KER))).reshape(-1, KER)
    if teams is not None:
        others = cross_groups(row_count, team)
        kernel_part = lax.psum(kernel_part, "rows", axis_index_groups=others)
        tail_part = lax.psum(tail_part.astype(F32), "rows", axis_index_groups=others)
        small = lax.psum(small, "rows", axis_index_groups=others)
    small_high = small.astype(BF)
    small_low = (small - small_high.astype(F32)).astype(BF)
    part_rows = kernel_part.shape[0] // 2
    part_low = kernel_part.astype(BF)
    masks = [1, 2, 6] if team == 8 else [1 << i for i in range(team.bit_length() - 1)]
    tail_low = tail_part.astype(BF).reshape(2, -1, KER)
    held_a, offsets_a = gather_team(
        jnp.concatenate([part_low[:part_rows], tail_low[0], small_high], axis=0),
        masks[1:] + masks[:1],
    )
    held_b, offsets_b = gather_team(
        jnp.concatenate([part_low[part_rows:], tail_low[1], small_low], axis=0), masks
    )
    order = jnp.array(
        [[offsets.index(x) for x in range(team)] for offsets in (offsets_a, offsets_b)], jnp.int32
    )
    if team == 8:
        holders = jnp.array([0, 1, 6, 7, 2, 3, 4, 5], jnp.int32)
    tail_order = order[:, holders ^ own_row]
    order = order[:, jnp.arange(team, dtype=jnp.int32) ^ own_row]
    kernel_total = assemble(order, held_a, held_b).transpose(2, 0, 1)
    tail_rows = tail_low.shape[1]
    small = jnp.sum(held_a[:, part_rows + tail_rows :].astype(F32), axis=0) + jnp.sum(
        held_b[:, part_rows + tail_rows :].astype(F32), axis=0
    )
    tail_total = jnp.stack(
        [
            held[:, part_rows : part_rows + tail_rows][tail_order[i]]
            for i, held in enumerate((held_a, held_b))
        ],
        axis=1,
    )
    tail_total = tail_total.reshape(-1, D).astype(F32)
    qkv_total = tail_total[: 3 * head_cols].reshape(3, head_cols, D).transpose(2, 0, 1)
    out_total = tail_total[3 * head_cols :]
    small = small.reshape(-1)[:small_size]
    sizes = [v.size for v in all_small + rows_small]
    ends = [sum(sizes[: i + 1]) for i in range(len(sizes))]
    cuts = [small[end - size : end] for size, end in zip(sizes, ends)]
    gain0_grad, bias0_grad, out_bias_grad, gain1_grad, bias1_grad = cuts[:5]
    down_bias_grad, gain2_grad, bias2_grad, conv_bias_grad, qv_grad, up_bias_grad = cuts[5:]
    feed_total = feed_total.astype(F32)
    return (
        block_out,
        frames_grad,
        kernel_total,
        conv_bias_grad,
        gain0_grad,
        bias0_grad,
        qkv_total,
        qv_grad.reshape(2, head_cols),
        out_total,
        out_bias_grad,
        gain1_grad,
        bias1_grad,
        feed_total[1],
        up_bias_grad,
        feed_total[0],
        down_bias_grad,
        gain2_grad,
        bias2_grad,
    )


def solution(mesh):
    return jax.shard_map(
        on_device,
        mesh=mesh,
        in_specs=(
            P(("rows", "tp"), None),
            P("rows", None),
            P(None, None, "tp"),
            P("tp"),
            P(),
            P(),
            P(None, None, "tp"),
            P(None, "tp"),
            P("tp", None),
            P(),
            P(),
            P(),
            P(None, "tp"),
            P("tp"),
            P("tp", None),
            P(),
            P(),
            P(),
            P(("rows", "tp"), None),
        ),
        out_specs=(
            P(("rows", "tp"), None),
            P(("rows", "tp"), None),
            P(None, None, "tp"),
            P("tp"),
            P(),
            P(),
            P(None, None, "tp"),
            P(None, "tp"),
            P("tp", None),
            P(),
            P(),
            P(),
            P(None, "tp"),
            P("tp"),
            P("tp", None),
            P(),
            P(),
            P(),
        ),
        check_vma=False,
    )
```

```python
import functools

import jax
import jax.numpy as jnp
import numpy as np
from jax import lax
from jax.experimental import pallas as pl
from jax.experimental.pallas import tpu as pltpu
from jax.sharding import PartitionSpec as P

D = 768
HD = 64
KER = 128
GROUPS = 16
LEN = 1024

EPSILON = 1e-05
ROOT_HALF = 0.7071067811865476
INV_ROOT_TAU = 0.3989422804014327
MASK_ROOT = 16384.0

GW = D // GROUPS
HALF = GW // 2
PH = 5
QN, PN = 17, 16
CORE = QN * PN
NJ = 27
LEAD = 13
EXT = (QN + NJ - 1) * PN
LANES = 256
GAP = KER // 2
SLOTS = PH * CORE
WIDE_MIB = 58

ORDER = (0, 2, 1, 3)

BF = jnp.bfloat16
F32 = jnp.float32


def iota(shape, dim):
    return lax.broadcasted_iota(jnp.int32, shape, dim)


def full(shape):
    return pl.BlockSpec(shape, lambda *index: (0,) * len(shape))


def block(shape, index_map):
    return pl.BlockSpec(shape, index_map)


def params(mib):
    return pltpu.CompilerParams(vmem_limit_bytes=mib * 2**20)


def cost(microseconds):
    return pl.CostEstimate(
        flops=int(microseconds * 1.1e9), bytes_accessed=int(microseconds * 1e6), transcendentals=0
    )


def dot(left, right):
    return jnp.dot(left, right, preferred_element_type=F32)


def dot_turned(left, right):
    return lax.dot_general(left, right, (((1,), (1,)), ((), ())), preferred_element_type=F32)


def phi_pair(v):
    cdf = 0.5 * (1.0 + lax.erf(v * ROOT_HALF))
    return v * cdf, cdf + v * INV_ROOT_TAU * jnp.exp(-0.5 * v * v)


def norm_stats(inputs):
    centered = inputs - jnp.mean(inputs, axis=-1, keepdims=True)
    inv_std = lax.rsqrt(jnp.mean(centered * centered, axis=-1, keepdims=True) + EPSILON)
    return centered * inv_std, inv_std


def spread_slots(segments):
    place = jnp.arange(LEN, dtype=jnp.int32) + GAP * segments
    at = place // PH
    return place % PH * CORE + at % QN * PN + at // QN


def extension():
    row, col = np.arange(EXT)[:, None], np.arange(CORE)[None, :]
    want = QN * (row % PN) + row // PN - LEAD
    have = QN * (col % PN) + col // PN
    return jnp.asarray((want == have).astype(np.float32), BF)


def toeplitz_kernel(w_ref, out_ref, wide_ref):
    g = pl.program_id(0)
    before = PH * GW
    after = wide_ref.shape[0] - before - KER * GW
    row, lane = iota((w_ref.shape[1], LANES), 0), iota((w_ref.shape[1], LANES), 1)
    spread = ((row == GW * g + lane % GW) & (lane < PH * GW)).astype(F32).astype(BF)
    wide_ref[0:before, :] = jnp.zeros((before, LANES), BF)
    wide_ref[before + KER * GW :, :] = jnp.zeros((after, LANES), BF)
    wide_ref[before : before + KER * GW, :] = dot(w_ref[...], spread).astype(BF)
    lane = iota((1, LANES), 1)
    masks = [(lane // GW == i).astype(F32).astype(BF) for i in range(PH)]

    def place(j, carry):
        for left in range(0, LANES, 128):
            lanes = slice(left, left + 128)
            total = None
            for i in range(left // GW, min((left + 127) // GW + 1, PH)):
                start = pl.multiple_of(before + PH * GW * j - GW * (1 + i), 16)
                part = wide_ref[pl.ds(start, PH * GW), lanes] * masks[i][:, lanes]
                total = part if total is None else total + part
            out_ref[0, pl.ds(pl.multiple_of(j * LANES, LANES), PH * GW), lanes] = total
        out_ref[0, pl.ds(pl.multiple_of(j * LANES + PH * GW, 16), LANES - PH * GW), :] = jnp.zeros(
            (LANES - PH * GW, LANES), BF
        )
        return carry

    lax.fori_loop(0, NJ, place, 0)


def toeplitz_weights(kernel_flat, groups):
    return pl.pallas_call(
        toeplitz_kernel,
        grid=(groups,),
        in_specs=[full((KER * GW, groups * GW))],
        out_specs=block((1, NJ * LANES, LANES), lambda g: (g, 0, 0)),
        out_shape=jax.ShapeDtypeStruct((groups, NJ * LANES, LANES), BF),
        scratch_shapes=[pltpu.VMEM((PH * GW + KER * GW + 288, LANES), BF)],
        compiler_params=params(WIDE_MIB),
        cost_estimate=cost(11),
    )(kernel_flat)


def fold_in(slots_ref, g):
    width = slots_ref.shape[1]
    row, lane = iota((width, LANES), 0), iota((width, LANES), 1)
    core = jnp.zeros((CORE, LANES), F32)
    for i in range(PH):
        pick = ((lane // GW == i) & (row == GW * g + lane % GW)).astype(F32).astype(BF)
        core = core + dot(slots_ref[i * CORE : (i + 1) * CORE, :], pick)
    return core


def fold_out(values, back_ref, g):
    width = back_ref.shape[1]
    row, col = iota((LANES, width), 0), iota((LANES, width), 1)
    for i in range(PH):
        pick = ((row // GW == i) & (col == GW * g + row % GW)).astype(F32).astype(BF)
        here = slice(i * CORE, (i + 1) * CORE)
        back_ref[here, :] = back_ref[here, :] + dot(values, pick).astype(BF)


def unspread(back_ref, put_ref):
    turned = back_ref[...].astype(F32).T.astype(BF)
    return dot(turned, put_ref[...]).T.astype(BF)


def conv_kernel(me_ref, f0_ref, f1_ref, f2_ref, f3_ref, put_ref, ext_ref, wt_ref, bias_ref,
                mixed_ref, slope_ref, core_ref, sig_ref, slots_ref, wide_ref, back_ref):
    g = pl.program_id(0)
    rows, features = f0_ref.shape
    width = sig_ref.shape[1]

    @pl.when(g == 0)
    def _():
        row, lane = iota((features, width), 0), iota((features, width), 1)
        pick = (row == lane + width * me_ref[0]).astype(F32).astype(BF)
        for n, ref in enumerate((f0_ref, f1_ref, f2_ref, f3_ref)):
            start = pl.multiple_of((me_ref[0] ^ ORDER[n]) * rows, rows)
            sig_ref[pl.ds(start, rows), :] = dot(ref[...], pick).astype(BF)
        slots_ref[...] = dot(put_ref[...], sig_ref[...]).astype(BF)
        back_ref[...] = jnp.zeros_like(back_ref)

    core = fold_in(slots_ref, g).astype(BF)
    core_ref[0] = core
    wide_ref[...] = dot(ext_ref[...], core).astype(BF)
    total = jnp.zeros((CORE, LANES), F32)
    for j in range(NJ):
        total = total + dot(
            wide_ref[PN * j : PN * j + CORE, :], wt_ref[0, j * LANES : (j + 1) * LANES, :]
        )
    value, slope = phi_pair(total + bias_ref[0])
    slope_ref[0] = slope
    fold_out(value.astype(BF), back_ref, g)

    @pl.when(g == pl.num_programs(0) - 1)
    def _():
        mixed_ref[...] = unspread(back_ref, put_ref)


def conv(me, frames, put, ext, toeplitz, bias_lanes):
    groups = toeplitz.shape[0]
    width = groups * GW
    return pl.pallas_call(
        conv_kernel,
        grid=(groups,),
        in_specs=[pl.BlockSpec(memory_space=pltpu.SMEM)]
        + [full(frames[0].shape)] * 4
        + [
            full((SLOTS, LEN)),
            full((EXT, CORE)),
            block((1, NJ * LANES, LANES), lambda g: (g, 0, 0)),
            block((1, 1, LANES), lambda g: (g, 0, 0)),
        ],
        out_specs=[
            full((LEN, width)),
            block((1, CORE, LANES), lambda g: (g, 0, 0)),
            block((1, CORE, LANES), lambda g: (g, 0, 0)),
        ],
        out_shape=[
            jax.ShapeDtypeStruct((LEN, width), BF),
            jax.ShapeDtypeStruct((groups, CORE, LANES), F32),
            jax.ShapeDtypeStruct((groups, CORE, LANES), BF),
        ],
        scratch_shapes=[
            pltpu.VMEM((LEN, width), BF),
            pltpu.VMEM((SLOTS, width), BF),
            pltpu.VMEM((EXT, LANES), BF),
            pltpu.VMEM((SLOTS, width), BF),
        ],
        compiler_params=params(WIDE_MIB),
        cost_estimate=cost(15),
    )(me, *frames, put, ext, toeplitz, bias_lanes)


def conv_grad_kernel(me_ref, keep_ref, far_ref, near_ref, put_ref, slope_ref, ext_ref,
                     wide_ref, half_ref, bias_ref, grad_ref, slots_ref):
    g = pl.program_id(0)
    rows = far_ref.shape[0] // 2

    @pl.when(g == 0)
    def _():
        for n, piece in enumerate(came_pieces(keep_ref, far_ref, near_ref)):
            start = pl.multiple_of((me_ref[0] ^ ORDER[n]) * rows, rows)
            grad_ref[pl.ds(start, rows), :] = piece
        slots_ref[...] = dot(put_ref[...], grad_ref[...]).astype(BF)

    grad = fold_in(slots_ref, g) * slope_ref[0]
    bias_ref[0] = jnp.sum(grad, axis=0, keepdims=True)
    low = grad.astype(BF)
    wide_ref[0] = dot(ext_ref[...], low).astype(BF)
    row, lane = iota((LANES, 128), 0), iota((LANES, 128), 1)
    for h in range(2):
        pick = (lane < PH * HALF) & (row == lane // HALF * GW + lane % HALF + h * HALF)
        half_ref[h] = dot(low, pick.astype(F32).astype(BF)).astype(BF)


def conv_grad(me, came, put, slope, ext):
    groups = slope.shape[0]
    width = came[0].shape[1]
    return pl.pallas_call(
        conv_grad_kernel,
        grid=(groups,),
        in_specs=[
            pl.BlockSpec(memory_space=pltpu.SMEM),
            full((LEN // 2, width)),
            full((LEN // 2, width)),
            full((LEN // 2, width)),
            full((SLOTS, LEN)),
            block((1, CORE, LANES), lambda g: (g, 0, 0)),
            full((EXT, CORE)),
        ],
        out_specs=[
            block((1, EXT, LANES), lambda g: (g, 0, 0)),
            block((2, CORE, 128), lambda g: (g, 0, 0)),
            block((1, 1, LANES), lambda g: (g, 0, 0)),
        ],
        out_shape=[
            jax.ShapeDtypeStruct((groups, EXT, LANES), BF),
            jax.ShapeDtypeStruct((2 * groups, CORE, 128), BF),
            jax.ShapeDtypeStruct((groups, 1, LANES), F32),
        ],
        scratch_shapes=[pltpu.VMEM((LEN, width), BF), pltpu.VMEM((SLOTS, width), BF)],
        compiler_params=params(WIDE_MIB),
        cost_estimate=cost(7),
    )(me, *came, put, slope, ext)


def signal_grad_kernel(me_ref, wide_ref, wt_ref, put_ref, keep_ref, near_ref, back_ref, all_ref):
    g = pl.program_id(0)
    rows = keep_ref.shape[0] // 2

    @pl.when(g == 0)
    def _():
        back_ref[...] = jnp.zeros_like(back_ref)

    total = jnp.zeros((CORE, LANES), F32)
    for j in range(NJ):
        m = NJ - 1 - j
        total = total + dot_turned(
            wide_ref[0, PN * j : PN * j + CORE, :], wt_ref[0, m * LANES : (m + 1) * LANES, :]
        )
    fold_out(total.astype(BF), back_ref, g)

    @pl.when(g == pl.num_programs(0) - 1)
    def _():
        all_ref[...] = unspread(back_ref, put_ref)
        for n in range(4):
            start = pl.multiple_of((me_ref[0] ^ ORDER[n]) * rows, rows)
            out_ref = keep_ref if n < 2 else near_ref
            out_ref[n % 2 * rows : (n % 2 + 1) * rows, :] = all_ref[pl.ds(start, rows), :]


def signal_grad(me, wide, toeplitz, put):
    groups = toeplitz.shape[0]
    width = groups * GW
    return pl.pallas_call(
        signal_grad_kernel,
        grid=(groups,),
        in_specs=[
            pl.BlockSpec(memory_space=pltpu.SMEM),
            block((1, EXT, LANES), lambda g: (g, 0, 0)),
            block((1, NJ * LANES, LANES), lambda g: (g, 0, 0)),
            full((SLOTS, LEN)),
        ],
        out_specs=[full((LEN // 2, width))] * 2,
        out_shape=[jax.ShapeDtypeStruct((LEN // 2, width), BF)] * 2,
        scratch_shapes=[pltpu.VMEM((SLOTS, width), BF), pltpu.VMEM((LEN, width), BF)],
        compiler_params=params(WIDE_MIB),
        cost_estimate=cost(12),
    )(me, wide, toeplitz, put)


def turn_core_kernel(sig_ref, ext_ref, out_ref, wide_ref):
    packs = sig_ref.shape[0]
    blocks = EXT // PN
    wide_ref[blocks:] = jnp.zeros((1, packs * PN, LANES), BF)
    for r in range(packs):
        rows = dot(ext_ref[...], sig_ref[r]).astype(BF)
        wide_ref[0:blocks, r * PN : (r + 1) * PN, :] = rows.reshape(blocks, PN, LANES)
    for q in range(blocks + 1):
        out_ref[:, q * 128 : (q + 1) * 128] = wide_ref[q].astype(F32).T.astype(BF)


def turn_core(sig, ext):
    packs = sig.shape[0]
    blocks = EXT // PN + 1
    return pl.pallas_call(
        turn_core_kernel,
        out_shape=jax.ShapeDtypeStruct((LANES, blocks * packs * PN), BF),
        scratch_shapes=[pltpu.VMEM((blocks, packs * PN, LANES), BF)],
        compiler_params=params(WIDE_MIB),
        cost_estimate=cost(6),
    )(sig, ext)


def tap_grad_kernel(sig_ref, grad_ref, out_ref, pair_ref, parts_ref, rows_ref):
    packs = grad_ref.shape[0]
    across = packs * PN
    pair_ref[QN, :, 0:128] = jnp.zeros((across, 128), BF)
    pair_ref[0, :, 128:] = jnp.zeros((across, 128), BF)
    for r in range(packs):
        rows = grad_ref[r].reshape(QN, PN, 128)
        pair_ref[0:QN, r * PN : (r + 1) * PN, 0:128] = rows
        pair_ref[1:, r * PN : (r + 1) * PN, 128:] = rows
    pair = pair_ref[...].reshape((QN + 1) * across, LANES)
    for j in range(0, NJ + 1, 2):
        part = dot(sig_ref[:, j * across : (j + QN + 1) * across], pair)
        parts_ref[PH * GW * j : PH * GW * (j + 1), :] = part[: PH * GW, 0:128]
        parts_ref[PH * GW * (j + 1) : PH * GW * (j + 2), :] = part[: PH * GW, 128:]
    phase = iota((1, 128), 1) // HALF
    chunk = 8 * GW

    def shift(step, carry):
        start = step * chunk
        total = jnp.zeros((chunk, 128), F32)
        for i in range(PH):
            rows = pl.ds(pl.multiple_of(start + GW * (1 + i), 8), chunk)
            total = jnp.where(phase == i, parts_ref[rows, :], total)
        rows_ref[pl.ds(pl.multiple_of(start, 8), chunk), :] = total
        return carry

    lax.fori_loop(0, KER * GW // chunk, shift, 0)
    for c in range(GW):
        taps = rows_ref[pl.ds(c, KER, stride=GW), :].T
        total = taps[0:HALF, :]
        for i in range(1, PH):
            total = total + taps[HALF * i : HALF * (i + 1), :]
        out_ref[c * HALF : (c + 1) * HALF, :] = total


def tap_grad(sig, grad):
    packs = grad.shape[0]
    return pl.pallas_call(
        tap_grad_kernel,
        out_shape=jax.ShapeDtypeStruct((GW * HALF, KER), F32),
        scratch_shapes=[
            pltpu.VMEM((QN + 1, packs * PN, LANES), BF),
            pltpu.VMEM(((NJ + 1) * PH * GW, 128), F32),
            pltpu.VMEM((KER * GW, 128), F32),
        ],
        compiler_params=params(WIDE_MIB),
        cost_estimate=cost(9),
    )(sig, grad)


def assemble_kernel(at_ref, a_ref, b_ref, out_ref, wide_ref):
    step = pl.program_id(0)
    packs = a_ref.shape[0]
    per_step = out_ref.shape[0]
    half_steps = pl.num_programs(0) // 2

    def place(held_ref, which):
        for r in range(packs):
            wide_ref[...] = held_ref[at_ref[which, r]].astype(F32)
            for c in range(per_step):
                out_ref[c, r * HALF : (r + 1) * HALF, :] = wide_ref[c * HALF : (c + 1) * HALF, :]

    @pl.when(step < half_steps)
    def _():
        place(a_ref, 0)

    @pl.when(step >= half_steps)
    def _():
        place(b_ref, 1)


def assemble(order, held_a, held_b):
    packs = held_a.shape[0]
    steps = 4
    per_step = GW // steps
    rows = per_step * HALF
    half = steps // 2
    return pl.pallas_call(
        assemble_kernel,
        grid=(steps,),
        in_specs=[
            pl.BlockSpec(memory_space=pltpu.SMEM),
            block((packs, rows, KER), lambda s: (0, jnp.minimum(s, half - 1), 0)),
            block((packs, rows, KER), lambda s: (0, jnp.maximum(s - half, 0), 0)),
        ],
        out_specs=block((per_step, packs * HALF, KER), lambda s: (s, 0, 0)),
        out_shape=jax.ShapeDtypeStruct((GW, packs * HALF, KER), F32),
        scratch_shapes=[pltpu.VMEM((rows, KER), F32)],
        compiler_params=params(WIDE_MIB),
        cost_estimate=cost(4),
    )(order, held_a, held_b)


def head_rows(turned, head, heads):
    pieces = [jnp.zeros((HD, turned.shape[1]), turned.dtype) for _ in range(heads)]
    pieces[head] = turned[HD * head : HD * (head + 1), :]
    return jnp.concatenate(pieces + [turned[HD * heads :, :]], axis=0)


def attention_kernel(q_block, heads, *refs):
    me_ref = refs[0]
    mixed = refs[1:5]
    frames = refs[5:9]
    (gain_ref, bias_ref, wq_ref, wk_ref, wv_ref, qb_ref, vb_ref, featq_ref, featk_ref) = refs[9:18]
    (att_ref, own_ref, hat_ref, inv_ref, all_out, low_out, q_out, qt_out, k_out, v_out, ot_ref,
     lse_ref) = refs[18:30]
    all_ref, low_ref, q_ref, qt_ref, k_ref, v_ref, vt_ref, sems = refs[30:]
    rows = frames[0].shape[0]
    part = mixed[0].shape[1]
    width = frames[0].shape[1]
    scale = HD ** (-0.5)
    me = me_ref[0]
    row, lane = iota((part, width), 0), iota((part, width), 1)
    spots = [(lane == row + part * (me ^ m)).astype(F32).astype(BF) for m in ORDER]
    for n in range(4):
        here = slice(n * rows, (n + 1) * rows)
        start = pl.multiple_of((me ^ ORDER[n]) * rows, rows)
        total = frames[n][...].astype(F32)
        for ref, spot in zip(mixed, spots):
            total = total + dot(ref[pl.ds(start, rows), :], spot)
        hat, inv = norm_stats(total)
        normed = hat * gain_ref[...] + bias_ref[...]
        if n == 0:
            own_ref[...] = normed
            hat_ref[...] = hat
            inv_ref[...] = jnp.broadcast_to(inv, inv_ref.shape)
        all_ref[here, :] = normed
        normed = normed.astype(BF)
        low_ref[here, :] = normed
        query = (dot_turned(normed, wq_ref[...]) + qb_ref[...]) * scale
        query = query + featq_ref[here, :].astype(F32)
        q_ref[here, :] = query.astype(BF)
        qt_ref[:, here] = query.T.astype(BF)
        key = dot_turned(normed, wk_ref[...])
        k_ref[here, :] = (key + featk_ref[here, :].astype(F32)).astype(BF)
        value = dot_turned(normed, wv_ref[...]) + vb_ref[...]
        v_ref[here, :] = value.astype(BF)
        vt_ref[:, here] = value.T.astype(BF)
    held = [all_ref, low_ref, q_ref, qt_ref, k_ref, v_ref]
    kept = [all_out, low_out, q_out, qt_out, k_out, v_out]
    copies = [
        pltpu.make_async_copy(src, dst, sems.at[i]) for i, (src, dst) in enumerate(zip(held, kept))
    ]
    for copy in copies:
        copy.start()
    total = 4 * rows
    for head in range(heads):
        for start in range(0, total, q_block):
            cols = slice(start, start + q_block)
            turned = head_rows(qt_ref[:, cols], head, heads)
            scores = dot(k_ref[...], turned)
            top = jnp.max(scores, axis=0, keepdims=True)
            weights = jnp.exp(scores - top)
            sums = jnp.sum(weights, axis=0, keepdims=True)
            value = dot(vt_ref[HD * head : HD * (head + 1), :], weights.astype(BF))
            ot_ref[HD * head : HD * (head + 1), cols] = value / sums
            lse_ref[head : head + 1, cols] = top + jnp.log(sums)
    lse_ref[heads:, :] = jnp.zeros((8 - heads, total), F32)
    for n in range(4):
        here = slice(n * rows, (n + 1) * rows)
        att_ref[here, :] = ot_ref[:, here].T.astype(BF)
    for copy in copies:
        copy.wait()


def attention(me, mixed, frames, norm, weights, biases, features, heads, q_block=512):
    rows, width = frames[0].shape
    total = 4 * rows
    cols = heads * HD
    vmem = pl.BlockSpec(memory_space=pltpu.VMEM)
    away = pl.BlockSpec(memory_space=pltpu.HBM)
    held = [
        ((total, width), F32),
        ((total, width), BF),
        ((total, LANES), BF),
        ((LANES, total), BF),
        ((total, LANES), BF),
        ((total, LANES), BF),
    ]
    return pl.pallas_call(
        functools.partial(attention_kernel, q_block, heads),
        in_specs=[pl.BlockSpec(memory_space=pltpu.SMEM)] + [vmem] * 17,
        out_specs=[vmem] * 4 + [away] * 6 + [vmem] * 2,
        out_shape=[
            jax.ShapeDtypeStruct((total, cols), BF),
            jax.ShapeDtypeStruct((rows, width), F32),
            jax.ShapeDtypeStruct((rows, width), F32),
            jax.ShapeDtypeStruct((rows, 128), F32),
        ]
        + [jax.ShapeDtypeStruct(shape, kind) for shape, kind in held]
        + [jax.ShapeDtypeStruct((cols, total), F32), jax.ShapeDtypeStruct((8, total), F32)],
        scratch_shapes=[pltpu.VMEM(shape, kind) for shape, kind in held]
        + [pltpu.VMEM((LANES, total), BF), pltpu.SemaphoreType.DMA((len(held),))],
        compiler_params=params(WIDE_MIB),
        cost_estimate=cost(14),
    )(me, *mixed, *frames, *norm, *weights, *biases, *features)


def attention_grad_kernel(q_block, heads, *refs):
    pieces = came_pieces(*refs[:3])
    (q_ref, qt_ref, k_ref, v_ref, ot_ref, lse_ref, wq_ref, wk_ref, wv_ref,
     keep_ref, near_ref, gq_ref, gk_ref, gv_ref, sum_ref,
     go_ref, got_ref, kt_ref, delta_ref, dqt_ref, dk_ref, dv_ref) = refs[3:]
    rows = pieces[0].shape[0]
    total = 4 * rows
    cols_all = heads * HD
    scale = HD ** (-0.5)
    go_ref[...] = jnp.zeros_like(go_ref)
    for n in range(4):
        go_ref[n * rows : (n + 1) * rows, :cols_all] = pieces[n]
    got_ref[...] = go_ref[...].astype(F32).T.astype(BF)
    kt_ref[...] = k_ref[...].astype(F32).T.astype(BF)
    for head in range(heads):
        own = slice(HD * head, HD * (head + 1))
        delta_ref[head : head + 1, :] = jnp.sum(
            got_ref[own, :].astype(F32) * ot_ref[own, :], axis=0, keepdims=True
        )
    lane = iota((1, LANES), 1)
    for head in range(heads):
        own = slice(HD * head, HD * (head + 1))
        mask = (lane // HD == head).astype(F32).astype(BF)
        for start in range(0, total, q_block):
            cols = slice(start, start + q_block)
            scores = dot(k_ref[...], head_rows(qt_ref[:, cols], head, heads))
            probs = jnp.exp(scores - lse_ref[head : head + 1, cols])
            prob_grad = dot(v_ref[...], head_rows(got_ref[:, cols], head, heads))
            score_grad = (probs * (prob_grad - delta_ref[head : head + 1, cols])).astype(BF)
            value_part = dot(probs.astype(BF), go_ref[cols, :] * mask)
            key_part = dot(score_grad, q_ref[cols, :] * mask)
            if head == 0 and start == 0:
                dv_ref[...] = value_part
                dk_ref[...] = key_part
            else:
                dv_ref[...] += value_part
                dk_ref[...] += key_part
            dqt_ref[own, cols] = dot(kt_ref[own, :], score_grad)
    dqt_ref[cols_all:, :] = jnp.zeros((LANES - cols_all, total), F32)
    sums_q = jnp.zeros((1, LANES), F32)
    sums_v = jnp.zeros((1, LANES), F32)
    for n in range(4):
        here = slice(n * rows, (n + 1) * rows)
        query_grad = dqt_ref[:, here].T * scale
        value_grad = dv_ref[here, :]
        sums_q = sums_q + jnp.sum(query_grad, axis=0, keepdims=True)
        sums_v = sums_v + jnp.sum(value_grad, axis=0, keepdims=True)
        low_q = query_grad.astype(BF)
        low_k = dk_ref[here, :].astype(BF)
        low_v = value_grad.astype(BF)
        gq_ref[here, :] = low_q[:, :cols_all]
        gk_ref[here, :] = low_k[:, :cols_all]
        gv_ref[here, :] = low_v[:, :cols_all]
        back = dot(low_q, wq_ref[...]) + dot(low_k, wk_ref[...]) + dot(low_v, wv_ref[...])
        out_ref = keep_ref if n < 2 else near_ref
        out_ref[n % 2 * rows : (n % 2 + 1) * rows, :] = back.astype(BF)
    sum_ref[0:1, :] = sums_q
    sum_ref[1:2, :] = sums_v
    sum_ref[2:, :] = jnp.zeros((6, LANES), F32)


def attention_grad(came, saved, weights, heads, q_block=512):
    half, cols = came[0].shape
    total = 2 * half
    width = weights[0].shape[1]
    return pl.pallas_call(
        functools.partial(attention_grad_kernel, q_block, heads),
        out_shape=[
            jax.ShapeDtypeStruct((half, width), BF),
            jax.ShapeDtypeStruct((half, width), BF),
            jax.ShapeDtypeStruct((total, cols), BF),
            jax.ShapeDtypeStruct((total, cols), BF),
            jax.ShapeDtypeStruct((total, cols), BF),
            jax.ShapeDtypeStruct((8, LANES), F32),
        ],
        scratch_shapes=[
            pltpu.VMEM((total, LANES), BF),
            pltpu.VMEM((LANES, total), BF),
            pltpu.VMEM((LANES, total), BF),
            pltpu.VMEM((8, total), F32),
            pltpu.VMEM((LANES, total), F32),
            pltpu.VMEM((total, LANES), F32),
            pltpu.VMEM((total, LANES), F32),
        ],
        compiler_params=params(WIDE_MIB),
        cost_estimate=cost(13),
    )(*came, *saved, *weights)


def put_half(n, value, keep_ref, near_ref):
    @pl.when(n < 2)
    def _():
        keep_ref[...] = value

    @pl.when(n >= 2)
    def _():
        near_ref[...] = value


def feed_kernel(a0_ref, a1_ref, a2_ref, a3_ref, normed_ref, o0_ref, o1_ref, o2_ref, o3_ref, ob_ref, gain_ref, bias_ref,
                up_ref, ub_ref, down_ref,
                low_ref, act_ref, slope_ref, keep_ref, near_ref, own_ref, hat_ref, inv_ref):
    n = pl.program_id(0)
    total = normed_ref[...] + ob_ref[...]
    out_refs = (o0_ref, o1_ref, o2_ref, o3_ref)
    for ref, out_ref in zip((a0_ref, a1_ref, a2_ref, a3_ref), out_refs):
        total = total + dot(ref[...], out_ref[...])
    hat, inv = norm_stats(total)
    normed = hat * gain_ref[...] + bias_ref[...]

    @pl.when(n == 0)
    def _():
        own_ref[...] = normed
        hat_ref[...] = hat
        inv_ref[...] = jnp.broadcast_to(inv, inv_ref.shape)

    low = normed.astype(BF)
    low_ref[...] = low
    value, slope = phi_pair(dot(low, up_ref[...]) + ub_ref[...])
    slope_ref[...] = slope
    value = value.astype(BF)
    act_ref[...] = value
    put_half(n, dot(value, down_ref[...]).astype(BF), keep_ref, near_ref)


def feed(attended, normed, out_pieces, out_bias, norm, up_weight, up_bias, down_weight):
    total, width = normed.shape
    rows = total // 4
    part = attended[0].shape[1]
    units = up_weight.shape[1]
    here = lambda n: (n, 0)
    return pl.pallas_call(
        feed_kernel,
        grid=(4,),
        in_specs=[block((rows, part), lambda n, i=i: (n ^ i, 0)) for i in range(4)]
        + [block((rows, width), here)]
        + [full((part, width))] * 4
        + [
            full((1, width)),
            full((1, width)),
            full((1, width)),
            full((width, units)),
            full((1, units)),
            full((units, width)),
        ],
        out_specs=[
            block((rows, width), here),
            block((rows, units), here),
            block((rows, units), here),
            block((rows, width), lambda n: (jnp.minimum(n, 1), 0)),
            block((rows, width), lambda n: (jnp.maximum(n - 2, 0), 0)),
            full((rows, width)),
            full((rows, width)),
            full((rows, 128)),
        ],
        out_shape=[
            jax.ShapeDtypeStruct((total, width), BF),
            jax.ShapeDtypeStruct((total, units), BF),
            jax.ShapeDtypeStruct((total, units), F32),
            jax.ShapeDtypeStruct((total // 2, width), BF),
            jax.ShapeDtypeStruct((total // 2, width), BF),
            jax.ShapeDtypeStruct((rows, width), F32),
            jax.ShapeDtypeStruct((rows, width), F32),
            jax.ShapeDtypeStruct((rows, 128), F32),
        ],
        compiler_params=params(WIDE_MIB),
        cost_estimate=cost(10),
    )(*attended, normed, *out_pieces, out_bias, *norm, up_weight, up_bias, down_weight)


def feed_grad_kernel(g0_ref, g1_ref, g2_ref, g3_ref, slope_ref, up_ref, down_ref,
                     all_ref, low_ref, keep_ref, near_ref, bias_ref):
    n = pl.program_id(0)
    for i, ref in enumerate((g0_ref, g1_ref, g2_ref, g3_ref)):

        @pl.when(n == i)
        def _():
            all_ref[...] = ref[...]

    grad = dot_turned(all_ref[...], down_ref[...]) * slope_ref[...]

    @pl.when(n == 0)
    def _():
        bias_ref[...] = jnp.zeros_like(bias_ref)

    bias_ref[...] += jnp.sum(grad, axis=0, keepdims=True)
    low = grad.astype(BF)
    low_ref[...] = low
    put_half(n, dot_turned(low, up_ref[...]).astype(BF), keep_ref, near_ref)


def feed_grad(grads, slope, up_weight, down_weight):
    total, units = slope.shape
    rows, width = grads[0].shape
    here = lambda n: (n, 0)
    return pl.pallas_call(
        feed_grad_kernel,
        grid=(4,),
        in_specs=[full((rows, width))] * 4
        + [block((rows, units), here), full((width, units)), full((units, width))],
        out_specs=[
            block((rows, width), here),
            block((rows, units), here),
            block((rows, width), lambda n: (jnp.minimum(n, 1), 0)),
            block((rows, width), lambda n: (jnp.maximum(n - 2, 0), 0)),
            full((1, units)),
        ],
        out_shape=[
            jax.ShapeDtypeStruct((total, width), BF),
            jax.ShapeDtypeStruct((total, units), BF),
            jax.ShapeDtypeStruct((total // 2, width), BF),
            jax.ShapeDtypeStruct((total // 2, width), BF),
            jax.ShapeDtypeStruct((1, units), F32),
        ],
        compiler_params=params(WIDE_MIB),
        cost_estimate=cost(6),
    )(*grads, slope, up_weight, down_weight)


def came_pieces(keep_ref, far_ref, near_ref):
    rows = far_ref.shape[0] // 2
    return [keep_ref[:rows, :], far_ref[:rows, :], near_ref[:rows, :], far_ref[rows:, :]]


def put_sums(sum_ref, *values):
    sum_ref[...] = jnp.zeros_like(sum_ref)
    for i, value in enumerate(values):
        sum_ref[i : i + 1, :] = jnp.sum(value, axis=0, keepdims=True)


def norm_grad(grad, hat, inv, gain):
    scaled = grad * gain
    return inv * (
        scaled
        - jnp.mean(scaled, axis=-1, keepdims=True)
        - hat * jnp.mean(scaled * hat, axis=-1, keepdims=True)
    )


def last_norm_kernel(keep_ref, near_ref, far_ref, normed_ref, cot_ref, down_ref, gain_ref, bias_ref,
                     out_ref, grad_ref, low_ref, sum_ref):
    total = keep_ref[...].astype(F32) + near_ref[...].astype(F32) + far_ref[...].astype(F32)
    hat, inv = norm_stats(normed_ref[...] + total + down_ref[...])
    gain = gain_ref[...]
    out_ref[...] = (hat * gain + bias_ref[...]).astype(BF)
    cot = cot_ref[...].astype(F32)
    grad = norm_grad(cot, hat, inv, gain)
    grad_ref[...] = grad
    low_ref[...] = grad.astype(BF)
    put_sums(sum_ref, cot * hat, cot, grad)


def last_norm(terms, normed, cotangent, down_bias, gain, bias):
    rows, width = normed.shape
    return pl.pallas_call(
        last_norm_kernel,
        grid=(1,),
        in_specs=[full((rows, width))] * 5 + [full((1, width))] * 3,
        out_specs=[full((rows, width))] * 3 + [full((8, width))],
        out_shape=[
            jax.ShapeDtypeStruct((rows, width), BF),
            jax.ShapeDtypeStruct((rows, width), F32),
            jax.ShapeDtypeStruct((rows, width), BF),
            jax.ShapeDtypeStruct((8, width), F32),
        ],
        compiler_params=params(WIDE_MIB),
        cost_estimate=cost(3),
    )(*terms, normed, cotangent, down_bias, gain, bias)


def middle_norm_kernel(keep_ref, near_ref, far_ref, grad_ref, hat_ref, inv_ref, gain_ref, o0_ref,
                       o1_ref, o2_ref, o3_ref, out_ref, low_ref, sum_ref, keep_out, near_out):
    rows = grad_ref.shape[0]
    total = keep_ref[...].astype(F32) + near_ref[...].astype(F32) + far_ref[...].astype(F32)
    total = total + grad_ref[...]
    hat = hat_ref[...]
    grad = norm_grad(total, hat, inv_ref[:, 0:1], gain_ref[...])
    out_ref[...] = grad
    low = grad.astype(BF)
    low_ref[...] = low
    put_sums(sum_ref, total * hat, total, grad)
    for n, ref in enumerate((o0_ref, o1_ref, o2_ref, o3_ref)):
        back = dot_turned(low, ref[...]).astype(BF)
        out = keep_out if n < 2 else near_out
        out[n % 2 * rows : (n % 2 + 1) * rows, :] = back


def middle_norm(terms, grad, hat, inv, gain, out_pieces):
    rows, width = grad.shape
    part = out_pieces[0].shape[0]
    return pl.pallas_call(
        middle_norm_kernel,
        grid=(1,),
        in_specs=[full((rows, width))] * 5
        + [full((rows, 128)), full((1, width))]
        + [full((part, width))] * 4,
        out_specs=[full((rows, width))] * 2 + [full((8, width))] + [full((2 * rows, part))] * 2,
        out_shape=[
            jax.ShapeDtypeStruct((rows, width), F32),
            jax.ShapeDtypeStruct((rows, width), BF),
            jax.ShapeDtypeStruct((8, width), F32),
            jax.ShapeDtypeStruct((2 * rows, part), BF),
            jax.ShapeDtypeStruct((2 * rows, part), BF),
        ],
        compiler_params=params(WIDE_MIB),
        cost_estimate=cost(3),
    )(*terms, grad, hat, inv, gain, *out_pieces)


def first_norm_kernel(me_ref, keep_ref, near_ref, far_ref, grad_ref, hat_ref, inv_ref, gain_ref,
                      out_ref, sum_ref, keep_out, near_out):
    rows, width = grad_ref.shape
    part = keep_out.shape[1]
    total = keep_ref[...].astype(F32) + near_ref[...].astype(F32) + far_ref[...].astype(F32)
    total = total + grad_ref[...]
    hat = hat_ref[...]
    grad = norm_grad(total, hat, inv_ref[:, 0:1], gain_ref[...])
    out_ref[...] = grad
    low = grad.astype(BF)
    put_sums(sum_ref, total * hat, total)
    row, lane = iota((width, part), 0), iota((width, part), 1)
    for n in range(4):
        pick = (row == lane + part * (me_ref[0] ^ ORDER[n])).astype(F32).astype(BF)
        out = keep_out if n < 2 else near_out
        out[n % 2 * rows : (n % 2 + 1) * rows, :] = dot(low, pick).astype(BF)


def first_norm(me, terms, grad, hat, inv, gain):
    rows, width = grad.shape
    part = width // 4
    return pl.pallas_call(
        first_norm_kernel,
        grid=(1,),
        in_specs=[pl.BlockSpec(memory_space=pltpu.SMEM)]
        + [full((rows, width))] * 5
        + [full((rows, 128)), full((1, width))],
        out_specs=[full((rows, width)), full((8, width))] + [full((2 * rows, part))] * 2,
        out_shape=[
            jax.ShapeDtypeStruct((rows, width), F32),
            jax.ShapeDtypeStruct((8, width), F32),
            jax.ShapeDtypeStruct((2 * rows, part), BF),
            jax.ShapeDtypeStruct((2 * rows, part), BF),
        ],
        compiler_params=params(WIDE_MIB),
        cost_estimate=cost(3),
    )(me, *terms, grad, hat, inv, gain)


def frames_grad_kernel(me_ref, keep_ref, far_ref, near_ref, grad_ref, out_ref):
    width = grad_ref.shape[1]
    part = keep_ref.shape[1]
    row, lane = iota((part, width), 0), iota((part, width), 1)
    total = grad_ref[...]
    for n, piece in enumerate(came_pieces(keep_ref, far_ref, near_ref)):
        spot = (lane == row + part * (me_ref[0] ^ ORDER[n])).astype(F32).astype(BF)
        total = total + dot(piece, spot)
    out_ref[...] = total


def add_frames_grad(me, came, grad):
    half, part = came[0].shape
    rows, width = grad.shape
    return pl.pallas_call(
        frames_grad_kernel,
        grid=(1,),
        in_specs=[pl.BlockSpec(memory_space=pltpu.SMEM)]
        + [full((half, part))] * 3
        + [full((rows, width))],
        out_specs=full((rows, width)),
        out_shape=jax.ShapeDtypeStruct((rows, width), F32),
        compiler_params=params(WIDE_MIB),
        cost_estimate=cost(2),
    )(me, *came, grad)


def swap(value, bit):
    return lax.ppermute(value, "tp", [(i, i ^ bit) for i in range(lax.axis_size("tp"))])


def gather_pieces(value):
    across = swap(value, 2)
    return [value, across, swap(value, 1), swap(across, 1)]


def scatter_terms(keep, near):
    piece = keep.shape[0] // 2
    came = swap(near, 1)
    pair = (keep[piece:].astype(F32) + came[piece:].astype(F32)).astype(BF)
    return [keep, came, swap(pair, 2)]


def exchange(keep, near):
    rows = keep.shape[0] // 2
    came = swap(near, 1)
    far = swap(jnp.concatenate([keep[rows:], came[rows:]], axis=0), 2)
    return [keep, far, came]


def after(value, *others):
    return lax.optimization_barrier((value, *others))[0]


def all_after(values, *others):
    return list(lax.optimization_barrier((*values, *others))[: len(values)])


def team_groups(row_count, team):
    if row_count == team:
        return None
    return [list(range(first, first + team)) for first in range(0, row_count, team)]


def cross_groups(row_count, team):
    return [list(range(first, row_count, team)) for first in range(team)]


def pair_rows(value, mask):
    count = lax.axis_size("rows")
    return lax.ppermute(value, "rows", [(i, i ^ mask) for i in range(count)])


FEED_MASKS = ((1, 2, 6), (2, 1, 6))


def side_of(index, mask):
    bits = [(index >> i) & 1 for i in range(3)]
    return {1: bits[0], 2: bits[1] ^ bits[2], 6: bits[2]}[mask]


def holders_of(masks):
    part = lambda index: sum(side_of(index, m) << (2 - i) for i, m in enumerate(masks))
    return sorted(range(8), key=part)


def halve(value, mask, side):
    half = value.shape[0] // 2
    kept = lax.dynamic_slice_in_dim(value, side * half, half, 0)
    sent = lax.dynamic_slice_in_dim(value, (1 - side) * half, half, 0)
    return kept, pair_rows(sent, mask)


def add_low(kept, came):
    return (kept.astype(F32) + came.astype(F32)).astype(BF)


def gather_team(value, masks):
    held, offsets = value[None], [0]
    for mask in masks:
        held = jnp.concatenate([held, pair_rows(held, mask)], axis=0)
        offsets = offsets + [x ^ mask for x in offsets]
    return held, offsets


def on_device(
    frames,
    seg_starts,
    conv_weight,
    conv_bias,
    norm_gain0,
    norm_bias0,
    qkv_weight,
    qv_bias,
    out_weight,
    out_bias,
    norm_gain1,
    norm_bias1,
    up_weight,
    up_bias,
    down_weight,
    down_bias,
    norm_gain2,
    norm_bias2,
    cotangent,
):
    head_cols = qkv_weight.shape[2]
    heads_here = head_cols // HD
    groups_here = conv_weight.shape[2] // GW
    team = 2 * groups_here
    row_count = lax.axis_size("rows")
    teams = team_groups(row_count, team)
    me = lax.axis_index("tp")
    me_word = me.reshape(1).astype(jnp.int32)
    own_row = lax.axis_index("rows") % team
    positions = jnp.arange(LEN, dtype=jnp.int32)
    segments = (
        jnp.sum((positions[:, None] >= seg_starts[0][None, :]).astype(jnp.int32), axis=1) - 1
    )
    line = lambda value: value.astype(F32).reshape(1, -1)

    slots = spread_slots(segments)
    put = (iota((SLOTS, LEN), 0) == slots[None, :]).astype(BF)
    ext = extension()
    conv_flat = conv_weight.reshape(KER * GW, -1)
    toeplitz = toeplitz_weights(conv_flat, groups_here)
    bias_lanes = jnp.tile(conv_bias.astype(F32).reshape(groups_here, 1, GW), (1, 1, PH))
    bias_lanes = jnp.pad(bias_lanes, ((0, 0), (0, 0), (0, LANES - PH * GW)))
    frames_pieces = gather_pieces(frames)
    out_pieces = gather_pieces(after(out_weight, frames_pieces[1]))
    mixed_low, slope0, core = conv(me_word, frames_pieces, put, ext, toeplitz, bias_lanes)
    mixed_low = after(mixed_low, *out_pieces)

    seg_rows = segments.reshape(4, -1)
    seg_own = jnp.concatenate(
        [lax.dynamic_index_in_dim(seg_rows, me ^ m, 0, keepdims=False) for m in ORDER]
    )
    lane = jnp.arange(LANES, dtype=jnp.int32)[None, :] - head_cols
    in_seg = lane == seg_own[:, None]
    of_seg = (lane >= 0) & (lane < seg_starts.shape[1])
    features = [
        jnp.where(in_seg, MASK_ROOT, 0.0).astype(BF),
        jnp.where(of_seg & ~in_seg, -MASK_ROOT, 0.0).astype(BF),
    ]
    qkv_padded = jnp.pad(
        qkv_weight.transpose(1, 2, 0), ((0, 0), (0, LANES - head_cols), (0, 0))
    )
    qkv_parts = [qkv_padded[0], qkv_padded[1], qkv_padded[2]]
    qv_padded = jnp.pad(qv_bias.astype(F32), ((0, 0), (0, LANES - head_cols)))
    gain0 = line(norm_gain0)
    mixed_pieces = gather_pieces(mixed_low)
    core_all = lax.all_to_all(
        jnp.repeat(core, 2, axis=0), "rows", 0, 0, axis_index_groups=teams, tiled=True
    )
    (attended, normed0, hat0, inv0, normed0_all, normed0_low, *saved) = attention(
        me_word,
        mixed_pieces,
        frames_pieces,
        [gain0, line(norm_bias0)],
        qkv_parts,
        [qv_padded[0:1], qv_padded[1:2]],
        features,
        heads_here,
    )

    attended = after(attended, core_all)
    attended_pieces = gather_pieces(attended)
    turned_core = turn_core(core_all, ext)
    attended_pieces = all_after(attended_pieces, turned_core)
    gain1 = line(norm_gain1)
    normed1_low, activated, slope1, keep, near, normed1, hat1, inv1 = feed(
        attended_pieces,
        normed0_all,
        out_pieces,
        line(out_bias),
        [gain1, line(norm_bias1)],
        up_weight,
        line(up_bias),
        down_weight,
    )
    block_out, grad2, grad2_low, sums2 = last_norm(
        scatter_terms(keep, near),
        normed1,
        cotangent,
        line(down_bias),
        line(norm_gain2),
        line(norm_bias2),
    )

    grad2_all, up_low, keep, near, up_bias_grad = feed_grad(
        gather_pieces(grad2_low), slope1, up_weight, down_weight
    )
    terms = scatter_terms(keep, near)
    down_grad = jnp.einsum("rf,rd->fd", activated, grad2_all, preferred_element_type=F32)
    up_grad = jnp.einsum("rd,rf->df", normed1_low, up_low, preferred_element_type=F32)
    feed_grads = [down_grad.astype(BF), up_grad.astype(BF)]
    terms = all_after(terms, *feed_grads)
    feed_steps = [[(mask, side_of(own_row, mask)) for mask in masks] for masks in FEED_MASKS]
    halves_1 = [halve(grad, *order[0]) for grad, order in zip(feed_grads, feed_steps)]

    grad1, grad1_low, sums1, keep, near = middle_norm(terms, grad2, hat1, inv1, gain1, out_pieces)
    came = exchange(keep, near)
    feed_sums = [add_low(*pair) for pair in halves_1]
    came = all_after(came, *feed_sums)
    halves_2 = [halve(grad, *order[1]) for grad, order in zip(feed_sums, feed_steps)]
    keep, near, query_grad, key_grad, value_grad, qv_sums = attention_grad(
        came, saved, qkv_parts, heads_here
    )
    grad1_pieces = gather_pieces(after(grad1_low, *came))
    feed_sums = [add_low(after(kept, near), other) for kept, other in halves_2]
    keep, near = all_after([keep, near], *grad1_pieces)
    halves_3 = [halve(grad, *order[2]) for grad, order in zip(feed_sums, feed_steps)]
    terms = scatter_terms(keep, near)
    out_grad = jnp.einsum(
        "rh,rd->hd", attended, jnp.concatenate(grad1_pieces, axis=0), preferred_element_type=F32
    )
    turned_grads = [
        jnp.einsum("rc,rd->cd", part, normed0_low, preferred_element_type=F32).astype(BF)
        for part in (query_grad, key_grad, value_grad)
    ]
    tail = jnp.concatenate(turned_grads + [out_grad.astype(BF)], axis=0)
    feed_sums = jnp.stack([add_low(*pair) for pair in halves_3])
    terms = all_after(terms, tail, feed_sums)
    qv_grad = qv_sums[:2, :head_cols]
    if teams is not None:
        feed_sums = lax.psum(feed_sums, "rows", axis_index_groups=cross_groups(row_count, team))
    feed_held = lax.all_gather(feed_sums, "rows", axis_index_groups=teams)
    tail_steps = feed_steps[0]
    tail_half = halve(tail, *tail_steps[0])
    grad0, sums0, keep, near = first_norm(me_word, terms, grad1, hat0, inv0, gain0)

    came = exchange(keep, near)
    tail_sum = add_low(*tail_half)
    came = all_after(came, tail_sum)
    tail_half = halve(tail_sum, *tail_steps[1])
    wide, halves, conv_bias_grad = conv_grad(me_word, came, put, slope0, ext)
    conv_bias_grad = conv_bias_grad[:, 0, : PH * GW].reshape(groups_here, PH, GW)
    conv_bias_grad = jnp.sum(conv_bias_grad, axis=1).reshape(-1)
    halves_all = lax.all_to_all(halves, "rows", 0, 0, axis_index_groups=teams, tiled=True)
    tail_sum = add_low(after(tail_half[0], halves), tail_half[1])
    tail_half = halve(tail_sum, *tail_steps[2])
    keep, near = signal_grad(me_word, after(wide, tail_sum), toeplitz, put)
    frames_grad = add_frames_grad(me_word, exchange(keep, near), grad0)
    halves_all = after(halves_all, near)
    kernel_part = tap_grad(turned_core, halves_all)
    tail_part = add_low(*tail_half)

    shared = jnp.concatenate([sums0[:2], sums1[:3], sums2[:3]], axis=0)
    all_small = [shared[i] for i in range(shared.shape[0])]
    rows_small = [conv_bias_grad, qv_grad, up_bias_grad]
    shared = shared + swap(shared, 1)
    shared = shared + swap(shared, 2)
    small = jnp.concatenate([shared.reshape(-1)] + [v.reshape(-1) for v in rows_small])
    small_size = small.size
    small = jnp.pad(small, (0, -small_size % (16 * KER))).reshape(-1, KER)
    if teams is not None:
        others = cross_groups(row_count, team)
        kernel_part = lax.psum(kernel_part, "rows", axis_index_groups=others)
        tail_part = lax.psum(tail_part.astype(F32), "rows", axis_index_groups=others)
        small = lax.psum(small, "rows", axis_index_groups=others)
    small_high = small.astype(BF)
    small_low = (small - small_high.astype(F32)).astype(BF)
    part_rows = kernel_part.shape[0] // 2
    part_low = kernel_part.astype(BF)
    masks = [1, 2, 6] if team == 8 else [1 << i for i in range(team.bit_length() - 1)]
    tail_low = tail_part.astype(BF).reshape(2, -1, KER)
    held_a, offsets_a = gather_team(
        jnp.concatenate([part_low[:part_rows], tail_low[0], small_high], axis=0),
        masks[1:] + masks[:1],
    )
    held_b, offsets_b = gather_team(
        jnp.concatenate([part_low[part_rows:], tail_low[1], small_low], axis=0), masks
    )
    order = jnp.array(
        [[offsets.index(x) for x in range(team)] for offsets in (offsets_a, offsets_b)], jnp.int32
    )
    order = order[:, jnp.arange(team, dtype=jnp.int32) ^ own_row]
    holders = [holders_of(masks) for masks in FEED_MASKS]
    kernel_total = assemble(order, held_a, held_b).transpose(2, 0, 1)
    tail_rows = tail_low.shape[1]
    small = jnp.sum(held_a[:, part_rows + tail_rows :].astype(F32), axis=0) + jnp.sum(
        held_b[:, part_rows + tail_rows :].astype(F32), axis=0
    )
    tail_total = jnp.stack(
        [
            held[:, part_rows : part_rows + tail_rows][order[i][jnp.array(holders[0])]]
            for i, held in enumerate((held_a, held_b))
        ],
        axis=1,
    )
    tail_total = tail_total.reshape(-1, D).astype(F32)
    qkv_total = tail_total[: 3 * head_cols].reshape(3, head_cols, D).transpose(2, 0, 1)
    out_total = tail_total[3 * head_cols :]
    small = small.reshape(-1)[:small_size]
    sizes = [v.size for v in all_small + rows_small]
    ends = [sum(sizes[: i + 1]) for i in range(len(sizes))]
    cuts = [small[end - size : end] for size, end in zip(sizes, ends)]
    gain0_grad, bias0_grad, gain1_grad, bias1_grad, out_bias_grad = cuts[:5]
    gain2_grad, bias2_grad, down_bias_grad, conv_bias_grad, qv_grad, up_bias_grad = cuts[5:]
    down_total, up_total = [
        jnp.concatenate([feed_held[r, i] for r in holders[i]], axis=0).astype(F32) for i in range(2)
    ]
    return (
        block_out,
        frames_grad,
        kernel_total,
        conv_bias_grad,
        gain0_grad,
        bias0_grad,
        qkv_total,
        qv_grad.reshape(2, head_cols),
        out_total,
        out_bias_grad,
        gain1_grad,
        bias1_grad,
        up_total,
        up_bias_grad,
        down_total,
        down_bias_grad,
        gain2_grad,
        bias2_grad,
    )


def solution(mesh):
    return jax.shard_map(
        on_device,
        mesh=mesh,
        in_specs=(
            P(("rows", "tp"), None),
            P("rows", None),
            P(None, None, "tp"),
            P("tp"),
            P(),
            P(),
            P(None, None, "tp"),
            P(None, "tp"),
            P("tp", None),
            P(),
            P(),
            P(),
            P(None, "tp"),
            P("tp"),
            P("tp", None),
            P(),
            P(),
            P(),
            P(("rows", "tp"), None),
        ),
        out_specs=(
            P(("rows", "tp"), None),
            P(("rows", "tp"), None),
            P(None, None, "tp"),
            P("tp"),
            P(),
            P(),
            P(None, None, "tp"),
            P(None, "tp"),
            P("tp", None),
            P(),
            P(),
            P(),
            P(None, "tp"),
            P("tp"),
            P("tp", None),
            P(),
            P(),
            P(),
        ),
        check_vma=False,
    )
```

```python
import functools

import jax
import jax.numpy as jnp
import numpy as np
from jax import lax
from jax.experimental import pallas as pl
from jax.experimental.pallas import tpu as pltpu
from jax.sharding import PartitionSpec as P

D = 768
HD = 64
KER = 128
GROUPS = 16
LEN = 1024

EPSILON = 1e-05
ROOT_HALF = 0.7071067811865476
INV_ROOT_TAU = 0.3989422804014327
MASK_ROOT = 16384.0

GW = D // GROUPS
HALF = GW // 2
PH = 5
QN, PN = 17, 16
CORE = QN * PN
NJ = 27
LEAD = 13
EXT = (QN + NJ - 1) * PN
LANES = 256
GAP = KER // 2
SLOTS = PH * CORE
WIDE_MIB = 58

ORDER = (0, 2, 1, 3)

BF = jnp.bfloat16
F32 = jnp.float32


def iota(shape, dim):
    return lax.broadcasted_iota(jnp.int32, shape, dim)


def full(shape):
    return pl.BlockSpec(shape, lambda *index: (0,) * len(shape))


def block(shape, index_map):
    return pl.BlockSpec(shape, index_map)


def params(mib):
    return pltpu.CompilerParams(vmem_limit_bytes=mib * 2**20)


def cost(microseconds):
    return pl.CostEstimate(
        flops=int(microseconds * 1.1e+09), bytes_accessed=int(microseconds * 1e+06), transcendentals=0
    )


def dot(left, right):
    return jnp.dot(left, right, preferred_element_type=F32)


def dot_turned(left, right):
    return lax.dot_general(left, right, (((1,), (1,)), ((), ())), preferred_element_type=F32)


def phi_pair(v):
    cdf = 0.5 * (1.0 + lax.erf(v * ROOT_HALF))
    return v * cdf, cdf + v * INV_ROOT_TAU * jnp.exp(-0.5 * v * v)


def norm_stats(inputs):
    centered = inputs - jnp.mean(inputs, axis=-1, keepdims=True)
    inv_std = lax.rsqrt(jnp.mean(centered * centered, axis=-1, keepdims=True) + EPSILON)
    return centered * inv_std, inv_std


def spread_slots(segments):
    place = jnp.arange(LEN, dtype=jnp.int32) + GAP * segments
    at = place // PH
    return place % PH * CORE + at % QN * PN + at // QN


def extension():
    row, col = np.arange(EXT)[:, None], np.arange(CORE)[None, :]
    want = QN * (row % PN) + row // PN - LEAD
    have = QN * (col % PN) + col // PN
    return jnp.asarray((want == have).astype(np.float32), BF)


def toeplitz_scratch():
    return [
        pltpu.VMEM((PH * GW + KER * GW + 288, LANES), BF),
        pltpu.VMEM((NJ * LANES, LANES), BF),
    ]


def fill_toeplitz(w_ref, step, g, wide_ref, wt_ref):
    before = PH * GW
    row, lane = iota((w_ref.shape[1], LANES), 0), iota((w_ref.shape[1], LANES), 1)
    spread = ((row == GW * g + lane % GW) & (lane < PH * GW)).astype(F32).astype(BF)

    @pl.when(step == 0)
    def _():
        rest = before + KER * GW
        wide_ref[0:before, :] = jnp.zeros((before, LANES), BF)
        wide_ref[rest:, :] = jnp.zeros((wide_ref.shape[0] - rest, LANES), BF)
        for j in range(NJ):
            gap = slice(j * LANES + PH * GW, (j + 1) * LANES)
            wt_ref[gap, :] = jnp.zeros((LANES - PH * GW, LANES), BF)

    wide_ref[before : before + KER * GW, :] = dot(w_ref[...], spread).astype(BF)
    lane = iota((1, LANES), 1)
    masks = [(lane // GW == i).astype(F32).astype(BF) for i in range(PH)]

    for j in range(NJ):
        for left in range(0, LANES, 128):
            lanes = slice(left, left + 128)
            total = None
            for i in range(left // GW, min((left + 127) // GW + 1, PH)):
                start = before + PH * GW * j - GW * (1 + i)
                part = wide_ref[start : start + PH * GW, lanes] * masks[i][:, lanes]
                total = part if total is None else total + part
            wt_ref[j * LANES : j * LANES + PH * GW, lanes] = total


def fold_in(slots_ref, g):
    width = slots_ref.shape[1]
    row, lane = iota((width, LANES), 0), iota((width, LANES), 1)
    core = jnp.zeros((CORE, LANES), F32)
    for i in range(PH):
        pick = ((lane // GW == i) & (row == GW * g + lane % GW)).astype(F32).astype(BF)
        core = core + dot(slots_ref[i * CORE : (i + 1) * CORE, :], pick)
    return core


def fold_out(values, back_ref, g):
    width = back_ref.shape[1]
    row, col = iota((LANES, width), 0), iota((LANES, width), 1)
    for i in range(PH):
        pick = ((row // GW == i) & (col == GW * g + row % GW)).astype(F32).astype(BF)
        here = slice(i * CORE, (i + 1) * CORE)
        back_ref[here, :] = back_ref[here, :] + dot(values, pick).astype(BF)


def unspread(back_ref, put_ref):
    turned = back_ref[...].astype(F32).T.astype(BF)
    return dot(turned, put_ref[...]).T.astype(BF)


def conv_kernel(me_ref, f0_ref, f1_ref, f2_ref, f3_ref, put_ref, ext_ref, w_ref, bias_ref,
                mixed_ref, slope_ref, core_ref, sig_ref, slots_ref, wide_ref, back_ref, taps_ref,
                wt_ref):
    g = pl.program_id(0)
    rows, features = f0_ref.shape
    width = sig_ref.shape[1]

    @pl.when(g == 0)
    def _():
        row, lane = iota((features, width), 0), iota((features, width), 1)
        pick = (row == lane + width * me_ref[0]).astype(F32).astype(BF)
        for n, ref in enumerate((f0_ref, f1_ref, f2_ref, f3_ref)):
            start = pl.multiple_of((me_ref[0] ^ ORDER[n]) * rows, rows)
            sig_ref[pl.ds(start, rows), :] = dot(ref[...], pick).astype(BF)
        slots_ref[...] = dot(put_ref[...], sig_ref[...]).astype(BF)
        back_ref[...] = jnp.zeros_like(back_ref)

    fill_toeplitz(w_ref, g, g, taps_ref, wt_ref)
    core = fold_in(slots_ref, g).astype(BF)
    core_ref[0] = core
    wide_ref[...] = dot(ext_ref[...], core).astype(BF)
    total = jnp.zeros((CORE, LANES), F32)
    for j in range(NJ):
        total = total + dot(
            wide_ref[PN * j : PN * j + CORE, :], wt_ref[j * LANES : (j + 1) * LANES, :]
        )
    value, slope = phi_pair(total + bias_ref[0])
    slope_ref[0] = slope
    fold_out(value.astype(BF), back_ref, g)

    @pl.when(g == pl.num_programs(0) - 1)
    def _():
        mixed_ref[...] = unspread(back_ref, put_ref)


def conv(me, frames, put, ext, taps, bias_lanes):
    width = taps.shape[1]
    groups = width // GW
    return pl.pallas_call(
        conv_kernel,
        grid=(groups,),
        in_specs=[pl.BlockSpec(memory_space=pltpu.SMEM)]
        + [full(frames[0].shape)] * 4
        + [
            full((SLOTS, LEN)),
            full((EXT, CORE)),
            full(taps.shape),
            block((1, 1, LANES), lambda g: (g, 0, 0)),
        ],
        out_specs=[
            full((LEN, width)),
            block((1, CORE, LANES), lambda g: (g, 0, 0)),
            block((1, CORE, LANES), lambda g: (g, 0, 0)),
        ],
        out_shape=[
            jax.ShapeDtypeStruct((LEN, width), BF),
            jax.ShapeDtypeStruct((groups, CORE, LANES), F32),
            jax.ShapeDtypeStruct((groups, CORE, LANES), BF),
        ],
        scratch_shapes=[
            pltpu.VMEM((LEN, width), BF),
            pltpu.VMEM((SLOTS, width), BF),
            pltpu.VMEM((EXT, LANES), BF),
            pltpu.VMEM((SLOTS, width), BF),
        ]
        + toeplitz_scratch(),
        compiler_params=params(WIDE_MIB),
        cost_estimate=cost(23),
    )(me, *frames, put, ext, taps, bias_lanes)


def conv_grad_kernel(me_ref, keep_ref, far_ref, near_ref, put_ref, slope_ref, ext_ref,
                     wide_ref, half_ref, bias_ref, grad_ref, slots_ref):
    g = pl.program_id(0)
    rows = far_ref.shape[0] // 2

    @pl.when(g == 0)
    def _():
        for n, piece in enumerate(came_pieces(keep_ref, far_ref, near_ref)):
            start = pl.multiple_of((me_ref[0] ^ ORDER[n]) * rows, rows)
            grad_ref[pl.ds(start, rows), :] = piece
        slots_ref[...] = dot(put_ref[...], grad_ref[...]).astype(BF)

    grad = fold_in(slots_ref, g) * slope_ref[0]
    bias_ref[0] = jnp.sum(grad, axis=0, keepdims=True)
    low = grad.astype(BF)
    wide_ref[0] = dot(ext_ref[...], low).astype(BF)
    row, lane = iota((LANES, 128), 0), iota((LANES, 128), 1)
    for h in range(2):
        pick = (lane < PH * HALF) & (row == lane // HALF * GW + lane % HALF + h * HALF)
        half_ref[h] = dot(low, pick.astype(F32).astype(BF)).astype(BF)


def conv_grad(me, came, put, slope, ext):
    groups = slope.shape[0]
    width = came[0].shape[1]
    return pl.pallas_call(
        conv_grad_kernel,
        grid=(groups,),
        in_specs=[
            pl.BlockSpec(memory_space=pltpu.SMEM),
            full((LEN // 2, width)),
            full((LEN // 2, width)),
            full((LEN // 2, width)),
            full((SLOTS, LEN)),
            block((1, CORE, LANES), lambda g: (g, 0, 0)),
            full((EXT, CORE)),
        ],
        out_specs=[
            block((1, EXT, LANES), lambda g: (g, 0, 0)),
            block((2, CORE, 128), lambda g: (g, 0, 0)),
            block((1, 1, LANES), lambda g: (g, 0, 0)),
        ],
        out_shape=[
            jax.ShapeDtypeStruct((groups, EXT, LANES), BF),
            jax.ShapeDtypeStruct((2 * groups, CORE, 128), BF),
            jax.ShapeDtypeStruct((groups, 1, LANES), F32),
        ],
        scratch_shapes=[pltpu.VMEM((LEN, width), BF), pltpu.VMEM((SLOTS, width), BF)],
        compiler_params=params(WIDE_MIB),
        cost_estimate=cost(0.1),
    )(me, *came, put, slope, ext)


def signal_grad_kernel(first, wide_ref, w_ref, *refs):
    back_ref, taps_ref, wt_ref = refs[-3:]
    step = pl.program_id(0)
    g = first + step
    fill_toeplitz(w_ref, step, g, taps_ref, wt_ref)

    @pl.when(step == 0)
    def _():
        if first == 0:
            back_ref[...] = jnp.zeros_like(back_ref)
        else:
            back_ref[...] = refs[0][...]

    total = jnp.zeros((CORE, LANES), F32)
    for j in range(NJ):
        m = NJ - 1 - j
        total = total + dot_turned(
            wide_ref[0, PN * j : PN * j + CORE, :], wt_ref[m * LANES : (m + 1) * LANES, :]
        )
    fold_out(total.astype(BF), back_ref, g)
    if first == 0:

        @pl.when(step == pl.num_programs(0) - 1)
        def _():
            refs[0][...] = back_ref[...]

        return
    _, put_ref, me_ref, keep_ref, near_ref, all_ref = refs[:6]
    rows = keep_ref.shape[0] // 2

    @pl.when(step == pl.num_programs(0) - 1)
    def _():
        all_ref[...] = unspread(back_ref, put_ref)
        for n in range(4):
            start = pl.multiple_of((me_ref[0] ^ ORDER[n]) * rows, rows)
            out_ref = keep_ref if n < 2 else near_ref
            out_ref[n % 2 * rows : (n % 2 + 1) * rows, :] = all_ref[pl.ds(start, rows), :]


def signal_grad(wide, taps, first, count, *rest):
    width = taps.shape[1]
    slots = jax.ShapeDtypeStruct((SLOTS, width), BF)
    piece = jax.ShapeDtypeStruct((LEN // 2, width), BF)
    own = [
        block((1, EXT, LANES), lambda g: (first + g, 0, 0)),
        full(taps.shape),
    ]
    more = [full(slots.shape), full((SLOTS, LEN)), pl.BlockSpec(memory_space=pltpu.SMEM)]
    scratch = [pltpu.VMEM(slots.shape, BF)] + toeplitz_scratch()
    return pl.pallas_call(
        functools.partial(signal_grad_kernel, first),
        grid=(count,),
        in_specs=own + (more if rest else []),
        out_specs=[full(piece.shape)] * 2 if rest else full(slots.shape),
        out_shape=[piece] * 2 if rest else slots,
        scratch_shapes=([pltpu.VMEM((LEN, width), BF)] if rest else []) + scratch,
        compiler_params=params(WIDE_MIB),
        cost_estimate=cost(0.1),
    )(wide, taps, *rest)


def turn_core_kernel(sig_ref, ext_ref, out_ref, wide_ref):
    packs = sig_ref.shape[0]
    blocks = EXT // PN
    wide_ref[blocks:] = jnp.zeros((1, packs * PN, LANES), BF)
    for r in range(packs):
        rows = dot(ext_ref[...], sig_ref[r]).astype(BF)
        wide_ref[0:blocks, r * PN : (r + 1) * PN, :] = rows.reshape(blocks, PN, LANES)
    for q in range(blocks + 1):
        out_ref[:, q * 128 : (q + 1) * 128] = wide_ref[q].astype(F32).T.astype(BF)


def turn_core(sig, ext):
    packs = sig.shape[0]
    blocks = EXT // PN + 1
    return pl.pallas_call(
        turn_core_kernel,
        out_shape=jax.ShapeDtypeStruct((LANES, blocks * packs * PN), BF),
        scratch_shapes=[pltpu.VMEM((blocks, packs * PN, LANES), BF)],
        compiler_params=params(WIDE_MIB),
        cost_estimate=cost(0.1),
    )(sig, ext)


def tap_grad_kernel(sig_ref, grad_ref, out_ref, pair_ref, parts_ref, rows_ref):
    packs = grad_ref.shape[0]
    across = packs * PN
    pair_ref[QN, :, 0:128] = jnp.zeros((across, 128), BF)
    pair_ref[0, :, 128:] = jnp.zeros((across, 128), BF)
    for r in range(packs):
        rows = grad_ref[r].reshape(QN, PN, 128)
        pair_ref[0:QN, r * PN : (r + 1) * PN, 0:128] = rows
        pair_ref[1:, r * PN : (r + 1) * PN, 128:] = rows
    pair = pair_ref[...].reshape((QN + 1) * across, LANES)
    for j in range(0, NJ + 1, 2):
        part = dot(sig_ref[:, j * across : (j + QN + 1) * across], pair)
        parts_ref[PH * GW * j : PH * GW * (j + 1), :] = part[: PH * GW, 0:128]
        parts_ref[PH * GW * (j + 1) : PH * GW * (j + 2), :] = part[: PH * GW, 128:]
    phase = iota((1, 128), 1) // HALF
    chunk = 8 * GW

    for start in range(0, KER * GW, chunk):
        total = jnp.zeros((chunk, 128), F32)
        for i in range(PH):
            rows = slice(start + GW * (1 + i), start + GW * (1 + i) + chunk)
            total = jnp.where(phase == i, parts_ref[rows, :], total)
        rows_ref[start : start + chunk, :] = total
    for c in range(GW):
        taps = rows_ref[pl.ds(c, KER, stride=GW), :].T
        total = taps[0:HALF, :]
        for i in range(1, PH):
            total = total + taps[HALF * i : HALF * (i + 1), :]
        out_ref[c * HALF : (c + 1) * HALF, :] = total


def tap_grad(sig, grad):
    packs = grad.shape[0]
    return pl.pallas_call(
        tap_grad_kernel,
        out_shape=jax.ShapeDtypeStruct((GW * HALF, KER), F32),
        scratch_shapes=[
            pltpu.VMEM((QN + 1, packs * PN, LANES), BF),
            pltpu.VMEM(((NJ + 1) * PH * GW, 128), F32),
            pltpu.VMEM((KER * GW, 128), F32),
        ],
        compiler_params=params(WIDE_MIB),
        cost_estimate=cost(0.1),
    )(sig, grad)


def assemble_kernel(at_ref, a0_ref, a1_ref, b0_ref, b1_ref, out_ref, wide_ref):
    step = pl.program_id(0)
    half = a0_ref.shape[0]
    packs = 2 * half
    per_step = out_ref.shape[0]
    half_steps = pl.num_programs(0) // 2

    def place(held_ref, came_ref, which):
        for r in range(packs):
            at = at_ref[which, r]

            @pl.when(at < half)
            def _():
                wide_ref[...] = held_ref[at].astype(F32)

            @pl.when(at >= half)
            def _():
                wide_ref[...] = came_ref[at - half].astype(F32)

            for c in range(per_step):
                out_ref[c, r * HALF : (r + 1) * HALF, :] = wide_ref[c * HALF : (c + 1) * HALF, :]

    @pl.when(step < half_steps)
    def _():
        place(a0_ref, a1_ref, 0)

    @pl.when(step >= half_steps)
    def _():
        place(b0_ref, b1_ref, 1)


def assemble(order, parts_a, parts_b):
    packs = 2 * parts_a[0].shape[0]
    steps = 4
    per_step = GW // steps
    rows = per_step * HALF
    half = steps // 2
    return pl.pallas_call(
        assemble_kernel,
        grid=(steps,),
        in_specs=[
            pl.BlockSpec(memory_space=pltpu.SMEM),
        ]
        + [block((packs // 2, rows, KER), lambda s: (0, jnp.minimum(s, half - 1), 0))] * 2
        + [block((packs // 2, rows, KER), lambda s: (0, jnp.maximum(s - half, 0), 0))] * 2,
        out_specs=block((per_step, packs * HALF, KER), lambda s: (s, 0, 0)),
        out_shape=jax.ShapeDtypeStruct((GW, packs * HALF, KER), F32),
        scratch_shapes=[pltpu.VMEM((rows, KER), F32)],
        compiler_params=params(WIDE_MIB),
        cost_estimate=cost(4),
    )(order, *parts_a, *parts_b)


def spread_parts_kernel(order_ref, held_d, came_d, held_u, came_u, down_ref, up_ref):
    part = pl.program_id(0)
    half = pl.num_programs(0) // 2
    for i, (held, came, out) in enumerate(((held_d, came_d, down_ref), (held_u, came_u, up_ref))):

        @pl.when(order_ref[i, part] < half)
        def _():
            out[...] = held[0, 0].astype(F32)

        @pl.when(order_ref[i, part] >= half)
        def _():
            out[...] = came[0, 0].astype(F32)


def spread_parts(order, held, came):
    half, _, rows, width = held.shape
    first = lambda i: block(
        (1, 1, rows, width), lambda p, at: (jnp.minimum(at[i, p], half - 1), i, 0, 0)
    )
    second = lambda i: block(
        (1, 1, rows, width), lambda p, at: (jnp.maximum(at[i, p] - half, 0), i, 0, 0)
    )
    out = jax.ShapeDtypeStruct((2 * half * rows, width), F32)
    return pl.pallas_call(
        spread_parts_kernel,
        grid_spec=pltpu.PrefetchScalarGridSpec(
            num_scalar_prefetch=1,
            grid=(2 * half,),
            in_specs=[first(0), second(0), first(1), second(1)],
            out_specs=[block((rows, width), lambda p, at: (p, 0))] * 2,
        ),
        out_shape=[out, out],
        compiler_params=params(WIDE_MIB),
        cost_estimate=cost(5),
    )(order, held, came, held, came)


def head_rows(turned, head, heads):
    pieces = [jnp.zeros((HD, turned.shape[1]), turned.dtype) for _ in range(heads)]
    pieces[head] = turned[HD * head : HD * (head + 1), :]
    return jnp.concatenate(pieces + [turned[HD * heads :, :]], axis=0)


def attention_kernel(q_block, heads, *refs):
    me_ref = refs[0]
    mixed = refs[1:5]
    frames = refs[5:9]
    (gain_ref, bias_ref, wq_ref, wk_ref, wv_ref, qb_ref, vb_ref, featq_ref, featk_ref) = refs[9:18]
    (att_ref, own_ref, hat_ref, inv_ref, all_out, low_out, q_out, qt_out, k_out, v_out, ot_ref,
     lse_ref) = refs[18:30]
    all_ref, low_ref, q_ref, qt_ref, k_ref, v_ref, vt_ref, sems = refs[30:]
    rows = frames[0].shape[0]
    part = mixed[0].shape[1]
    width = frames[0].shape[1]
    scale = HD ** (-0.5)
    me = me_ref[0]
    row, lane = iota((part, width), 0), iota((part, width), 1)
    spots = [(lane == row + part * (me ^ m)).astype(F32).astype(BF) for m in ORDER]
    for n in range(4):
        here = slice(n * rows, (n + 1) * rows)
        start = pl.multiple_of((me ^ ORDER[n]) * rows, rows)
        total = frames[n][...].astype(F32)
        for ref, spot in zip(mixed, spots):
            total = total + dot(ref[pl.ds(start, rows), :], spot)
        hat, inv = norm_stats(total)
        normed = hat * gain_ref[...] + bias_ref[...]
        if n == 0:
            own_ref[...] = normed
            hat_ref[...] = hat
            inv_ref[...] = jnp.broadcast_to(inv, inv_ref.shape)
        all_ref[here, :] = normed
        normed = normed.astype(BF)
        low_ref[here, :] = normed
        query = (dot_turned(normed, wq_ref[...]) + qb_ref[...]) * scale
        query = query + featq_ref[here, :].astype(F32)
        q_ref[here, :] = query.astype(BF)
        qt_ref[:, here] = query.T.astype(BF)
        key = dot_turned(normed, wk_ref[...])
        k_ref[here, :] = (key + featk_ref[here, :].astype(F32)).astype(BF)
        value = dot_turned(normed, wv_ref[...]) + vb_ref[...]
        v_ref[here, :] = value.astype(BF)
        vt_ref[:, here] = value.T.astype(BF)
    held = [all_ref, low_ref, q_ref, qt_ref, k_ref, v_ref]
    kept = [all_out, low_out, q_out, qt_out, k_out, v_out]
    copies = [
        pltpu.make_async_copy(src, dst, sems.at[i]) for i, (src, dst) in enumerate(zip(held, kept))
    ]
    for copy in copies:
        copy.start()
    total = 4 * rows
    for head in range(heads):
        for start in range(0, total, q_block):
            cols = slice(start, start + q_block)
            turned = head_rows(qt_ref[:, cols], head, heads)
            scores = dot(k_ref[...], turned)
            top = jnp.max(scores, axis=0, keepdims=True)
            weights = jnp.exp(scores - top)
            sums = jnp.sum(weights, axis=0, keepdims=True)
            value = dot(vt_ref[HD * head : HD * (head + 1), :], weights.astype(BF))
            ot_ref[HD * head : HD * (head + 1), cols] = value / sums
            lse_ref[head : head + 1, cols] = top + jnp.log(sums)
    lse_ref[heads:, :] = jnp.zeros((8 - heads, total), F32)
    for n in range(4):
        here = slice(n * rows, (n + 1) * rows)
        att_ref[here, :] = ot_ref[:, here].T.astype(BF)
    for copy in copies:
        copy.wait()


def attention(me, mixed, frames, norm, weights, biases, features, heads, q_block=512):
    rows, width = frames[0].shape
    total = 4 * rows
    cols = heads * HD
    vmem = pl.BlockSpec(memory_space=pltpu.VMEM)
    away = pl.BlockSpec(memory_space=pltpu.HBM)
    held = [
        ((total, width), F32),
        ((total, width), BF),
        ((total, LANES), BF),
        ((LANES, total), BF),
        ((total, LANES), BF),
        ((total, LANES), BF),
    ]
    return pl.pallas_call(
        functools.partial(attention_kernel, q_block, heads),
        in_specs=[pl.BlockSpec(memory_space=pltpu.SMEM)] + [vmem] * 17,
        out_specs=[vmem] * 4 + [away] * 6 + [vmem] * 2,
        out_shape=[
            jax.ShapeDtypeStruct((total, cols), BF),
            jax.ShapeDtypeStruct((rows, width), F32),
            jax.ShapeDtypeStruct((rows, width), F32),
            jax.ShapeDtypeStruct((rows, 128), F32),
        ]
        + [jax.ShapeDtypeStruct(shape, kind) for shape, kind in held]
        + [jax.ShapeDtypeStruct((cols, total), F32), jax.ShapeDtypeStruct((8, total), F32)],
        scratch_shapes=[pltpu.VMEM(shape, kind) for shape, kind in held]
        + [pltpu.VMEM((LANES, total), BF), pltpu.SemaphoreType.DMA((len(held),))],
        compiler_params=params(WIDE_MIB),
        cost_estimate=cost(14),
    )(me, *mixed, *frames, *norm, *weights, *biases, *features)


def attention_grad_kernel(q_block, heads, *refs):
    pieces = came_pieces(*refs[:3])
    (q_ref, qt_ref, k_ref, v_ref, ot_ref, lse_ref, wq_ref, wk_ref, wv_ref,
     keep_ref, near_ref, gq_ref, gk_ref, gv_ref, sum_ref,
     go_ref, got_ref, kt_ref, delta_ref, dqt_ref, dk_ref, dv_ref) = refs[3:]
    rows = pieces[0].shape[0]
    total = 4 * rows
    cols_all = heads * HD
    scale = HD ** (-0.5)
    go_ref[...] = jnp.zeros_like(go_ref)
    for n in range(4):
        go_ref[n * rows : (n + 1) * rows, :cols_all] = pieces[n]
    got_ref[...] = go_ref[...].astype(F32).T.astype(BF)
    kt_ref[...] = k_ref[...].astype(F32).T.astype(BF)
    for head in range(heads):
        own = slice(HD * head, HD * (head + 1))
        delta_ref[head : head + 1, :] = jnp.sum(
            got_ref[own, :].astype(F32) * ot_ref[own, :], axis=0, keepdims=True
        )
    lane = iota((1, LANES), 1)
    for head in range(heads):
        own = slice(HD * head, HD * (head + 1))
        mask = (lane // HD == head).astype(F32).astype(BF)
        for start in range(0, total, q_block):
            cols = slice(start, start + q_block)
            scores = dot(k_ref[...], head_rows(qt_ref[:, cols], head, heads))
            probs = jnp.exp(scores - lse_ref[head : head + 1, cols])
            prob_grad = dot(v_ref[...], head_rows(got_ref[:, cols], head, heads))
            score_grad = (probs * (prob_grad - delta_ref[head : head + 1, cols])).astype(BF)
            value_part = dot(probs.astype(BF), go_ref[cols, :] * mask)
            key_part = dot(score_grad, q_ref[cols, :] * mask)
            if head == 0 and start == 0:
                dv_ref[...] = value_part
                dk_ref[...] = key_part
            else:
                dv_ref[...] += value_part
                dk_ref[...] += key_part
            dqt_ref[own, cols] = dot(kt_ref[own, :], score_grad)
    dqt_ref[cols_all:, :] = jnp.zeros((LANES - cols_all, total), F32)
    sums_q = jnp.zeros((1, LANES), F32)
    sums_v = jnp.zeros((1, LANES), F32)
    for n in range(4):
        here = slice(n * rows, (n + 1) * rows)
        query_grad = dqt_ref[:, here].T * scale
        value_grad = dv_ref[here, :]
        sums_q = sums_q + jnp.sum(query_grad, axis=0, keepdims=True)
        sums_v = sums_v + jnp.sum(value_grad, axis=0, keepdims=True)
        low_q = query_grad.astype(BF)
        low_k = dk_ref[here, :].astype(BF)
        low_v = value_grad.astype(BF)
        gq_ref[here, :] = low_q[:, :cols_all]
        gk_ref[here, :] = low_k[:, :cols_all]
        gv_ref[here, :] = low_v[:, :cols_all]
        back = dot(low_q, wq_ref[...]) + dot(low_k, wk_ref[...]) + dot(low_v, wv_ref[...])
        out_ref = keep_ref if n < 2 else near_ref
        out_ref[n % 2 * rows : (n % 2 + 1) * rows, :] = back.astype(BF)
    sum_ref[0:1, :] = sums_q
    sum_ref[1:2, :] = sums_v
    sum_ref[2:, :] = jnp.zeros((6, LANES), F32)


def attention_grad(came, saved, weights, heads, q_block=512):
    half, cols = came[0].shape
    total = 2 * half
    width = weights[0].shape[1]
    return pl.pallas_call(
        functools.partial(attention_grad_kernel, q_block, heads),
        out_shape=[
            jax.ShapeDtypeStruct((half, width), BF),
            jax.ShapeDtypeStruct((half, width), BF),
            jax.ShapeDtypeStruct((total, cols), BF),
            jax.ShapeDtypeStruct((total, cols), BF),
            jax.ShapeDtypeStruct((total, cols), BF),
            jax.ShapeDtypeStruct((8, LANES), F32),
        ],
        scratch_shapes=[
            pltpu.VMEM((total, LANES), BF),
            pltpu.VMEM((LANES, total), BF),
            pltpu.VMEM((LANES, total), BF),
            pltpu.VMEM((8, total), F32),
            pltpu.VMEM((LANES, total), F32),
            pltpu.VMEM((total, LANES), F32),
            pltpu.VMEM((total, LANES), F32),
        ],
        compiler_params=params(WIDE_MIB),
        cost_estimate=cost(0.1),
    )(*came, *saved, *weights)


def put_half(n, value, keep_ref, near_ref):
    @pl.when(n < 2)
    def _():
        keep_ref[...] = value

    @pl.when(n >= 2)
    def _():
        near_ref[...] = value


def feed_kernel(a0_ref, a1_ref, a2_ref, a3_ref, normed_ref, o0_ref, o1_ref, o2_ref, o3_ref, ob_ref, gain_ref, bias_ref,
                up_ref, ub_ref, down_ref,
                low_ref, act_ref, slope_ref, keep_ref, near_ref, own_ref, hat_ref, inv_ref):
    n = pl.program_id(0)
    total = normed_ref[...] + ob_ref[...]
    out_refs = (o0_ref, o1_ref, o2_ref, o3_ref)
    for ref, out_ref in zip((a0_ref, a1_ref, a2_ref, a3_ref), out_refs):
        total = total + dot(ref[...], out_ref[...])
    hat, inv = norm_stats(total)
    normed = hat * gain_ref[...] + bias_ref[...]

    @pl.when(n == 0)
    def _():
        own_ref[...] = normed
        hat_ref[...] = hat
        inv_ref[...] = jnp.broadcast_to(inv, inv_ref.shape)

    low = normed.astype(BF)
    low_ref[...] = low
    value, slope = phi_pair(dot(low, up_ref[...]) + ub_ref[...])
    slope_ref[...] = slope
    value = value.astype(BF)
    act_ref[...] = value
    put_half(n, dot(value, down_ref[...]).astype(BF), keep_ref, near_ref)


def feed(attended, normed, out_pieces, out_bias, norm, up_weight, up_bias, down_weight):
    total, width = normed.shape
    rows = total // 4
    part = attended[0].shape[1]
    units = up_weight.shape[1]
    here = lambda n: (n, 0)
    return pl.pallas_call(
        feed_kernel,
        grid=(4,),
        in_specs=[block((rows, part), lambda n, i=i: (n ^ i, 0)) for i in range(4)]
        + [block((rows, width), here)]
        + [full((part, width))] * 4
        + [
            full((1, width)),
            full((1, width)),
            full((1, width)),
            full((width, units)),
            full((1, units)),
            full((units, width)),
        ],
        out_specs=[
            block((rows, width), here),
            block((rows, units), here),
            block((rows, units), here),
            block((rows, width), lambda n: (jnp.minimum(n, 1), 0)),
            block((rows, width), lambda n: (jnp.maximum(n - 2, 0), 0)),
            full((rows, width)),
            full((rows, width)),
            full((rows, 128)),
        ],
        out_shape=[
            jax.ShapeDtypeStruct((total, width), BF),
            jax.ShapeDtypeStruct((total, units), BF),
            jax.ShapeDtypeStruct((total, units), F32),
            jax.ShapeDtypeStruct((total // 2, width), BF),
            jax.ShapeDtypeStruct((total // 2, width), BF),
            jax.ShapeDtypeStruct((rows, width), F32),
            jax.ShapeDtypeStruct((rows, width), F32),
            jax.ShapeDtypeStruct((rows, 128), F32),
        ],
        compiler_params=params(WIDE_MIB),
        cost_estimate=cost(10),
    )(*attended, normed, *out_pieces, out_bias, *norm, up_weight, up_bias, down_weight)


def feed_grad_kernel(g0_ref, g1_ref, g2_ref, g3_ref, slope_ref, up_ref, down_ref,
                     all_ref, low_ref, keep_ref, near_ref, bias_ref):
    n = pl.program_id(0)
    for i, ref in enumerate((g0_ref, g1_ref, g2_ref, g3_ref)):

        @pl.when(n == i)
        def _():
            all_ref[...] = ref[...]

    grad = dot_turned(all_ref[...], down_ref[...]) * slope_ref[...]

    @pl.when(n == 0)
    def _():
        bias_ref[...] = jnp.zeros_like(bias_ref)

    bias_ref[...] += jnp.sum(grad, axis=0, keepdims=True)
    low = grad.astype(BF)
    low_ref[...] = low
    put_half(n, dot_turned(low, up_ref[...]).astype(BF), keep_ref, near_ref)


def feed_grad(grads, slope, up_weight, down_weight):
    total, units = slope.shape
    rows, width = grads[0].shape
    here = lambda n: (n, 0)
    return pl.pallas_call(
        feed_grad_kernel,
        grid=(4,),
        in_specs=[full((rows, width))] * 4
        + [block((rows, units), here), full((width, units)), full((units, width))],
        out_specs=[
            block((rows, width), here),
            block((rows, units), here),
            block((rows, width), lambda n: (jnp.minimum(n, 1), 0)),
            block((rows, width), lambda n: (jnp.maximum(n - 2, 0), 0)),
            full((1, units)),
        ],
        out_shape=[
            jax.ShapeDtypeStruct((total, width), BF),
            jax.ShapeDtypeStruct((total, units), BF),
            jax.ShapeDtypeStruct((total // 2, width), BF),
            jax.ShapeDtypeStruct((total // 2, width), BF),
            jax.ShapeDtypeStruct((1, units), F32),
        ],
        compiler_params=params(WIDE_MIB),
        cost_estimate=cost(6),
    )(*grads, slope, up_weight, down_weight)


def came_pieces(keep_ref, far_ref, near_ref):
    rows = far_ref.shape[0] // 2
    return [keep_ref[:rows, :], far_ref[:rows, :], near_ref[:rows, :], far_ref[rows:, :]]


def put_sums(sum_ref, *values):
    sum_ref[...] = jnp.zeros_like(sum_ref)
    for i, value in enumerate(values):
        sum_ref[i : i + 1, :] = jnp.sum(value, axis=0, keepdims=True)


def norm_grad(grad, hat, inv, gain):
    scaled = grad * gain
    return inv * (
        scaled
        - jnp.mean(scaled, axis=-1, keepdims=True)
        - hat * jnp.mean(scaled * hat, axis=-1, keepdims=True)
    )


def last_norm_kernel(keep_ref, near_ref, far_ref, normed_ref, cot_ref, down_ref, gain_ref, bias_ref,
                     out_ref, grad_ref, low_ref, sum_ref):
    total = keep_ref[...].astype(F32) + near_ref[...].astype(F32) + far_ref[...].astype(F32)
    hat, inv = norm_stats(normed_ref[...] + total + down_ref[...])
    gain = gain_ref[...]
    out_ref[...] = (hat * gain + bias_ref[...]).astype(BF)
    cot = cot_ref[...].astype(F32)
    grad = norm_grad(cot, hat, inv, gain)
    grad_ref[...] = grad
    low_ref[...] = grad.astype(BF)
    put_sums(sum_ref, cot * hat, cot, grad)


def last_norm(terms, normed, cotangent, down_bias, gain, bias):
    rows, width = normed.shape
    return pl.pallas_call(
        last_norm_kernel,
        grid=(1,),
        in_specs=[full((rows, width))] * 5 + [full((1, width))] * 3,
        out_specs=[full((rows, width))] * 3 + [full((8, width))],
        out_shape=[
            jax.ShapeDtypeStruct((rows, width), BF),
            jax.ShapeDtypeStruct((rows, width), F32),
            jax.ShapeDtypeStruct((rows, width), BF),
            jax.ShapeDtypeStruct((8, width), F32),
        ],
        compiler_params=params(WIDE_MIB),
        cost_estimate=cost(3),
    )(*terms, normed, cotangent, down_bias, gain, bias)


def middle_norm_kernel(keep_ref, near_ref, far_ref, grad_ref, hat_ref, inv_ref, gain_ref, o0_ref,
                       o1_ref, o2_ref, o3_ref, out_ref, low_ref, sum_ref, keep_out, near_out):
    rows = grad_ref.shape[0]
    total = keep_ref[...].astype(F32) + near_ref[...].astype(F32) + far_ref[...].astype(F32)
    total = total + grad_ref[...]
    hat = hat_ref[...]
    grad = norm_grad(total, hat, inv_ref[:, 0:1], gain_ref[...])
    out_ref[...] = grad
    low = grad.astype(BF)
    low_ref[...] = low
    put_sums(sum_ref, total * hat, total, grad)
    for n, ref in enumerate((o0_ref, o1_ref, o2_ref, o3_ref)):
        back = dot_turned(low, ref[...]).astype(BF)
        out = keep_out if n < 2 else near_out
        out[n % 2 * rows : (n % 2 + 1) * rows, :] = back


def middle_norm(terms, grad, hat, inv, gain, out_pieces):
    rows, width = grad.shape
    part = out_pieces[0].shape[0]
    return pl.pallas_call(
        middle_norm_kernel,
        grid=(1,),
        in_specs=[full((rows, width))] * 5
        + [full((rows, 128)), full((1, width))]
        + [full((part, width))] * 4,
        out_specs=[full((rows, width))] * 2 + [full((8, width))] + [full((2 * rows, part))] * 2,
        out_shape=[
            jax.ShapeDtypeStruct((rows, width), F32),
            jax.ShapeDtypeStruct((rows, width), BF),
            jax.ShapeDtypeStruct((8, width), F32),
            jax.ShapeDtypeStruct((2 * rows, part), BF),
            jax.ShapeDtypeStruct((2 * rows, part), BF),
        ],
        compiler_params=params(WIDE_MIB),
        cost_estimate=cost(0.1),
    )(*terms, grad, hat, inv, gain, *out_pieces)


def first_norm_kernel(me_ref, keep_ref, near_ref, far_ref, grad_ref, hat_ref, inv_ref, gain_ref,
                      out_ref, sum_ref, keep_out, near_out):
    rows, width = grad_ref.shape
    part = keep_out.shape[1]
    total = keep_ref[...].astype(F32) + near_ref[...].astype(F32) + far_ref[...].astype(F32)
    total = total + grad_ref[...]
    hat = hat_ref[...]
    grad = norm_grad(total, hat, inv_ref[:, 0:1], gain_ref[...])
    out_ref[...] = grad
    low = grad.astype(BF)
    put_sums(sum_ref, total * hat, total)
    row, lane = iota((width, part), 0), iota((width, part), 1)
    for n in range(4):
        pick = (row == lane + part * (me_ref[0] ^ ORDER[n])).astype(F32).astype(BF)
        out = keep_out if n < 2 else near_out
        out[n % 2 * rows : (n % 2 + 1) * rows, :] = dot(low, pick).astype(BF)


def first_norm(me, terms, grad, hat, inv, gain):
    rows, width = grad.shape
    part = width // 4
    return pl.pallas_call(
        first_norm_kernel,
        grid=(1,),
        in_specs=[pl.BlockSpec(memory_space=pltpu.SMEM)]
        + [full((rows, width))] * 5
        + [full((rows, 128)), full((1, width))],
        out_specs=[full((rows, width)), full((8, width))] + [full((2 * rows, part))] * 2,
        out_shape=[
            jax.ShapeDtypeStruct((rows, width), F32),
            jax.ShapeDtypeStruct((8, width), F32),
            jax.ShapeDtypeStruct((2 * rows, part), BF),
            jax.ShapeDtypeStruct((2 * rows, part), BF),
        ],
        compiler_params=params(WIDE_MIB),
        cost_estimate=cost(0.1),
    )(me, *terms, grad, hat, inv, gain)


def frames_grad_kernel(me_ref, keep_ref, far_ref, near_ref, grad_ref, out_ref):
    width = grad_ref.shape[1]
    part = keep_ref.shape[1]
    row, lane = iota((part, width), 0), iota((part, width), 1)
    total = grad_ref[...]
    for n, piece in enumerate(came_pieces(keep_ref, far_ref, near_ref)):
        spot = (lane == row + part * (me_ref[0] ^ ORDER[n])).astype(F32).astype(BF)
        total = total + dot(piece, spot)
    out_ref[...] = total


def add_frames_grad(me, came, grad):
    half, part = came[0].shape
    rows, width = grad.shape
    return pl.pallas_call(
        frames_grad_kernel,
        grid=(1,),
        in_specs=[pl.BlockSpec(memory_space=pltpu.SMEM)]
        + [full((half, part))] * 3
        + [full((rows, width))],
        out_specs=full((rows, width)),
        out_shape=jax.ShapeDtypeStruct((rows, width), F32),
        compiler_params=params(WIDE_MIB),
        cost_estimate=cost(0.1),
    )(me, *came, grad)


def swap(value, bit):
    return lax.ppermute(value, "tp", [(i, i ^ bit) for i in range(lax.axis_size("tp"))])


def gather_pieces(value):
    across = swap(value, 2)
    return [value, across, swap(value, 1), swap(across, 1)]


def scatter_terms(keep, near):
    piece = keep.shape[0] // 2
    came = swap(near, 1)
    pair = (keep[piece:].astype(F32) + came[piece:].astype(F32)).astype(BF)
    return [keep, came, swap(pair, 2)], pair


def exchange(keep, near, *ahead):
    rows = keep.shape[0] // 2
    came = swap(near, 1)
    pair = after(jnp.concatenate([keep[rows:], came[rows:]], axis=0), *ahead)
    return [keep, swap(pair, 2), came], pair


def after(value, *others):
    return lax.optimization_barrier((value, *others))[0]


def all_after(values, *others):
    return list(lax.optimization_barrier((*values, *others))[: len(values)])


def team_groups(row_count, team):
    if row_count == team:
        return None
    return [list(range(first, first + team)) for first in range(0, row_count, team)]


def cross_groups(row_count, team):
    return [list(range(first, row_count, team)) for first in range(team)]


def pair_rows(value, mask):
    count = lax.axis_size("rows")
    return lax.ppermute(value, "rows", [(i, i ^ mask) for i in range(count)])


FEED_MASKS = ((1, 2, 6), (2, 1, 6))


def side_of(index, mask):
    bits = [(index >> i) & 1 for i in range(3)]
    return {1: bits[0], 2: bits[1] ^ bits[2], 6: bits[2]}[mask]


def holders_of(masks):
    part = lambda index: sum(side_of(index, m) << (2 - i) for i, m in enumerate(masks))
    return sorted(range(8), key=part)


def halve(value, mask, side):
    half = value.shape[0] // 2
    kept = lax.dynamic_slice_in_dim(value, side * half, half, 0)
    sent = lax.dynamic_slice_in_dim(value, (1 - side) * half, half, 0)
    return kept, pair_rows(sent, mask)


def add_low(kept, came):
    return (kept.astype(F32) + came.astype(F32)).astype(BF)


def gather_step(held, offsets, mask):
    held = jnp.concatenate([held, pair_rows(held, mask)], axis=0)
    return held, offsets + [x ^ mask for x in offsets]


def on_device(
    frames,
    seg_starts,
    conv_weight,
    conv_bias,
    norm_gain0,
    norm_bias0,
    qkv_weight,
    qv_bias,
    out_weight,
    out_bias,
    norm_gain1,
    norm_bias1,
    up_weight,
    up_bias,
    down_weight,
    down_bias,
    norm_gain2,
    norm_bias2,
    cotangent,
):
    head_cols = qkv_weight.shape[2]
    heads_here = head_cols // HD
    groups_here = conv_weight.shape[2] // GW
    team = 2 * groups_here
    row_count = lax.axis_size("rows")
    teams = team_groups(row_count, team)
    me = lax.axis_index("tp")
    me_word = me.reshape(1).astype(jnp.int32)
    own_row = lax.axis_index("rows") % team
    positions = jnp.arange(LEN, dtype=jnp.int32)
    segments = (
        jnp.sum((positions[:, None] >= seg_starts[0][None, :]).astype(jnp.int32), axis=1) - 1
    )
    line = lambda value: value.astype(F32).reshape(1, -1)

    slots = spread_slots(segments)
    conv_flat = lax.optimization_barrier(conv_weight.reshape(KER * GW, -1))
    put = (iota((SLOTS, LEN), 0) == after(slots, conv_flat)[None, :]).astype(BF)
    ext = extension()
    bias_lanes = jnp.tile(conv_bias.astype(F32).reshape(groups_here, 1, GW), (1, 1, PH))
    bias_lanes = jnp.pad(bias_lanes, ((0, 0), (0, 0), (0, LANES - PH * GW)))
    frames_pieces = gather_pieces(frames)
    lane = jnp.arange(LANES, dtype=jnp.int32)[None, :] - head_cols
    seg_rows = segments.reshape(4, -1)
    seg_own = jnp.concatenate(
        [lax.dynamic_index_in_dim(seg_rows, me ^ m, 0, keepdims=False) for m in ORDER]
    )
    in_seg = lane == seg_own[:, None]
    of_seg = (lane >= 0) & (lane < seg_starts.shape[1])
    features = [
        jnp.where(in_seg, MASK_ROOT, 0.0).astype(BF),
        jnp.where(of_seg & ~in_seg, -MASK_ROOT, 0.0).astype(BF),
    ]
    qkv_padded = jnp.pad(
        qkv_weight.transpose(1, 2, 0), ((0, 0), (0, LANES - head_cols), (0, 0))
    )
    qkv_parts = [qkv_padded[0], qkv_padded[1], qkv_padded[2]]
    out_pieces = gather_pieces(out_weight)
    frames_pieces = all_after(frames_pieces, *features, qkv_padded, out_pieces[1])
    mixed_low, slope0, core = conv(me_word, frames_pieces, put, ext, conv_flat, bias_lanes)

    qv_padded = jnp.pad(qv_bias.astype(F32), ((0, 0), (0, LANES - head_cols)))
    gain0 = line(norm_gain0)
    mixed_pieces = gather_pieces(mixed_low)
    (attended, normed0, hat0, inv0, normed0_all, normed0_low, *saved) = attention(
        me_word,
        mixed_pieces,
        frames_pieces,
        [gain0, line(norm_bias0)],
        qkv_parts,
        [qv_padded[0:1], qv_padded[1:2]],
        features,
        heads_here,
    )

    core_all = lax.all_to_all(
        jnp.repeat(core, 2, axis=0), "rows", 0, 0, axis_index_groups=teams, tiled=True
    )
    attended = after(attended, core_all)
    attended_pieces = gather_pieces(attended)
    gain1 = line(norm_gain1)
    normed1_low, activated, slope1, keep, near, normed1, hat1, inv1 = feed(
        attended_pieces,
        normed0_all,
        out_pieces,
        line(out_bias),
        [gain1, line(norm_bias1)],
        up_weight,
        line(up_bias),
        down_weight,
    )
    terms, pair = scatter_terms(keep, near)
    block_out, grad2, grad2_low, sums2 = last_norm(
        terms,
        normed1,
        cotangent,
        line(down_bias),
        line(norm_gain2),
        line(norm_bias2),
    )

    grad2_all, up_low, keep, near, up_bias_grad = feed_grad(
        gather_pieces(grad2_low), slope1, up_weight, down_weight
    )
    terms, pair = scatter_terms(keep, near)
    activated, normed1_low = all_after([activated, normed1_low], pair)
    down_grad = jnp.einsum("rf,rd->fd", activated, grad2_all, preferred_element_type=F32)
    up_grad = jnp.einsum("rd,rf->df", normed1_low, up_low, preferred_element_type=F32)
    feed_grads = [down_grad.astype(BF), up_grad.astype(BF)]
    terms = all_after(terms, *feed_grads)
    feed_steps = [[(mask, side_of(own_row, mask)) for mask in masks] for masks in FEED_MASKS]
    halves_1 = [halve(grad, *order[0]) for grad, order in zip(feed_grads, feed_steps)]

    grad1, grad1_low, sums1, keep, near = middle_norm(terms, grad2, hat1, inv1, gain1, out_pieces)
    came, pair = exchange(keep, near, *[other for kept, other in halves_1])
    feed_sums = [add_low(after(kept, pair), other) for kept, other in halves_1]
    came = all_after(came, *feed_sums)
    halves_2 = [halve(grad, *order[1]) for grad, order in zip(feed_sums, feed_steps)]
    keep, near, query_grad, key_grad, value_grad, qv_sums = attention_grad(
        came, saved, qkv_parts, heads_here
    )
    grad1_pieces = gather_pieces(after(grad1_low, *came))
    feed_sums = [add_low(after(kept, keep), other) for kept, other in halves_2]
    near = after(near, *feed_sums, grad1_pieces[1], grad1_pieces[2])
    terms, pair = scatter_terms(keep, near)
    halves_3 = [halve(grad, *order[2]) for grad, order in zip(feed_sums, feed_steps)]
    out_grad = jnp.einsum(
        "rh,rd->hd",
        after(attended, pair),
        jnp.concatenate(grad1_pieces, axis=0),
        preferred_element_type=F32,
    )
    normed0_low = after(normed0_low, pair)
    turned_grads = [
        jnp.einsum("rc,rd->cd", part, normed0_low, preferred_element_type=F32).astype(BF)
        for part in (query_grad, key_grad, value_grad)
    ]
    tail = jnp.concatenate(turned_grads + [out_grad.astype(BF)], axis=0)
    feed_sums = jnp.stack([add_low(after(kept, pair), other) for kept, other in halves_3])
    if teams is not None:
        feed_sums = lax.psum(feed_sums, "rows", axis_index_groups=cross_groups(row_count, team))
    terms = all_after(terms, tail, feed_sums)
    feed_held, offsets_f = feed_sums[None], [0]
    feed_came = pair_rows(feed_held, 2)
    qv_grad = qv_sums[:2, :head_cols]
    tail_steps = feed_steps[0]
    tail_half = halve(tail, *tail_steps[0])
    grad0, sums0, keep, near = first_norm(me_word, terms, grad1, hat0, inv0, gain0)

    near = after(near, feed_came)
    feed_held = jnp.concatenate([feed_held, feed_came], axis=0)
    offsets_f = offsets_f + [x ^ 2 for x in offsets_f]
    came, pair = exchange(keep, near)
    feed_came = pair_rows(after(feed_held, pair), 6)
    tail_sum = add_low(after(tail_half[0], pair), tail_half[1])
    came = all_after(came, tail_sum)
    tail_half = halve(tail_sum, *tail_steps[1])
    wide, halves, conv_bias_grad = conv_grad(me_word, came, put, slope0, ext)
    conv_bias_grad = conv_bias_grad[:, 0, : PH * GW].reshape(groups_here, PH, GW)
    conv_bias_grad = jnp.sum(conv_bias_grad, axis=1).reshape(-1)
    halves_all = lax.all_to_all(halves, "rows", 0, 0, axis_index_groups=teams, tiled=True)
    turned_core = turn_core(after(core_all, halves), ext)
    wide = after(wide, feed_came)
    feed_held = jnp.concatenate([feed_held, feed_came], axis=0)
    offsets_f = offsets_f + [x ^ 6 for x in offsets_f]
    feed_came = pair_rows(feed_held, 1)
    offsets_f = offsets_f + [x ^ 1 for x in offsets_f]
    signal_slots = signal_grad(wide, conv_flat, 0, groups_here // 2)
    tail_sum = add_low(after(tail_half[0], signal_slots), tail_half[1])
    tail_half = halve(tail_sum, *tail_steps[2])
    halves_all = after(halves_all, signal_slots, tail_sum)
    kernel_part = tap_grad(turned_core, halves_all)
    tail_part = add_low(after(tail_half[0], kernel_part), tail_half[1])

    shared = jnp.concatenate([sums0[:2], sums1[:3], sums2[:3]], axis=0)
    all_small = [shared[i] for i in range(shared.shape[0])]
    rows_small = [conv_bias_grad, qv_grad, up_bias_grad]
    shared = shared + swap(shared, 1)
    shared = shared + swap(shared, 2)
    small = jnp.concatenate([shared.reshape(-1)] + [v.reshape(-1) for v in rows_small])
    small_size = small.size
    small = jnp.pad(small, (0, -small_size % (16 * KER))).reshape(-1, KER)
    if teams is not None:
        others = cross_groups(row_count, team)
        kernel_part = lax.psum(kernel_part, "rows", axis_index_groups=others)
        tail_part = lax.psum(tail_part.astype(F32), "rows", axis_index_groups=others)
        small = lax.psum(small, "rows", axis_index_groups=others)
    small_high = small.astype(BF)
    small_low = (small - small_high.astype(F32)).astype(BF)
    part_rows = kernel_part.shape[0] // 2
    part_low = kernel_part.astype(BF)
    tail_low = tail_part.astype(BF).reshape(2, -1, KER)
    held_a = jnp.concatenate([part_low[:part_rows], tail_low[0], small_high], axis=0)[None]
    held_b = jnp.concatenate([part_low[part_rows:], tail_low[1], small_low], axis=0)[None]
    held_a, offsets_a = gather_step(held_a, [0], 2)
    held_b, offsets_b = gather_step(held_b, [0], 1)
    keep, near = signal_grad(
        after(wide, kernel_part),
        conv_flat,
        groups_here // 2,
        groups_here - groups_here // 2,
        signal_slots,
        put,
        me_word,
    )
    held_a, held_b, keep, near = all_after([held_a, held_b, keep, near], feed_came)
    held_a, offsets_a = gather_step(held_a, offsets_a, 6)
    held_b, offsets_b = gather_step(held_b, offsets_b, 2)
    came, pair = exchange(keep, near)
    frames_grad = add_frames_grad(me_word, came, grad0)
    order_f = jnp.array(
        [
            [[offsets_f.index(r ^ own) for r in holders_of(masks)] for masks in FEED_MASKS]
            for own in range(team)
        ],
        jnp.int32,
    )
    down_total, up_total = spread_parts(
        lax.dynamic_index_in_dim(order_f, own_row, 0, keepdims=False),
        after(feed_held, held_a, held_b),
        feed_came,
    )
    came_a, came_b = pair_rows(held_a, 1), pair_rows(held_b, 6)
    offsets_a = offsets_a + [x ^ 1 for x in offsets_a]
    offsets_b = offsets_b + [x ^ 6 for x in offsets_b]
    order = jnp.array(
        [[offsets.index(x) for x in range(team)] for offsets in (offsets_a, offsets_b)], jnp.int32
    )
    order = order[:, jnp.arange(team, dtype=jnp.int32) ^ own_row]
    kernel_total = assemble(order, [held_a, came_a], [held_b, came_b]).transpose(2, 0, 1)
    tail_rows = tail_low.shape[1]
    small = sum(
        jnp.sum(value[:, part_rows + tail_rows :].astype(F32), axis=0)
        for value in (held_a, came_a, held_b, came_b)
    )
    tail_total = jnp.stack(
        [
            jnp.concatenate(
                [value[:, part_rows : part_rows + tail_rows] for value in values], axis=0
            )[order[i][jnp.array(holders_of(FEED_MASKS[0]))]]
            for i, values in enumerate(((held_a, came_a), (held_b, came_b)))
        ],
        axis=1,
    )
    tail_total = tail_total.reshape(-1, D).astype(F32)
    qkv_total = tail_total[: 3 * head_cols].reshape(3, head_cols, D).transpose(2, 0, 1)
    out_total = tail_total[3 * head_cols :]
    small = small.reshape(-1)[:small_size]
    sizes = [v.size for v in all_small + rows_small]
    ends = [sum(sizes[: i + 1]) for i in range(len(sizes))]
    cuts = [small[end - size : end] for size, end in zip(sizes, ends)]
    gain0_grad, bias0_grad, gain1_grad, bias1_grad, out_bias_grad = cuts[:5]
    gain2_grad, bias2_grad, down_bias_grad, conv_bias_grad, qv_grad, up_bias_grad = cuts[5:]
    return (
        block_out,
        frames_grad,
        kernel_total,
        conv_bias_grad,
        gain0_grad,
        bias0_grad,
        qkv_total,
        qv_grad.reshape(2, head_cols),
        out_total,
        out_bias_grad,
        gain1_grad,
        bias1_grad,
        up_total,
        up_bias_grad,
        down_total,
        down_bias_grad,
        gain2_grad,
        bias2_grad,
    )


def solution(mesh):
    return jax.shard_map(
        on_device,
        mesh=mesh,
        in_specs=(
            P(("rows", "tp"), None),
            P("rows", None),
            P(None, None, "tp"),
            P("tp"),
            P(),
            P(),
            P(None, None, "tp"),
            P(None, "tp"),
            P("tp", None),
            P(),
            P(),
            P(),
            P(None, "tp"),
            P("tp"),
            P("tp", None),
            P(),
            P(),
            P(),
            P(("rows", "tp"), None),
        ),
        out_specs=(
            P(("rows", "tp"), None),
            P(("rows", "tp"), None),
            P(None, None, "tp"),
            P("tp"),
            P(),
            P(),
            P(None, None, "tp"),
            P(None, "tp"),
            P("tp", None),
            P(),
            P(),
            P(),
            P(None, "tp"),
            P("tp"),
            P("tp", None),
            P(),
            P(),
            P(),
        ),
        check_vma=False,
    )
```

```python
import functools

import jax
import jax.numpy as jnp
import numpy as np
from jax import lax
from jax.experimental import pallas as pl
from jax.experimental.pallas import tpu as pltpu
from jax.sharding import PartitionSpec as P

D = 768
HD = 64
KER = 128
GROUPS = 16
LEN = 1024

EPSILON = 1e-05
ROOT_HALF = 0.7071067811865476
INV_ROOT_TAU = 0.3989422804014327
MASK_ROOT = 16384.0

GW = D // GROUPS
HALF = GW // 2
PH = 5
QN, PN = 17, 16
CORE = QN * PN
NJ = 27
LEAD = 13
EXT = (QN + NJ - 1) * PN
LANES = 256
GAP = KER // 2
SLOTS = PH * CORE
WIDE_MIB = 58

ORDER = (0, 2, 1, 3)

BF = jnp.bfloat16
F32 = jnp.float32


def iota(shape, dim):
    return lax.broadcasted_iota(jnp.int32, shape, dim)


def full(shape):
    return pl.BlockSpec(shape, lambda *index: (0,) * len(shape))


def block(shape, index_map):
    return pl.BlockSpec(shape, index_map)


def params(mib):
    return pltpu.CompilerParams(vmem_limit_bytes=mib * 2**20)


def cost(microseconds):
    return pl.CostEstimate(
        flops=int(microseconds * 1.1e+09), bytes_accessed=int(microseconds * 1e+06), transcendentals=0
    )


def dot(left, right):
    return jnp.dot(left, right, preferred_element_type=F32)


def dot_turned(left, right):
    return lax.dot_general(left, right, (((1,), (1,)), ((), ())), preferred_element_type=F32)


def phi_pair(v):
    cdf = 0.5 * (1.0 + lax.erf(v * ROOT_HALF))
    return v * cdf, cdf + v * INV_ROOT_TAU * jnp.exp(-0.5 * v * v)


def norm_stats(inputs):
    centered = inputs - jnp.mean(inputs, axis=-1, keepdims=True)
    inv_std = lax.rsqrt(jnp.mean(centered * centered, axis=-1, keepdims=True) + EPSILON)
    return centered * inv_std, inv_std


def spread_slots(segments):
    place = jnp.arange(LEN, dtype=jnp.int32) + GAP * segments
    at = place // PH
    return place % PH * CORE + at % QN * PN + at // QN


def extension():
    row, col = np.arange(EXT)[:, None], np.arange(CORE)[None, :]
    want = QN * (row % PN) + row // PN - LEAD
    have = QN * (col % PN) + col // PN
    return jnp.asarray((want == have).astype(np.float32), BF)


def toeplitz_scratch():
    return [
        pltpu.VMEM((PH * GW + KER * GW + 288, LANES), BF),
        pltpu.VMEM((NJ * LANES, LANES), BF),
    ]


def fill_toeplitz(w_ref, step, g, wide_ref, wt_ref):
    before = PH * GW
    row, lane = iota((w_ref.shape[1], LANES), 0), iota((w_ref.shape[1], LANES), 1)
    spread = ((row == GW * g + lane % GW) & (lane < PH * GW)).astype(F32).astype(BF)

    @pl.when(step == 0)
    def _():
        rest = before + KER * GW
        wide_ref[0:before, :] = jnp.zeros((before, LANES), BF)
        wide_ref[rest:, :] = jnp.zeros((wide_ref.shape[0] - rest, LANES), BF)
        for j in range(NJ):
            gap = slice(j * LANES + PH * GW, (j + 1) * LANES)
            wt_ref[gap, :] = jnp.zeros((LANES - PH * GW, LANES), BF)

    wide_ref[before : before + KER * GW, :] = dot(w_ref[...], spread).astype(BF)
    lane = iota((1, LANES), 1)
    masks = [(lane // GW == i).astype(F32).astype(BF) for i in range(PH)]

    for j in range(NJ):
        for left in range(0, LANES, 128):
            lanes = slice(left, left + 128)
            total = None
            for i in range(left // GW, min((left + 127) // GW + 1, PH)):
                start = before + PH * GW * j - GW * (1 + i)
                part = wide_ref[start : start + PH * GW, lanes] * masks[i][:, lanes]
                total = part if total is None else total + part
            wt_ref[j * LANES : j * LANES + PH * GW, lanes] = total


def fold_in(slots_ref, g):
    width = slots_ref.shape[1]
    row, lane = iota((width, LANES), 0), iota((width, LANES), 1)
    core = jnp.zeros((CORE, LANES), F32)
    for i in range(PH):
        pick = ((lane // GW == i) & (row == GW * g + lane % GW)).astype(F32).astype(BF)
        core = core + dot(slots_ref[i * CORE : (i + 1) * CORE, :], pick)
    return core


def fold_out(values, back_ref, g):
    width = back_ref.shape[1]
    row, col = iota((LANES, width), 0), iota((LANES, width), 1)
    for i in range(PH):
        pick = ((row // GW == i) & (col == GW * g + row % GW)).astype(F32).astype(BF)
        here = slice(i * CORE, (i + 1) * CORE)
        back_ref[here, :] = back_ref[here, :] + dot(values, pick).astype(BF)


def unspread(back_ref, put_ref):
    turned = back_ref[...].astype(F32).T.astype(BF)
    return dot(turned, put_ref[...]).T.astype(BF)


def conv_kernel(me_ref, f0_ref, f1_ref, f2_ref, f3_ref, put_ref, ext_ref, w_ref, bias_ref,
                mixed_ref, slope_ref, core_ref, sig_ref, slots_ref, wide_ref, back_ref, taps_ref,
                wt_ref):
    g = pl.program_id(0)
    rows, features = f0_ref.shape
    width = sig_ref.shape[1]

    @pl.when(g == 0)
    def _():
        row, lane = iota((features, width), 0), iota((features, width), 1)
        pick = (row == lane + width * me_ref[0]).astype(F32).astype(BF)
        for n, ref in enumerate((f0_ref, f1_ref, f2_ref, f3_ref)):
            start = pl.multiple_of((me_ref[0] ^ ORDER[n]) * rows, rows)
            sig_ref[pl.ds(start, rows), :] = dot(ref[...], pick).astype(BF)
        slots_ref[...] = dot(put_ref[...], sig_ref[...]).astype(BF)
        back_ref[...] = jnp.zeros_like(back_ref)

    fill_toeplitz(w_ref, g, g, taps_ref, wt_ref)
    core = fold_in(slots_ref, g).astype(BF)
    core_ref[0] = core
    wide_ref[...] = dot(ext_ref[...], core).astype(BF)
    total = jnp.zeros((CORE, LANES), F32)
    for j in range(NJ):
        total = total + dot(
            wide_ref[PN * j : PN * j + CORE, :], wt_ref[j * LANES : (j + 1) * LANES, :]
        )
    value, slope = phi_pair(total + bias_ref[0])
    slope_ref[0] = slope
    fold_out(value.astype(BF), back_ref, g)

    @pl.when(g == pl.num_programs(0) - 1)
    def _():
        mixed_ref[...] = unspread(back_ref, put_ref)


def conv(me, frames, put, ext, taps, bias_lanes):
    width = taps.shape[1]
    groups = width // GW
    return pl.pallas_call(
        conv_kernel,
        grid=(groups,),
        in_specs=[pl.BlockSpec(memory_space=pltpu.SMEM)]
        + [full(frames[0].shape)] * 4
        + [
            full((SLOTS, LEN)),
            full((EXT, CORE)),
            full(taps.shape),
            block((1, 1, LANES), lambda g: (g, 0, 0)),
        ],
        out_specs=[
            full((LEN, width)),
            block((1, CORE, LANES), lambda g: (g, 0, 0)),
            block((1, CORE, LANES), lambda g: (g, 0, 0)),
        ],
        out_shape=[
            jax.ShapeDtypeStruct((LEN, width), BF),
            jax.ShapeDtypeStruct((groups, CORE, LANES), F32),
            jax.ShapeDtypeStruct((groups, CORE, LANES), BF),
        ],
        scratch_shapes=[
            pltpu.VMEM((LEN, width), BF),
            pltpu.VMEM((SLOTS, width), BF),
            pltpu.VMEM((EXT, LANES), BF),
            pltpu.VMEM((SLOTS, width), BF),
        ]
        + toeplitz_scratch(),
        compiler_params=params(WIDE_MIB),
        cost_estimate=cost(0.1),
    )(me, *frames, put, ext, taps, bias_lanes)


def conv_grad_kernel(me_ref, keep_ref, far_ref, near_ref, put_ref, slope_ref, ext_ref,
                     wide_ref, half_ref, bias_ref, grad_ref, slots_ref):
    g = pl.program_id(0)
    rows = far_ref.shape[0] // 2

    @pl.when(g == 0)
    def _():
        for n, piece in enumerate(came_pieces(keep_ref, far_ref, near_ref)):
            start = pl.multiple_of((me_ref[0] ^ ORDER[n]) * rows, rows)
            grad_ref[pl.ds(start, rows), :] = piece
        slots_ref[...] = dot(put_ref[...], grad_ref[...]).astype(BF)

    grad = fold_in(slots_ref, g) * slope_ref[0]
    bias_ref[0] = jnp.sum(grad, axis=0, keepdims=True)
    low = grad.astype(BF)
    wide_ref[0] = dot(ext_ref[...], low).astype(BF)
    row, lane = iota((LANES, 128), 0), iota((LANES, 128), 1)
    for h in range(2):
        pick = (lane < PH * HALF) & (row == lane // HALF * GW + lane % HALF + h * HALF)
        half_ref[h] = dot(low, pick.astype(F32).astype(BF)).astype(BF)


def conv_grad(me, came, put, slope, ext):
    groups = slope.shape[0]
    width = came[0].shape[1]
    return pl.pallas_call(
        conv_grad_kernel,
        grid=(groups,),
        in_specs=[
            pl.BlockSpec(memory_space=pltpu.SMEM),
            full((LEN // 2, width)),
            full((LEN // 2, width)),
            full((LEN // 2, width)),
            full((SLOTS, LEN)),
            block((1, CORE, LANES), lambda g: (g, 0, 0)),
            full((EXT, CORE)),
        ],
        out_specs=[
            block((1, EXT, LANES), lambda g: (g, 0, 0)),
            block((2, CORE, 128), lambda g: (g, 0, 0)),
            block((1, 1, LANES), lambda g: (g, 0, 0)),
        ],
        out_shape=[
            jax.ShapeDtypeStruct((groups, EXT, LANES), BF),
            jax.ShapeDtypeStruct((2 * groups, CORE, 128), BF),
            jax.ShapeDtypeStruct((groups, 1, LANES), F32),
        ],
        scratch_shapes=[pltpu.VMEM((LEN, width), BF), pltpu.VMEM((SLOTS, width), BF)],
        compiler_params=params(WIDE_MIB),
        cost_estimate=cost(0.1),
    )(me, *came, put, slope, ext)


def signal_grad_kernel(first, wide_ref, w_ref, *refs):
    back_ref, taps_ref, wt_ref = refs[-3:]
    step = pl.program_id(0)
    g = first + step
    fill_toeplitz(w_ref, step, g, taps_ref, wt_ref)

    @pl.when(step == 0)
    def _():
        if first == 0:
            back_ref[...] = jnp.zeros_like(back_ref)
        else:
            back_ref[...] = refs[0][...]

    total = jnp.zeros((CORE, LANES), F32)
    for j in range(NJ):
        m = NJ - 1 - j
        total = total + dot_turned(
            wide_ref[0, PN * j : PN * j + CORE, :], wt_ref[m * LANES : (m + 1) * LANES, :]
        )
    fold_out(total.astype(BF), back_ref, g)
    if first == 0:

        @pl.when(step == pl.num_programs(0) - 1)
        def _():
            refs[0][...] = back_ref[...]

        return
    _, put_ref, me_ref, keep_ref, near_ref, all_ref = refs[:6]
    rows = keep_ref.shape[0] // 2

    @pl.when(step == pl.num_programs(0) - 1)
    def _():
        all_ref[...] = unspread(back_ref, put_ref)
        for n in range(4):
            start = pl.multiple_of((me_ref[0] ^ ORDER[n]) * rows, rows)
            out_ref = keep_ref if n < 2 else near_ref
            out_ref[n % 2 * rows : (n % 2 + 1) * rows, :] = all_ref[pl.ds(start, rows), :]


def signal_grad(wide, taps, first, count, *rest):
    width = taps.shape[1]
    slots = jax.ShapeDtypeStruct((SLOTS, width), BF)
    piece = jax.ShapeDtypeStruct((LEN // 2, width), BF)
    own = [
        block((1, EXT, LANES), lambda g: (first + g, 0, 0)),
        full(taps.shape),
    ]
    more = [full(slots.shape), full((SLOTS, LEN)), pl.BlockSpec(memory_space=pltpu.SMEM)]
    scratch = [pltpu.VMEM(slots.shape, BF)] + toeplitz_scratch()
    return pl.pallas_call(
        functools.partial(signal_grad_kernel, first),
        grid=(count,),
        in_specs=own + (more if rest else []),
        out_specs=[full(piece.shape)] * 2 if rest else full(slots.shape),
        out_shape=[piece] * 2 if rest else slots,
        scratch_shapes=([pltpu.VMEM((LEN, width), BF)] if rest else []) + scratch,
        compiler_params=params(WIDE_MIB),
        cost_estimate=cost(0.1),
    )(wide, taps, *rest)


def turn_core_kernel(sig_ref, ext_ref, out_ref, wide_ref):
    packs = sig_ref.shape[0]
    blocks = EXT // PN
    wide_ref[blocks:] = jnp.zeros((1, packs * PN, LANES), BF)
    for r in range(packs):
        rows = dot(ext_ref[...], sig_ref[r]).astype(BF)
        wide_ref[0:blocks, r * PN : (r + 1) * PN, :] = rows.reshape(blocks, PN, LANES)
    for q in range(blocks + 1):
        out_ref[:, q * 128 : (q + 1) * 128] = wide_ref[q].astype(F32).T.astype(BF)


def turn_core(sig, ext):
    packs = sig.shape[0]
    blocks = EXT // PN + 1
    return pl.pallas_call(
        turn_core_kernel,
        out_shape=jax.ShapeDtypeStruct((LANES, blocks * packs * PN), BF),
        scratch_shapes=[pltpu.VMEM((blocks, packs * PN, LANES), BF)],
        compiler_params=params(WIDE_MIB),
        cost_estimate=cost(0.1),
    )(sig, ext)


def tap_grad_kernel(sig_ref, grad_ref, out_ref, pair_ref, parts_ref, rows_ref):
    packs = grad_ref.shape[0]
    across = packs * PN
    pair_ref[QN, :, 0:128] = jnp.zeros((across, 128), BF)
    pair_ref[0, :, 128:] = jnp.zeros((across, 128), BF)
    for r in range(packs):
        rows = grad_ref[r].reshape(QN, PN, 128)
        pair_ref[0:QN, r * PN : (r + 1) * PN, 0:128] = rows
        pair_ref[1:, r * PN : (r + 1) * PN, 128:] = rows
    pair = pair_ref[...].reshape((QN + 1) * across, LANES)
    for j in range(0, NJ + 1, 2):
        part = dot(sig_ref[:, j * across : (j + QN + 1) * across], pair)
        parts_ref[PH * GW * j : PH * GW * (j + 1), :] = part[: PH * GW, 0:128]
        parts_ref[PH * GW * (j + 1) : PH * GW * (j + 2), :] = part[: PH * GW, 128:]
    phase = iota((1, 128), 1) // HALF
    chunk = 8 * GW

    for start in range(0, KER * GW, chunk):
        total = jnp.zeros((chunk, 128), F32)
        for i in range(PH):
            rows = slice(start + GW * (1 + i), start + GW * (1 + i) + chunk)
            total = jnp.where(phase == i, parts_ref[rows, :], total)
        rows_ref[start : start + chunk, :] = total
    for c in range(GW):
        taps = rows_ref[pl.ds(c, KER, stride=GW), :].T
        total = taps[0:HALF, :]
        for i in range(1, PH):
            total = total + taps[HALF * i : HALF * (i + 1), :]
        out_ref[c * HALF : (c + 1) * HALF, :] = total


def tap_grad(sig, grad):
    packs = grad.shape[0]
    return pl.pallas_call(
        tap_grad_kernel,
        out_shape=jax.ShapeDtypeStruct((GW * HALF, KER), F32),
        scratch_shapes=[
            pltpu.VMEM((QN + 1, packs * PN, LANES), BF),
            pltpu.VMEM(((NJ + 1) * PH * GW, 128), F32),
            pltpu.VMEM((KER * GW, 128), F32),
        ],
        compiler_params=params(WIDE_MIB),
        cost_estimate=cost(0.1),
    )(sig, grad)


def assemble_kernel(at_ref, a0_ref, a1_ref, b0_ref, b1_ref, out_ref, wide_ref):
    step = pl.program_id(0)
    half = a0_ref.shape[0]
    packs = 2 * half
    per_step = out_ref.shape[0]
    half_steps = pl.num_programs(0) // 2

    def place(held_ref, came_ref, which):
        for r in range(packs):
            at = at_ref[which, r]

            @pl.when(at < half)
            def _():
                wide_ref[...] = held_ref[at].astype(F32)

            @pl.when(at >= half)
            def _():
                wide_ref[...] = came_ref[at - half].astype(F32)

            for c in range(per_step):
                out_ref[c, r * HALF : (r + 1) * HALF, :] = wide_ref[c * HALF : (c + 1) * HALF, :]

    @pl.when(step < half_steps)
    def _():
        place(a0_ref, a1_ref, 0)

    @pl.when(step >= half_steps)
    def _():
        place(b0_ref, b1_ref, 1)


def assemble(order, parts_a, parts_b):
    packs = 2 * parts_a[0].shape[0]
    steps = 4
    per_step = GW // steps
    rows = per_step * HALF
    half = steps // 2
    return pl.pallas_call(
        assemble_kernel,
        grid=(steps,),
        in_specs=[
            pl.BlockSpec(memory_space=pltpu.SMEM),
        ]
        + [block((packs // 2, rows, KER), lambda s: (0, jnp.minimum(s, half - 1), 0))] * 2
        + [block((packs // 2, rows, KER), lambda s: (0, jnp.maximum(s - half, 0), 0))] * 2,
        out_specs=block((per_step, packs * HALF, KER), lambda s: (s, 0, 0)),
        out_shape=jax.ShapeDtypeStruct((GW, packs * HALF, KER), F32),
        scratch_shapes=[pltpu.VMEM((rows, KER), F32)],
        compiler_params=params(WIDE_MIB),
        cost_estimate=cost(4),
    )(order, *parts_a, *parts_b)


def spread_parts_kernel(order_ref, held_d, came_d, held_u, came_u, down_ref, up_ref):
    part = pl.program_id(0)
    half = pl.num_programs(0) // 2
    for i, (held, came, out) in enumerate(((held_d, came_d, down_ref), (held_u, came_u, up_ref))):

        @pl.when(order_ref[i, part] < half)
        def _():
            out[...] = held[0, 0].astype(F32)

        @pl.when(order_ref[i, part] >= half)
        def _():
            out[...] = came[0, 0].astype(F32)


def spread_parts(order, held, came):
    half, _, rows, width = held.shape
    first = lambda i: block(
        (1, 1, rows, width), lambda p, at: (jnp.minimum(at[i, p], half - 1), i, 0, 0)
    )
    second = lambda i: block(
        (1, 1, rows, width), lambda p, at: (jnp.maximum(at[i, p] - half, 0), i, 0, 0)
    )
    out = jax.ShapeDtypeStruct((2 * half * rows, width), F32)
    return pl.pallas_call(
        spread_parts_kernel,
        grid_spec=pltpu.PrefetchScalarGridSpec(
            num_scalar_prefetch=1,
            grid=(2 * half,),
            in_specs=[first(0), second(0), first(1), second(1)],
            out_specs=[block((rows, width), lambda p, at: (p, 0))] * 2,
        ),
        out_shape=[out, out],
        compiler_params=params(WIDE_MIB),
        cost_estimate=cost(5),
    )(order, held, came, held, came)


def spread_tail_kernel(first, order_ref, held_ref, came_ref, first_ref, last_ref):
    part = pl.program_id(0)
    half = pl.num_programs(0) // 2
    value = jnp.where(order_ref[part] < half, held_ref[0].astype(F32), came_ref[0].astype(F32))

    @pl.when(part < first)
    def _():
        first_ref[...] = value

    @pl.when(part >= first)
    def _():
        last_ref[...] = value


def spread_tail(order, held, came, split):
    half, rows, width = held.shape
    first = split // rows
    return pl.pallas_call(
        functools.partial(spread_tail_kernel, first),
        grid_spec=pltpu.PrefetchScalarGridSpec(
            num_scalar_prefetch=1,
            grid=(2 * half,),
            in_specs=[
                block((1, rows, width), lambda p, at: (jnp.minimum(at[p], half - 1), 0, 0)),
                block((1, rows, width), lambda p, at: (jnp.maximum(at[p] - half, 0), 0, 0)),
            ],
            out_specs=[
                block((rows, width), lambda p, at: (jnp.minimum(p, first - 1), 0)),
                block((rows, width), lambda p, at: (jnp.maximum(p - first, 0), 0)),
            ],
        ),
        out_shape=[
            jax.ShapeDtypeStruct((split, width), F32),
            jax.ShapeDtypeStruct((2 * half * rows - split, width), F32),
        ],
        compiler_params=params(WIDE_MIB),
        cost_estimate=cost(3),
    )(order, held, came)


def head_rows(turned, head, heads):
    pieces = [jnp.zeros((HD, turned.shape[1]), turned.dtype) for _ in range(heads)]
    pieces[head] = turned[HD * head : HD * (head + 1), :]
    return jnp.concatenate(pieces + [turned[HD * heads :, :]], axis=0)


def attention_kernel(q_block, heads, *refs):
    me_ref = refs[0]
    mixed = refs[1:5]
    frames = refs[5:9]
    (vec_ref, wq_ref, wk_ref, wv_ref, qv_ref, featq_ref, featk_ref) = refs[9:16]
    (att_ref, own_ref, hat_ref, inv_ref, all_out, low_out, q_out, qt_out, k_out, v_out, ot_ref,
     lse_ref) = refs[16:28]
    all_ref, low_ref, q_ref, qt_ref, k_ref, v_ref, vt_ref, sems = refs[28:]
    rows = frames[0].shape[0]
    part = mixed[0].shape[1]
    width = frames[0].shape[1]
    scale = HD ** (-0.5)
    me = me_ref[0]
    row, lane = iota((part, width), 0), iota((part, width), 1)
    spots = [(lane == row + part * (me ^ m)).astype(F32).astype(BF) for m in ORDER]
    for n in range(4):
        here = slice(n * rows, (n + 1) * rows)
        start = pl.multiple_of((me ^ ORDER[n]) * rows, rows)
        total = frames[n][...].astype(F32)
        for ref, spot in zip(mixed, spots):
            total = total + dot(ref[pl.ds(start, rows), :], spot)
        hat, inv = norm_stats(total)
        normed = hat * vec_ref[0:1, :] + vec_ref[1:2, :]
        if n == 0:
            own_ref[...] = normed
            hat_ref[...] = hat
            inv_ref[...] = jnp.broadcast_to(inv, inv_ref.shape)
        all_ref[here, :] = normed
        normed = normed.astype(BF)
        low_ref[here, :] = normed
        query = (dot_turned(normed, wq_ref[...]) + qv_ref[0:1, :]) * scale
        query = query + featq_ref[here, :].astype(F32)
        q_ref[here, :] = query.astype(BF)
        qt_ref[:, here] = query.T.astype(BF)
        key = dot_turned(normed, wk_ref[...])
        k_ref[here, :] = (key + featk_ref[here, :].astype(F32)).astype(BF)
        value = dot_turned(normed, wv_ref[...]) + qv_ref[1:2, :]
        v_ref[here, :] = value.astype(BF)
        vt_ref[:, here] = value.T.astype(BF)
    held = [all_ref, low_ref, q_ref, qt_ref, k_ref, v_ref]
    kept = [all_out, low_out, q_out, qt_out, k_out, v_out]
    copies = [
        pltpu.make_async_copy(src, dst, sems.at[i]) for i, (src, dst) in enumerate(zip(held, kept))
    ]
    for copy in copies:
        copy.start()
    total = 4 * rows
    for head in range(heads):
        for start in range(0, total, q_block):
            cols = slice(start, start + q_block)
            turned = head_rows(qt_ref[:, cols], head, heads)
            scores = dot(k_ref[...], turned)
            top = jnp.max(scores, axis=0, keepdims=True)
            weights = jnp.exp(scores - top)
            sums = jnp.sum(weights, axis=0, keepdims=True)
            value = dot(vt_ref[HD * head : HD * (head + 1), :], weights.astype(BF))
            ot_ref[HD * head : HD * (head + 1), cols] = value / sums
            lse_ref[head : head + 1, cols] = top + jnp.log(sums)
    lse_ref[heads:, :] = jnp.zeros((8 - heads, total), F32)
    for n in range(4):
        here = slice(n * rows, (n + 1) * rows)
        att_ref[here, :] = ot_ref[:, here].T.astype(BF)
    for copy in copies:
        copy.wait()


def attention(me, mixed, frames, vectors, weights, qv, features, heads, q_block=512):
    rows, width = frames[0].shape
    total = 4 * rows
    cols = heads * HD
    vmem = pl.BlockSpec(memory_space=pltpu.VMEM)
    away = pl.BlockSpec(memory_space=pltpu.HBM)
    held = [
        ((total, width), F32),
        ((total, width), BF),
        ((total, LANES), BF),
        ((LANES, total), BF),
        ((total, LANES), BF),
        ((total, LANES), BF),
    ]
    return pl.pallas_call(
        functools.partial(attention_kernel, q_block, heads),
        in_specs=[pl.BlockSpec(memory_space=pltpu.SMEM)] + [vmem] * 15,
        out_specs=[vmem] * 4 + [away] * 6 + [vmem] * 2,
        out_shape=[
            jax.ShapeDtypeStruct((total, cols), BF),
            jax.ShapeDtypeStruct((rows, width), F32),
            jax.ShapeDtypeStruct((rows, width), F32),
            jax.ShapeDtypeStruct((rows, 128), F32),
        ]
        + [jax.ShapeDtypeStruct(shape, kind) for shape, kind in held]
        + [jax.ShapeDtypeStruct((cols, total), F32), jax.ShapeDtypeStruct((8, total), F32)],
        scratch_shapes=[pltpu.VMEM(shape, kind) for shape, kind in held]
        + [pltpu.VMEM((LANES, total), BF), pltpu.SemaphoreType.DMA((len(held),))],
        compiler_params=params(WIDE_MIB),
        cost_estimate=cost(4),
    )(me, *mixed, *frames, vectors, *weights, qv, *features)


def attention_grad_kernel(q_block, heads, *refs):
    pieces = came_pieces(*refs[:3])
    (q_ref, qt_ref, k_ref, v_ref, ot_ref, lse_ref, wq_ref, wk_ref, wv_ref,
     keep_ref, near_ref, gq_ref, gk_ref, gv_ref, sum_ref,
     go_ref, got_ref, kt_ref, delta_ref, dqt_ref, dk_ref, dv_ref) = refs[3:]
    rows = pieces[0].shape[0]
    total = 4 * rows
    cols_all = heads * HD
    scale = HD ** (-0.5)
    go_ref[...] = jnp.zeros_like(go_ref)
    for n in range(4):
        go_ref[n * rows : (n + 1) * rows, :cols_all] = pieces[n]
    got_ref[...] = go_ref[...].astype(F32).T.astype(BF)
    kt_ref[...] = k_ref[...].astype(F32).T.astype(BF)
    for head in range(heads):
        own = slice(HD * head, HD * (head + 1))
        delta_ref[head : head + 1, :] = jnp.sum(
            got_ref[own, :].astype(F32) * ot_ref[own, :], axis=0, keepdims=True
        )
    lane = iota((1, LANES), 1)
    for head in range(heads):
        own = slice(HD * head, HD * (head + 1))
        mask = (lane // HD == head).astype(F32).astype(BF)
        for start in range(0, total, q_block):
            cols = slice(start, start + q_block)
            scores = dot(k_ref[...], head_rows(qt_ref[:, cols], head, heads))
            probs = jnp.exp(scores - lse_ref[head : head + 1, cols])
            prob_grad = dot(v_ref[...], head_rows(got_ref[:, cols], head, heads))
            score_grad = (probs * (prob_grad - delta_ref[head : head + 1, cols])).astype(BF)
            value_part = dot(probs.astype(BF), go_ref[cols, :] * mask)
            key_part = dot(score_grad, q_ref[cols, :] * mask)
            if head == 0 and start == 0:
                dv_ref[...] = value_part
                dk_ref[...] = key_part
            else:
                dv_ref[...] += value_part
                dk_ref[...] += key_part
            dqt_ref[own, cols] = dot(kt_ref[own, :], score_grad)
    dqt_ref[cols_all:, :] = jnp.zeros((LANES - cols_all, total), F32)
    sums_q = jnp.zeros((1, LANES), F32)
    sums_v = jnp.zeros((1, LANES), F32)
    for n in range(4):
        here = slice(n * rows, (n + 1) * rows)
        query_grad = dqt_ref[:, here].T * scale
        value_grad = dv_ref[here, :]
        sums_q = sums_q + jnp.sum(query_grad, axis=0, keepdims=True)
        sums_v = sums_v + jnp.sum(value_grad, axis=0, keepdims=True)
        low_q = query_grad.astype(BF)
        low_k = dk_ref[here, :].astype(BF)
        low_v = value_grad.astype(BF)
        gq_ref[here, :] = low_q[:, :cols_all]
        gk_ref[here, :] = low_k[:, :cols_all]
        gv_ref[here, :] = low_v[:, :cols_all]
        back = dot(low_q, wq_ref[...]) + dot(low_k, wk_ref[...]) + dot(low_v, wv_ref[...])
        out_ref = keep_ref if n < 2 else near_ref
        out_ref[n % 2 * rows : (n % 2 + 1) * rows, :] = back.astype(BF)
    sum_ref[0:1, :] = sums_q
    sum_ref[1:2, :] = sums_v
    sum_ref[2:, :] = jnp.zeros((6, LANES), F32)


def attention_grad(came, saved, weights, heads, q_block=512):
    half, cols = came[0].shape
    total = 2 * half
    width = weights[0].shape[1]
    return pl.pallas_call(
        functools.partial(attention_grad_kernel, q_block, heads),
        out_shape=[
            jax.ShapeDtypeStruct((half, width), BF),
            jax.ShapeDtypeStruct((half, width), BF),
            jax.ShapeDtypeStruct((total, cols), BF),
            jax.ShapeDtypeStruct((total, cols), BF),
            jax.ShapeDtypeStruct((total, cols), BF),
            jax.ShapeDtypeStruct((8, LANES), F32),
        ],
        scratch_shapes=[
            pltpu.VMEM((total, LANES), BF),
            pltpu.VMEM((LANES, total), BF),
            pltpu.VMEM((LANES, total), BF),
            pltpu.VMEM((8, total), F32),
            pltpu.VMEM((LANES, total), F32),
            pltpu.VMEM((total, LANES), F32),
            pltpu.VMEM((total, LANES), F32),
        ],
        compiler_params=params(WIDE_MIB),
        cost_estimate=cost(0.1),
    )(*came, *saved, *weights)


def put_half(n, value, keep_ref, near_ref):
    @pl.when(n < 2)
    def _():
        keep_ref[...] = value

    @pl.when(n >= 2)
    def _():
        near_ref[...] = value


def feed_kernel(a0_ref, a1_ref, a2_ref, a3_ref, normed_ref, o0_ref, o1_ref, o2_ref, o3_ref, vec_ref,
                up_ref, down_ref,
                low_ref, act_ref, slope_ref, keep_ref, near_ref, own_ref, hat_ref, inv_ref):
    n = pl.program_id(0)
    total = normed_ref[...] + vec_ref[6:7, :]
    out_refs = (o0_ref, o1_ref, o2_ref, o3_ref)
    for ref, out_ref in zip((a0_ref, a1_ref, a2_ref, a3_ref), out_refs):
        total = total + dot(ref[...], out_ref[...])
    hat, inv = norm_stats(total)
    normed = hat * vec_ref[2:3, :] + vec_ref[3:4, :]

    @pl.when(n == 0)
    def _():
        own_ref[...] = normed
        hat_ref[...] = hat
        inv_ref[...] = jnp.broadcast_to(inv, inv_ref.shape)

    low = normed.astype(BF)
    low_ref[...] = low
    value, slope = phi_pair(dot(low, up_ref[...]) + vec_ref[8:9, :])
    slope_ref[...] = slope
    value = value.astype(BF)
    act_ref[...] = value
    put_half(n, dot(value, down_ref[...]).astype(BF), keep_ref, near_ref)


def feed(attended, normed, out_pieces, vectors, up_weight, down_weight):
    total, width = normed.shape
    rows = total // 4
    part = attended[0].shape[1]
    units = up_weight.shape[1]
    here = lambda n: (n, 0)
    return pl.pallas_call(
        feed_kernel,
        grid=(4,),
        in_specs=[block((rows, part), lambda n, i=i: (n ^ i, 0)) for i in range(4)]
        + [block((rows, width), here)]
        + [full((part, width))] * 4
        + [
            full((16, width)),
            full((width, units)),
            full((units, width)),
        ],
        out_specs=[
            block((rows, width), here),
            block((rows, units), here),
            block((rows, units), here),
            block((rows, width), lambda n: (jnp.minimum(n, 1), 0)),
            block((rows, width), lambda n: (jnp.maximum(n - 2, 0), 0)),
            full((rows, width)),
            full((rows, width)),
            full((rows, 128)),
        ],
        out_shape=[
            jax.ShapeDtypeStruct((total, width), BF),
            jax.ShapeDtypeStruct((total, units), BF),
            jax.ShapeDtypeStruct((total, units), F32),
            jax.ShapeDtypeStruct((total // 2, width), BF),
            jax.ShapeDtypeStruct((total // 2, width), BF),
            jax.ShapeDtypeStruct((rows, width), F32),
            jax.ShapeDtypeStruct((rows, width), F32),
            jax.ShapeDtypeStruct((rows, 128), F32),
        ],
        compiler_params=params(WIDE_MIB),
        cost_estimate=cost(10),
    )(*attended, normed, *out_pieces, vectors, up_weight, down_weight)


def feed_grad_kernel(g0_ref, g1_ref, g2_ref, g3_ref, slope_ref, up_ref, down_ref,
                     all_ref, low_ref, keep_ref, near_ref, bias_ref):
    n = pl.program_id(0)
    for i, ref in enumerate((g0_ref, g1_ref, g2_ref, g3_ref)):

        @pl.when(n == i)
        def _():
            all_ref[...] = ref[...]

    grad = dot_turned(all_ref[...], down_ref[...]) * slope_ref[...]

    @pl.when(n == 0)
    def _():
        bias_ref[...] = jnp.zeros_like(bias_ref)

    bias_ref[...] += jnp.sum(grad, axis=0, keepdims=True)
    low = grad.astype(BF)
    low_ref[...] = low
    put_half(n, dot_turned(low, up_ref[...]).astype(BF), keep_ref, near_ref)


def feed_grad(grads, slope, up_weight, down_weight):
    total, units = slope.shape
    rows, width = grads[0].shape
    here = lambda n: (n, 0)
    return pl.pallas_call(
        feed_grad_kernel,
        grid=(4,),
        in_specs=[full((rows, width))] * 4
        + [block((rows, units), here), full((width, units)), full((units, width))],
        out_specs=[
            block((rows, width), here),
            block((rows, units), here),
            block((rows, width), lambda n: (jnp.minimum(n, 1), 0)),
            block((rows, width), lambda n: (jnp.maximum(n - 2, 0), 0)),
            full((1, units)),
        ],
        out_shape=[
            jax.ShapeDtypeStruct((total, width), BF),
            jax.ShapeDtypeStruct((total, units), BF),
            jax.ShapeDtypeStruct((total // 2, width), BF),
            jax.ShapeDtypeStruct((total // 2, width), BF),
            jax.ShapeDtypeStruct((1, units), F32),
        ],
        compiler_params=params(WIDE_MIB),
        cost_estimate=cost(6),
    )(*grads, slope, up_weight, down_weight)


def came_pieces(keep_ref, far_ref, near_ref):
    rows = far_ref.shape[0] // 2
    return [keep_ref[:rows, :], far_ref[:rows, :], near_ref[:rows, :], far_ref[rows:, :]]


def put_sums(sum_ref, *values):
    sum_ref[...] = jnp.zeros_like(sum_ref)
    for i, value in enumerate(values):
        sum_ref[i : i + 1, :] = jnp.sum(value, axis=0, keepdims=True)


def norm_grad(grad, hat, inv, gain):
    scaled = grad * gain
    return inv * (
        scaled
        - jnp.mean(scaled, axis=-1, keepdims=True)
        - hat * jnp.mean(scaled * hat, axis=-1, keepdims=True)
    )


def last_norm_kernel(keep_ref, near_ref, far_ref, normed_ref, cot_ref, vec_ref, out_ref, grad_ref, low_ref, sum_ref):
    total = keep_ref[...].astype(F32) + near_ref[...].astype(F32) + far_ref[...].astype(F32)
    hat, inv = norm_stats(normed_ref[...] + total + vec_ref[7:8, :])
    gain = vec_ref[4:5, :]
    out_ref[...] = (hat * gain + vec_ref[5:6, :]).astype(BF)
    cot = cot_ref[...].astype(F32)
    grad = norm_grad(cot, hat, inv, gain)
    grad_ref[...] = grad
    low_ref[...] = grad.astype(BF)
    put_sums(sum_ref, cot * hat, cot, grad)


def last_norm(terms, normed, cotangent, vectors):
    rows, width = normed.shape
    return pl.pallas_call(
        last_norm_kernel,
        grid=(1,),
        in_specs=[full((rows, width))] * 5 + [full((16, width))],
        out_specs=[full((rows, width))] * 3 + [full((8, width))],
        out_shape=[
            jax.ShapeDtypeStruct((rows, width), BF),
            jax.ShapeDtypeStruct((rows, width), F32),
            jax.ShapeDtypeStruct((rows, width), BF),
            jax.ShapeDtypeStruct((8, width), F32),
        ],
        compiler_params=params(WIDE_MIB),
        cost_estimate=cost(3),
    )(*terms, normed, cotangent, vectors)


def middle_norm_kernel(keep_ref, near_ref, far_ref, grad_ref, hat_ref, inv_ref, vec_ref, o0_ref,
                       o1_ref, o2_ref, o3_ref, out_ref, low_ref, sum_ref, keep_out, near_out):
    rows = grad_ref.shape[0]
    total = keep_ref[...].astype(F32) + near_ref[...].astype(F32) + far_ref[...].astype(F32)
    total = total + grad_ref[...]
    hat = hat_ref[...]
    grad = norm_grad(total, hat, inv_ref[:, 0:1], vec_ref[2:3, :])
    out_ref[...] = grad
    low = grad.astype(BF)
    low_ref[...] = low
    put_sums(sum_ref, total * hat, total, grad)
    for n, ref in enumerate((o0_ref, o1_ref, o2_ref, o3_ref)):
        back = dot_turned(low, ref[...]).astype(BF)
        out = keep_out if n < 2 else near_out
        out[n % 2 * rows : (n % 2 + 1) * rows, :] = back


def middle_norm(terms, grad, hat, inv, vectors, out_pieces):
    rows, width = grad.shape
    part = out_pieces[0].shape[0]
    return pl.pallas_call(
        middle_norm_kernel,
        grid=(1,),
        in_specs=[full((rows, width))] * 5
        + [full((rows, 128)), full((16, width))]
        + [full((part, width))] * 4,
        out_specs=[full((rows, width))] * 2 + [full((8, width))] + [full((2 * rows, part))] * 2,
        out_shape=[
            jax.ShapeDtypeStruct((rows, width), F32),
            jax.ShapeDtypeStruct((rows, width), BF),
            jax.ShapeDtypeStruct((8, width), F32),
            jax.ShapeDtypeStruct((2 * rows, part), BF),
            jax.ShapeDtypeStruct((2 * rows, part), BF),
        ],
        compiler_params=params(WIDE_MIB),
        cost_estimate=cost(0.1),
    )(*terms, grad, hat, inv, vectors, *out_pieces)


def first_norm_kernel(me_ref, keep_ref, near_ref, far_ref, grad_ref, hat_ref, inv_ref, vec_ref,
                      out_ref, sum_ref, keep_out, near_out):
    rows, width = grad_ref.shape
    part = keep_out.shape[1]
    total = keep_ref[...].astype(F32) + near_ref[...].astype(F32) + far_ref[...].astype(F32)
    total = total + grad_ref[...]
    hat = hat_ref[...]
    grad = norm_grad(total, hat, inv_ref[:, 0:1], vec_ref[0:1, :])
    out_ref[...] = grad
    low = grad.astype(BF)
    put_sums(sum_ref, total * hat, total)
    row, lane = iota((width, part), 0), iota((width, part), 1)
    for n in range(4):
        pick = (row == lane + part * (me_ref[0] ^ ORDER[n])).astype(F32).astype(BF)
        out = keep_out if n < 2 else near_out
        out[n % 2 * rows : (n % 2 + 1) * rows, :] = dot(low, pick).astype(BF)


def first_norm(me, terms, grad, hat, inv, vectors):
    rows, width = grad.shape
    part = width // 4
    return pl.pallas_call(
        first_norm_kernel,
        grid=(1,),
        in_specs=[pl.BlockSpec(memory_space=pltpu.SMEM)]
        + [full((rows, width))] * 5
        + [full((rows, 128)), full((16, width))],
        out_specs=[full((rows, width)), full((8, width))] + [full((2 * rows, part))] * 2,
        out_shape=[
            jax.ShapeDtypeStruct((rows, width), F32),
            jax.ShapeDtypeStruct((8, width), F32),
            jax.ShapeDtypeStruct((2 * rows, part), BF),
            jax.ShapeDtypeStruct((2 * rows, part), BF),
        ],
        compiler_params=params(WIDE_MIB),
        cost_estimate=cost(0.1),
    )(me, *terms, grad, hat, inv, vectors)


def frames_grad_kernel(me_ref, keep_ref, far_ref, near_ref, grad_ref, out_ref):
    width = grad_ref.shape[1]
    part = keep_ref.shape[1]
    row, lane = iota((part, width), 0), iota((part, width), 1)
    total = grad_ref[...]
    for n, piece in enumerate(came_pieces(keep_ref, far_ref, near_ref)):
        spot = (lane == row + part * (me_ref[0] ^ ORDER[n])).astype(F32).astype(BF)
        total = total + dot(piece, spot)
    out_ref[...] = total


def add_frames_grad(me, came, grad):
    half, part = came[0].shape
    rows, width = grad.shape
    return pl.pallas_call(
        frames_grad_kernel,
        grid=(1,),
        in_specs=[pl.BlockSpec(memory_space=pltpu.SMEM)]
        + [full((half, part))] * 3
        + [full((rows, width))],
        out_specs=full((rows, width)),
        out_shape=jax.ShapeDtypeStruct((rows, width), F32),
        compiler_params=params(WIDE_MIB),
        cost_estimate=cost(0.1),
    )(me, *came, grad)


def swap(value, bit):
    return lax.ppermute(value, "tp", [(i, i ^ bit) for i in range(lax.axis_size("tp"))])


def gather_pieces(value):
    across = swap(value, 2)
    return [value, across, swap(value, 1), swap(across, 1)]


def scatter_terms(keep, near):
    piece = keep.shape[0] // 2
    came = swap(near, 1)
    pair = (keep[piece:].astype(F32) + came[piece:].astype(F32)).astype(BF)
    return [keep, came, swap(pair, 2)], pair


def exchange(keep, near, *ahead):
    rows = keep.shape[0] // 2
    came = swap(near, 1)
    pair = after(jnp.concatenate([keep[rows:], came[rows:]], axis=0), *ahead)
    return [keep, swap(pair, 2), came], pair


def after(value, *others):
    return lax.optimization_barrier((value, *others))[0]


def all_after(values, *others):
    return list(lax.optimization_barrier((*values, *others))[: len(values)])


def team_groups(row_count, team):
    if row_count == team:
        return None
    return [list(range(first, first + team)) for first in range(0, row_count, team)]


def cross_groups(row_count, team):
    return [list(range(first, row_count, team)) for first in range(team)]


def pair_rows(value, mask):
    count = lax.axis_size("rows")
    return lax.ppermute(value, "rows", [(i, i ^ mask) for i in range(count)])


FEED_MASKS = ((1, 4, 2), (2, 1, 4))
TAIL_MASKS = (1, 2, 4)


def side_of(index, mask):
    return (index >> {1: 0, 2: 1, 4: 2}[mask]) & 1


def holders_of(masks):
    part = lambda index: sum(side_of(index, m) << (2 - i) for i, m in enumerate(masks))
    return sorted(range(8), key=part)


def halve(value, mask, side):
    half = value.shape[0] // 2
    kept = lax.dynamic_slice_in_dim(value, side * half, half, 0)
    sent = lax.dynamic_slice_in_dim(value, (1 - side) * half, half, 0)
    return kept, pair_rows(sent, mask)


def add_low(kept, came):
    return (kept.astype(F32) + came.astype(F32)).astype(BF)


def gather_join(held, came, offsets, mask):
    held = jnp.concatenate([held, came], axis=0)
    return held, offsets + [x ^ mask for x in offsets]


def on_device(
    frames,
    seg_starts,
    conv_weight,
    conv_bias,
    norm_gain0,
    norm_bias0,
    qkv_weight,
    qv_bias,
    out_weight,
    out_bias,
    norm_gain1,
    norm_bias1,
    up_weight,
    up_bias,
    down_weight,
    down_bias,
    norm_gain2,
    norm_bias2,
    cotangent,
):
    head_cols = qkv_weight.shape[2]
    heads_here = head_cols // HD
    groups_here = conv_weight.shape[2] // GW
    team = 2 * groups_here
    row_count = lax.axis_size("rows")
    teams = team_groups(row_count, team)
    me = lax.axis_index("tp")
    me_word = me.reshape(1).astype(jnp.int32)
    own_row = lax.axis_index("rows") % team
    positions = jnp.arange(LEN, dtype=jnp.int32)
    segments = (
        jnp.sum((positions[:, None] >= seg_starts[0][None, :]).astype(jnp.int32), axis=1) - 1
    )
    vectors = [norm_gain0, norm_bias0, norm_gain1, norm_bias1, norm_gain2, norm_bias2]
    vectors = jnp.stack(vectors + [out_bias, down_bias, up_bias]).astype(F32)
    vectors = jnp.pad(vectors, ((0, 16 - vectors.shape[0]), (0, 0)))

    slots = spread_slots(segments)
    conv_flat = lax.optimization_barrier(conv_weight.reshape(KER * GW, -1))
    put = (iota((SLOTS, LEN), 0) == after(slots, conv_flat)[None, :]).astype(BF)
    ext = extension()
    bias_lanes = jnp.tile(conv_bias.astype(F32).reshape(groups_here, 1, GW), (1, 1, PH))
    bias_lanes = jnp.pad(bias_lanes, ((0, 0), (0, 0), (0, LANES - PH * GW)))
    frames_pieces = gather_pieces(frames)
    lane = jnp.arange(LANES, dtype=jnp.int32)[None, :] - head_cols
    seg_rows = segments.reshape(4, -1)
    seg_own = jnp.concatenate(
        [lax.dynamic_index_in_dim(seg_rows, me ^ m, 0, keepdims=False) for m in ORDER]
    )
    in_seg = lane == seg_own[:, None]
    of_seg = (lane >= 0) & (lane < seg_starts.shape[1])
    features = [
        jnp.where(in_seg, MASK_ROOT, 0.0).astype(BF),
        jnp.where(of_seg & ~in_seg, -MASK_ROOT, 0.0).astype(BF),
    ]
    qkv_padded = jnp.pad(
        qkv_weight.transpose(1, 2, 0), ((0, 0), (0, LANES - head_cols), (0, 0))
    )
    qkv_parts = [qkv_padded[0], qkv_padded[1], qkv_padded[2]]
    out_pieces = gather_pieces(out_weight)
    qv_padded = jnp.pad(qv_bias.astype(F32), ((0, 0), (0, LANES - head_cols)))
    frames_pieces = all_after(frames_pieces, *features, *qkv_parts, qv_padded, vectors)
    mixed_low, slope0, core = conv(me_word, frames_pieces, put, ext, conv_flat, bias_lanes)

    mixed_low = after(mixed_low, out_pieces[1], out_pieces[2])
    mixed_pieces = gather_pieces(mixed_low)
    (attended, normed0, hat0, inv0, normed0_all, normed0_low, *saved) = attention(
        me_word,
        mixed_pieces,
        frames_pieces,
        vectors,
        qkv_parts,
        qv_padded,
        features,
        heads_here,
    )

    core_all = lax.all_to_all(
        jnp.repeat(core, 2, axis=0), "rows", 0, 0, axis_index_groups=teams, tiled=True
    )
    attended_pieces = all_after(gather_pieces(attended), core_all)
    normed1_low, activated, slope1, keep, near, normed1, hat1, inv1 = feed(
        attended_pieces, normed0_all, out_pieces, vectors, up_weight, down_weight
    )
    terms, pair = scatter_terms(keep, near)
    turned_core = turn_core(after(core_all, pair), ext)
    terms = all_after(terms, turned_core)
    block_out, grad2, grad2_low, sums2 = last_norm(terms, normed1, cotangent, vectors)

    grad2_all, up_low, keep, near, up_bias_grad = feed_grad(
        gather_pieces(grad2_low), slope1, up_weight, down_weight
    )
    terms, pair = scatter_terms(keep, near)
    activated, normed1_low = all_after([activated, normed1_low], pair)
    down_grad = jnp.einsum("rf,rd->fd", activated, grad2_all, preferred_element_type=F32)
    up_grad = jnp.einsum("rd,rf->df", normed1_low, up_low, preferred_element_type=F32)
    feed_grads = [down_grad.astype(BF), up_grad.astype(BF)]
    terms = all_after(terms, *feed_grads)
    feed_steps = [[(mask, side_of(own_row, mask)) for mask in masks] for masks in FEED_MASKS]
    halves_1 = [halve(grad, *order[0]) for grad, order in zip(feed_grads, feed_steps)]

    grad1, grad1_low, sums1, keep, near = middle_norm(
        terms, grad2, hat1, inv1, vectors, out_pieces
    )
    came, pair = exchange(keep, near, *[other for kept, other in halves_1])
    feed_sums = [add_low(after(kept, pair), other) for kept, other in halves_1]
    came = all_after(came, *feed_sums)
    halves_2 = [halve(grad, *order[1]) for grad, order in zip(feed_sums, feed_steps)]
    keep, near, query_grad, key_grad, value_grad, qv_sums = attention_grad(
        came, saved, qkv_parts, heads_here
    )
    grad1_pieces = gather_pieces(after(grad1_low, *came))
    feed_sums = [add_low(after(kept, keep), other) for kept, other in halves_2]
    near = after(near, *feed_sums, grad1_pieces[1], grad1_pieces[2])
    terms, pair = scatter_terms(keep, near)
    halves_3 = [halve(grad, *order[2]) for grad, order in zip(feed_sums, feed_steps)]
    out_grad = jnp.einsum(
        "rh,rd->hd",
        after(attended, pair),
        jnp.concatenate(grad1_pieces, axis=0),
        preferred_element_type=F32,
    )
    normed0_low = after(normed0_low, pair)
    turned_grads = [
        jnp.einsum("rc,rd->cd", part, normed0_low, preferred_element_type=F32).astype(BF)
        for part in (query_grad, key_grad, value_grad)
    ]
    tail = jnp.concatenate(turned_grads + [out_grad.astype(BF)], axis=0)
    terms = all_after(terms, tail)
    qv_grad = qv_sums[:2, :head_cols]
    tail_steps = [(mask, side_of(own_row, mask)) for mask in TAIL_MASKS]
    tail_half = halve(tail, *tail_steps[0])
    grad0, sums0, keep, near = first_norm(me_word, terms, grad1, hat0, inv0, vectors)

    near = after(near, tail_half[1], *[other for kept, other in halves_3])
    came, pair = exchange(keep, near)
    feed_sums = jnp.stack([add_low(after(kept, pair), other) for kept, other in halves_3])
    tail_sum = add_low(after(tail_half[0], pair), tail_half[1])
    came = all_after(came, tail_sum, feed_sums)
    tail_half = halve(tail_sum, *tail_steps[1])
    if teams is not None:
        feed_sums = lax.psum(feed_sums, "rows", axis_index_groups=cross_groups(row_count, team))
    feed_held, offsets_f = feed_sums[None], [0]
    feed_came = pair_rows(feed_held, 4)
    wide, halves, conv_bias_grad = conv_grad(me_word, came, put, slope0, ext)
    conv_bias_grad = conv_bias_grad[:, 0, : PH * GW].reshape(groups_here, PH, GW)
    conv_bias_grad = jnp.sum(conv_bias_grad, axis=1).reshape(-1)
    halves_all = lax.all_to_all(halves, "rows", 0, 0, axis_index_groups=teams, tiled=True)
    tail_sum = add_low(after(tail_half[0], halves), tail_half[1])
    tail_half = halve(tail_sum, *tail_steps[2])
    feed_held, offsets_f = gather_join(feed_held, after(feed_came, halves), offsets_f, 4)
    feed_came = pair_rows(feed_held, 2)
    signal_slots = signal_grad(after(wide, tail_sum, feed_held), conv_flat, 0, groups_here // 2)
    tail_part = add_low(after(tail_half[0], signal_slots), tail_half[1])
    halves_all = after(halves_all, signal_slots, tail_part)
    kernel_part = tap_grad(turned_core, halves_all)
    feed_held, offsets_f = gather_join(feed_held, after(feed_came, kernel_part), offsets_f, 2)
    feed_came = pair_rows(feed_held, 1)
    offsets_f = offsets_f + [x ^ 1 for x in offsets_f]
    if teams is not None:
        others = cross_groups(row_count, team)
        tail_part = lax.psum(tail_part.astype(F32), "rows", axis_index_groups=others).astype(BF)
    tail_held, offsets_t = tail_part[None], [0]
    tail_came = pair_rows(tail_held, 4)

    shared = jnp.concatenate([sums0[:2], sums1[:3], sums2[:3]], axis=0)
    all_small = [shared[i] for i in range(shared.shape[0])]
    rows_small = [conv_bias_grad, qv_grad, up_bias_grad]
    shared = shared + swap(shared, 1)
    shared = shared + swap(shared, 2)
    small = jnp.concatenate([shared.reshape(-1)] + [v.reshape(-1) for v in rows_small])
    small_size = small.size
    small = jnp.pad(small, (0, -small_size % (16 * KER))).reshape(-1, KER)
    if teams is not None:
        others = cross_groups(row_count, team)
        kernel_part = lax.psum(kernel_part, "rows", axis_index_groups=others)
        small = lax.psum(small, "rows", axis_index_groups=others)
    small_high = small.astype(BF)
    small_low = (small - small_high.astype(F32)).astype(BF)
    part_rows = kernel_part.shape[0] // 2
    part_low = kernel_part.astype(BF)
    held_a = jnp.concatenate([part_low[:part_rows], small_high], axis=0)[None]
    held_b = jnp.concatenate([part_low[part_rows:], small_low], axis=0)[None]
    came_a, came_b = pair_rows(held_a, 4), pair_rows(held_b, 4)
    tail_held, offsets_t = gather_join(
        tail_held, after(tail_came, held_a, held_b), offsets_t, 4
    )
    tail_came = pair_rows(tail_held, 2)
    keep, near = signal_grad(
        after(wide, kernel_part, tail_held, feed_held),
        conv_flat,
        groups_here // 2,
        groups_here - groups_here // 2,
        signal_slots,
        put,
        me_word,
    )
    came_a, came_b, keep, near = all_after([came_a, came_b, keep, near], feed_came, tail_came)
    held_a, offsets_a = gather_join(held_a, came_a, [0], 4)
    held_b, offsets_b = gather_join(held_b, came_b, [0], 4)
    came_a, came_b = pair_rows(held_a, 2), pair_rows(held_b, 1)
    tail_held, offsets_t = gather_join(tail_held, tail_came, offsets_t, 2)
    tail_came = pair_rows(tail_held, 1)
    offsets_t = offsets_t + [x ^ 1 for x in offsets_t]
    came, pair = exchange(keep, near)
    frames_grad = add_frames_grad(me_word, came, grad0)
    held_a, offsets_a = gather_join(held_a, came_a, offsets_a, 2)
    held_b, offsets_b = gather_join(held_b, came_b, offsets_b, 1)
    part_order = jnp.array(
        [
            [
                [offsets.index(r ^ own) for r in holders_of(masks)]
                for offsets, masks in (
                    (offsets_f, FEED_MASKS[0]),
                    (offsets_f, FEED_MASKS[1]),
                    (offsets_t, TAIL_MASKS),
                )
            ]
            for own in range(team)
        ],
        jnp.int32,
    )
    part_order = lax.dynamic_index_in_dim(part_order, own_row, 0, keepdims=False)
    down_total, up_total = spread_parts(
        part_order[:2], after(feed_held, held_a, held_b), feed_came
    )
    qkv_total, out_total = spread_tail(
        part_order[2], after(tail_held, held_a, held_b), tail_came, 3 * head_cols
    )
    qkv_total = qkv_total.reshape(3, head_cols, D).transpose(2, 0, 1)
    came_a, came_b = pair_rows(held_a, 1), pair_rows(held_b, 2)
    offsets_a = offsets_a + [x ^ 1 for x in offsets_a]
    offsets_b = offsets_b + [x ^ 2 for x in offsets_b]
    order = jnp.array(
        [[offsets.index(x) for x in range(team)] for offsets in (offsets_a, offsets_b)], jnp.int32
    )
    order = order[:, jnp.arange(team, dtype=jnp.int32) ^ own_row]
    kernel_total = assemble(order, [held_a, came_a], [held_b, came_b]).transpose(2, 0, 1)
    small = sum(
        jnp.sum(value[:, part_rows:].astype(F32), axis=0)
        for value in (held_a, came_a, held_b, came_b)
    )
    small = small.reshape(-1)[:small_size]
    sizes = [v.size for v in all_small + rows_small]
    ends = [sum(sizes[: i + 1]) for i in range(len(sizes))]
    cuts = [small[end - size : end] for size, end in zip(sizes, ends)]
    gain0_grad, bias0_grad, gain1_grad, bias1_grad, out_bias_grad = cuts[:5]
    gain2_grad, bias2_grad, down_bias_grad, conv_bias_grad, qv_grad, up_bias_grad = cuts[5:]
    return (
        block_out,
        frames_grad,
        kernel_total,
        conv_bias_grad,
        gain0_grad,
        bias0_grad,
        qkv_total,
        qv_grad.reshape(2, head_cols),
        out_total,
        out_bias_grad,
        gain1_grad,
        bias1_grad,
        up_total,
        up_bias_grad,
        down_total,
        down_bias_grad,
        gain2_grad,
        bias2_grad,
    )


def solution(mesh):
    return jax.shard_map(
        on_device,
        mesh=mesh,
        in_specs=(
            P(("rows", "tp"), None),
            P("rows", None),
            P(None, None, "tp"),
            P("tp"),
            P(),
            P(),
            P(None, None, "tp"),
            P(None, "tp"),
            P("tp", None),
            P(),
            P(),
            P(),
            P(None, "tp"),
            P("tp"),
            P("tp", None),
            P(),
            P(),
            P(),
            P(("rows", "tp"), None),
        ),
        out_specs=(
            P(("rows", "tp"), None),
            P(("rows", "tp"), None),
            P(None, None, "tp"),
            P("tp"),
            P(),
            P(),
            P(None, None, "tp"),
            P(None, "tp"),
            P("tp", None),
            P(),
            P(),
            P(),
            P(None, "tp"),
            P("tp"),
            P("tp", None),
            P(),
            P(),
            P(),
        ),
        check_vma=False,
    )
```

```python
import functools

import jax
import jax.numpy as jnp
import numpy as np
from jax import lax
from jax.experimental import pallas as pl
from jax.experimental.pallas import tpu as pltpu
from jax.sharding import PartitionSpec as P

D = 768
HD = 64
KER = 128
GROUPS = 16
LEN = 1024

EPSILON = 1e-05
ROOT_HALF = 0.7071067811865476
INV_ROOT_TAU = 0.3989422804014327
MASK_ROOT = 16384.0

GW = D // GROUPS
HALF = GW // 2
PH = 5
QN, PN = 17, 16
CORE = QN * PN
NJ = 27
LEAD = 13
EXT = (QN + NJ - 1) * PN
LANES = 256
GAP = KER // 2
SLOTS = PH * CORE
WIDE_MIB = 58

ORDER = (0, 2, 1, 3)

BF = jnp.bfloat16
F32 = jnp.float32


def iota(shape, dim):
    return lax.broadcasted_iota(jnp.int32, shape, dim)


def full(shape):
    return pl.BlockSpec(shape, lambda *index: (0,) * len(shape))


def block(shape, index_map):
    return pl.BlockSpec(shape, index_map)


def params(mib):
    return pltpu.CompilerParams(vmem_limit_bytes=mib * 2**20)


def cost(microseconds):
    return pl.CostEstimate(
        flops=int(microseconds * 1.1e+09), bytes_accessed=int(microseconds * 1e+06), transcendentals=0
    )


def dot(left, right):
    return jnp.dot(left, right, preferred_element_type=F32)


def dot_turned(left, right):
    return lax.dot_general(left, right, (((1,), (1,)), ((), ())), preferred_element_type=F32)


def phi_pair(v):
    cdf = 0.5 * (1.0 + lax.erf(v * ROOT_HALF))
    return v * cdf, cdf + v * INV_ROOT_TAU * jnp.exp(-0.5 * v * v)


def norm_stats(inputs):
    centered = inputs - jnp.mean(inputs, axis=-1, keepdims=True)
    inv_std = lax.rsqrt(jnp.mean(centered * centered, axis=-1, keepdims=True) + EPSILON)
    return centered * inv_std, inv_std


def segment_row(starts_ref):
    frame = iota((1, LEN), 1)
    total = jnp.full((1, LEN), -1, jnp.int32)
    for j in range(starts_ref.shape[1]):
        total = total + (frame >= starts_ref[0, j]).astype(jnp.int32)
    return total


def fill_put(starts_ref, put_ref):
    place = iota((1, LEN), 1) + GAP * segment_row(starts_ref)
    at = (place * 52429) >> 18
    high = (at * 61681) >> 20
    slot = (place - PH * at) * CORE + (at - QN * high) * PN + high
    for i in range(PH):
        rows = iota((CORE, LEN), 0) + i * CORE
        put_ref[i * CORE : (i + 1) * CORE, :] = (rows == slot).astype(F32).astype(BF)


def extension():
    row, col = np.arange(EXT)[:, None], np.arange(CORE)[None, :]
    want = QN * (row % PN) + row // PN - LEAD
    have = QN * (col % PN) + col // PN
    return jnp.asarray((want == have).astype(np.float32), BF)


def toeplitz_scratch():
    return [
        pltpu.VMEM((PH * GW + KER * GW + 288, LANES), BF),
        pltpu.VMEM((NJ * LANES, LANES), BF),
    ]


def fill_toeplitz(w_ref, step, g, wide_ref, wt_ref):
    before = PH * GW
    row, lane = iota((w_ref.shape[1], LANES), 0), iota((w_ref.shape[1], LANES), 1)
    spread = ((row == GW * g + lane % GW) & (lane < PH * GW)).astype(F32).astype(BF)

    @pl.when(step == 0)
    def _():
        rest = before + KER * GW
        wide_ref[0:before, :] = jnp.zeros((before, LANES), BF)
        wide_ref[rest:, :] = jnp.zeros((wide_ref.shape[0] - rest, LANES), BF)
        for j in range(NJ):
            gap = slice(j * LANES + PH * GW, (j + 1) * LANES)
            wt_ref[gap, :] = jnp.zeros((LANES - PH * GW, LANES), BF)

    wide_ref[before : before + KER * GW, :] = dot(w_ref[...], spread).astype(BF)
    lane = iota((1, LANES), 1)
    masks = [(lane // GW == i).astype(F32).astype(BF) for i in range(PH)]

    for j in range(NJ):
        for left in range(0, LANES, 128):
            lanes = slice(left, left + 128)
            total = None
            for i in range(left // GW, min((left + 127) // GW + 1, PH)):
                start = before + PH * GW * j - GW * (1 + i)
                part = wide_ref[start : start + PH * GW, lanes] * masks[i][:, lanes]
                total = part if total is None else total + part
            wt_ref[j * LANES : j * LANES + PH * GW, lanes] = total


def fold_in(slots_ref, g):
    width = slots_ref.shape[1]
    row, lane = iota((width, LANES), 0), iota((width, LANES), 1)
    core = jnp.zeros((CORE, LANES), F32)
    for i in range(PH):
        pick = ((lane // GW == i) & (row == GW * g + lane % GW)).astype(F32).astype(BF)
        core = core + dot(slots_ref[i * CORE : (i + 1) * CORE, :], pick)
    return core


def fold_out(values, back_ref, g):
    width = back_ref.shape[1]
    row, col = iota((LANES, width), 0), iota((LANES, width), 1)
    for i in range(PH):
        pick = ((row // GW == i) & (col == GW * g + row % GW)).astype(F32).astype(BF)
        here = slice(i * CORE, (i + 1) * CORE)
        back_ref[here, :] = back_ref[here, :] + dot(values, pick).astype(BF)


def unspread(back_ref, put_ref):
    turned = back_ref[...].astype(F32).T.astype(BF)
    return dot(turned, put_ref[...]).T.astype(BF)


def conv_kernel(me_ref, starts_ref, f0_ref, f1_ref, f2_ref, f3_ref, ext_ref, w_ref, bias_ref,
                mixed_ref, slope_ref, core_ref, sig_ref, slots_ref, wide_ref, back_ref, put_ref,
                taps_ref, wt_ref):
    g = pl.program_id(0)
    rows, features = f0_ref.shape
    width = sig_ref.shape[1]

    @pl.when(g == 0)
    def _():
        fill_put(starts_ref, put_ref)
        row, lane = iota((features, width), 0), iota((features, width), 1)
        pick = (row == lane + width * me_ref[0]).astype(F32).astype(BF)
        for n, ref in enumerate((f0_ref, f1_ref, f2_ref, f3_ref)):
            start = pl.multiple_of((me_ref[0] ^ ORDER[n]) * rows, rows)
            sig_ref[pl.ds(start, rows), :] = dot(ref[...], pick).astype(BF)
        slots_ref[...] = dot(put_ref[...], sig_ref[...]).astype(BF)
        back_ref[...] = jnp.zeros_like(back_ref)

    fill_toeplitz(w_ref, g, g, taps_ref, wt_ref)
    core = fold_in(slots_ref, g).astype(BF)
    core_ref[0] = core
    wide_ref[...] = dot(ext_ref[...], core).astype(BF)
    total = jnp.zeros((CORE, LANES), F32)
    for j in range(NJ):
        total = total + dot(
            wide_ref[PN * j : PN * j + CORE, :], wt_ref[j * LANES : (j + 1) * LANES, :]
        )
    value, slope = phi_pair(total + bias_ref[0])
    slope_ref[0] = slope
    fold_out(value.astype(BF), back_ref, g)

    @pl.when(g == pl.num_programs(0) - 1)
    def _():
        mixed_ref[...] = unspread(back_ref, put_ref)


def conv(me, starts, frames, ext, taps, bias_lanes):
    width = taps.shape[1]
    groups = width // GW
    return pl.pallas_call(
        conv_kernel,
        grid=(groups,),
        in_specs=[pl.BlockSpec(memory_space=pltpu.SMEM)] * 2
        + [full(frames[0].shape)] * 4
        + [
            full((EXT, CORE)),
            full(taps.shape),
            block((1, 1, LANES), lambda g: (g, 0, 0)),
        ],
        out_specs=[
            full((LEN, width)),
            block((1, CORE, LANES), lambda g: (g, 0, 0)),
            block((1, CORE, LANES), lambda g: (g, 0, 0)),
        ],
        out_shape=[
            jax.ShapeDtypeStruct((LEN, width), BF),
            jax.ShapeDtypeStruct((groups, CORE, LANES), F32),
            jax.ShapeDtypeStruct((groups, CORE, LANES), BF),
        ],
        scratch_shapes=[
            pltpu.VMEM((LEN, width), BF),
            pltpu.VMEM((SLOTS, width), BF),
            pltpu.VMEM((EXT, LANES), BF),
            pltpu.VMEM((SLOTS, width), BF),
            pltpu.VMEM((SLOTS, LEN), BF),
        ]
        + toeplitz_scratch(),
        compiler_params=params(WIDE_MIB),
        cost_estimate=cost(0.1),
    )(me, starts, *frames, ext, taps, bias_lanes)


def conv_grad_kernel(me_ref, starts_ref, keep_ref, far_ref, near_ref, slope_ref, ext_ref,
                     wide_ref, half_ref, bias_ref, grad_ref, slots_ref, put_ref):
    g = pl.program_id(0)
    rows = far_ref.shape[0] // 2

    @pl.when(g == 0)
    def _():
        fill_put(starts_ref, put_ref)
        for n, piece in enumerate(came_pieces(keep_ref, far_ref, near_ref)):
            start = pl.multiple_of((me_ref[0] ^ ORDER[n]) * rows, rows)
            grad_ref[pl.ds(start, rows), :] = piece
        slots_ref[...] = dot(put_ref[...], grad_ref[...]).astype(BF)

    grad = fold_in(slots_ref, g) * slope_ref[0]
    bias_ref[0] = jnp.sum(grad, axis=0, keepdims=True)
    low = grad.astype(BF)
    wide_ref[0] = dot(ext_ref[...], low).astype(BF)
    row, lane = iota((LANES, 128), 0), iota((LANES, 128), 1)
    for h in range(2):
        pick = (lane < PH * HALF) & (row == lane // HALF * GW + lane % HALF + h * HALF)
        half_ref[h] = dot(low, pick.astype(F32).astype(BF)).astype(BF)


def conv_grad(me, starts, came, slope, ext):
    groups = slope.shape[0]
    width = came[0].shape[1]
    return pl.pallas_call(
        conv_grad_kernel,
        grid=(groups,),
        in_specs=[
            pl.BlockSpec(memory_space=pltpu.SMEM),
            pl.BlockSpec(memory_space=pltpu.SMEM),
            full((LEN // 2, width)),
            full((LEN // 2, width)),
            full((LEN // 2, width)),
            block((1, CORE, LANES), lambda g: (g, 0, 0)),
            full((EXT, CORE)),
        ],
        out_specs=[
            block((1, EXT, LANES), lambda g: (g, 0, 0)),
            block((2, CORE, 128), lambda g: (g, 0, 0)),
            block((1, 1, LANES), lambda g: (g, 0, 0)),
        ],
        out_shape=[
            jax.ShapeDtypeStruct((groups, EXT, LANES), BF),
            jax.ShapeDtypeStruct((2 * groups, CORE, 128), BF),
            jax.ShapeDtypeStruct((groups, 1, LANES), F32),
        ],
        scratch_shapes=[
            pltpu.VMEM((LEN, width), BF),
            pltpu.VMEM((SLOTS, width), BF),
            pltpu.VMEM((SLOTS, LEN), BF),
        ],
        compiler_params=params(WIDE_MIB),
        cost_estimate=cost(0.1),
    )(me, starts, *came, slope, ext)


def signal_grad_kernel(first, wide_ref, w_ref, *refs):
    back_ref, taps_ref, wt_ref = refs[-3:]
    step = pl.program_id(0)
    g = first + step
    fill_toeplitz(w_ref, step, g, taps_ref, wt_ref)

    @pl.when(step == 0)
    def _():
        if first == 0:
            back_ref[...] = jnp.zeros_like(back_ref)
        else:
            back_ref[...] = refs[0][...]

    total = jnp.zeros((CORE, LANES), F32)
    for j in range(NJ):
        m = NJ - 1 - j
        total = total + dot_turned(
            wide_ref[0, PN * j : PN * j + CORE, :], wt_ref[m * LANES : (m + 1) * LANES, :]
        )
    fold_out(total.astype(BF), back_ref, g)
    if first == 0:

        @pl.when(step == pl.num_programs(0) - 1)
        def _():
            refs[0][...] = back_ref[...]

        return
    _, starts_ref, me_ref, keep_ref, near_ref, all_ref, put_ref = refs[:7]
    rows = keep_ref.shape[0] // 2

    @pl.when(step == pl.num_programs(0) - 1)
    def _():
        fill_put(starts_ref, put_ref)
        all_ref[...] = unspread(back_ref, put_ref)
        for n in range(4):
            start = pl.multiple_of((me_ref[0] ^ ORDER[n]) * rows, rows)
            out_ref = keep_ref if n < 2 else near_ref
            out_ref[n % 2 * rows : (n % 2 + 1) * rows, :] = all_ref[pl.ds(start, rows), :]


def signal_grad(wide, taps, first, count, *rest):
    width = taps.shape[1]
    slots = jax.ShapeDtypeStruct((SLOTS, width), BF)
    piece = jax.ShapeDtypeStruct((LEN // 2, width), BF)
    own = [
        block((1, EXT, LANES), lambda g: (first + g, 0, 0)),
        full(taps.shape),
    ]
    more = [full(slots.shape)] + [pl.BlockSpec(memory_space=pltpu.SMEM)] * 2
    scratch = [pltpu.VMEM(slots.shape, BF)] + toeplitz_scratch()
    return pl.pallas_call(
        functools.partial(signal_grad_kernel, first),
        grid=(count,),
        in_specs=own + (more if rest else []),
        out_specs=[full(piece.shape)] * 2 if rest else full(slots.shape),
        out_shape=[piece] * 2 if rest else slots,
        scratch_shapes=([pltpu.VMEM((LEN, width), BF), pltpu.VMEM((SLOTS, LEN), BF)] if rest else [])
        + scratch,
        compiler_params=params(WIDE_MIB),
        cost_estimate=cost(0.1),
    )(wide, taps, *rest)


def turn_core_kernel(sig_ref, ext_ref, out_ref, wide_ref):
    packs = sig_ref.shape[0]
    blocks = EXT // PN
    wide_ref[blocks:] = jnp.zeros((1, packs * PN, LANES), BF)
    for r in range(packs):
        rows = dot(ext_ref[...], sig_ref[r]).astype(BF)
        wide_ref[0:blocks, r * PN : (r + 1) * PN, :] = rows.reshape(blocks, PN, LANES)
    for q in range(blocks + 1):
        out_ref[:, q * 128 : (q + 1) * 128] = wide_ref[q].astype(F32).T.astype(BF)


def turn_core(sig, ext):
    packs = sig.shape[0]
    blocks = EXT // PN + 1
    return pl.pallas_call(
        turn_core_kernel,
        out_shape=jax.ShapeDtypeStruct((LANES, blocks * packs * PN), BF),
        scratch_shapes=[pltpu.VMEM((blocks, packs * PN, LANES), BF)],
        compiler_params=params(WIDE_MIB),
        cost_estimate=cost(0.1),
    )(sig, ext)


def tap_grad_kernel(sig_ref, grad_ref, out_ref, pair_ref, parts_ref, rows_ref):
    packs = grad_ref.shape[0]
    across = packs * PN
    pair_ref[QN, :, 0:128] = jnp.zeros((across, 128), BF)
    pair_ref[0, :, 128:] = jnp.zeros((across, 128), BF)
    for r in range(packs):
        rows = grad_ref[r].reshape(QN, PN, 128)
        pair_ref[0:QN, r * PN : (r + 1) * PN, 0:128] = rows
        pair_ref[1:, r * PN : (r + 1) * PN, 128:] = rows
    pair = pair_ref[...].reshape((QN + 1) * across, LANES)
    for j in range(0, NJ + 1, 2):
        part = dot(sig_ref[:, j * across : (j + QN + 1) * across], pair)
        parts_ref[PH * GW * j : PH * GW * (j + 1), :] = part[: PH * GW, 0:128]
        parts_ref[PH * GW * (j + 1) : PH * GW * (j + 2), :] = part[: PH * GW, 128:]
    phase = iota((1, 128), 1) // HALF
    chunk = 8 * GW

    for start in range(0, KER * GW, chunk):
        total = jnp.zeros((chunk, 128), F32)
        for i in range(PH):
            rows = slice(start + GW * (1 + i), start + GW * (1 + i) + chunk)
            total = jnp.where(phase == i, parts_ref[rows, :], total)
        rows_ref[start : start + chunk, :] = total
    for c in range(GW):
        taps = rows_ref[pl.ds(c, KER, stride=GW), :].T
        total = taps[0:HALF, :]
        for i in range(1, PH):
            total = total + taps[HALF * i : HALF * (i + 1), :]
        out_ref[c * HALF : (c + 1) * HALF, :] = total


def tap_grad(sig, grad):
    packs = grad.shape[0]
    return pl.pallas_call(
        tap_grad_kernel,
        out_shape=jax.ShapeDtypeStruct((GW * HALF, KER), F32),
        scratch_shapes=[
            pltpu.VMEM((QN + 1, packs * PN, LANES), BF),
            pltpu.VMEM(((NJ + 1) * PH * GW, 128), F32),
            pltpu.VMEM((KER * GW, 128), F32),
        ],
        compiler_params=params(WIDE_MIB),
        cost_estimate=cost(0.1),
    )(sig, grad)


def assemble_kernel(at_ref, a0_ref, a1_ref, b0_ref, b1_ref, out_ref, wide_ref):
    step = pl.program_id(0)
    half = a0_ref.shape[0]
    packs = 2 * half
    per_step = out_ref.shape[0]
    half_steps = pl.num_programs(0) // 2

    def place(held_ref, came_ref, which):
        for r in range(packs):
            at = at_ref[which, r]

            @pl.when(at < half)
            def _():
                wide_ref[...] = held_ref[at].astype(F32)

            @pl.when(at >= half)
            def _():
                wide_ref[...] = came_ref[at - half].astype(F32)

            for c in range(per_step):
                out_ref[c, r * HALF : (r + 1) * HALF, :] = wide_ref[c * HALF : (c + 1) * HALF, :]

    @pl.when(step < half_steps)
    def _():
        place(a0_ref, a1_ref, 0)

    @pl.when(step >= half_steps)
    def _():
        place(b0_ref, b1_ref, 1)


def assemble(order, parts_a, parts_b):
    packs = 2 * parts_a[0].shape[0]
    steps = 4
    per_step = GW // steps
    rows = per_step * HALF
    half = steps // 2
    return pl.pallas_call(
        assemble_kernel,
        grid=(steps,),
        in_specs=[
            pl.BlockSpec(memory_space=pltpu.SMEM),
        ]
        + [block((packs // 2, rows, KER), lambda s: (0, jnp.minimum(s, half - 1), 0))] * 2
        + [block((packs // 2, rows, KER), lambda s: (0, jnp.maximum(s - half, 0), 0))] * 2,
        out_specs=block((per_step, packs * HALF, KER), lambda s: (s, 0, 0)),
        out_shape=jax.ShapeDtypeStruct((GW, packs * HALF, KER), F32),
        scratch_shapes=[pltpu.VMEM((rows, KER), F32)],
        compiler_params=params(WIDE_MIB),
        cost_estimate=cost(4),
    )(order, *parts_a, *parts_b)


def spread_parts_kernel(order_ref, held_d, came_d, held_u, came_u, down_ref, up_ref):
    part = pl.program_id(0)
    half = pl.num_programs(0) // 2
    for i, (held, came, out) in enumerate(((held_d, came_d, down_ref), (held_u, came_u, up_ref))):

        @pl.when(order_ref[i, part] < half)
        def _():
            out[...] = held[0, 0].astype(F32)

        @pl.when(order_ref[i, part] >= half)
        def _():
            out[...] = came[0, 0].astype(F32)


def spread_parts(order, held, came):
    half, _, rows, width = held.shape
    first = lambda i: block(
        (1, 1, rows, width), lambda p, at: (jnp.minimum(at[i, p], half - 1), i, 0, 0)
    )
    second = lambda i: block(
        (1, 1, rows, width), lambda p, at: (jnp.maximum(at[i, p] - half, 0), i, 0, 0)
    )
    out = jax.ShapeDtypeStruct((2 * half * rows, width), F32)
    return pl.pallas_call(
        spread_parts_kernel,
        grid_spec=pltpu.PrefetchScalarGridSpec(
            num_scalar_prefetch=1,
            grid=(2 * half,),
            in_specs=[first(0), second(0), first(1), second(1)],
            out_specs=[block((rows, width), lambda p, at: (p, 0))] * 2,
        ),
        out_shape=[out, out],
        compiler_params=params(WIDE_MIB),
        cost_estimate=cost(5),
    )(order, held, came, held, came)


def spread_tail_kernel(first, order_ref, held_ref, came_ref, first_ref, last_ref):
    part = pl.program_id(0)
    half = pl.num_programs(0) // 2
    value = jnp.where(order_ref[part] < half, held_ref[0].astype(F32), came_ref[0].astype(F32))

    @pl.when(part < first)
    def _():
        first_ref[...] = value

    @pl.when(part >= first)
    def _():
        last_ref[...] = value


def spread_tail(order, held, came, split):
    half, rows, width = held.shape
    first = split // rows
    return pl.pallas_call(
        functools.partial(spread_tail_kernel, first),
        grid_spec=pltpu.PrefetchScalarGridSpec(
            num_scalar_prefetch=1,
            grid=(2 * half,),
            in_specs=[
                block((1, rows, width), lambda p, at: (jnp.minimum(at[p], half - 1), 0, 0)),
                block((1, rows, width), lambda p, at: (jnp.maximum(at[p] - half, 0), 0, 0)),
            ],
            out_specs=[
                block((rows, width), lambda p, at: (jnp.minimum(p, first - 1), 0)),
                block((rows, width), lambda p, at: (jnp.maximum(p - first, 0), 0)),
            ],
        ),
        out_shape=[
            jax.ShapeDtypeStruct((split, width), F32),
            jax.ShapeDtypeStruct((2 * half * rows - split, width), F32),
        ],
        compiler_params=params(WIDE_MIB),
        cost_estimate=cost(3),
    )(order, held, came)


def head_rows(turned, head, heads):
    pieces = [jnp.zeros((HD, turned.shape[1]), turned.dtype) for _ in range(heads)]
    pieces[head] = turned[HD * head : HD * (head + 1), :]
    return jnp.concatenate(pieces + [turned[HD * heads :, :]], axis=0)


def attention_kernel(q_block, heads, *refs):
    me_ref, starts_ref = refs[:2]
    mixed = refs[2:6]
    frames = refs[6:10]
    (vec_ref, wq_ref, wk_ref, wv_ref, qv_ref) = refs[10:15]
    (att_ref, own_ref, hat_ref, inv_ref, all_out, low_out, q_out, qt_out, k_out, v_out, ot_ref,
     lse_ref) = refs[15:27]
    all_ref, low_ref, q_ref, qt_ref, k_ref, v_ref, vt_ref, sems, seg_ref = refs[27:]
    rows = frames[0].shape[0]
    part = mixed[0].shape[1]
    width = frames[0].shape[1]
    scale = HD ** (-0.5)
    me = me_ref[0]
    row, lane = iota((part, width), 0), iota((part, width), 1)
    spots = [(lane == row + part * (me ^ m)).astype(F32).astype(BF) for m in ORDER]
    seg_ref[0:1, :] = segment_row(starts_ref)
    behind = iota((LANES, rows), 0) - heads * HD
    of_seg = (behind >= 0) & (behind < starts_ref.shape[1])
    for n in range(4):
        here = slice(n * rows, (n + 1) * rows)
        start = pl.multiple_of((me ^ ORDER[n]) * rows, rows)
        total = frames[n][...].astype(F32)
        for ref, spot in zip(mixed, spots):
            total = total + dot(ref[pl.ds(start, rows), :], spot)
        hat, inv = norm_stats(total)
        normed = hat * vec_ref[0:1, :] + vec_ref[1:2, :]
        if n == 0:
            own_ref[...] = normed
            hat_ref[...] = hat
            inv_ref[...] = jnp.broadcast_to(inv, inv_ref.shape)
        all_ref[here, :] = normed
        normed = normed.astype(BF)
        low_ref[here, :] = normed
        query = (dot_turned(normed, wq_ref[...]) + qv_ref[0:1, :]) * scale
        in_seg = behind == seg_ref[0:1, pl.ds(start, rows)]
        q_ref[here, :] = query.astype(BF)
        qt_ref[:, here] = (query.T + jnp.where(in_seg, MASK_ROOT, 0.0)).astype(BF)
        key = dot_turned(normed, wk_ref[...])
        k_ref[here, :] = (key + jnp.where(of_seg & ~in_seg, -MASK_ROOT, 0.0).T).astype(BF)
        value = dot_turned(normed, wv_ref[...]) + qv_ref[1:2, :]
        v_ref[here, :] = value.astype(BF)
        vt_ref[:, here] = value.T.astype(BF)
    held = [all_ref, low_ref, q_ref, qt_ref, k_ref, v_ref]
    kept = [all_out, low_out, q_out, qt_out, k_out, v_out]
    copies = [
        pltpu.make_async_copy(src, dst, sems.at[i]) for i, (src, dst) in enumerate(zip(held, kept))
    ]
    for copy in copies:
        copy.start()
    total = 4 * rows
    for head in range(heads):
        for start in range(0, total, q_block):
            cols = slice(start, start + q_block)
            turned = head_rows(qt_ref[:, cols], head, heads)
            scores = dot(k_ref[...], turned)
            top = jnp.max(scores, axis=0, keepdims=True)
            weights = jnp.exp(scores - top)
            sums = jnp.sum(weights, axis=0, keepdims=True)
            value = dot(vt_ref[HD * head : HD * (head + 1), :], weights.astype(BF))
            ot_ref[HD * head : HD * (head + 1), cols] = value / sums
            lse_ref[head : head + 1, cols] = top + jnp.log(sums)
    lse_ref[heads:, :] = jnp.zeros((8 - heads, total), F32)
    for n in range(4):
        here = slice(n * rows, (n + 1) * rows)
        att_ref[here, :] = ot_ref[:, here].T.astype(BF)
    for copy in copies:
        copy.wait()


def attention(me, starts, mixed, frames, vectors, weights, qv, heads, q_block=512):
    rows, width = frames[0].shape
    total = 4 * rows
    cols = heads * HD
    vmem = pl.BlockSpec(memory_space=pltpu.VMEM)
    away = pl.BlockSpec(memory_space=pltpu.HBM)
    held = [
        ((total, width), F32),
        ((total, width), BF),
        ((total, LANES), BF),
        ((LANES, total), BF),
        ((total, LANES), BF),
        ((total, LANES), BF),
    ]
    return pl.pallas_call(
        functools.partial(attention_kernel, q_block, heads),
        in_specs=[pl.BlockSpec(memory_space=pltpu.SMEM)] * 2 + [vmem] * 13,
        out_specs=[vmem] * 4 + [away] * 6 + [vmem] * 2,
        out_shape=[
            jax.ShapeDtypeStruct((total, cols), BF),
            jax.ShapeDtypeStruct((rows, width), F32),
            jax.ShapeDtypeStruct((rows, width), F32),
            jax.ShapeDtypeStruct((rows, 128), F32),
        ]
        + [jax.ShapeDtypeStruct(shape, kind) for shape, kind in held]
        + [jax.ShapeDtypeStruct((cols, total), F32), jax.ShapeDtypeStruct((8, total), F32)],
        scratch_shapes=[pltpu.VMEM(shape, kind) for shape, kind in held]
        + [
            pltpu.VMEM((LANES, total), BF),
            pltpu.SemaphoreType.DMA((len(held),)),
            pltpu.VMEM((8, total), jnp.int32),
        ],
        compiler_params=params(WIDE_MIB),
        cost_estimate=cost(4),
    )(me, starts, *mixed, *frames, vectors, *weights, qv)


def attention_grad_kernel(q_block, heads, *refs):
    pieces = came_pieces(*refs[:3])
    (q_ref, qt_ref, k_ref, v_ref, ot_ref, lse_ref, wq_ref, wk_ref, wv_ref,
     keep_ref, near_ref, gq_ref, gk_ref, gv_ref, sum_ref,
     go_ref, got_ref, kt_ref, delta_ref, dqt_ref, dk_ref, dv_ref) = refs[3:]
    rows = pieces[0].shape[0]
    total = 4 * rows
    cols_all = heads * HD
    scale = HD ** (-0.5)
    go_ref[...] = jnp.zeros_like(go_ref)
    for n in range(4):
        go_ref[n * rows : (n + 1) * rows, :cols_all] = pieces[n]
    got_ref[...] = go_ref[...].astype(F32).T.astype(BF)
    kt_ref[...] = k_ref[...].astype(F32).T.astype(BF)
    for head in range(heads):
        own = slice(HD * head, HD * (head + 1))
        delta_ref[head : head + 1, :] = jnp.sum(
            got_ref[own, :].astype(F32) * ot_ref[own, :], axis=0, keepdims=True
        )
    lane = iota((1, LANES), 1)
    for head in range(heads):
        own = slice(HD * head, HD * (head + 1))
        mask = (lane // HD == head).astype(F32).astype(BF)
        for start in range(0, total, q_block):
            cols = slice(start, start + q_block)
            scores = dot(k_ref[...], head_rows(qt_ref[:, cols], head, heads))
            probs = jnp.exp(scores - lse_ref[head : head + 1, cols])
            prob_grad = dot(v_ref[...], head_rows(got_ref[:, cols], head, heads))
            score_grad = (probs * (prob_grad - delta_ref[head : head + 1, cols])).astype(BF)
            value_part = dot(probs.astype(BF), go_ref[cols, :] * mask)
            key_part = dot(score_grad, q_ref[cols, :] * mask)
            if head == 0 and start == 0:
                dv_ref[...] = value_part
                dk_ref[...] = key_part
            else:
                dv_ref[...] += value_part
                dk_ref[...] += key_part
            dqt_ref[own, cols] = dot(kt_ref[own, :], score_grad)
    dqt_ref[cols_all:, :] = jnp.zeros((LANES - cols_all, total), F32)
    sums_q = jnp.zeros((1, LANES), F32)
    sums_v = jnp.zeros((1, LANES), F32)
    for n in range(4):
        here = slice(n * rows, (n + 1) * rows)
        query_grad = dqt_ref[:, here].T * scale
        value_grad = dv_ref[here, :]
        sums_q = sums_q + jnp.sum(query_grad, axis=0, keepdims=True)
        sums_v = sums_v + jnp.sum(value_grad, axis=0, keepdims=True)
        low_q = query_grad.astype(BF)
        low_k = dk_ref[here, :].astype(BF)
        low_v = value_grad.astype(BF)
        gq_ref[here, :] = low_q[:, :cols_all]
        gk_ref[here, :] = low_k[:, :cols_all]
        gv_ref[here, :] = low_v[:, :cols_all]
        back = dot(low_q, wq_ref[...]) + dot(low_k, wk_ref[...]) + dot(low_v, wv_ref[...])
        out_ref = keep_ref if n < 2 else near_ref
        out_ref[n % 2 * rows : (n % 2 + 1) * rows, :] = back.astype(BF)
    sum_ref[0:1, :] = sums_q
    sum_ref[1:2, :] = sums_v
    sum_ref[2:, :] = jnp.zeros((6, LANES), F32)


def attention_grad(came, saved, weights, heads, q_block=512):
    half, cols = came[0].shape
    total = 2 * half
    width = weights[0].shape[1]
    return pl.pallas_call(
        functools.partial(attention_grad_kernel, q_block, heads),
        out_shape=[
            jax.ShapeDtypeStruct((half, width), BF),
            jax.ShapeDtypeStruct((half, width), BF),
            jax.ShapeDtypeStruct((total, cols), BF),
            jax.ShapeDtypeStruct((total, cols), BF),
            jax.ShapeDtypeStruct((total, cols), BF),
            jax.ShapeDtypeStruct((8, LANES), F32),
        ],
        scratch_shapes=[
            pltpu.VMEM((total, LANES), BF),
            pltpu.VMEM((LANES, total), BF),
            pltpu.VMEM((LANES, total), BF),
            pltpu.VMEM((8, total), F32),
            pltpu.VMEM((LANES, total), F32),
            pltpu.VMEM((total, LANES), F32),
            pltpu.VMEM((total, LANES), F32),
        ],
        compiler_params=params(WIDE_MIB),
        cost_estimate=cost(0.1),
    )(*came, *saved, *weights)


def put_half(n, value, keep_ref, near_ref):
    @pl.when(n < 2)
    def _():
        keep_ref[...] = value

    @pl.when(n >= 2)
    def _():
        near_ref[...] = value


def feed_kernel(a0_ref, a1_ref, a2_ref, a3_ref, normed_ref, o0_ref, o1_ref, o2_ref, o3_ref, vec_ref,
                up_ref, down_ref,
                low_ref, act_ref, slope_ref, keep_ref, near_ref, own_ref, hat_ref, inv_ref):
    n = pl.program_id(0)
    total = normed_ref[...] + vec_ref[6:7, :]
    out_refs = (o0_ref, o1_ref, o2_ref, o3_ref)
    for ref, out_ref in zip((a0_ref, a1_ref, a2_ref, a3_ref), out_refs):
        total = total + dot(ref[...], out_ref[...])
    hat, inv = norm_stats(total)
    normed = hat * vec_ref[2:3, :] + vec_ref[3:4, :]

    @pl.when(n == 0)
    def _():
        own_ref[...] = normed
        hat_ref[...] = hat
        inv_ref[...] = jnp.broadcast_to(inv, inv_ref.shape)

    low = normed.astype(BF)
    low_ref[...] = low
    value, slope = phi_pair(dot(low, up_ref[...]) + vec_ref[8:9, :])
    slope_ref[...] = slope
    value = value.astype(BF)
    act_ref[...] = value
    put_half(n, dot(value, down_ref[...]).astype(BF), keep_ref, near_ref)


def feed(attended, normed, out_pieces, vectors, up_weight, down_weight):
    total, width = normed.shape
    rows = total // 4
    part = attended[0].shape[1]
    units = up_weight.shape[1]
    here = lambda n: (n, 0)
    return pl.pallas_call(
        feed_kernel,
        grid=(4,),
        in_specs=[block((rows, part), lambda n, i=i: (n ^ i, 0)) for i in range(4)]
        + [block((rows, width), here)]
        + [full((part, width))] * 4
        + [
            full((16, width)),
            full((width, units)),
            full((units, width)),
        ],
        out_specs=[
            block((rows, width), here),
            block((rows, units), here),
            block((rows, units), here),
            block((rows, width), lambda n: (jnp.minimum(n, 1), 0)),
            block((rows, width), lambda n: (jnp.maximum(n - 2, 0), 0)),
            full((rows, width)),
            full((rows, width)),
            full((rows, 128)),
        ],
        out_shape=[
            jax.ShapeDtypeStruct((total, width), BF),
            jax.ShapeDtypeStruct((total, units), BF),
            jax.ShapeDtypeStruct((total, units), F32),
            jax.ShapeDtypeStruct((total // 2, width), BF),
            jax.ShapeDtypeStruct((total // 2, width), BF),
            jax.ShapeDtypeStruct((rows, width), F32),
            jax.ShapeDtypeStruct((rows, width), F32),
            jax.ShapeDtypeStruct((rows, 128), F32),
        ],
        compiler_params=params(WIDE_MIB),
        cost_estimate=cost(10),
    )(*attended, normed, *out_pieces, vectors, up_weight, down_weight)


def feed_grad_kernel(g0_ref, g1_ref, g2_ref, g3_ref, slope_ref, up_ref, down_ref,
                     all_ref, low_ref, keep_ref, near_ref, bias_ref):
    n = pl.program_id(0)
    for i, ref in enumerate((g0_ref, g1_ref, g2_ref, g3_ref)):

        @pl.when(n == i)
        def _():
            all_ref[...] = ref[...]

    grad = dot_turned(all_ref[...], down_ref[...]) * slope_ref[...]

    @pl.when(n == 0)
    def _():
        bias_ref[...] = jnp.zeros_like(bias_ref)

    bias_ref[...] += jnp.sum(grad, axis=0, keepdims=True)
    low = grad.astype(BF)
    low_ref[...] = low
    put_half(n, dot_turned(low, up_ref[...]).astype(BF), keep_ref, near_ref)


def feed_grad(grads, slope, up_weight, down_weight):
    total, units = slope.shape
    rows, width = grads[0].shape
    here = lambda n: (n, 0)
    return pl.pallas_call(
        feed_grad_kernel,
        grid=(4,),
        in_specs=[full((rows, width))] * 4
        + [block((rows, units), here), full((width, units)), full((units, width))],
        out_specs=[
            block((rows, width), here),
            block((rows, units), here),
            block((rows, width), lambda n: (jnp.minimum(n, 1), 0)),
            block((rows, width), lambda n: (jnp.maximum(n - 2, 0), 0)),
            full((1, units)),
        ],
        out_shape=[
            jax.ShapeDtypeStruct((total, width), BF),
            jax.ShapeDtypeStruct((total, units), BF),
            jax.ShapeDtypeStruct((total // 2, width), BF),
            jax.ShapeDtypeStruct((total // 2, width), BF),
            jax.ShapeDtypeStruct((1, units), F32),
        ],
        compiler_params=params(WIDE_MIB),
        cost_estimate=cost(6),
    )(*grads, slope, up_weight, down_weight)


def came_pieces(keep_ref, far_ref, near_ref):
    rows = far_ref.shape[0] // 2
    return [keep_ref[:rows, :], far_ref[:rows, :], near_ref[:rows, :], far_ref[rows:, :]]


def put_sums(sum_ref, *values):
    sum_ref[...] = jnp.zeros_like(sum_ref)
    for i, value in enumerate(values):
        sum_ref[i : i + 1, :] = jnp.sum(value, axis=0, keepdims=True)


def norm_grad(grad, hat, inv, gain):
    scaled = grad * gain
    return inv * (
        scaled
        - jnp.mean(scaled, axis=-1, keepdims=True)
        - hat * jnp.mean(scaled * hat, axis=-1, keepdims=True)
    )


def last_norm_kernel(keep_ref, near_ref, far_ref, normed_ref, cot_ref, vec_ref, out_ref, grad_ref, low_ref, sum_ref):
    total = keep_ref[...].astype(F32) + near_ref[...].astype(F32) + far_ref[...].astype(F32)
    hat, inv = norm_stats(normed_ref[...] + total + vec_ref[7:8, :])
    gain = vec_ref[4:5, :]
    out_ref[...] = (hat * gain + vec_ref[5:6, :]).astype(BF)
    cot = cot_ref[...].astype(F32)
    grad = norm_grad(cot, hat, inv, gain)
    grad_ref[...] = grad
    low_ref[...] = grad.astype(BF)
    put_sums(sum_ref, cot * hat, cot, grad)


def last_norm(terms, normed, cotangent, vectors):
    rows, width = normed.shape
    return pl.pallas_call(
        last_norm_kernel,
        grid=(1,),
        in_specs=[full((rows, width))] * 5 + [full((16, width))],
        out_specs=[full((rows, width))] * 3 + [full((8, width))],
        out_shape=[
            jax.ShapeDtypeStruct((rows, width), BF),
            jax.ShapeDtypeStruct((rows, width), F32),
            jax.ShapeDtypeStruct((rows, width), BF),
            jax.ShapeDtypeStruct((8, width), F32),
        ],
        compiler_params=params(WIDE_MIB),
        cost_estimate=cost(3),
    )(*terms, normed, cotangent, vectors)


def middle_norm_kernel(keep_ref, near_ref, far_ref, grad_ref, hat_ref, inv_ref, vec_ref, o0_ref,
                       o1_ref, o2_ref, o3_ref, out_ref, low_ref, sum_ref, keep_out, near_out):
    rows = grad_ref.shape[0]
    total = keep_ref[...].astype(F32) + near_ref[...].astype(F32) + far_ref[...].astype(F32)
    total = total + grad_ref[...]
    hat = hat_ref[...]
    grad = norm_grad(total, hat, inv_ref[:, 0:1], vec_ref[2:3, :])
    out_ref[...] = grad
    low = grad.astype(BF)
    low_ref[...] = low
    put_sums(sum_ref, total * hat, total, grad)
    for n, ref in enumerate((o0_ref, o1_ref, o2_ref, o3_ref)):
        back = dot_turned(low, ref[...]).astype(BF)
        out = keep_out if n < 2 else near_out
        out[n % 2 * rows : (n % 2 + 1) * rows, :] = back


def middle_norm(terms, grad, hat, inv, vectors, out_pieces):
    rows, width = grad.shape
    part = out_pieces[0].shape[0]
    return pl.pallas_call(
        middle_norm_kernel,
        grid=(1,),
        in_specs=[full((rows, width))] * 5
        + [full((rows, 128)), full((16, width))]
        + [full((part, width))] * 4,
        out_specs=[full((rows, width))] * 2 + [full((8, width))] + [full((2 * rows, part))] * 2,
        out_shape=[
            jax.ShapeDtypeStruct((rows, width), F32),
            jax.ShapeDtypeStruct((rows, width), BF),
            jax.ShapeDtypeStruct((8, width), F32),
            jax.ShapeDtypeStruct((2 * rows, part), BF),
            jax.ShapeDtypeStruct((2 * rows, part), BF),
        ],
        compiler_params=params(WIDE_MIB),
        cost_estimate=cost(0.1),
    )(*terms, grad, hat, inv, vectors, *out_pieces)


def first_norm_kernel(me_ref, keep_ref, near_ref, far_ref, grad_ref, hat_ref, inv_ref, vec_ref,
                      out_ref, sum_ref, keep_out, near_out):
    rows, width = grad_ref.shape
    part = keep_out.shape[1]
    total = keep_ref[...].astype(F32) + near_ref[...].astype(F32) + far_ref[...].astype(F32)
    total = total + grad_ref[...]
    hat = hat_ref[...]
    grad = norm_grad(total, hat, inv_ref[:, 0:1], vec_ref[0:1, :])
    out_ref[...] = grad
    low = grad.astype(BF)
    put_sums(sum_ref, total * hat, total)
    row, lane = iota((width, part), 0), iota((width, part), 1)
    for n in range(4):
        pick = (row == lane + part * (me_ref[0] ^ ORDER[n])).astype(F32).astype(BF)
        out = keep_out if n < 2 else near_out
        out[n % 2 * rows : (n % 2 + 1) * rows, :] = dot(low, pick).astype(BF)


def first_norm(me, terms, grad, hat, inv, vectors):
    rows, width = grad.shape
    part = width // 4
    return pl.pallas_call(
        first_norm_kernel,
        grid=(1,),
        in_specs=[pl.BlockSpec(memory_space=pltpu.SMEM)]
        + [full((rows, width))] * 5
        + [full((rows, 128)), full((16, width))],
        out_specs=[full((rows, width)), full((8, width))] + [full((2 * rows, part))] * 2,
        out_shape=[
            jax.ShapeDtypeStruct((rows, width), F32),
            jax.ShapeDtypeStruct((8, width), F32),
            jax.ShapeDtypeStruct((2 * rows, part), BF),
            jax.ShapeDtypeStruct((2 * rows, part), BF),
        ],
        compiler_params=params(WIDE_MIB),
        cost_estimate=cost(0.1),
    )(me, *terms, grad, hat, inv, vectors)


def frames_grad_kernel(me_ref, keep_ref, far_ref, near_ref, grad_ref, out_ref):
    width = grad_ref.shape[1]
    part = keep_ref.shape[1]
    row, lane = iota((part, width), 0), iota((part, width), 1)
    total = grad_ref[...]
    for n, piece in enumerate(came_pieces(keep_ref, far_ref, near_ref)):
        spot = (lane == row + part * (me_ref[0] ^ ORDER[n])).astype(F32).astype(BF)
        total = total + dot(piece, spot)
    out_ref[...] = total


def add_frames_grad(me, came, grad):
    half, part = came[0].shape
    rows, width = grad.shape
    return pl.pallas_call(
        frames_grad_kernel,
        grid=(1,),
        in_specs=[pl.BlockSpec(memory_space=pltpu.SMEM)]
        + [full((half, part))] * 3
        + [full((rows, width))],
        out_specs=full((rows, width)),
        out_shape=jax.ShapeDtypeStruct((rows, width), F32),
        compiler_params=params(WIDE_MIB),
        cost_estimate=cost(0.1),
    )(me, *came, grad)


def swap(value, bit):
    return lax.ppermute(value, "tp", [(i, i ^ bit) for i in range(lax.axis_size("tp"))])


def gather_pieces(value):
    across = swap(value, 2)
    return [value, across, swap(value, 1), swap(across, 1)]


def scatter_terms(keep, near):
    piece = keep.shape[0] // 2
    came = swap(near, 1)
    pair = (keep[piece:].astype(F32) + came[piece:].astype(F32)).astype(BF)
    return [keep, came, swap(pair, 2)], pair


def exchange(keep, near, *ahead):
    rows = keep.shape[0] // 2
    came = swap(near, 1)
    pair = after(jnp.concatenate([keep[rows:], came[rows:]], axis=0), *ahead)
    return [keep, swap(pair, 2), came], pair


def after(value, *others):
    return lax.optimization_barrier((value, *others))[0]


def all_after(values, *others):
    return list(lax.optimization_barrier((*values, *others))[: len(values)])


def team_groups(row_count, team):
    if row_count == team:
        return None
    return [list(range(first, first + team)) for first in range(0, row_count, team)]


def cross_groups(row_count, team):
    return [list(range(first, row_count, team)) for first in range(team)]


def pair_rows(value, mask):
    count = lax.axis_size("rows")
    return lax.ppermute(value, "rows", [(i, i ^ mask) for i in range(count)])


FEED_MASKS = ((1, 4, 2), (2, 1, 4))
TAIL_MASKS = (1, 2, 4)


def side_of(index, mask):
    return (index >> {1: 0, 2: 1, 4: 2}[mask]) & 1


def holders_of(masks):
    part = lambda index: sum(side_of(index, m) << (2 - i) for i, m in enumerate(masks))
    return sorted(range(8), key=part)


def halve(value, mask, side):
    half = value.shape[0] // 2
    kept = lax.dynamic_slice_in_dim(value, side * half, half, 0)
    sent = lax.dynamic_slice_in_dim(value, (1 - side) * half, half, 0)
    return kept, pair_rows(sent, mask)


def add_low(kept, came):
    return (kept.astype(F32) + came.astype(F32)).astype(BF)


def gather_join(held, came, offsets, mask):
    held = jnp.concatenate([held, came], axis=0)
    return held, offsets + [x ^ mask for x in offsets]


def on_device(
    frames,
    seg_starts,
    conv_weight,
    conv_bias,
    norm_gain0,
    norm_bias0,
    qkv_weight,
    qv_bias,
    out_weight,
    out_bias,
    norm_gain1,
    norm_bias1,
    up_weight,
    up_bias,
    down_weight,
    down_bias,
    norm_gain2,
    norm_bias2,
    cotangent,
):
    head_cols = qkv_weight.shape[2]
    heads_here = head_cols // HD
    groups_here = conv_weight.shape[2] // GW
    team = 2 * groups_here
    row_count = lax.axis_size("rows")
    teams = team_groups(row_count, team)
    me = lax.axis_index("tp")
    me_word = me.reshape(1).astype(jnp.int32)
    own_row = lax.axis_index("rows") % team
    vectors = [norm_gain0, norm_bias0, norm_gain1, norm_bias1, norm_gain2, norm_bias2]
    vectors = jnp.concatenate(vectors + [out_bias, down_bias, up_bias]).astype(F32)
    vectors = jnp.pad(vectors.reshape(-1, D), ((0, 7), (0, 0)))

    ext = extension()
    conv_flat = lax.optimization_barrier(conv_weight.reshape(KER * GW, -1))
    starts = seg_starts
    bias_lanes = jnp.tile(conv_bias.astype(F32).reshape(groups_here, 1, GW), (1, 1, PH))
    bias_lanes = jnp.pad(bias_lanes, ((0, 0), (0, 0), (0, LANES - PH * GW)))
    bias_lanes = after(bias_lanes, starts)
    across = swap(frames, 2)
    frames_pieces = [frames, across, swap(frames, 1), swap(after(across, conv_flat), 1)]
    out_pieces = gather_pieces(out_weight)
    mixed_low, slope0, core = conv(me_word, starts, frames_pieces, ext, conv_flat, bias_lanes)

    mixed_low = after(mixed_low, out_pieces[1], out_pieces[2])
    qkv_padded = jnp.pad(
        after(qkv_weight, mixed_low).transpose(1, 2, 0),
        ((0, 0), (0, LANES - head_cols), (0, 0)),
    )
    qkv_parts = [qkv_padded[0], qkv_padded[1], qkv_padded[2]]
    qv_padded = jnp.pad(
        after(qv_bias, mixed_low).astype(F32), ((0, 0), (0, LANES - head_cols))
    )
    vectors = after(vectors, mixed_low)
    mixed_pieces = gather_pieces(mixed_low)
    (attended, normed0, hat0, inv0, normed0_all, normed0_low, *saved) = attention(
        me_word,
        seg_starts,
        mixed_pieces,
        frames_pieces,
        vectors,
        qkv_parts,
        qv_padded,
        heads_here,
    )

    core_all = lax.all_to_all(
        jnp.repeat(core, 2, axis=0), "rows", 0, 0, axis_index_groups=teams, tiled=True
    )
    attended_pieces = all_after(gather_pieces(attended), core_all)
    normed1_low, activated, slope1, keep, near, normed1, hat1, inv1 = feed(
        attended_pieces, normed0_all, out_pieces, vectors, up_weight, down_weight
    )
    terms, pair = scatter_terms(keep, near)
    turned_core = turn_core(after(core_all, pair), ext)
    terms = all_after(terms, turned_core)
    block_out, grad2, grad2_low, sums2 = last_norm(terms, normed1, cotangent, vectors)

    grad2_all, up_low, keep, near, up_bias_grad = feed_grad(
        gather_pieces(grad2_low), slope1, up_weight, down_weight
    )
    terms, pair = scatter_terms(keep, near)
    activated, normed1_low = all_after([activated, normed1_low], pair)
    down_grad = jnp.einsum("rf,rd->fd", activated, grad2_all, preferred_element_type=F32)
    up_grad = jnp.einsum("rd,rf->df", normed1_low, up_low, preferred_element_type=F32)
    feed_grads = [down_grad.astype(BF), up_grad.astype(BF)]
    terms = all_after(terms, *feed_grads)
    feed_steps = [[(mask, side_of(own_row, mask)) for mask in masks] for masks in FEED_MASKS]
    halves_1 = [halve(grad, *order[0]) for grad, order in zip(feed_grads, feed_steps)]

    grad1, grad1_low, sums1, keep, near = middle_norm(
        terms, grad2, hat1, inv1, vectors, out_pieces
    )
    came, pair = exchange(keep, near, *[other for kept, other in halves_1])
    feed_sums = [add_low(after(kept, pair), other) for kept, other in halves_1]
    came = all_after(came, *feed_sums)
    halves_2 = [halve(grad, *order[1]) for grad, order in zip(feed_sums, feed_steps)]
    keep, near, query_grad, key_grad, value_grad, qv_sums = attention_grad(
        came, saved, qkv_parts, heads_here
    )
    grad1_pieces = gather_pieces(after(grad1_low, *came))
    feed_sums = [add_low(after(kept, keep), other) for kept, other in halves_2]
    near = after(near, *feed_sums, grad1_pieces[1], grad1_pieces[2])
    terms, pair = scatter_terms(keep, near)
    halves_3 = [halve(grad, *order[2]) for grad, order in zip(feed_sums, feed_steps)]
    out_grad = jnp.einsum(
        "rh,rd->hd",
        after(attended, pair),
        jnp.concatenate(grad1_pieces, axis=0),
        preferred_element_type=F32,
    )
    normed0_low = after(normed0_low, pair)
    turned_grads = [
        jnp.einsum("rc,rd->cd", part, normed0_low, preferred_element_type=F32).astype(BF)
        for part in (query_grad, key_grad, value_grad)
    ]
    tail = jnp.concatenate(turned_grads + [out_grad.astype(BF)], axis=0)
    terms = all_after(terms, tail)
    qv_grad = qv_sums[:2, :head_cols]
    tail_steps = [(mask, side_of(own_row, mask)) for mask in TAIL_MASKS]
    tail_half = halve(tail, *tail_steps[0])
    grad0, sums0, keep, near = first_norm(me_word, terms, grad1, hat0, inv0, vectors)

    near = after(near, tail_half[1], *[other for kept, other in halves_3])
    came, pair = exchange(keep, near)
    feed_sums = jnp.stack([add_low(after(kept, pair), other) for kept, other in halves_3])
    tail_sum = add_low(after(tail_half[0], pair), tail_half[1])
    came = all_after(came, tail_sum, feed_sums)
    tail_half = halve(tail_sum, *tail_steps[1])
    if teams is not None:
        feed_sums = lax.psum(feed_sums, "rows", axis_index_groups=cross_groups(row_count, team))
    feed_held, offsets_f = feed_sums[None], [0]
    feed_came = pair_rows(feed_held, 4)
    wide, halves, conv_bias_grad = conv_grad(me_word, seg_starts, came, slope0, ext)
    conv_bias_grad = conv_bias_grad[:, 0, : PH * GW].reshape(groups_here, PH, GW)
    conv_bias_grad = jnp.sum(conv_bias_grad, axis=1).reshape(-1)
    halves_all = lax.all_to_all(halves, "rows", 0, 0, axis_index_groups=teams, tiled=True)
    tail_sum = add_low(after(tail_half[0], halves), tail_half[1])
    tail_half = halve(tail_sum, *tail_steps[2])
    feed_held, offsets_f = gather_join(feed_held, after(feed_came, halves), offsets_f, 4)
    feed_came = pair_rows(feed_held, 2)
    signal_slots = signal_grad(after(wide, tail_sum, feed_held), conv_flat, 0, groups_here // 2)
    tail_part = add_low(after(tail_half[0], signal_slots), tail_half[1])
    halves_all = after(halves_all, signal_slots, tail_part)
    kernel_part = tap_grad(turned_core, halves_all)
    feed_held, offsets_f = gather_join(feed_held, after(feed_came, kernel_part), offsets_f, 2)
    feed_came = pair_rows(feed_held, 1)
    offsets_f = offsets_f + [x ^ 1 for x in offsets_f]
    if teams is not None:
        others = cross_groups(row_count, team)
        tail_part = lax.psum(tail_part.astype(F32), "rows", axis_index_groups=others).astype(BF)
    tail_held, offsets_t = tail_part[None], [0]
    tail_came = pair_rows(tail_held, 4)

    shared = jnp.concatenate([sums0[:2], sums1[:3], sums2[:3]], axis=0)
    all_small = [shared[i] for i in range(shared.shape[0])]
    rows_small = [conv_bias_grad, qv_grad, up_bias_grad]
    shared = shared + swap(shared, 1)
    shared = shared + swap(shared, 2)
    small = jnp.concatenate([shared.reshape(-1)] + [v.reshape(-1) for v in rows_small])
    small_size = small.size
    small = jnp.pad(small, (0, -small_size % (16 * KER))).reshape(-1, KER)
    if teams is not None:
        others = cross_groups(row_count, team)
        kernel_part = lax.psum(kernel_part, "rows", axis_index_groups=others)
        small = lax.psum(small, "rows", axis_index_groups=others)
    small_high = small.astype(BF)
    small_low = (small - small_high.astype(F32)).astype(BF)
    part_rows = kernel_part.shape[0] // 2
    part_low = kernel_part.astype(BF)
    held_a = jnp.concatenate([part_low[:part_rows], small_high], axis=0)[None]
    held_b = jnp.concatenate([part_low[part_rows:], small_low], axis=0)[None]
    came_a, came_b = pair_rows(held_a, 4), pair_rows(held_b, 4)
    tail_held, offsets_t = gather_join(
        tail_held, after(tail_came, held_a, held_b), offsets_t, 4
    )
    tail_came = pair_rows(tail_held, 2)
    keep, near = signal_grad(
        after(wide, kernel_part, tail_held, feed_held),
        conv_flat,
        groups_here // 2,
        groups_here - groups_here // 2,
        signal_slots,
        seg_starts,
        me_word,
    )
    came_a, came_b, keep, near = all_after([came_a, came_b, keep, near], feed_came, tail_came)
    held_a, offsets_a = gather_join(held_a, came_a, [0], 4)
    held_b, offsets_b = gather_join(held_b, came_b, [0], 4)
    came_a, came_b = pair_rows(held_a, 2), pair_rows(held_b, 1)
    tail_held, offsets_t = gather_join(tail_held, tail_came, offsets_t, 2)
    tail_came = pair_rows(tail_held, 1)
    offsets_t = offsets_t + [x ^ 1 for x in offsets_t]
    came, pair = exchange(keep, near)
    frames_grad = add_frames_grad(me_word, came, grad0)
    held_a, offsets_a = gather_join(held_a, came_a, offsets_a, 2)
    held_b, offsets_b = gather_join(held_b, came_b, offsets_b, 1)
    part_order = jnp.array(
        [
            [
                [offsets.index(r ^ own) for r in holders_of(masks)]
                for offsets, masks in (
                    (offsets_f, FEED_MASKS[0]),
                    (offsets_f, FEED_MASKS[1]),
                    (offsets_t, TAIL_MASKS),
                )
            ]
            for own in range(team)
        ],
        jnp.int32,
    )
    part_order = lax.dynamic_index_in_dim(part_order, own_row, 0, keepdims=False)
    down_total, up_total = spread_parts(
        part_order[:2], after(feed_held, held_a, held_b), feed_came
    )
    qkv_total, out_total = spread_tail(
        part_order[2], after(tail_held, held_a, held_b), tail_came, 3 * head_cols
    )
    qkv_total = qkv_total.reshape(3, head_cols, D).transpose(2, 0, 1)
    came_a, came_b = pair_rows(held_a, 1), pair_rows(held_b, 2)
    offsets_a = offsets_a + [x ^ 1 for x in offsets_a]
    offsets_b = offsets_b + [x ^ 2 for x in offsets_b]
    order = jnp.array(
        [[offsets.index(x) for x in range(team)] for offsets in (offsets_a, offsets_b)], jnp.int32
    )
    order = order[:, jnp.arange(team, dtype=jnp.int32) ^ own_row]
    kernel_total = assemble(order, [held_a, came_a], [held_b, came_b]).transpose(2, 0, 1)
    small = sum(
        jnp.sum(value[:, part_rows:].astype(F32), axis=0)
        for value in (held_a, came_a, held_b, came_b)
    )
    small = small.reshape(-1)[:small_size]
    sizes = [v.size for v in all_small + rows_small]
    ends = [sum(sizes[: i + 1]) for i in range(len(sizes))]
    cuts = [small[end - size : end] for size, end in zip(sizes, ends)]
    gain0_grad, bias0_grad, gain1_grad, bias1_grad, out_bias_grad = cuts[:5]
    gain2_grad, bias2_grad, down_bias_grad, conv_bias_grad, qv_grad, up_bias_grad = cuts[5:]
    return (
        block_out,
        frames_grad,
        kernel_total,
        conv_bias_grad,
        gain0_grad,
        bias0_grad,
        qkv_total,
        qv_grad.reshape(2, head_cols),
        out_total,
        out_bias_grad,
        gain1_grad,
        bias1_grad,
        up_total,
        up_bias_grad,
        down_total,
        down_bias_grad,
        gain2_grad,
        bias2_grad,
    )


def solution(mesh):
    return jax.shard_map(
        on_device,
        mesh=mesh,
        in_specs=(
            P(("rows", "tp"), None),
            P("rows", None),
            P(None, None, "tp"),
            P("tp"),
            P(),
            P(),
            P(None, None, "tp"),
            P(None, "tp"),
            P("tp", None),
            P(),
            P(),
            P(),
            P(None, "tp"),
            P("tp"),
            P("tp", None),
            P(),
            P(),
            P(),
            P(("rows", "tp"), None),
        ),
        out_specs=(
            P(("rows", "tp"), None),
            P(("rows", "tp"), None),
            P(None, None, "tp"),
            P("tp"),
            P(),
            P(),
            P(None, None, "tp"),
            P(None, "tp"),
            P("tp", None),
            P(),
            P(),
            P(),
            P(None, "tp"),
            P("tp"),
            P("tp", None),
            P(),
            P(),
            P(),
        ),
        check_vma=False,
    )
```

```python
import functools

import jax
import jax.numpy as jnp
import numpy as np
from jax import lax
from jax.experimental import pallas as pl
from jax.experimental.pallas import tpu as pltpu
from jax.sharding import PartitionSpec as P

D = 768
HD = 64
KER = 128
GROUPS = 16
LEN = 1024

EPSILON = 1e-05
ROOT_HALF = 0.7071067811865476
INV_ROOT_TAU = 0.3989422804014327
MASK_ROOT = 16384.0

GW = D // GROUPS
HALF = GW // 2
PH = 5
QN, PN = 17, 16
CORE = QN * PN
NJ = 27
LEAD = 13
EXT = (QN + NJ - 1) * PN
LANES = 256
GAP = KER // 2
SLOTS = PH * CORE
WIDE_MIB = 58

ORDER = (0, 2, 1, 3)

BF = jnp.bfloat16
F32 = jnp.float32


def iota(shape, dim):
    return lax.broadcasted_iota(jnp.int32, shape, dim)


def full(shape):
    return pl.BlockSpec(shape, lambda *index: (0,) * len(shape))


def block(shape, index_map):
    return pl.BlockSpec(shape, index_map)


def params(mib):
    return pltpu.CompilerParams(vmem_limit_bytes=mib * 2**20)


def cost(microseconds):
    return pl.CostEstimate(
        flops=int(microseconds * 1.1e+09), bytes_accessed=int(microseconds * 1e+06), transcendentals=0
    )


def dot(left, right):
    return jnp.dot(left, right, preferred_element_type=F32)


def dot_turned(left, right):
    return lax.dot_general(left, right, (((1,), (1,)), ((), ())), preferred_element_type=F32)


def phi_pair(v):
    cdf = 0.5 * (1.0 + lax.erf(v * ROOT_HALF))
    return v * cdf, cdf + v * INV_ROOT_TAU * jnp.exp(-0.5 * v * v)


def norm_stats(inputs):
    centered = inputs - jnp.mean(inputs, axis=-1, keepdims=True)
    inv_std = lax.rsqrt(jnp.mean(centered * centered, axis=-1, keepdims=True) + EPSILON)
    return centered * inv_std, inv_std


def segment_row(starts_ref):
    frame = iota((1, LEN), 1)
    total = jnp.full((1, LEN), -1, jnp.int32)
    for j in range(starts_ref.shape[1]):
        total = total + (frame >= starts_ref[0, j]).astype(jnp.int32)
    return total


def fill_put(starts_ref, put_ref):
    place = iota((1, LEN), 1) + GAP * segment_row(starts_ref)
    at = (place * 52429) >> 18
    high = (at * 61681) >> 20
    slot = (place - PH * at) * CORE + (at - QN * high) * PN + high
    for i in range(PH):
        rows = iota((CORE, LEN), 0) + i * CORE
        put_ref[i * CORE : (i + 1) * CORE, :] = (rows == slot).astype(F32).astype(BF)


def extension():
    row, col = np.arange(EXT)[:, None], np.arange(CORE)[None, :]
    want = QN * (row % PN) + row // PN - LEAD
    have = QN * (col % PN) + col // PN
    return jnp.asarray((want == have).astype(np.float32), BF)


def toeplitz_scratch():
    return [
        pltpu.VMEM((PH * GW + KER * GW + 288, LANES), BF),
        pltpu.VMEM((NJ * LANES, LANES), BF),
    ]


def fill_toeplitz(w_ref, step, g, wide_ref, wt_ref):
    before = PH * GW
    row, lane = iota((w_ref.shape[1], LANES), 0), iota((w_ref.shape[1], LANES), 1)
    spread = ((row == GW * g + lane % GW) & (lane < PH * GW)).astype(F32).astype(BF)

    @pl.when(step == 0)
    def _():
        rest = before + KER * GW
        wide_ref[0:before, :] = jnp.zeros((before, LANES), BF)
        wide_ref[rest:, :] = jnp.zeros((wide_ref.shape[0] - rest, LANES), BF)
        for j in range(NJ):
            gap = slice(j * LANES + PH * GW, (j + 1) * LANES)
            wt_ref[gap, :] = jnp.zeros((LANES - PH * GW, LANES), BF)

    wide_ref[before : before + KER * GW, :] = dot(w_ref[...], spread).astype(BF)
    lane = iota((1, LANES), 1)
    masks = [(lane // GW == i).astype(F32).astype(BF) for i in range(PH)]

    for j in range(NJ):
        for left in range(0, LANES, 128):
            lanes = slice(left, left + 128)
            total = None
            for i in range(left // GW, min((left + 127) // GW + 1, PH)):
                start = before + PH * GW * j - GW * (1 + i)
                part = wide_ref[start : start + PH * GW, lanes] * masks[i][:, lanes]
                total = part if total is None else total + part
            wt_ref[j * LANES : j * LANES + PH * GW, lanes] = total


def fold_in(slots_ref, g):
    width = slots_ref.shape[1]
    row, lane = iota((width, LANES), 0), iota((width, LANES), 1)
    core = jnp.zeros((CORE, LANES), F32)
    for i in range(PH):
        pick = ((lane // GW == i) & (row == GW * g + lane % GW)).astype(F32).astype(BF)
        core = core + dot(slots_ref[i * CORE : (i + 1) * CORE, :], pick)
    return core


def fold_out(values, back_ref, g):
    width = back_ref.shape[1]
    row, col = iota((LANES, width), 0), iota((LANES, width), 1)
    for i in range(PH):
        pick = ((row // GW == i) & (col == GW * g + row % GW)).astype(F32).astype(BF)
        here = slice(i * CORE, (i + 1) * CORE)
        back_ref[here, :] = back_ref[here, :] + dot(values, pick).astype(BF)


def unspread(back_ref, put_ref):
    turned = back_ref[...].astype(F32).T.astype(BF)
    return dot(turned, put_ref[...]).T.astype(BF)


def conv_kernel(me_ref, starts_ref, f0_ref, f1_ref, f2_ref, f3_ref, ext_ref, w_ref, bias_ref,
                mixed_ref, slope_ref, core_ref, sig_ref, slots_ref, wide_ref, back_ref, put_ref,
                taps_ref, wt_ref):
    g = pl.program_id(0)
    rows, features = f0_ref.shape
    width = sig_ref.shape[1]

    @pl.when(g == 0)
    def _():
        fill_put(starts_ref, put_ref)
        row, lane = iota((features, width), 0), iota((features, width), 1)
        pick = (row == lane + width * me_ref[0]).astype(F32).astype(BF)
        for n, ref in enumerate((f0_ref, f1_ref, f2_ref, f3_ref)):
            start = pl.multiple_of((me_ref[0] ^ ORDER[n]) * rows, rows)
            sig_ref[pl.ds(start, rows), :] = dot(ref[...], pick).astype(BF)
        slots_ref[...] = dot(put_ref[...], sig_ref[...]).astype(BF)
        back_ref[...] = jnp.zeros_like(back_ref)

    fill_toeplitz(w_ref, g, g, taps_ref, wt_ref)
    core = fold_in(slots_ref, g).astype(BF)
    core_ref[0] = core
    wide_ref[...] = dot(ext_ref[...], core).astype(BF)
    total = jnp.zeros((CORE, LANES), F32)
    for j in range(NJ):
        total = total + dot(
            wide_ref[PN * j : PN * j + CORE, :], wt_ref[j * LANES : (j + 1) * LANES, :]
        )
    value, slope = phi_pair(total + bias_ref[0])
    slope_ref[0] = slope
    fold_out(value.astype(BF), back_ref, g)

    @pl.when(g == pl.num_programs(0) - 1)
    def _():
        mixed_ref[...] = unspread(back_ref, put_ref)


def conv(me, starts, frames, ext, taps, bias_lanes):
    width = taps.shape[1]
    groups = width // GW
    return pl.pallas_call(
        conv_kernel,
        grid=(groups,),
        in_specs=[pl.BlockSpec(memory_space=pltpu.SMEM)] * 2
        + [full(frames[0].shape)] * 4
        + [
            full((EXT, CORE)),
            full(taps.shape),
            block((1, 1, LANES), lambda g: (g, 0, 0)),
        ],
        out_specs=[
            full((LEN, width)),
            block((1, CORE, LANES), lambda g: (g, 0, 0)),
            block((1, CORE, LANES), lambda g: (g, 0, 0)),
        ],
        out_shape=[
            jax.ShapeDtypeStruct((LEN, width), BF),
            jax.ShapeDtypeStruct((groups, CORE, LANES), F32),
            jax.ShapeDtypeStruct((groups, CORE, LANES), BF),
        ],
        scratch_shapes=[
            pltpu.VMEM((LEN, width), BF),
            pltpu.VMEM((SLOTS, width), BF),
            pltpu.VMEM((EXT, LANES), BF),
            pltpu.VMEM((SLOTS, width), BF),
            pltpu.VMEM((SLOTS, LEN), BF),
        ]
        + toeplitz_scratch(),
        compiler_params=params(WIDE_MIB),
        cost_estimate=cost(0.1),
    )(me, starts, *frames, ext, taps, bias_lanes)


def conv_grad_kernel(me_ref, starts_ref, keep_ref, far_ref, near_ref, slope_ref, ext_ref,
                     wide_ref, half_ref, bias_ref, grad_ref, slots_ref, put_ref):
    g = pl.program_id(0)
    rows = far_ref.shape[0] // 2

    @pl.when(g == 0)
    def _():
        fill_put(starts_ref, put_ref)
        for n, piece in enumerate(came_pieces(keep_ref, far_ref, near_ref)):
            start = pl.multiple_of((me_ref[0] ^ ORDER[n]) * rows, rows)
            grad_ref[pl.ds(start, rows), :] = piece
        slots_ref[...] = dot(put_ref[...], grad_ref[...]).astype(BF)

    grad = fold_in(slots_ref, g) * slope_ref[0]
    bias_ref[0] = jnp.sum(grad, axis=0, keepdims=True)
    low = grad.astype(BF)
    wide_ref[0] = dot(ext_ref[...], low).astype(BF)
    row, lane = iota((LANES, 128), 0), iota((LANES, 128), 1)
    for h in range(2):
        pick = (lane < PH * HALF) & (row == lane // HALF * GW + lane % HALF + h * HALF)
        half_ref[h] = dot(low, pick.astype(F32).astype(BF)).astype(BF)


def conv_grad(me, starts, came, slope, ext):
    groups = slope.shape[0]
    width = came[0].shape[1]
    return pl.pallas_call(
        conv_grad_kernel,
        grid=(groups,),
        in_specs=[
            pl.BlockSpec(memory_space=pltpu.SMEM),
            pl.BlockSpec(memory_space=pltpu.SMEM),
            full((LEN // 2, width)),
            full((LEN // 2, width)),
            full((LEN // 2, width)),
            block((1, CORE, LANES), lambda g: (g, 0, 0)),
            full((EXT, CORE)),
        ],
        out_specs=[
            block((1, EXT, LANES), lambda g: (g, 0, 0)),
            block((2, CORE, 128), lambda g: (g, 0, 0)),
            block((1, 1, LANES), lambda g: (g, 0, 0)),
        ],
        out_shape=[
            jax.ShapeDtypeStruct((groups, EXT, LANES), BF),
            jax.ShapeDtypeStruct((2 * groups, CORE, 128), BF),
            jax.ShapeDtypeStruct((groups, 1, LANES), F32),
        ],
        scratch_shapes=[
            pltpu.VMEM((LEN, width), BF),
            pltpu.VMEM((SLOTS, width), BF),
            pltpu.VMEM((SLOTS, LEN), BF),
        ],
        compiler_params=params(WIDE_MIB),
        cost_estimate=cost(0.1),
    )(me, starts, *came, slope, ext)


def signal_grad_kernel(first, wide_ref, w_ref, *refs):
    back_ref, taps_ref, wt_ref = refs[-3:]
    step = pl.program_id(0)
    g = first + step
    fill_toeplitz(w_ref, step, g, taps_ref, wt_ref)

    @pl.when(step == 0)
    def _():
        if first == 0:
            back_ref[...] = jnp.zeros_like(back_ref)
        else:
            back_ref[...] = refs[0][...]

    total = jnp.zeros((CORE, LANES), F32)
    for j in range(NJ):
        m = NJ - 1 - j
        total = total + dot_turned(
            wide_ref[0, PN * j : PN * j + CORE, :], wt_ref[m * LANES : (m + 1) * LANES, :]
        )
    fold_out(total.astype(BF), back_ref, g)
    if first == 0:

        @pl.when(step == pl.num_programs(0) - 1)
        def _():
            refs[0][...] = back_ref[...]

        return
    _, starts_ref, me_ref, keep_ref, near_ref, all_ref, put_ref = refs[:7]
    rows = keep_ref.shape[0] // 2

    @pl.when(step == pl.num_programs(0) - 1)
    def _():
        fill_put(starts_ref, put_ref)
        all_ref[...] = unspread(back_ref, put_ref)
        for n in range(4):
            start = pl.multiple_of((me_ref[0] ^ ORDER[n]) * rows, rows)
            out_ref = keep_ref if n < 2 else near_ref
            out_ref[n % 2 * rows : (n % 2 + 1) * rows, :] = all_ref[pl.ds(start, rows), :]


def signal_grad(wide, taps, first, count, *rest):
    width = taps.shape[1]
    slots = jax.ShapeDtypeStruct((SLOTS, width), BF)
    piece = jax.ShapeDtypeStruct((LEN // 2, width), BF)
    own = [
        block((1, EXT, LANES), lambda g: (first + g, 0, 0)),
        full(taps.shape),
    ]
    more = [full(slots.shape)] + [pl.BlockSpec(memory_space=pltpu.SMEM)] * 2
    scratch = [pltpu.VMEM(slots.shape, BF)] + toeplitz_scratch()
    return pl.pallas_call(
        functools.partial(signal_grad_kernel, first),
        grid=(count,),
        in_specs=own + (more if rest else []),
        out_specs=[full(piece.shape)] * 2 if rest else full(slots.shape),
        out_shape=[piece] * 2 if rest else slots,
        scratch_shapes=([pltpu.VMEM((LEN, width), BF), pltpu.VMEM((SLOTS, LEN), BF)] if rest else [])
        + scratch,
        compiler_params=params(WIDE_MIB),
        cost_estimate=cost(0.1),
    )(wide, taps, *rest)


def turn_core_kernel(sig_ref, ext_ref, out_ref, wide_ref):
    packs = sig_ref.shape[0]
    blocks = EXT // PN
    wide_ref[blocks:] = jnp.zeros((1, packs * PN, LANES), BF)
    for r in range(packs):
        rows = dot(ext_ref[...], sig_ref[r]).astype(BF)
        wide_ref[0:blocks, r * PN : (r + 1) * PN, :] = rows.reshape(blocks, PN, LANES)
    for q in range(blocks + 1):
        out_ref[:, q * 128 : (q + 1) * 128] = wide_ref[q].astype(F32).T.astype(BF)


def turn_core(sig, ext):
    packs = sig.shape[0]
    blocks = EXT // PN + 1
    return pl.pallas_call(
        turn_core_kernel,
        out_shape=jax.ShapeDtypeStruct((LANES, blocks * packs * PN), BF),
        scratch_shapes=[pltpu.VMEM((blocks, packs * PN, LANES), BF)],
        compiler_params=params(WIDE_MIB),
        cost_estimate=cost(0.1),
    )(sig, ext)


def tap_grad_kernel(sig_ref, grad_ref, out_ref, pair_ref, parts_ref, rows_ref):
    packs = grad_ref.shape[0]
    across = packs * PN
    pair_ref[QN, :, 0:128] = jnp.zeros((across, 128), BF)
    pair_ref[0, :, 128:] = jnp.zeros((across, 128), BF)
    for r in range(packs):
        rows = grad_ref[r].reshape(QN, PN, 128)
        pair_ref[0:QN, r * PN : (r + 1) * PN, 0:128] = rows
        pair_ref[1:, r * PN : (r + 1) * PN, 128:] = rows
    pair = pair_ref[...].reshape((QN + 1) * across, LANES)
    for j in range(0, NJ + 1, 2):
        part = dot(sig_ref[:, j * across : (j + QN + 1) * across], pair)
        parts_ref[PH * GW * j : PH * GW * (j + 1), :] = part[: PH * GW, 0:128]
        parts_ref[PH * GW * (j + 1) : PH * GW * (j + 2), :] = part[: PH * GW, 128:]
    phase = iota((1, 128), 1) // HALF
    chunk = 8 * GW

    for start in range(0, KER * GW, chunk):
        total = jnp.zeros((chunk, 128), F32)
        for i in range(PH):
            rows = slice(start + GW * (1 + i), start + GW * (1 + i) + chunk)
            total = jnp.where(phase == i, parts_ref[rows, :], total)
        rows_ref[start : start + chunk, :] = total
    for c in range(GW):
        taps = rows_ref[pl.ds(c, KER, stride=GW), :].T
        total = taps[0:HALF, :]
        for i in range(1, PH):
            total = total + taps[HALF * i : HALF * (i + 1), :]
        out_ref[c * HALF : (c + 1) * HALF, :] = total


def tap_grad(sig, grad):
    packs = grad.shape[0]
    return pl.pallas_call(
        tap_grad_kernel,
        out_shape=jax.ShapeDtypeStruct((GW * HALF, KER), F32),
        scratch_shapes=[
            pltpu.VMEM((QN + 1, packs * PN, LANES), BF),
            pltpu.VMEM(((NJ + 1) * PH * GW, 128), F32),
            pltpu.VMEM((KER * GW, 128), F32),
        ],
        compiler_params=params(WIDE_MIB),
        cost_estimate=cost(0.1),
    )(sig, grad)


def assemble_kernel(at_ref, a0_ref, a1_ref, b0_ref, b1_ref, out_ref, wide_ref):
    step = pl.program_id(0)
    half = a0_ref.shape[0]
    packs = 2 * half
    per_step = out_ref.shape[0]
    half_steps = pl.num_programs(0) // 2

    def place(held_ref, came_ref, which):
        for r in range(packs):
            at = at_ref[which, r]

            @pl.when(at < half)
            def _():
                wide_ref[...] = held_ref[at].astype(F32)

            @pl.when(at >= half)
            def _():
                wide_ref[...] = came_ref[at - half].astype(F32)

            for c in range(per_step):
                out_ref[c, r * HALF : (r + 1) * HALF, :] = wide_ref[c * HALF : (c + 1) * HALF, :]

    @pl.when(step < half_steps)
    def _():
        place(a0_ref, a1_ref, 0)

    @pl.when(step >= half_steps)
    def _():
        place(b0_ref, b1_ref, 1)


def assemble(order, parts_a, parts_b):
    packs = 2 * parts_a[0].shape[0]
    steps = 4
    per_step = GW // steps
    rows = per_step * HALF
    half = steps // 2
    return pl.pallas_call(
        assemble_kernel,
        grid=(steps,),
        in_specs=[
            pl.BlockSpec(memory_space=pltpu.SMEM),
        ]
        + [block((packs // 2, rows, KER), lambda s: (0, jnp.minimum(s, half - 1), 0))] * 2
        + [block((packs // 2, rows, KER), lambda s: (0, jnp.maximum(s - half, 0), 0))] * 2,
        out_specs=block((per_step, packs * HALF, KER), lambda s: (s, 0, 0)),
        out_shape=jax.ShapeDtypeStruct((GW, packs * HALF, KER), F32),
        scratch_shapes=[pltpu.VMEM((rows, KER), F32)],
        compiler_params=params(WIDE_MIB),
        cost_estimate=cost(4),
    )(order, *parts_a, *parts_b)


def spread_parts_kernel(order_ref, held_d, came_d, held_u, came_u, down_ref, up_ref):
    part = pl.program_id(0)
    half = pl.num_programs(0) // 2
    for i, (held, came, out) in enumerate(((held_d, came_d, down_ref), (held_u, came_u, up_ref))):

        @pl.when(order_ref[i, part] < half)
        def _():
            out[...] = held[0, 0].astype(F32)

        @pl.when(order_ref[i, part] >= half)
        def _():
            out[...] = came[0, 0].astype(F32)


def spread_parts(order, held, came):
    half, _, rows, width = held.shape
    first = lambda i: block(
        (1, 1, rows, width), lambda p, at: (jnp.minimum(at[i, p], half - 1), i, 0, 0)
    )
    second = lambda i: block(
        (1, 1, rows, width), lambda p, at: (jnp.maximum(at[i, p] - half, 0), i, 0, 0)
    )
    out = jax.ShapeDtypeStruct((2 * half * rows, width), F32)
    return pl.pallas_call(
        spread_parts_kernel,
        grid_spec=pltpu.PrefetchScalarGridSpec(
            num_scalar_prefetch=1,
            grid=(2 * half,),
            in_specs=[first(0), second(0), first(1), second(1)],
            out_specs=[block((rows, width), lambda p, at: (p, 0))] * 2,
        ),
        out_shape=[out, out],
        compiler_params=params(WIDE_MIB),
        cost_estimate=cost(5),
    )(order, held, came, held, came)


def spread_tail_kernel(first, order_ref, held_ref, came_ref, first_ref, last_ref):
    part = pl.program_id(0)
    half = pl.num_programs(0) // 2
    value = jnp.where(order_ref[part] < half, held_ref[0].astype(F32), came_ref[0].astype(F32))

    @pl.when(part < first)
    def _():
        first_ref[...] = value

    @pl.when(part >= first)
    def _():
        last_ref[...] = value


def spread_tail(order, held, came, split):
    half, rows, width = held.shape
    first = split // rows
    return pl.pallas_call(
        functools.partial(spread_tail_kernel, first),
        grid_spec=pltpu.PrefetchScalarGridSpec(
            num_scalar_prefetch=1,
            grid=(2 * half,),
            in_specs=[
                block((1, rows, width), lambda p, at: (jnp.minimum(at[p], half - 1), 0, 0)),
                block((1, rows, width), lambda p, at: (jnp.maximum(at[p] - half, 0), 0, 0)),
            ],
            out_specs=[
                block((rows, width), lambda p, at: (jnp.minimum(p, first - 1), 0)),
                block((rows, width), lambda p, at: (jnp.maximum(p - first, 0), 0)),
            ],
        ),
        out_shape=[
            jax.ShapeDtypeStruct((split, width), F32),
            jax.ShapeDtypeStruct((2 * half * rows - split, width), F32),
        ],
        compiler_params=params(WIDE_MIB),
        cost_estimate=cost(3),
    )(order, held, came)


def head_rows(turned, head, heads):
    pieces = [jnp.zeros((HD, turned.shape[1]), turned.dtype) for _ in range(heads)]
    pieces[head] = turned[HD * head : HD * (head + 1), :]
    return jnp.concatenate(pieces + [turned[HD * heads :, :]], axis=0)


def attention_kernel(q_block, heads, *refs):
    me_ref, starts_ref = refs[:2]
    mixed = refs[2:6]
    frames = refs[6:10]
    (vec_ref, wq_ref, wk_ref, wv_ref, qv_ref) = refs[10:15]
    (att_ref, own_ref, hat_ref, inv_ref, all_out, low_out, q_out, qt_out, k_out, v_out, ot_ref,
     lse_ref) = refs[15:27]
    all_ref, low_ref, q_ref, qt_ref, k_ref, v_ref, vt_ref, sems, seg_ref = refs[27:]
    rows = frames[0].shape[0]
    part = mixed[0].shape[1]
    width = frames[0].shape[1]
    scale = HD ** (-0.5)
    me = me_ref[0]
    row, lane = iota((part, width), 0), iota((part, width), 1)
    spots = [(lane == row + part * (me ^ m)).astype(F32).astype(BF) for m in ORDER]
    seg_ref[0:1, :] = segment_row(starts_ref)
    behind = iota((LANES, rows), 0) - heads * HD
    of_seg = (behind >= 0) & (behind < starts_ref.shape[1])
    for n in range(4):
        here = slice(n * rows, (n + 1) * rows)
        start = pl.multiple_of((me ^ ORDER[n]) * rows, rows)
        total = frames[n][...].astype(F32)
        for ref, spot in zip(mixed, spots):
            total = total + dot(ref[pl.ds(start, rows), :], spot)
        hat, inv = norm_stats(total)
        normed = hat * vec_ref[0:1, :] + vec_ref[1:2, :]
        if n == 0:
            own_ref[...] = normed
            hat_ref[...] = hat
            inv_ref[...] = jnp.broadcast_to(inv, inv_ref.shape)
        all_ref[here, :] = normed
        normed = normed.astype(BF)
        low_ref[here, :] = normed
        query = (dot_turned(normed, wq_ref[...]) + qv_ref[0:1, :]) * scale
        in_seg = behind == seg_ref[0:1, pl.ds(start, rows)]
        q_ref[here, :] = query.astype(BF)
        qt_ref[:, here] = (query.T + jnp.where(in_seg, MASK_ROOT, 0.0)).astype(BF)
        key = dot_turned(normed, wk_ref[...])
        k_ref[here, :] = (key + jnp.where(of_seg & ~in_seg, -MASK_ROOT, 0.0).T).astype(BF)
        value = dot_turned(normed, wv_ref[...]) + qv_ref[1:2, :]
        v_ref[here, :] = value.astype(BF)
        vt_ref[:, here] = value.T.astype(BF)
    held = [all_ref, low_ref, q_ref, qt_ref, k_ref, v_ref]
    kept = [all_out, low_out, q_out, qt_out, k_out, v_out]
    copies = [
        pltpu.make_async_copy(src, dst, sems.at[i]) for i, (src, dst) in enumerate(zip(held, kept))
    ]
    for copy in copies:
        copy.start()
    total = 4 * rows
    for head in range(heads):
        for start in range(0, total, q_block):
            cols = slice(start, start + q_block)
            turned = head_rows(qt_ref[:, cols], head, heads)
            scores = dot(k_ref[...], turned)
            top = jnp.max(scores, axis=0, keepdims=True)
            weights = jnp.exp(scores - top)
            sums = jnp.sum(weights, axis=0, keepdims=True)
            value = dot(vt_ref[HD * head : HD * (head + 1), :], weights.astype(BF))
            ot_ref[HD * head : HD * (head + 1), cols] = value / sums
            lse_ref[head : head + 1, cols] = top + jnp.log(sums)
    lse_ref[heads:, :] = jnp.zeros((8 - heads, total), F32)
    for n in range(4):
        here = slice(n * rows, (n + 1) * rows)
        att_ref[here, :] = ot_ref[:, here].T.astype(BF)
    for copy in copies:
        copy.wait()


def attention(me, starts, mixed, frames, vectors, weights, qv, heads, q_block=512):
    rows, width = frames[0].shape
    total = 4 * rows
    cols = heads * HD
    vmem = pl.BlockSpec(memory_space=pltpu.VMEM)
    away = pl.BlockSpec(memory_space=pltpu.HBM)
    held = [
        ((total, width), F32),
        ((total, width), BF),
        ((total, LANES), BF),
        ((LANES, total), BF),
        ((total, LANES), BF),
        ((total, LANES), BF),
    ]
    return pl.pallas_call(
        functools.partial(attention_kernel, q_block, heads),
        in_specs=[pl.BlockSpec(memory_space=pltpu.SMEM)] * 2 + [vmem] * 13,
        out_specs=[vmem] * 4 + [away] * 6 + [vmem] * 2,
        out_shape=[
            jax.ShapeDtypeStruct((total, cols), BF),
            jax.ShapeDtypeStruct((rows, width), F32),
            jax.ShapeDtypeStruct((rows, width), F32),
            jax.ShapeDtypeStruct((rows, 128), F32),
        ]
        + [jax.ShapeDtypeStruct(shape, kind) for shape, kind in held]
        + [jax.ShapeDtypeStruct((cols, total), F32), jax.ShapeDtypeStruct((8, total), F32)],
        scratch_shapes=[pltpu.VMEM(shape, kind) for shape, kind in held]
        + [
            pltpu.VMEM((LANES, total), BF),
            pltpu.SemaphoreType.DMA((len(held),)),
            pltpu.VMEM((8, total), jnp.int32),
        ],
        compiler_params=params(WIDE_MIB),
        cost_estimate=cost(4),
    )(me, starts, *mixed, *frames, vectors, *weights, qv)


def attention_grad_kernel(q_block, heads, *refs):
    pieces = came_pieces(*refs[:3])
    (q_ref, qt_ref, k_ref, v_ref, ot_ref, lse_ref, wq_ref, wk_ref, wv_ref,
     keep_ref, near_ref, gq_ref, gk_ref, gv_ref, sum_ref,
     go_ref, got_ref, kt_ref, delta_ref, dqt_ref, dk_ref, dv_ref) = refs[3:]
    rows = pieces[0].shape[0]
    total = 4 * rows
    cols_all = heads * HD
    scale = HD ** (-0.5)
    go_ref[...] = jnp.zeros_like(go_ref)
    for n in range(4):
        go_ref[n * rows : (n + 1) * rows, :cols_all] = pieces[n]
    got_ref[...] = go_ref[...].astype(F32).T.astype(BF)
    kt_ref[...] = k_ref[...].astype(F32).T.astype(BF)
    for head in range(heads):
        own = slice(HD * head, HD * (head + 1))
        delta_ref[head : head + 1, :] = jnp.sum(
            got_ref[own, :].astype(F32) * ot_ref[own, :], axis=0, keepdims=True
        )
    lane = iota((1, LANES), 1)
    for head in range(heads):
        own = slice(HD * head, HD * (head + 1))
        mask = (lane // HD == head).astype(F32).astype(BF)
        for start in range(0, total, q_block):
            cols = slice(start, start + q_block)
            scores = dot(k_ref[...], head_rows(qt_ref[:, cols], head, heads))
            probs = jnp.exp(scores - lse_ref[head : head + 1, cols])
            prob_grad = dot(v_ref[...], head_rows(got_ref[:, cols], head, heads))
            score_grad = (probs * (prob_grad - delta_ref[head : head + 1, cols])).astype(BF)
            value_part = dot(probs.astype(BF), go_ref[cols, :] * mask)
            key_part = dot(score_grad, q_ref[cols, :] * mask)
            if head == 0 and start == 0:
                dv_ref[...] = value_part
                dk_ref[...] = key_part
            else:
                dv_ref[...] += value_part
                dk_ref[...] += key_part
            dqt_ref[own, cols] = dot(kt_ref[own, :], score_grad)
    dqt_ref[cols_all:, :] = jnp.zeros((LANES - cols_all, total), F32)
    sums_q = jnp.zeros((1, LANES), F32)
    sums_v = jnp.zeros((1, LANES), F32)
    for n in range(4):
        here = slice(n * rows, (n + 1) * rows)
        query_grad = dqt_ref[:, here].T * scale
        value_grad = dv_ref[here, :]
        sums_q = sums_q + jnp.sum(query_grad, axis=0, keepdims=True)
        sums_v = sums_v + jnp.sum(value_grad, axis=0, keepdims=True)
        low_q = query_grad.astype(BF)
        low_k = dk_ref[here, :].astype(BF)
        low_v = value_grad.astype(BF)
        gq_ref[here, :] = low_q[:, :cols_all]
        gk_ref[here, :] = low_k[:, :cols_all]
        gv_ref[here, :] = low_v[:, :cols_all]
        back = dot(low_q, wq_ref[...]) + dot(low_k, wk_ref[...]) + dot(low_v, wv_ref[...])
        out_ref = keep_ref if n < 2 else near_ref
        out_ref[n % 2 * rows : (n % 2 + 1) * rows, :] = back.astype(BF)
    sum_ref[0:1, :] = sums_q
    sum_ref[1:2, :] = sums_v
    sum_ref[2:, :] = jnp.zeros((6, LANES), F32)


def attention_grad(came, saved, weights, heads, q_block=512):
    half, cols = came[0].shape
    total = 2 * half
    width = weights[0].shape[1]
    return pl.pallas_call(
        functools.partial(attention_grad_kernel, q_block, heads),
        out_shape=[
            jax.ShapeDtypeStruct((half, width), BF),
            jax.ShapeDtypeStruct((half, width), BF),
            jax.ShapeDtypeStruct((total, cols), BF),
            jax.ShapeDtypeStruct((total, cols), BF),
            jax.ShapeDtypeStruct((total, cols), BF),
            jax.ShapeDtypeStruct((8, LANES), F32),
        ],
        scratch_shapes=[
            pltpu.VMEM((total, LANES), BF),
            pltpu.VMEM((LANES, total), BF),
            pltpu.VMEM((LANES, total), BF),
            pltpu.VMEM((8, total), F32),
            pltpu.VMEM((LANES, total), F32),
            pltpu.VMEM((total, LANES), F32),
            pltpu.VMEM((total, LANES), F32),
        ],
        compiler_params=params(WIDE_MIB),
        cost_estimate=cost(0.1),
    )(*came, *saved, *weights)


def put_half(n, value, keep_ref, near_ref):
    @pl.when(n < 2)
    def _():
        keep_ref[...] = value

    @pl.when(n >= 2)
    def _():
        near_ref[...] = value


def feed_kernel(a0_ref, a1_ref, a2_ref, a3_ref, normed_ref, o0_ref, o1_ref, o2_ref, o3_ref, vec_ref,
                up_ref, down_ref,
                low_ref, act_ref, slope_ref, keep_ref, near_ref, own_ref, hat_ref, inv_ref):
    n = pl.program_id(0)
    total = normed_ref[...] + vec_ref[6:7, :]
    out_refs = (o0_ref, o1_ref, o2_ref, o3_ref)
    for ref, out_ref in zip((a0_ref, a1_ref, a2_ref, a3_ref), out_refs):
        total = total + dot(ref[...], out_ref[...])
    hat, inv = norm_stats(total)
    normed = hat * vec_ref[2:3, :] + vec_ref[3:4, :]

    @pl.when(n == 0)
    def _():
        own_ref[...] = normed
        hat_ref[...] = hat
        inv_ref[...] = jnp.broadcast_to(inv, inv_ref.shape)

    low = normed.astype(BF)
    low_ref[...] = low
    value, slope = phi_pair(dot(low, up_ref[...]) + vec_ref[8:9, :])
    slope_ref[...] = slope
    value = value.astype(BF)
    act_ref[...] = value
    put_half(n, dot(value, down_ref[...]).astype(BF), keep_ref, near_ref)


def feed(attended, normed, out_pieces, vectors, up_weight, down_weight):
    total, width = normed.shape
    rows = total // 4
    part = attended[0].shape[1]
    units = up_weight.shape[1]
    here = lambda n: (n, 0)
    return pl.pallas_call(
        feed_kernel,
        grid=(4,),
        in_specs=[block((rows, part), lambda n, i=i: (n ^ i, 0)) for i in range(4)]
        + [block((rows, width), here)]
        + [full((part, width))] * 4
        + [
            full((16, width)),
            full((width, units)),
            full((units, width)),
        ],
        out_specs=[
            block((rows, width), here),
            block((rows, units), here),
            block((rows, units), here),
            block((rows, width), lambda n: (jnp.minimum(n, 1), 0)),
            block((rows, width), lambda n: (jnp.maximum(n - 2, 0), 0)),
            full((rows, width)),
            full((rows, width)),
            full((rows, 128)),
        ],
        out_shape=[
            jax.ShapeDtypeStruct((total, width), BF),
            jax.ShapeDtypeStruct((total, units), BF),
            jax.ShapeDtypeStruct((total, units), F32),
            jax.ShapeDtypeStruct((total // 2, width), BF),
            jax.ShapeDtypeStruct((total // 2, width), BF),
            jax.ShapeDtypeStruct((rows, width), F32),
            jax.ShapeDtypeStruct((rows, width), F32),
            jax.ShapeDtypeStruct((rows, 128), F32),
        ],
        compiler_params=params(WIDE_MIB),
        cost_estimate=cost(10),
    )(*attended, normed, *out_pieces, vectors, up_weight, down_weight)


def feed_grad_kernel(g0_ref, g1_ref, g2_ref, g3_ref, slope_ref, up_ref, down_ref,
                     all_ref, low_ref, keep_ref, near_ref, bias_ref):
    n = pl.program_id(0)
    for i, ref in enumerate((g0_ref, g1_ref, g2_ref, g3_ref)):

        @pl.when(n == i)
        def _():
            all_ref[...] = ref[...]

    grad = dot_turned(all_ref[...], down_ref[...]) * slope_ref[...]

    @pl.when(n == 0)
    def _():
        bias_ref[...] = jnp.zeros_like(bias_ref)

    bias_ref[...] += jnp.sum(grad, axis=0, keepdims=True)
    low = grad.astype(BF)
    low_ref[...] = low
    put_half(n, dot_turned(low, up_ref[...]).astype(BF), keep_ref, near_ref)


def feed_grad(grads, slope, up_weight, down_weight):
    total, units = slope.shape
    rows, width = grads[0].shape
    here = lambda n: (n, 0)
    return pl.pallas_call(
        feed_grad_kernel,
        grid=(4,),
        in_specs=[full((rows, width))] * 4
        + [block((rows, units), here), full((width, units)), full((units, width))],
        out_specs=[
            block((rows, width), here),
            block((rows, units), here),
            block((rows, width), lambda n: (jnp.minimum(n, 1), 0)),
            block((rows, width), lambda n: (jnp.maximum(n - 2, 0), 0)),
            full((1, units)),
        ],
        out_shape=[
            jax.ShapeDtypeStruct((total, width), BF),
            jax.ShapeDtypeStruct((total, units), BF),
            jax.ShapeDtypeStruct((total // 2, width), BF),
            jax.ShapeDtypeStruct((total // 2, width), BF),
            jax.ShapeDtypeStruct((1, units), F32),
        ],
        compiler_params=params(WIDE_MIB),
        cost_estimate=cost(6),
    )(*grads, slope, up_weight, down_weight)


def came_pieces(keep_ref, far_ref, near_ref):
    rows = far_ref.shape[0] // 2
    return [keep_ref[:rows, :], far_ref[:rows, :], near_ref[:rows, :], far_ref[rows:, :]]


def put_sums(sum_ref, *values):
    sum_ref[...] = jnp.zeros_like(sum_ref)
    for i, value in enumerate(values):
        sum_ref[i : i + 1, :] = jnp.sum(value, axis=0, keepdims=True)


def norm_grad(grad, hat, inv, gain):
    scaled = grad * gain
    return inv * (
        scaled
        - jnp.mean(scaled, axis=-1, keepdims=True)
        - hat * jnp.mean(scaled * hat, axis=-1, keepdims=True)
    )


def last_norm_kernel(keep_ref, near_ref, far_ref, normed_ref, cot_ref, vec_ref, out_ref, grad_ref, low_ref, sum_ref):
    total = keep_ref[...].astype(F32) + near_ref[...].astype(F32) + far_ref[...].astype(F32)
    hat, inv = norm_stats(normed_ref[...] + total + vec_ref[7:8, :])
    gain = vec_ref[4:5, :]
    out_ref[...] = (hat * gain + vec_ref[5:6, :]).astype(BF)
    cot = cot_ref[...].astype(F32)
    grad = norm_grad(cot, hat, inv, gain)
    grad_ref[...] = grad
    low_ref[...] = grad.astype(BF)
    put_sums(sum_ref, cot * hat, cot, grad)


def last_norm(terms, normed, cotangent, vectors):
    rows, width = normed.shape
    return pl.pallas_call(
        last_norm_kernel,
        grid=(1,),
        in_specs=[full((rows, width))] * 5 + [full((16, width))],
        out_specs=[full((rows, width))] * 3 + [full((8, width))],
        out_shape=[
            jax.ShapeDtypeStruct((rows, width), BF),
            jax.ShapeDtypeStruct((rows, width), F32),
            jax.ShapeDtypeStruct((rows, width), BF),
            jax.ShapeDtypeStruct((8, width), F32),
        ],
        compiler_params=params(WIDE_MIB),
        cost_estimate=cost(3),
    )(*terms, normed, cotangent, vectors)


def middle_norm_kernel(keep_ref, near_ref, far_ref, grad_ref, hat_ref, inv_ref, vec_ref, o0_ref,
                       o1_ref, o2_ref, o3_ref, out_ref, low_ref, sum_ref, keep_out, near_out):
    rows = grad_ref.shape[0]
    total = keep_ref[...].astype(F32) + near_ref[...].astype(F32) + far_ref[...].astype(F32)
    total = total + grad_ref[...]
    hat = hat_ref[...]
    grad = norm_grad(total, hat, inv_ref[:, 0:1], vec_ref[2:3, :])
    out_ref[...] = grad
    low = grad.astype(BF)
    low_ref[...] = low
    put_sums(sum_ref, total * hat, total, grad)
    for n, ref in enumerate((o0_ref, o1_ref, o2_ref, o3_ref)):
        back = dot_turned(low, ref[...]).astype(BF)
        out = keep_out if n < 2 else near_out
        out[n % 2 * rows : (n % 2 + 1) * rows, :] = back


def middle_norm(terms, grad, hat, inv, vectors, out_pieces):
    rows, width = grad.shape
    part = out_pieces[0].shape[0]
    return pl.pallas_call(
        middle_norm_kernel,
        grid=(1,),
        in_specs=[full((rows, width))] * 5
        + [full((rows, 128)), full((16, width))]
        + [full((part, width))] * 4,
        out_specs=[full((rows, width))] * 2 + [full((8, width))] + [full((2 * rows, part))] * 2,
        out_shape=[
            jax.ShapeDtypeStruct((rows, width), F32),
            jax.ShapeDtypeStruct((rows, width), BF),
            jax.ShapeDtypeStruct((8, width), F32),
            jax.ShapeDtypeStruct((2 * rows, part), BF),
            jax.ShapeDtypeStruct((2 * rows, part), BF),
        ],
        compiler_params=params(WIDE_MIB),
        cost_estimate=cost(0.1),
    )(*terms, grad, hat, inv, vectors, *out_pieces)


def first_norm_kernel(me_ref, keep_ref, near_ref, far_ref, grad_ref, hat_ref, inv_ref, vec_ref,
                      out_ref, sum_ref, keep_out, near_out):
    rows, width = grad_ref.shape
    part = keep_out.shape[1]
    total = keep_ref[...].astype(F32) + near_ref[...].astype(F32) + far_ref[...].astype(F32)
    total = total + grad_ref[...]
    hat = hat_ref[...]
    grad = norm_grad(total, hat, inv_ref[:, 0:1], vec_ref[0:1, :])
    out_ref[...] = grad
    low = grad.astype(BF)
    put_sums(sum_ref, total * hat, total)
    row, lane = iota((width, part), 0), iota((width, part), 1)
    for n in range(4):
        pick = (row == lane + part * (me_ref[0] ^ ORDER[n])).astype(F32).astype(BF)
        out = keep_out if n < 2 else near_out
        out[n % 2 * rows : (n % 2 + 1) * rows, :] = dot(low, pick).astype(BF)


def first_norm(me, terms, grad, hat, inv, vectors):
    rows, width = grad.shape
    part = width // 4
    return pl.pallas_call(
        first_norm_kernel,
        grid=(1,),
        in_specs=[pl.BlockSpec(memory_space=pltpu.SMEM)]
        + [full((rows, width))] * 5
        + [full((rows, 128)), full((16, width))],
        out_specs=[full((rows, width)), full((8, width))] + [full((2 * rows, part))] * 2,
        out_shape=[
            jax.ShapeDtypeStruct((rows, width), F32),
            jax.ShapeDtypeStruct((8, width), F32),
            jax.ShapeDtypeStruct((2 * rows, part), BF),
            jax.ShapeDtypeStruct((2 * rows, part), BF),
        ],
        compiler_params=params(WIDE_MIB),
        cost_estimate=cost(0.1),
    )(me, *terms, grad, hat, inv, vectors)


def frames_grad_kernel(me_ref, keep_ref, far_ref, near_ref, grad_ref, out_ref):
    width = grad_ref.shape[1]
    part = keep_ref.shape[1]
    row, lane = iota((part, width), 0), iota((part, width), 1)
    total = grad_ref[...]
    for n, piece in enumerate(came_pieces(keep_ref, far_ref, near_ref)):
        spot = (lane == row + part * (me_ref[0] ^ ORDER[n])).astype(F32).astype(BF)
        total = total + dot(piece, spot)
    out_ref[...] = total


def add_frames_grad(me, came, grad):
    half, part = came[0].shape
    rows, width = grad.shape
    return pl.pallas_call(
        frames_grad_kernel,
        grid=(1,),
        in_specs=[pl.BlockSpec(memory_space=pltpu.SMEM)]
        + [full((half, part))] * 3
        + [full((rows, width))],
        out_specs=full((rows, width)),
        out_shape=jax.ShapeDtypeStruct((rows, width), F32),
        compiler_params=params(WIDE_MIB),
        cost_estimate=cost(0.1),
    )(me, *came, grad)


def swap(value, bit):
    return lax.ppermute(value, "tp", [(i, i ^ bit) for i in range(lax.axis_size("tp"))])


def gather_pieces(value):
    across = swap(value, 2)
    return [value, across, swap(value, 1), swap(across, 1)]


def scatter_terms(keep, near):
    piece = keep.shape[0] // 2
    came = swap(near, 1)
    pair = (keep[piece:].astype(F32) + came[piece:].astype(F32)).astype(BF)
    return [keep, came, swap(pair, 2)], pair


def exchange(keep, near, *ahead):
    rows = keep.shape[0] // 2
    came = swap(near, 1)
    pair = after(jnp.concatenate([keep[rows:], came[rows:]], axis=0), *ahead)
    return [keep, swap(pair, 2), came], pair


def after(value, *others):
    return lax.optimization_barrier((value, *others))[0]


def all_after(values, *others):
    return list(lax.optimization_barrier((*values, *others))[: len(values)])


def team_groups(row_count, team):
    if row_count == team:
        return None
    return [list(range(first, first + team)) for first in range(0, row_count, team)]


def cross_groups(row_count, team):
    return [list(range(first, row_count, team)) for first in range(team)]


def pair_rows(value, mask):
    count = lax.axis_size("rows")
    return lax.ppermute(value, "rows", [(i, i ^ mask) for i in range(count)])


FEED_MASKS = ((1, 4, 2), (2, 1, 4))
TAIL_MASKS = (1, 2, 4)


def side_of(index, mask):
    return (index >> {1: 0, 2: 1, 4: 2}[mask]) & 1


def holders_of(masks):
    part = lambda index: sum(side_of(index, m) << (2 - i) for i, m in enumerate(masks))
    return sorted(range(8), key=part)


def halve(value, mask, side):
    half = value.shape[0] // 2
    kept = lax.dynamic_slice_in_dim(value, side * half, half, 0)
    sent = lax.dynamic_slice_in_dim(value, (1 - side) * half, half, 0)
    return kept, pair_rows(sent, mask)


def add_low(kept, came):
    return (kept.astype(F32) + came.astype(F32)).astype(BF)


def gather_join(held, came, offsets, mask):
    held = jnp.concatenate([held, came], axis=0)
    return held, offsets + [x ^ mask for x in offsets]


def on_device(
    frames,
    seg_starts,
    conv_weight,
    conv_bias,
    norm_gain0,
    norm_bias0,
    qkv_weight,
    qv_bias,
    out_weight,
    out_bias,
    norm_gain1,
    norm_bias1,
    up_weight,
    up_bias,
    down_weight,
    down_bias,
    norm_gain2,
    norm_bias2,
    cotangent,
):
    head_cols = qkv_weight.shape[2]
    heads_here = head_cols // HD
    groups_here = conv_weight.shape[2] // GW
    team = 2 * groups_here
    row_count = lax.axis_size("rows")
    teams = team_groups(row_count, team)
    me = lax.axis_index("tp")
    me_word = me.reshape(1).astype(jnp.int32)
    own_row = lax.axis_index("rows") % team
    vectors = [norm_gain0, norm_bias0, norm_gain1, norm_bias1, norm_gain2, norm_bias2]
    vectors = jnp.concatenate(vectors + [out_bias, down_bias, up_bias]).astype(F32)
    vectors = jnp.pad(vectors.reshape(-1, D), ((0, 7), (0, 0)))

    ext = extension()
    conv_flat = lax.optimization_barrier(conv_weight.reshape(KER * GW, -1))
    starts = seg_starts
    bias_lanes = jnp.tile(conv_bias.astype(F32).reshape(groups_here, 1, GW), (1, 1, PH))
    bias_lanes = jnp.pad(bias_lanes, ((0, 0), (0, 0), (0, LANES - PH * GW)))
    bias_lanes = after(bias_lanes, starts)
    across = swap(frames, 2)
    frames_pieces = [frames, across, swap(frames, 1), swap(after(across, conv_flat), 1)]
    out_pieces = gather_pieces(out_weight)
    mixed_low, slope0, core = conv(me_word, starts, frames_pieces, ext, conv_flat, bias_lanes)

    mixed_low = after(mixed_low, out_pieces[1], out_pieces[2])
    qkv_padded = jnp.pad(
        after(qkv_weight, mixed_low).transpose(1, 2, 0),
        ((0, 0), (0, LANES - head_cols), (0, 0)),
    )
    qkv_parts = [qkv_padded[0], qkv_padded[1], qkv_padded[2]]
    qv_padded = jnp.pad(
        after(qv_bias, mixed_low).astype(F32), ((0, 0), (0, LANES - head_cols))
    )
    vectors = after(vectors, mixed_low)
    mixed_pieces = gather_pieces(mixed_low)
    (attended, normed0, hat0, inv0, normed0_all, normed0_low, *saved) = attention(
        me_word,
        seg_starts,
        mixed_pieces,
        frames_pieces,
        vectors,
        qkv_parts,
        qv_padded,
        heads_here,
    )

    core_all = lax.all_to_all(
        jnp.repeat(core, 2, axis=0), "rows", 0, 0, axis_index_groups=teams, tiled=True
    )
    attended_pieces = all_after(gather_pieces(attended), core_all)
    normed1_low, activated, slope1, keep, near, normed1, hat1, inv1 = feed(
        attended_pieces, normed0_all, out_pieces, vectors, up_weight, down_weight
    )
    terms, pair = scatter_terms(keep, near)
    turned_core = turn_core(after(core_all, pair), ext)
    terms = all_after(terms, turned_core)
    block_out, grad2, grad2_low, sums2 = last_norm(terms, normed1, cotangent, vectors)

    grad2_all, up_low, keep, near, up_bias_grad = feed_grad(
        gather_pieces(grad2_low), slope1, up_weight, down_weight
    )
    terms, pair = scatter_terms(keep, near)
    activated, normed1_low = all_after([activated, normed1_low], pair)
    down_grad = jnp.einsum("rf,rd->fd", activated, grad2_all, preferred_element_type=F32)
    up_grad = jnp.einsum("rd,rf->df", normed1_low, up_low, preferred_element_type=F32)
    feed_grads = [down_grad.astype(BF), up_grad.astype(BF)]
    terms = all_after(terms, *feed_grads)
    feed_steps = [[(mask, side_of(own_row, mask)) for mask in masks] for masks in FEED_MASKS]
    halves_1 = [halve(grad, *order[0]) for grad, order in zip(feed_grads, feed_steps)]

    grad1, grad1_low, sums1, keep, near = middle_norm(
        terms, grad2, hat1, inv1, vectors, out_pieces
    )
    came, pair = exchange(keep, near, *[other for kept, other in halves_1])
    feed_sums = [add_low(after(kept, pair), other) for kept, other in halves_1]
    came = all_after(came, *feed_sums)
    halves_2 = [halve(grad, *order[1]) for grad, order in zip(feed_sums, feed_steps)]
    keep, near, query_grad, key_grad, value_grad, qv_sums = attention_grad(
        came, saved, qkv_parts, heads_here
    )
    grad1_pieces = gather_pieces(after(grad1_low, *came))
    feed_sums = [add_low(after(kept, keep), other) for kept, other in halves_2]
    near = after(near, *feed_sums, grad1_pieces[1], grad1_pieces[2])
    terms, pair = scatter_terms(keep, near)
    halves_3 = [halve(grad, *order[2]) for grad, order in zip(feed_sums, feed_steps)]
    out_grad = jnp.einsum(
        "rh,rd->hd",
        after(attended, pair),
        jnp.concatenate(grad1_pieces, axis=0),
        preferred_element_type=F32,
    )
    normed0_low = after(normed0_low, pair)
    turned_grads = [
        jnp.einsum("rc,rd->cd", part, normed0_low, preferred_element_type=F32).astype(BF)
        for part in (query_grad, key_grad, value_grad)
    ]
    tail = jnp.concatenate(turned_grads + [out_grad.astype(BF)], axis=0)
    terms = all_after(terms, tail)
    qv_grad = qv_sums[:2, :head_cols]
    tail_steps = [(mask, side_of(own_row, mask)) for mask in TAIL_MASKS]
    tail_half = halve(after(tail, terms[2]), *tail_steps[0])
    grad0, sums0, keep, near = first_norm(me_word, terms, grad1, hat0, inv0, vectors)

    near = after(near, *[other for kept, other in halves_3])
    came, pair = exchange(keep, near)
    feed_sums = jnp.stack([add_low(after(kept, pair), other) for kept, other in halves_3])
    tail_sum = add_low(after(tail_half[0], pair), tail_half[1])
    shared = after(jnp.concatenate([sums0[:2], sums1[:3], sums2[:3]], axis=0), pair)
    shared = shared + swap(shared, 1)
    shared = shared + swap(shared, 2)
    came = all_after(came, tail_sum, feed_sums, shared)
    tail_half = halve(tail_sum, *tail_steps[1])
    if teams is not None:
        feed_sums = lax.psum(feed_sums, "rows", axis_index_groups=cross_groups(row_count, team))
    feed_held, offsets_f = feed_sums[None], [0]
    feed_came = pair_rows(feed_held, 4)
    wide, halves, conv_bias_grad = conv_grad(me_word, seg_starts, came, slope0, ext)
    conv_bias_grad = conv_bias_grad[:, 0, : PH * GW].reshape(groups_here, PH, GW)
    conv_bias_grad = jnp.sum(conv_bias_grad, axis=1).reshape(-1)
    halves_all = lax.all_to_all(halves, "rows", 0, 0, axis_index_groups=teams, tiled=True)
    tail_sum = add_low(after(tail_half[0], halves), tail_half[1])
    tail_half = halve(tail_sum, *tail_steps[2])
    feed_held, offsets_f = gather_join(feed_held, after(feed_came, halves), offsets_f, 4)
    feed_came = pair_rows(feed_held, 2)
    signal_slots = signal_grad(after(wide, tail_sum, feed_held), conv_flat, 0, groups_here // 2)
    tail_part = add_low(after(tail_half[0], signal_slots), tail_half[1])
    halves_all = after(halves_all, signal_slots, tail_part)
    kernel_part = tap_grad(turned_core, halves_all)
    if teams is not None:
        others = cross_groups(row_count, team)
        tail_part = lax.psum(tail_part.astype(F32), "rows", axis_index_groups=others).astype(BF)
    tail_held, offsets_t = tail_part[None], [0]
    tail_came = pair_rows(tail_held, 4)
    feed_held, offsets_f = gather_join(feed_held, after(feed_came, kernel_part, tail_came), offsets_f, 2)
    feed_came = pair_rows(feed_held, 1)
    offsets_f = offsets_f + [x ^ 1 for x in offsets_f]

    all_small = [shared[i] for i in range(shared.shape[0])]
    rows_small = [conv_bias_grad, qv_grad, up_bias_grad]
    small = jnp.concatenate([shared.reshape(-1)] + [v.reshape(-1) for v in rows_small])
    small_size = small.size
    small = jnp.pad(small, (0, -small_size % (16 * KER))).reshape(-1, KER)
    if teams is not None:
        others = cross_groups(row_count, team)
        kernel_part = lax.psum(kernel_part, "rows", axis_index_groups=others)
        small = lax.psum(small, "rows", axis_index_groups=others)
    small_high = small.astype(BF)
    small_low = (small - small_high.astype(F32)).astype(BF)
    part_rows = kernel_part.shape[0] // 2
    part_low = kernel_part.astype(BF)
    held_a = jnp.concatenate([part_low[:part_rows], small_high], axis=0)[None]
    held_b = jnp.concatenate([part_low[part_rows:], small_low], axis=0)[None]
    came_a, came_b = pair_rows(held_a, 4), pair_rows(held_b, 4)
    tail_held, offsets_t = gather_join(
        tail_held, after(tail_came, held_a, held_b), offsets_t, 4
    )
    tail_came = pair_rows(tail_held, 2)
    keep, near = signal_grad(
        after(wide, kernel_part, tail_held, feed_held),
        conv_flat,
        groups_here // 2,
        groups_here - groups_here // 2,
        signal_slots,
        seg_starts,
        me_word,
    )
    came_a, came_b, keep, near = all_after([came_a, came_b, keep, near], feed_came, tail_came)
    held_a, offsets_a = gather_join(held_a, came_a, [0], 4)
    held_b, offsets_b = gather_join(held_b, came_b, [0], 4)
    came_a, came_b = pair_rows(held_a, 2), pair_rows(held_b, 1)
    tail_held, offsets_t = gather_join(tail_held, tail_came, offsets_t, 2)
    tail_came = pair_rows(tail_held, 1)
    offsets_t = offsets_t + [x ^ 1 for x in offsets_t]
    came, pair = exchange(keep, near)
    frames_grad = add_frames_grad(me_word, came, grad0)
    held_a, offsets_a = gather_join(held_a, came_a, offsets_a, 2)
    held_b, offsets_b = gather_join(held_b, came_b, offsets_b, 1)
    part_order = jnp.array(
        [
            [
                [offsets.index(r ^ own) for r in holders_of(masks)]
                for offsets, masks in (
                    (offsets_f, FEED_MASKS[0]),
                    (offsets_f, FEED_MASKS[1]),
                    (offsets_t, TAIL_MASKS),
                )
            ]
            for own in range(team)
        ],
        jnp.int32,
    )
    part_order = lax.dynamic_index_in_dim(part_order, own_row, 0, keepdims=False)
    down_total, up_total = spread_parts(
        part_order[:2], after(feed_held, held_a, held_b), feed_came
    )
    qkv_total, out_total = spread_tail(
        part_order[2], after(tail_held, held_a, held_b), tail_came, 3 * head_cols
    )
    qkv_total = qkv_total.reshape(3, head_cols, D).transpose(2, 0, 1)
    came_a, came_b = pair_rows(held_a, 1), pair_rows(held_b, 2)
    offsets_a = offsets_a + [x ^ 1 for x in offsets_a]
    offsets_b = offsets_b + [x ^ 2 for x in offsets_b]
    order = jnp.array(
        [[offsets.index(x) for x in range(team)] for offsets in (offsets_a, offsets_b)], jnp.int32
    )
    order = order[:, jnp.arange(team, dtype=jnp.int32) ^ own_row]
    kernel_total = assemble(order, [held_a, came_a], [held_b, came_b]).transpose(2, 0, 1)
    small = sum(
        jnp.sum(value[:, part_rows:].astype(F32), axis=0)
        for value in (held_a, came_a, held_b, came_b)
    )
    small = small.reshape(-1)[:small_size]
    sizes = [v.size for v in all_small + rows_small]
    ends = [sum(sizes[: i + 1]) for i in range(len(sizes))]
    cuts = [small[end - size : end] for size, end in zip(sizes, ends)]
    gain0_grad, bias0_grad, gain1_grad, bias1_grad, out_bias_grad = cuts[:5]
    gain2_grad, bias2_grad, down_bias_grad, conv_bias_grad, qv_grad, up_bias_grad = cuts[5:]
    return (
        block_out,
        frames_grad,
        kernel_total,
        conv_bias_grad,
        gain0_grad,
        bias0_grad,
        qkv_total,
        qv_grad.reshape(2, head_cols),
        out_total,
        out_bias_grad,
        gain1_grad,
        bias1_grad,
        up_total,
        up_bias_grad,
        down_total,
        down_bias_grad,
        gain2_grad,
        bias2_grad,
    )


def solution(mesh):
    return jax.shard_map(
        on_device,
        mesh=mesh,
        in_specs=(
            P(("rows", "tp"), None),
            P("rows", None),
            P(None, None, "tp"),
            P("tp"),
            P(),
            P(),
            P(None, None, "tp"),
            P(None, "tp"),
            P("tp", None),
            P(),
            P(),
            P(),
            P(None, "tp"),
            P("tp"),
            P("tp", None),
            P(),
            P(),
            P(),
            P(("rows", "tp"), None),
        ),
        out_specs=(
            P(("rows", "tp"), None),
            P(("rows", "tp"), None),
            P(None, None, "tp"),
            P("tp"),
            P(),
            P(),
            P(None, None, "tp"),
            P(None, "tp"),
            P("tp", None),
            P(),
            P(),
            P(),
            P(None, "tp"),
            P("tp"),
            P("tp", None),
            P(),
            P(),
            P(),
        ),
        check_vma=False,
    )
```
